32 devices in a mesh: dp: 8 (over y, x, core), mp: 4 (over z).
Axes of the slice: x: 2, y: 2, z: 4, core: 2. Of those that a mesh axis runs over, the one named last changes fastest.
Arguments:
- tokens: bfloat16 [2, 16, 944, 768], P(None, 'dp', 'mp'), may hold values from -6 to 6
- w_qkv: bfloat16 [3, 768, 768], P(None, 'dp', 'mp'), may hold values from -0.21875 to 0.21875
- w_up: bfloat16 [768, 3072], P('dp', 'mp'), may hold values from -0.21875 to 0.21875
- w_proj: bfloat16 [768, 768], P('mp', 'dp'), may hold values from -1.75 to 1.75
- w_down: bfloat16 [3072, 768], P('mp', 'dp'), may hold values from -0.109375 to 0.109375
- norm_gain: float32 [768], replicated, may hold values from 0.25 to 1.75
- query_gain: float32 [64], replicated, may hold values from 0.25 to 1.75
- key_gain: float32 [64], replicated, may hold values from 0.25 to 1.75
- image_ids: int32 [2, 16, 944], P(None, 'dp'), may hold values from 0 to 7, never falling along the last dimension, each value on 1 to 709 neighbouring positions
- cotangent: bfloat16 [2, 16, 944, 768], P(None, 'dp', 'mp'), may hold values from -6 to 6
Outputs:
- output: bfloat16 [2, 16, 944, 768], P(None, 'dp', 'mp')
- input_grad: float32 [2, 16, 944, 768], P(None, 'dp', 'mp')
- grad_qkv: float32 [3, 768, 768], P(None, 'dp', 'mp')
- grad_up: float32 [768, 3072], P('dp', 'mp')
- grad_proj: float32 [768, 768], P('mp', 'dp')
- grad_down: float32 [3072, 768], P('mp', 'dp')
- grad_norm_gain: float32 [768], replicated
- grad_query_gain: float32 [64], replicated
- grad_key_gain: float32 [64], replicated
The draws below stay inside these ranges and needn't reach their ends.
Inputs may be any that keep to these rules, and one draw needn't show every extreme that they name: `image_ids`: within each sequence the numbers never fall, start at 0 and rise by one from image to image; each image holds 1 to 709 tokens and one image of every sequence holds exactly 709.
All inputs are finite; a program needn't handle non-finite values.
Results may differ from the reference program's by a relative error of at most 0.011.
Values may be sent and summed in bfloat16 or wider, within the bound.
A program may use at most 320 MiB of HBM per device.

```python
import math
import jax
import jax.numpy as jnp
import numpy as np
from jax import lax

D = 768
H = 12
HD = 64
FF = 3072
L = 944
MICRO = 2
IMAGES = 8
MOST = 709
SEQUENCES = 16


def with_spikes(values, rng, source, target, shards_of, factor):
    def block_of(position):
        return (jnp.arange(values.shape[position]) // (values.shape[position] // shards_of)).reshape((-1,) + (1,) * (values.ndim - 1 - position))

    near = jax.random.permutation(rng, shards_of)[block_of(target)]
    other_side = (block_of(target) + shards_of // 2) % shards_of
    return jnp.where((block_of(source) == near) | (block_of(source) == other_side), factor * values, values)


def steps_of(rng, dims, shards, smallest, largest):
    loudness, own = 1.0, jax.random.fold_in(rng, 6)
    for position, blocks in shards:
        heights = jnp.exp(jax.random.uniform(jax.random.fold_in(own, position), (blocks,), jnp.float32, smallest / len(shards), largest / len(shards)))
        loudness = loudness * jnp.repeat(heights, dims[position] // blocks).reshape([-1 if axis == position else 1 for axis in range(len(dims))])
    return loudness


def length_profile(number_of, total, limit, slope):
    loads = [(1 << 20) // math.isqrt(standing ** slope) + 1 for standing in range(2, number_of + 1)]
    spare, given = total - limit - (number_of - 1), [1] * (number_of - 1)
    while spare > 0:
        free = [i for i in range(number_of - 1) if given[i] < limit]
        whole, remaining = sum([loads[i] for i in free]), spare
        for i in free:
            more = min(limit - given[i], max(1, remaining * loads[i] // whole), spare)
            given[i] = given[i] + more
            spare = spare - more
    return np.array([limit] + given)


def uneven(own_key, number_of, total, limit, slope):
    if number_of == 2:
        one = jax.random.randint(own_key, (), max(1, total - limit), min(limit, total - 1) + 1)
        return jnp.stack([one, total - one])
    tallies = jnp.asarray(length_profile(number_of, total, limit, slope), jnp.int32)
    pairs = (number_of - 1) // 2
    donor, taker = tallies[1:1 + 2 * pairs:2], tallies[2:2 + 2 * pairs:2]
    slack = jnp.minimum(donor - 1, limit - taker)
    shifted = jax.random.randint(jax.random.fold_in(own_key, 1), (pairs,), 0, 1 << 20) % (slack + 1)
    tallies = tallies.at[1:1 + 2 * pairs:2].set(donor - shifted).at[2:2 + 2 * pairs:2].set(taker + shifted)
    return tallies[jax.random.permutation(jax.random.fold_in(own_key, 2), number_of)]


def centred(own_key, extent, scale, bound, cuts=(), kind=jnp.bfloat16):
    values = jax.random.normal(own_key, extent, jnp.float32) * scale
    if len(cuts) > 0:
        values = steps_of(own_key, extent, cuts, -0.22, 0.18) * values
    return jnp.clip(values, min=-bound, max=bound).astype(kind)


def gaussian_with(rng, extent, scale, bound, cuts, heavy, dtype=jnp.bfloat16):
    entries = scale * jax.random.normal(rng, extent, jnp.float32)
    if cuts:
        entries = entries * steps_of(rng, extent, cuts, -0.22, 0.18)
    return jnp.clip(with_spikes(entries, jax.random.fold_in(rng, 3), *heavy), -bound, bound).astype(dtype)


def setup_inputs(seed: int = 0) -> dict:
    splits = jax.random.split(jax.random.key(seed), 11)
    tokens = gaussian_with(splits[0], (MICRO, SEQUENCES, L, D), 1.0, 6.0, ((1, 8), (2, 4)), (1, 3, 8, 2.0))
    w_qkv = centred(splits[1], (3, D, H * HD), D ** -0.5, 0.21875, ((1, 8), (2, 4)))
    w_up = centred(splits[2], (D, FF), D ** -0.5, 0.21875, ((0, 8), (1, 4)))
    w_proj = centred(splits[3], (H * HD, D), (max(H * HD // 64, 1)) ** -0.5, 1.75, ((0, 4), (1, 8)))
    w_down = centred(splits[4], (FF, D), FF ** -0.5, 0.109375, ((0, 4), (1, 8)))
    norm_gain = jnp.clip(1.0 + 0.15 * jax.random.normal(splits[5], (D,), jnp.float32), 0.25, 1.75)
    query_gain = jnp.clip(1.0 + 0.15 * jax.random.normal(splits[6], (HD,), jnp.float32), 0.25, 1.75)
    key_gain = jnp.clip(1.0 + 0.15 * jax.random.normal(splits[7], (HD,), jnp.float32), 0.25, 1.75)
    image_ids = jax.vmap(lambda own: jnp.searchsorted(jnp.cumsum(uneven(own, IMAGES, L, MOST, 0)), jnp.arange(L), side="right"))(jax.random.split(splits[8], MICRO * SEQUENCES)).reshape((MICRO, SEQUENCES, L)).astype(jnp.int32)
    cotangent = gaussian_with(splits[9], (MICRO, SEQUENCES, L, D), 1.0, 6.0, ((1, 8), (2, 4)), (1, 3, 8, 2.0))
    return dict(tokens=tokens, w_qkv=w_qkv, w_up=w_up, w_proj=w_proj, w_down=w_down, norm_gain=norm_gain, query_gain=query_gain, key_gain=key_gain, image_ids=image_ids, cotangent=cotangent)


@jax.custom_vjp
def low(v):
    return lax.optimization_barrier(v.astype(jnp.bfloat16)).astype(jnp.float32)

@jax.custom_vjp
def low_back(v):
    return v

def low_keep(v):
    return (low(v), None)

def low_pass(kept, grad):
    return (grad,)

def back_keep(v):
    return (v, None)

def back_low(kept, grad):
    return (low(grad),)
low.defvjp(low_keep, low_pass)
low_back.defvjp(back_keep, back_low)
precise = lax.Precision.HIGHEST

def norm_rows(values, gain):
    centered = values - lax.optimization_barrier(jnp.mean(values, axis=-1, keepdims=True))
    spread = lax.rsqrt(lax.optimization_barrier(jnp.mean(centered * centered, axis=-1, keepdims=True)) + 1e-06)
    return centered * spread * gain

def block_forward(token_rows, image_rows, w_qkv, w_up, w_proj, w_down, norm_gain, query_gain, key_gain):
    seq_count = token_rows.shape[0]
    flat_rows = token_rows.reshape(seq_count * L, D)
    normed = low(norm_rows(flat_rows, norm_gain))
    projected = jnp.einsum('rd,cdh->crh', normed, w_qkv, precision=precise)
    query_heads = low(norm_rows(low_back(projected[0]).reshape(seq_count, L, H, HD), query_gain))
    key_heads = low(norm_rows(low_back(projected[1]).reshape(seq_count, L, H, HD), key_gain))
    value_heads = low(low_back(projected[2])).reshape(seq_count, L, H, HD)
    scores = jnp.einsum('sqhd,skhd->shqk', query_heads, key_heads, precision=precise) * HD ** (-0.5)
    same_image = image_rows[:, None, :, None] == image_rows[:, None, None, :]
    scores = low_back(jnp.where(same_image, scores, -1e+30))
    attn_probs = low(jax.nn.softmax(scores, axis=-1))
    attended = jnp.einsum('shqk,skhd->sqhd', attn_probs, value_heads, precision=precise)
    attended = low(low_back(attended.reshape(seq_count * L, H * HD)))
    upper_proj = low_back(jnp.dot(normed, w_up, precision=precise))
    hidden = low(jax.nn.gelu(upper_proj, approximate=True))
    branch = jnp.dot(attended, w_proj, precision=precise) + jnp.dot(hidden, w_down, precision=precise)
    return (flat_rows + branch).reshape(seq_count, L, D)

def reference(tokens, w_qkv, w_up, w_proj, w_down, norm_gain, query_gain, key_gain, image_ids, cotangent):
    weights = tuple((array.astype(jnp.float32) for array in (w_qkv, w_up, w_proj, w_down, norm_gain, query_gain, key_gain)))
    token_blocks = tokens.astype(jnp.float32).reshape(-1, 2, L, D)
    image_blocks = image_ids.reshape(-1, 2, L)

    def forward(token_blocks, *weights):

        def one_block(packed):
            return block_forward(packed[0], packed[1], *weights)
        return lax.map(jax.checkpoint(one_block), (token_blocks, image_blocks))
    result, back = jax.vjp(forward, token_blocks, *weights)
    grads = back(cotangent.astype(jnp.float32).reshape(-1, 2, L, D))
    output = result.reshape(tokens.shape).astype(jnp.bfloat16)
    input_grad = grads[0].reshape(tokens.shape)
    return (output, input_grad, grads[1], grads[2], grads[3], grads[4], grads[5], grads[6], grads[7])
```

```python
import functools

import jax
import jax.numpy as jnp
from jax import lax
from jax.experimental import pallas as pl
from jax.experimental.pallas import tpu as pltpu
from jax.sharding import PartitionSpec as P

HD = 64
MOST = 709
IMAGES = 8
PIECE = 240
BIG = 768
REST = 256
ROWS = BIG + REST
VMEM = 60 * 1024 * 1024
F32 = jnp.float32
BF16 = jnp.bfloat16


def nn(left, right):
    return lax.dot_general(left, right, (((1,), (0,)), ((), ())), preferred_element_type=F32)


def nt(left, right):
    return lax.dot_general(left, right, (((1,), (1,)), ((), ())), preferred_element_type=F32)


def norm_kernel(place, tok, cot, gain, normed, grads, send1, send2, send3):
    step = pl.program_id(0)
    part = tok.shape[1]
    x = tok[0].astype(F32)
    centered = x - jnp.mean(x, axis=-1, keepdims=True)
    spread = lax.rsqrt(jnp.mean(centered * centered, axis=-1, keepdims=True) + 1e-6)
    value = (centered * spread * gain[...]).astype(BF16)
    normed[...] = jnp.zeros_like(normed)
    grads[...] = jnp.zeros_like(grads)
    normed[0, :part] = value
    grads[0, :part] = cot[0]
    for index, send in ((1, send1), (2, send2), (3, send3)):

        @pl.when(step == index)
        def _():
            send[0] = normed[0]
            send[1] = grads[0]


def norm_call(place, tokens, cotangent, gain):
    count, part, width = tokens.shape
    block = lambda k, place: (lax.rem(place[0] + k, count), 0, 0)
    fixed = lambda k, place: (0, 0, 0)
    return pl.pallas_call(
        norm_kernel,
        grid_spec=pltpu.PrefetchScalarGridSpec(
            num_scalar_prefetch=1,
            grid=(count,),
            in_specs=[
                pl.BlockSpec((1, part, width), block),
                pl.BlockSpec((1, part, width), block),
                pl.BlockSpec((1, width), lambda k, place: (0, 0)),
            ],
            out_specs=[pl.BlockSpec((1, PIECE, width), lambda k, place: (k, 0, 0))] * 2
            + [pl.BlockSpec((2, PIECE, width), fixed)] * 3,
        ),
        out_shape=[jax.ShapeDtypeStruct((count, PIECE, width), BF16)] * 2
        + [jax.ShapeDtypeStruct((2, PIECE, width), BF16)] * 3,
        compiler_params=pltpu.CompilerParams(vmem_limit_bytes=VMEM),
        name="norm_rows",
    )(place, tokens, cotangent, gain)


def feed_kernel(normed, grads, w_up, w_down, branch, d_normed, g_up, g_down, xt, dt):
    step = pl.program_id(0)
    x = normed[...]
    dy = grads[...]

    @pl.when(step == 0)
    def _():
        xt[...] = x.T
        dt[...] = dy.T

    up = nn(x, w_up[0])
    inner = 0.7978845608028654 * (up + 0.044715 * up * up * up)
    th = jnp.tanh(inner)
    half = 0.5 * (1.0 + th)
    hidden = (up * half).astype(BF16)
    slope = half + 0.5 * up * (1.0 - th * th) * (
        0.7978845608028654 * (1.0 + 3 * 0.044715 * up * up)
    )
    d_up = (nn(dy, w_down[0]) * slope).astype(BF16)
    g_up[0] = nn(xt[...], d_up).astype(BF16)
    g_down[0] = nn(dt[...], hidden).astype(BF16)
    out = nt(hidden, w_down[0])
    back = nt(d_up, w_up[0])

    @pl.when(step == 0)
    def _():
        branch[...] = out
        d_normed[...] = back

    @pl.when(step > 0)
    def _():
        branch[...] += out
        d_normed[...] += back


def feed_call(normed, grads, w_up, w_down):
    rows, width = normed.shape
    chunks, _, hidden = w_up.shape
    whole = pl.BlockSpec((rows, width), lambda m: (0, 0))
    chunk = pl.BlockSpec((1, width, hidden), lambda m: (m, 0, 0))
    return pl.pallas_call(
        feed_kernel,
        grid=(chunks,),
        in_specs=[whole, whole, chunk, chunk],
        out_specs=[whole, whole, chunk, chunk],
        out_shape=[jax.ShapeDtypeStruct((rows, width), F32)] * 2
        + [jax.ShapeDtypeStruct(w_up.shape, BF16)] * 2,
        scratch_shapes=[pltpu.VMEM((width, rows), BF16)] * 2,
        compiler_params=pltpu.CompilerParams(vmem_limit_bytes=VMEM),
        cost_estimate=pl.CostEstimate(
            flops=12 * rows * width * hidden * chunks,
            bytes_accessed=4 * chunks * width * hidden * 2,
            transcendentals=rows * hidden * chunks,
        ),
        name="feed_forward",
    )(normed, grads, w_up, w_down)


def iota(shape, axis):
    return lax.broadcasted_iota(jnp.int32, shape, axis)


def source_of(index, start, total):
    rest = index - BIG
    other = jnp.where(rest < start, rest, rest + MOST)
    held = jnp.where(index < MOST, start + index, -1)
    return jnp.where((rest >= 0) & (rest < total - MOST), other, held)


def attention_kernel(
    part, place, own_x, own_dy, in1, in2, in3, ids, gains, weights,
    out0, out1, out2, out3, g_weights, g_gains,
    x_ref, dy_ref, xt, dt, feat_q, feat_k, pt, raw, d_raw, d_att, att, d_normed, branch,
):
    step = pl.program_id(0)
    mp = ids.shape[1]
    total = mp * part
    me = place[0]
    lane = iota((1, 128), 1)

    @pl.when(step == 0)
    def _():
        numbers = ids[0]
        start = jnp.zeros((1, 1), jnp.int32)
        for image in range(IMAGES):
            count = jnp.sum(
                (numbers == image).astype(F32), axis=(0, 1), keepdims=True
            )
            ahead = jnp.sum(
                ((numbers >= 0) & (numbers < image)).astype(F32), axis=(0, 1), keepdims=True
            )
            start = start + jnp.where(count == MOST, ahead, 0.0).astype(jnp.int32)
        column = source_of(iota((ROWS, 1), 0), start, total)
        line = source_of(iota((1, ROWS), 1), start, total)
        x_sum, dy_sum, feats = 0.0, 0.0, 0.0
        pieces = ((own_x, own_dy), (in1,), (in2,), (in3,))
        for k, piece in enumerate(pieces):
            chunk = lax.rem(me - k + mp, mp)
            offset = iota((1, PIECE), 1)
            pos = jnp.where(offset < part, chunk * part + offset, -2)
            pick = (column == pos).astype(F32).astype(BF16)
            offset = iota((PIECE, 1), 0)
            pos = jnp.where(offset < part, chunk * part + offset, -2)
            pt[k] = (line == pos).astype(F32).astype(BF16)
            x_piece = piece[0][0]
            dy_piece = piece[1][0] if k == 0 else piece[0][1]
            x_sum = x_sum + nn(pick, x_piece)
            dy_sum = dy_sum + nn(pick, dy_piece)
            marks = (iota((128, 1), 0) - HD == ids[0, pl.ds(chunk, 1), :]).astype(F32)
            feats = feats + nt(pick, marks.astype(BF16))
        x = x_sum.astype(BF16)
        dy = dy_sum.astype(BF16)
        x_ref[...] = x
        dy_ref[...] = dy
        xt[...] = x.T
        dt[...] = dy.T
        feat_q[...] = (feats * 128.0).astype(BF16)
        marked = (lane >= HD) & (lane < HD + IMAGES)
        feat_k[...] = jnp.where(marked, (feats - 1.0) * 256.0, 0.0).astype(BF16)
        d_normed[...] = jnp.zeros_like(d_normed)
        branch[...] = jnp.zeros_like(branch)
        g_gains[...] = jnp.zeros_like(g_gains)

    raw[...] = nn(x_ref[...], weights[0, :, :640])
    d_att[...] = nn(dy_ref[...], weights[0, :, 512:])
    low = lane < HD
    same = (iota((128, 128), 0) // HD == iota((128, 128), 1) // HD).astype(F32)
    mean_of = (same * (1.0 / HD)).astype(BF16)
    gain = gains[...]

    def half_mean(value):
        return nn(value.astype(BF16), mean_of)

    d_gain = jnp.zeros((1, 128), F32)
    for head in range(3):
        qk = raw[:, 128 * head:128 * head + 128]
        high = qk.astype(BF16)
        mean = nn(high, mean_of) + half_mean(qk - high.astype(F32))
        centered = qk - mean
        spread = lax.rsqrt(half_mean(centered * centered) + 1e-6)
        unit = centered * spread
        rounded = (unit * gain).astype(BF16).astype(F32)
        q_aug = jnp.where(low, rounded * 0.125, feat_q[...].astype(F32)).astype(BF16)
        k_aug = jnp.where(low, pltpu.roll(rounded, HD, 1), feat_k[...].astype(F32)).astype(BF16)
        v_tile = 384 + 128 * (head // 2)
        v = raw[:, v_tile:v_tile + 128]
        if head == 1:
            v = pltpu.roll(v, HD, 1)
        one = ((lane == HD) | (lane == HD + 1)).astype(F32)
        v_aug = jnp.where(low, v, one).astype(BF16)
        a_tile = 128 * ((head + 1) // 2)
        da = d_att[:, a_tile:a_tile + 128]
        if head != 1:
            da = pltpu.roll(da, HD, 1)
        q_t = q_aug.astype(F32).T.astype(BF16)
        d_queries, attended, d_keys, d_values = [], [], [], []
        for base, count in ((0, BIG), (BIG, REST)):
            keys = k_aug[base:base + count]
            values = v_aug[base:base + count]
            dk_t = jnp.zeros((128, count), F32)
            dv_t = jnp.zeros((128, count), F32)
            for row in range(base, base + count, 256):
                rows = slice(row, row + 256)
                prob = jnp.exp(nt(q_aug[rows], keys))
                prob_low = prob.astype(BF16)
                gathered = nn(prob_low, values)
                inverse = 1.0 / gathered[:, HD:HD + 1]
                out = jnp.where(low, gathered * inverse, 0.0)
                attended.append(out)
                scaled = jnp.where(low, da[rows] * inverse, 0.0).astype(BF16).astype(F32)
                dot = jnp.sum(scaled * out, axis=-1, keepdims=True)
                dot_high = dot.astype(BF16).astype(F32)
                d_aug = jnp.where(
                    lane == HD, -dot_high, jnp.where(lane == HD + 1, dot_high - dot, scaled)
                )
                d_low = d_aug.astype(BF16)
                d_score = (prob * nt(d_low, values)).astype(BF16)
                d_queries.append(nn(d_score, keys))
                dk_t = dk_t + nn(q_t[:, rows], d_score)
                dv_t = dv_t + nn(d_aug.T.astype(BF16), prob_low)
            d_keys.append(dk_t.T)
            d_values.append(dv_t.T)
        d_query = jnp.concatenate(d_queries, axis=0) * 0.125
        d_key = jnp.concatenate(d_keys, axis=0)
        d_value = jnp.concatenate(d_values, axis=0)
        attend = jnp.concatenate(attended, axis=0)
        d_qk = jnp.where(low, d_query, pltpu.roll(d_key, HD, 1))
        d_gain = d_gain + jnp.sum(d_qk * unit, axis=0, keepdims=True)
        scaled = d_qk * gain
        d_qk = spread * (scaled - half_mean(scaled) - unit * half_mean(scaled * unit))
        d_raw[:, 128 * head:128 * head + 128] = d_qk.astype(BF16)
        if head == 0:
            first_value = d_value
            att[:, 0:128] = jnp.where(low, 0.0, pltpu.roll(attend, HD, 1)).astype(BF16)
        elif head == 1:
            both = jnp.where(low, first_value, pltpu.roll(d_value, HD, 1))
            d_raw[:, 384:512] = both.astype(BF16)
            first_att = attend
        else:
            d_raw[:, 512:640] = jnp.where(low, d_value, 0.0).astype(BF16)
            both = jnp.where(low, first_att, pltpu.roll(attend, HD, 1))
            att[:, 128:256] = both.astype(BF16)
    g_gains[...] += d_gain
    d_projected = d_raw[...]
    attended = att[...]
    d_normed[...] += nt(d_projected, weights[0, :, :640])
    branch[...] += nt(attended, weights[0, :, 512:])
    left = nn(xt[...], d_projected)
    right = nn(dt[...], attended)
    g_weights[0, :, :512] = left[:, :512].astype(BF16)
    g_weights[0, :, 512:640] = (left[:, 512:] + right[:, :128]).astype(BF16)
    g_weights[0, :, 640:] = right[:, 128:].astype(BF16)

    @pl.when(step == pl.num_programs(0) - 1)
    def _():
        d_rows = d_normed[...].astype(BF16)
        b_rows = branch[...].astype(BF16)
        for k, out in enumerate((out0, out1, out2, out3)):
            out[0] = nn(pt[k], d_rows).astype(BF16)
            out[1] = nn(pt[k], b_rows).astype(BF16)


def attention_call(place, part, normed, grads, received, ids, gains, weights):
    width = normed.shape[-1]
    chunks = weights.shape[0]
    mp = ids.shape[1]
    own = pl.BlockSpec((1, PIECE, width), lambda m, place: (0, 0, 0))
    pair = pl.BlockSpec((2, PIECE, width), lambda m, place: (0, 0, 0))
    chunk = pl.BlockSpec((1, width, width), lambda m, place: (m, 0, 0))
    line = pl.BlockSpec((1, 128), lambda m, place: (0, 0))
    return pl.pallas_call(
        functools.partial(attention_kernel, part),
        grid_spec=pltpu.PrefetchScalarGridSpec(
            num_scalar_prefetch=1,
            grid=(chunks,),
            in_specs=[own, own, pair, pair, pair,
                      pl.BlockSpec((1, mp, PIECE), lambda m, place: (place[0], 0, 0)),
                      line, chunk],
            out_specs=[pair] * 4 + [chunk, line],
            scratch_shapes=[
                pltpu.VMEM((ROWS, width), BF16),
                pltpu.VMEM((ROWS, width), BF16),
                pltpu.VMEM((width, ROWS), BF16),
                pltpu.VMEM((width, ROWS), BF16),
                pltpu.VMEM((ROWS, 128), BF16),
                pltpu.VMEM((ROWS, 128), BF16),
                pltpu.VMEM((mp, PIECE, ROWS), BF16),
                pltpu.VMEM((ROWS, 640), F32),
                pltpu.VMEM((ROWS, 640), BF16),
                pltpu.VMEM((ROWS, 256), F32),
                pltpu.VMEM((ROWS, 256), BF16),
                pltpu.VMEM((ROWS, width), F32),
                pltpu.VMEM((ROWS, width), F32),
            ],
        ),
        out_shape=[jax.ShapeDtypeStruct((2, PIECE, width), BF16)] * 4
        + [jax.ShapeDtypeStruct(weights.shape, BF16), jax.ShapeDtypeStruct((1, 128), F32)],
        compiler_params=pltpu.CompilerParams(vmem_limit_bytes=VMEM),
        cost_estimate=pl.CostEstimate(
            flops=60_000_000_000, bytes_accessed=4 * chunks * width * width,
            transcendentals=ROWS * ROWS * 12,
        ),
        name="attention",
    )(place, normed, grads, *received, ids, gains, weights)


def finish_kernel(
    place, tok, cot, gain, branch, d_ff, ret0, ret1, ret2, ret3, output, input_grad, g_gain
):
    step = pl.program_id(0)
    part = tok.shape[1]

    @pl.when(step == 0)
    def _():
        g_gain[...] = jnp.zeros_like(g_gain)

    for index, back in enumerate((ret0, ret1, ret2, ret3)):

        @pl.when(step == index)
        def _():
            x = tok[0].astype(F32)
            output[0] = (x + (branch[0] + back[1].astype(F32))[:part]).astype(BF16)
            d_normed = (d_ff[0] + back[0].astype(F32))[:part]
            centered = x - jnp.mean(x, axis=-1, keepdims=True)
            spread = lax.rsqrt(jnp.mean(centered * centered, axis=-1, keepdims=True) + 1e-6)
            unit = centered * spread
            g_gain[...] += jnp.sum(d_normed * unit, axis=0, keepdims=True)
            scaled = d_normed * gain[...]
            d_x = spread * (
                scaled
                - jnp.mean(scaled, axis=-1, keepdims=True)
                - unit * jnp.mean(scaled * unit, axis=-1, keepdims=True)
            )
            input_grad[0] = cot[0].astype(F32) + d_x


def finish_call(place, tokens, cotangent, gain, branch, d_ff, returned):
    count, part, width = tokens.shape
    block = pl.BlockSpec(
        (1, part, width), lambda k, place: (lax.rem(place[0] + k, count), 0, 0)
    )
    padded = pl.BlockSpec((1, PIECE, width), lambda k, place: (k, 0, 0))
    pair = pl.BlockSpec((2, PIECE, width), lambda k, place: (0, 0, 0))
    line = pl.BlockSpec((1, width), lambda k, place: (0, 0))
    return pl.pallas_call(
        finish_kernel,
        grid_spec=pltpu.PrefetchScalarGridSpec(
            num_scalar_prefetch=1,
            grid=(count,),
            in_specs=[block, block, line, padded, padded] + [pair] * 4,
            out_specs=[block, block, line],
        ),
        out_shape=[
            jax.ShapeDtypeStruct(tokens.shape, BF16),
            jax.ShapeDtypeStruct(tokens.shape, F32),
            jax.ShapeDtypeStruct((1, width), F32),
        ],
        compiler_params=pltpu.CompilerParams(vmem_limit_bytes=VMEM),
        name="finish",
    )(place, tokens, cotangent, gain, branch, d_ff, *returned)


def pack_attention(w_qkv, w_proj):
    rows, wide = w_qkv.shape[1:]
    heads = wide // HD
    qk = w_qkv[:2].reshape(2, rows, heads, HD).transpose(1, 2, 0, 3).reshape(rows, 2 * wide)
    return jnp.concatenate([qk, w_qkv[2], w_proj.T], axis=1)


def unpack_attention(grad, wide):
    rows = grad.shape[0]
    heads = wide // HD
    qk = grad[:, :2 * wide].reshape(rows, heads, 2, HD).transpose(2, 0, 1, 3)
    qk = qk.reshape(2, rows, wide)
    g_qkv = jnp.concatenate([qk, grad[None, :, 2 * wide:3 * wide]], axis=0)
    return g_qkv, grad[:, 3 * wide:].T


def body(
    mp, tokens, w_qkv, w_up, w_proj, w_down, norm_gain, query_gain, key_gain, image_ids, cotangent
):
    micro, seqs, part, width = tokens.shape
    count = micro * seqs
    shard = w_up.shape[0]
    me = lax.axis_index("mp")
    place = me.astype(jnp.int32)[None]
    both = ("mp", "dp")
    w_attn = lax.all_gather(pack_attention(w_qkv, w_proj), both).reshape(mp, width, width)
    w_ff = lax.all_gather(jnp.stack([w_up, w_down.T]), both)
    w_ff = w_ff.reshape(mp, -1, 2, shard, width)
    w_upper = w_ff[:, :, 0].reshape(mp, width, width)
    w_lower = w_ff[:, :, 1].reshape(mp, width, width)

    tok = tokens.reshape(count, part, width)
    cot = cotangent.reshape(count, part, width)
    gain = norm_gain.reshape(1, width)
    normed, grads, *sends = norm_call(place, tok, cot, gain)
    received = [
        lax.ppermute(send, "mp", [(i, (i + k) % mp) for i in range(mp)])
        for k, send in enumerate(sends, 1)
    ]
    ids = image_ids.reshape(count, mp, part)
    ids = jnp.pad(ids, ((0, 0), (0, 0), (0, PIECE - part)), constant_values=-1)
    gains = jnp.concatenate([query_gain, key_gain]).reshape(1, 2 * HD)
    *outs, g_attn, g_gains = attention_call(
        place, part, normed, grads, received, ids, gains, w_attn
    )
    returned = [outs[0]] + [
        lax.ppermute(out, "mp", [(i, (i - k) % mp) for i in range(mp)])
        for k, out in enumerate(outs[1:], 1)
    ]
    branch, d_ff, g_up, g_down = feed_call(
        normed.reshape(count * PIECE, width), grads.reshape(count * PIECE, width), w_upper, w_lower
    )
    output, input_grad, g_norm = finish_call(
        place, tok, cot, gain,
        branch.reshape(count, PIECE, width), d_ff.reshape(count, PIECE, width), returned,
    )

    def scatter(grad):
        grad = grad.reshape(-1, shard, width)
        return lax.psum_scatter(grad, both, scatter_dimension=0).astype(F32)

    g_attn, g_up, g_down = scatter(g_attn), scatter(g_up), scatter(g_down)
    g_qkv, g_proj = unpack_attention(g_attn, w_qkv.shape[2])
    g_norm, g_gains = lax.psum((g_norm[0], g_gains[0]), ("dp", "mp"))
    return (
        output.reshape(tokens.shape),
        input_grad.reshape(tokens.shape),
        g_qkv,
        g_up,
        g_proj,
        g_down.T,
        g_norm,
        g_gains[:HD],
        g_gains[HD:],
    )


def solution(mesh):
    rows = P(None, "dp", "mp", None)
    weights = (P(None, "dp", "mp"), P("dp", "mp"), P("mp", "dp"), P("mp", "dp"))
    gains = (P(), P(), P())
    return jax.shard_map(
        functools.partial(body, mesh.shape["mp"]),
        mesh=mesh,
        in_specs=(rows,) + weights + gains + (P(None, "dp", None), rows),
        out_specs=(rows, rows) + weights + gains,
        check_vma=False,
    )
```

```python
import functools

import jax
import jax.numpy as jnp
from jax import lax
from jax.experimental import pallas as pl
from jax.experimental.pallas import tpu as pltpu
from jax.sharding import PartitionSpec as P

HD = 64
MOST = 709
IMAGES = 8
PIECE = 240
BIG = 768
REST = 256
ROWS = BIG + REST
VMEM = 60 * 1024 * 1024
F32 = jnp.float32
BF16 = jnp.bfloat16


def nn(left, right):
    return lax.dot_general(left, right, (((1,), (0,)), ((), ())), preferred_element_type=F32)


def nt(left, right):
    return lax.dot_general(left, right, (((1,), (1,)), ((), ())), preferred_element_type=F32)


def norm_kernel(place, tok, cot, gain, normed, grads, send1, send2, send3):
    step = pl.program_id(0)
    part = tok.shape[1]
    x = tok[0].astype(F32)
    centered = x - jnp.mean(x, axis=-1, keepdims=True)
    spread = lax.rsqrt(jnp.mean(centered * centered, axis=-1, keepdims=True) + 1e-6)
    value = (centered * spread * gain[...]).astype(BF16)
    normed[...] = jnp.zeros_like(normed)
    grads[...] = jnp.zeros_like(grads)
    normed[0, :part] = value
    grads[0, :part] = cot[0]
    for index, send in ((1, send1), (2, send2), (3, send3)):

        @pl.when(step == index)
        def _():
            send[0] = normed[0]
            send[1] = grads[0]


def norm_call(place, tokens, cotangent, gain):
    count, part, width = tokens.shape
    block = lambda k, place: (lax.rem(place[0] + k, count), 0, 0)
    fixed = lambda k, place: (0, 0, 0)
    return pl.pallas_call(
        norm_kernel,
        grid_spec=pltpu.PrefetchScalarGridSpec(
            num_scalar_prefetch=1,
            grid=(count,),
            in_specs=[
                pl.BlockSpec((1, part, width), block),
                pl.BlockSpec((1, part, width), block),
                pl.BlockSpec((1, width), lambda k, place: (0, 0)),
            ],
            out_specs=[pl.BlockSpec((1, PIECE, width), lambda k, place: (k, 0, 0))] * 2
            + [pl.BlockSpec((2, PIECE, width), fixed)] * 3,
        ),
        out_shape=[jax.ShapeDtypeStruct((count, PIECE, width), BF16)] * 2
        + [jax.ShapeDtypeStruct((2, PIECE, width), BF16)] * 3,
        compiler_params=pltpu.CompilerParams(vmem_limit_bytes=VMEM),
        name="norm_rows",
    )(place, tokens, cotangent, gain)


def feed_kernel(normed, grads, w_up, w_down, branch, d_normed, g_up, g_down, xt, dt):
    step = pl.program_id(0)
    x = normed[...]
    dy = grads[...]

    @pl.when(step == 0)
    def _():
        xt[...] = x.T
        dt[...] = dy.T

    up = nn(x, w_up[0])
    value, slope = gelu_parts(up)
    hidden = value.astype(BF16)
    d_up = (nn(dy, w_down[0]) * slope).astype(BF16)
    g_up[0] = nn(xt[...], d_up).astype(BF16)
    g_down[0] = nn(dt[...], hidden).astype(BF16)
    out = nt(hidden, w_down[0])
    back = nt(d_up, w_up[0])

    @pl.when(step == 0)
    def _():
        branch[...] = out
        d_normed[...] = back

    @pl.when(step > 0)
    def _():
        branch[...] += out
        d_normed[...] += back


def feed_call(normed, grads, w_up, w_down):
    rows, width = normed.shape
    chunks, _, hidden = w_up.shape
    whole = pl.BlockSpec((rows, width), lambda m: (0, 0))
    chunk = pl.BlockSpec((1, width, hidden), lambda m: (m, 0, 0))
    return pl.pallas_call(
        feed_kernel,
        grid=(chunks,),
        in_specs=[whole, whole, chunk, chunk],
        out_specs=[whole, whole, chunk, chunk],
        out_shape=[jax.ShapeDtypeStruct((rows, width), F32)] * 2
        + [jax.ShapeDtypeStruct(w_up.shape, BF16)] * 2,
        scratch_shapes=[pltpu.VMEM((width, rows), BF16)] * 2,
        compiler_params=pltpu.CompilerParams(vmem_limit_bytes=VMEM),
        cost_estimate=pl.CostEstimate(
            flops=12 * rows * width * hidden * chunks,
            bytes_accessed=4 * chunks * width * hidden * 2,
            transcendentals=rows * hidden * chunks,
        ),
        name="feed_forward",
    )(normed, grads, w_up, w_down)


def gelu_parts(up):
    inner = 0.7978845608028654 * (up + 0.044715 * up * up * up)
    th = jnp.tanh(inner)
    half = 0.5 * (1.0 + th)
    slope = half + 0.5 * up * (1.0 - th * th) * (
        0.7978845608028654 * (1.0 + 3 * 0.044715 * up * up)
    )
    return up * half, slope


def feed_remote_kernel(
    x_ref, dy_ref, w_hbm, g_attn, gain, gains_in,
    branch, d_normed, out_attn, out_up, out_down, out_gains,
    xt, dt, w_buf, g_ff, got_core, got_first, got_second, got_z, sums, got_sums, z_sums,
    w_sem, send_sem, recv_sem, z_send, z_recv, sum_send, sum_recv,
):
    width = x_ref.shape[1]
    steps, shard = w_hbm.shape[0], w_hbm.shape[3]
    d = lax.axis_index("dp")
    z = lax.axis_index("mp")
    core, x, y = d % 2, (d // 2) % 2, d // 4
    sibling, beside, above = d + 1 - 2 * core, d + 2 - 4 * x, d + 4 - 8 * y
    half = width // 2
    items = ((0, slice(0, half), True), (0, slice(half, width), False),
             (1, slice(0, width), True), (2, slice(0, width), False))

    def part_of(step):
        return lax.rem(z + 1 + step, steps)

    barrier = pltpu.get_barrier_semaphore()
    for other in (sibling, beside, above):
        pl.semaphore_signal(barrier, 1, device_id={"dp": other, "mp": z},
                            device_id_type=pl.DeviceIdType.MESH)
    for k in range(1, steps):
        pl.semaphore_signal(barrier, 1, device_id={"dp": d, "mp": lax.rem(z + k, steps)},
                            device_id_type=pl.DeviceIdType.MESH)
    pl.semaphore_wait(barrier, steps + 2)

    def remote(src, dst, send, recv, dp_to, z_to):
        return pltpu.make_async_remote_copy(
            src_ref=src, dst_ref=dst, send_sem=send, recv_sem=recv,
            device_id={"dp": dp_to, "mp": z_to}, device_id_type=pl.DeviceIdType.MESH,
        )

    def core_copy(step, item):
        kind, cols, _ = items[item]
        if kind == 0:
            src = g_attn.at[part_of(step), :, :, 1 - core, :, cols]
        else:
            src = g_ff.at[step, kind - 1, :, :, 1 - core, :, cols]
        dst = got_core.at[step, kind, :, :, :, cols]
        sem = (0, item, step)
        return remote(src, dst, send_sem.at[sem], recv_sem.at[sem], sibling, z)

    def first_copy(step, item):
        kind, cols, x_first = items[item]
        dst = got_first.at[step, kind, :, :, cols]
        sem = (1, item, step)
        if x_first:
            src = got_core.at[step, kind, :, 1 - x, :, cols]
        else:
            src = got_core.at[step, kind, 1 - y, :, :, cols]
        return remote(src, dst, send_sem.at[sem], recv_sem.at[sem], beside if x_first else above, z)

    def second_copy(step, item):
        kind, cols, x_first = items[item]
        src = got_first.at[step, kind, 1 - y if x_first else 1 - x, :, cols]
        dst = got_second.at[step, kind, :, cols]
        sem = (2, item, step)
        return remote(src, dst, send_sem.at[sem], recv_sem.at[sem], above if x_first else beside, z)

    def z_copy(step, kind):
        return remote(got_second.at[step, kind], got_z.at[kind, step],
                      z_send.at[kind, step], z_recv.at[kind, step], d, part_of(step))

    def after_core(step, chosen):
        for item in chosen:
            kind, cols, _ = items[item]
            core_copy(step, item).wait_recv()
            for row in ((0, 0), (0, 1), (1, 0), (1, 1)):
                if kind == 0:
                    own = g_attn[(part_of(step), *row, core, slice(None), cols)]
                else:
                    own = g_ff[(step, kind - 1, *row, core, slice(None), cols)]
                place = (step, kind, *row, slice(None), cols)
                got_core[place] = (own.astype(F32) + got_core[place].astype(F32)).astype(BF16)
            first_copy(step, item).start()

    def after_first(step, chosen):
        for item in chosen:
            kind, cols, x_first = items[item]
            first_copy(step, item).wait_recv()
            for row in range(2):
                if x_first:
                    own = got_core[step, kind, row, x, :, cols]
                else:
                    own = got_core[step, kind, y, row, :, cols]
                total = own.astype(F32) + got_first[step, kind, row, :, cols].astype(F32)
                got_first[step, kind, row, :, cols] = total.astype(BF16)
            second_copy(step, item).start()

    def second_sum(step, item):
        kind, cols, x_first = items[item]
        second_copy(step, item).wait_recv()
        own = got_first[step, kind, y if x_first else x, :, cols]
        return own.astype(F32) + got_second[step, kind, :, cols].astype(F32)

    def after_second(step, chosen):
        for item in chosen:
            kind, cols, _ = items[item]
            got_second[step, kind, :, cols] = second_sum(step, item).astype(BF16)
        for kind in sorted({items[item][0] for item in chosen}):
            z_copy(step, kind).start()

    def finish_sum(chosen, out):
        step = steps - 1
        for item in chosen:
            kind, cols, _ = items[item]
            total = second_sum(step, item)
            for slot in range(steps - 1):
                total = total + got_z[kind, slot, :, cols].astype(F32)
            out[:, cols] = total

    def w_copy(step, kind):
        slot = lax.rem(step, 2)
        return pltpu.make_async_copy(
            w_hbm.at[part_of(step), :, kind], w_buf.at[slot, kind], w_sem.at[slot, kind]
        )

    def feed_half(step, index):
        cols = slice(half * index, half * index + half)
        slot = lax.rem(step, 2)
        upper = w_buf[slot, 0, :, :, cols].reshape(width, half)
        lower = w_buf[slot, 1, :, :, cols].reshape(width, half)
        value, slope = gelu_parts(nn(x_ref[...], upper))
        hidden = value.astype(BF16)
        d_up = (nn(dy_ref[...], lower) * slope).astype(BF16)
        split = (2, 2, 2, shard, half)
        g_ff[step, 0, :, :, :, :, cols] = nn(xt[...], d_up).astype(BF16).reshape(split)
        g_ff[step, 1, :, :, :, :, cols] = nn(dt[...], hidden).astype(BF16).reshape(split)
        branch[...] += nt(hidden, lower)
        d_normed[...] += nt(d_up, upper)

    attn, feed = (0, 1), (2, 3)
    for step in range(steps):
        for item in attn:
            core_copy(step, item).start()
    for kind in range(2):
        w_copy(0, kind).start()
    xt[...] = x_ref[...].T
    dt[...] = dy_ref[...].T
    branch[...] = jnp.zeros_like(branch)
    d_normed[...] = jnp.zeros_like(d_normed)

    def one_step(step, carry):
        for kind in range(2):
            w_copy(step, kind).wait()

        @pl.when(step + 1 < steps)
        def _():
            for kind in range(2):
                w_copy(step + 1, kind).start()

        feed_half(step, 0)

        @pl.when(step >= 1)
        def _():
            after_core(step - 1, feed)

        after_core(step, attn)

        @pl.when(step >= 2)
        def _():
            after_second(step - 2, feed)

        feed_half(step, 1)
        for item in feed:
            core_copy(step, item).start()

        @pl.when(step >= 1)
        def _():
            after_first(step - 1, feed)

        after_first(step, attn)

        @pl.when(step >= 1)
        def _():
            after_second(step - 1, attn)

        return carry

    lax.fori_loop(0, steps, one_step, 0)
    last = steps - 1

    sums[0] = gains_in[...]
    store_gain(sums.at[0], d_normed[...], x_ref[...], gain[...])

    def sum_copy(stage):
        to = (sibling, beside, above)[stage]
        return remote(sums.at[stage], got_sums.at[stage], sum_send.at[stage], sum_recv.at[stage],
                      to, z)

    def sum_z_copy(k):
        return remote(sums.at[3], z_sums.at[z], sum_send.at[2 + k], sum_recv.at[2 + k],
                      d, lax.rem(z + k, steps))

    def next_sum(stage):
        sum_copy(stage).wait_recv()
        sums[stage + 1] = sums[stage] + got_sums[stage]

    sum_copy(0).start()
    after_core(last, feed)
    next_sum(0)
    sum_copy(1).start()
    after_second(last - 1, feed)
    next_sum(1)
    sum_copy(2).start()
    after_first(last, feed)
    next_sum(2)
    for k in range(1, steps):
        sum_z_copy(k).start()
    z_sums[z] = sums[3]
    for step in range(last):
        z_copy(step, 0).wait_recv()
    finish_sum(attn, out_attn)
    for step in range(last):
        z_copy(step, 1).wait_recv()
        z_copy(step, 2).wait_recv()
    finish_sum(feed[:1], out_up)
    finish_sum(feed[1:], out_down)
    for k in range(1, steps):
        sum_z_copy(k).wait_recv()
    total = z_sums[0]
    for k in range(1, steps):
        total = total + z_sums[k]
    out_gains[...] = total

    for step in range(steps):
        for item in range(4):
            core_copy(step, item).wait_send()
            first_copy(step, item).wait_send()
            second_copy(step, item).wait_send()
    for step in range(last):
        for kind in range(3):
            z_copy(step, kind).wait_send()
    for stage in range(3):
        sum_copy(stage).wait_send()
    for k in range(1, steps):
        sum_z_copy(k).wait_send()


def feed_remote_call(normed, grads, w_ff, g_attn, gain, gains):
    rows, width = normed.shape
    steps, _, _, shard, _ = w_ff.shape
    vmem = pl.BlockSpec(memory_space=pltpu.VMEM)
    return pl.pallas_call(
        feed_remote_kernel,
        in_specs=[vmem, vmem, pl.BlockSpec(memory_space=pl.ANY), vmem, vmem, vmem],
        out_specs=[vmem] * 6,
        out_shape=[jax.ShapeDtypeStruct((rows, width), F32)] * 2
        + [jax.ShapeDtypeStruct((shard, width), F32)] * 3
        + [jax.ShapeDtypeStruct((8, 128), F32)],
        scratch_shapes=[
            pltpu.VMEM((width, rows), BF16),
            pltpu.VMEM((width, rows), BF16),
            pltpu.VMEM((2, 2, 8, shard, width), BF16),
            pltpu.VMEM((steps, 2, 2, 2, 2, shard, width), BF16),
            pltpu.VMEM((steps, 3, 2, 2, shard, width), BF16),
            pltpu.VMEM((steps, 3, 2, shard, width), BF16),
            pltpu.VMEM((steps, 3, shard, width), BF16),
            pltpu.VMEM((3, steps - 1, shard, width), BF16),
            pltpu.VMEM((4, 8, 128), F32),
            pltpu.VMEM((3, 8, 128), F32),
            pltpu.VMEM((steps, 8, 128), F32),
            pltpu.SemaphoreType.DMA((2, 2)),
            pltpu.SemaphoreType.DMA((3, 4, steps)),
            pltpu.SemaphoreType.DMA((3, 4, steps)),
            pltpu.SemaphoreType.DMA((3, steps - 1)),
            pltpu.SemaphoreType.DMA((3, steps - 1)),
            pltpu.SemaphoreType.DMA((6,)),
            pltpu.SemaphoreType.DMA((6,)),
        ],
        compiler_params=pltpu.CompilerParams(
            collective_id=0, has_side_effects=True, vmem_limit_bytes=VMEM
        ),
        cost_estimate=pl.CostEstimate(
            flops=12 * rows * width * width * steps,
            bytes_accessed=4 * steps * width * width * 2,
            transcendentals=rows * width * steps,
        ),
        name="feed_forward_scatter",
    )(normed, grads, w_ff, g_attn, gain, gains)


def iota(shape, axis):
    return lax.broadcasted_iota(jnp.int32, shape, axis)


def source_of(index, start, total):
    rest = index - BIG
    other = jnp.where(rest < start, rest, rest + MOST)
    held = jnp.where(index < MOST, start + index, -1)
    return jnp.where((rest >= 0) & (rest < total - MOST), other, held)


def store_gain(out, d_normed, normed, gain):
    total = jnp.sum(d_normed * normed.astype(F32), axis=0, keepdims=True) / gain
    for row in range(total.shape[1] // 128):
        out[row:row + 1] += total[:, 128 * row:128 * row + 128]


def attention_kernel(
    part, place, own_x, own_dy, in1, in2, in3, ids, gains, norm_gain, weights,
    out0, out1, out2, out3, g_weights, g_gains,
    x_ref, dy_ref, xt, dt, feat_q, feat_k, pt, raw, d_raw, d_att, att, d_normed, branch,
):
    step = pl.program_id(0)
    mp = ids.shape[1]
    total = mp * part
    me = place[0]
    lane = iota((1, 128), 1)

    @pl.when(step == 0)
    def _():
        numbers = ids[0]
        start = jnp.zeros((1, 1), jnp.int32)
        for image in range(IMAGES):
            count = jnp.sum(
                (numbers == image).astype(F32), axis=(0, 1), keepdims=True
            )
            ahead = jnp.sum(
                ((numbers >= 0) & (numbers < image)).astype(F32), axis=(0, 1), keepdims=True
            )
            start = start + jnp.where(count == MOST, ahead, 0.0).astype(jnp.int32)
        column = source_of(iota((ROWS, 1), 0), start, total)
        line = source_of(iota((1, ROWS), 1), start, total)
        x_sum, dy_sum, feats = 0.0, 0.0, 0.0
        pieces = ((own_x, own_dy), (in1,), (in2,), (in3,))
        for k, piece in enumerate(pieces):
            chunk = lax.rem(me - k + mp, mp)
            offset = iota((1, PIECE), 1)
            pos = jnp.where(offset < part, chunk * part + offset, -2)
            pick = (column == pos).astype(F32).astype(BF16)
            offset = iota((PIECE, 1), 0)
            pos = jnp.where(offset < part, chunk * part + offset, -2)
            pt[k] = (line == pos).astype(F32).astype(BF16)
            x_piece = piece[0][0]
            dy_piece = piece[1][0] if k == 0 else piece[0][1]
            x_sum = x_sum + nn(pick, x_piece)
            dy_sum = dy_sum + nn(pick, dy_piece)
            marks = (iota((128, 1), 0) - HD == ids[0, pl.ds(chunk, 1), :]).astype(F32)
            feats = feats + nt(pick, marks.astype(BF16))
        x = x_sum.astype(BF16)
        dy = dy_sum.astype(BF16)
        x_ref[...] = x
        dy_ref[...] = dy
        xt[...] = x.T
        dt[...] = dy.T
        feat_q[...] = (feats * 128.0).astype(BF16)
        marked = (lane >= HD) & (lane < HD + IMAGES)
        feat_k[...] = jnp.where(marked, (feats - 1.0) * 256.0, 0.0).astype(BF16)
        d_normed[...] = jnp.zeros_like(d_normed)
        branch[...] = jnp.zeros_like(branch)
        g_gains[...] = jnp.zeros_like(g_gains)

    raw[...] = nn(x_ref[...], weights[0, :, :640])
    d_att[...] = nn(dy_ref[...], weights[0, :, 512:])
    low = lane < HD
    same = (iota((128, 128), 0) // HD == iota((128, 128), 1) // HD).astype(F32)
    mean_of = (same * (1.0 / HD)).astype(BF16)
    gain = gains[...]

    def half_mean(value):
        return nn(value.astype(BF16), mean_of)

    d_gain = jnp.zeros((1, 128), F32)
    for head in range(3):
        qk = raw[:, 128 * head:128 * head + 128]
        high = qk.astype(BF16)
        mean = nn(high, mean_of) + half_mean(qk - high.astype(F32))
        centered = qk - mean
        spread = lax.rsqrt(half_mean(centered * centered) + 1e-6)
        unit = centered * spread
        rounded = (unit * gain).astype(BF16).astype(F32)
        q_aug = jnp.where(low, rounded * 0.125, feat_q[...].astype(F32)).astype(BF16)
        k_aug = jnp.where(low, pltpu.roll(rounded, HD, 1), feat_k[...].astype(F32)).astype(BF16)
        v_tile = 384 + 128 * (head // 2)
        v = raw[:, v_tile:v_tile + 128]
        if head == 1:
            v = pltpu.roll(v, HD, 1)
        one = ((lane == HD) | (lane == HD + 1)).astype(F32)
        v_aug = jnp.where(low, v, one).astype(BF16)
        a_tile = 128 * ((head + 1) // 2)
        da = d_att[:, a_tile:a_tile + 128]
        if head != 1:
            da = pltpu.roll(da, HD, 1)
        q_t = q_aug.astype(F32).T.astype(BF16)
        d_queries, attended, d_keys, d_values = [], [], [], []
        for base, count in ((0, BIG), (BIG, REST)):
            keys = k_aug[base:base + count]
            values = v_aug[base:base + count]
            dk_t = jnp.zeros((128, count), F32)
            dv_t = jnp.zeros((128, count), F32)
            for row in range(base, base + count, 256):
                rows = slice(row, row + 256)
                prob = jnp.exp(nt(q_aug[rows], keys))
                prob_low = prob.astype(BF16)
                gathered = nn(prob_low, values)
                inverse = 1.0 / gathered[:, HD:HD + 1]
                out = jnp.where(low, gathered * inverse, 0.0)
                attended.append(out)
                scaled = jnp.where(low, da[rows] * inverse, 0.0).astype(BF16).astype(F32)
                dot = jnp.sum(scaled * out, axis=-1, keepdims=True)
                dot_high = dot.astype(BF16).astype(F32)
                d_aug = jnp.where(
                    lane == HD, -dot_high, jnp.where(lane == HD + 1, dot_high - dot, scaled)
                )
                d_low = d_aug.astype(BF16)
                d_score = (prob * nt(d_low, values)).astype(BF16)
                d_queries.append(nn(d_score, keys))
                dk_t = dk_t + nn(q_t[:, rows], d_score)
                dv_t = dv_t + nn(d_aug.T.astype(BF16), prob_low)
            d_keys.append(dk_t.T)
            d_values.append(dv_t.T)
        d_query = jnp.concatenate(d_queries, axis=0) * 0.125
        d_key = jnp.concatenate(d_keys, axis=0)
        d_value = jnp.concatenate(d_values, axis=0)
        attend = jnp.concatenate(attended, axis=0)
        d_qk = jnp.where(low, d_query, pltpu.roll(d_key, HD, 1))
        d_gain = d_gain + jnp.sum(d_qk * unit, axis=0, keepdims=True)
        scaled = d_qk * gain
        d_qk = spread * (scaled - half_mean(scaled) - unit * half_mean(scaled * unit))
        d_raw[:, 128 * head:128 * head + 128] = d_qk.astype(BF16)
        if head == 0:
            first_value = d_value
            att[:, 0:128] = jnp.where(low, 0.0, pltpu.roll(attend, HD, 1)).astype(BF16)
        elif head == 1:
            both = jnp.where(low, first_value, pltpu.roll(d_value, HD, 1))
            d_raw[:, 384:512] = both.astype(BF16)
            first_att = attend
        else:
            d_raw[:, 512:640] = jnp.where(low, d_value, 0.0).astype(BF16)
            both = jnp.where(low, first_att, pltpu.roll(attend, HD, 1))
            att[:, 128:256] = both.astype(BF16)
    g_gains[6:7] += d_gain
    d_projected = d_raw[...]
    attended = att[...]
    d_normed[...] += nt(d_projected, weights[0, :, :640])
    branch[...] += nt(attended, weights[0, :, 512:])
    left = nn(xt[...], d_projected)
    right = nn(dt[...], attended)
    g_weights[0, :, :512] = left[:, :512].astype(BF16)
    g_weights[0, :, 512:640] = (left[:, 512:] + right[:, :128]).astype(BF16)
    g_weights[0, :, 640:] = right[:, 128:].astype(BF16)

    @pl.when(step == pl.num_programs(0) - 1)
    def _():
        store_gain(g_gains, d_normed[...], x_ref[...], norm_gain[...])
        d_rows = d_normed[...].astype(BF16)
        b_rows = branch[...].astype(BF16)
        for k, out in enumerate((out0, out1, out2, out3)):
            out[0] = nn(pt[k], d_rows).astype(BF16)
            out[1] = nn(pt[k], b_rows).astype(BF16)


def attention_call(place, part, normed, grads, received, ids, gains, norm_gain, weights):
    width = normed.shape[-1]
    chunks = weights.shape[0]
    mp = ids.shape[1]
    own = pl.BlockSpec((1, PIECE, width), lambda m, place: (0, 0, 0))
    pair = pl.BlockSpec((2, PIECE, width), lambda m, place: (0, 0, 0))
    chunk = pl.BlockSpec((1, width, width), lambda m, place: (m, 0, 0))
    line = pl.BlockSpec((1, 128), lambda m, place: (0, 0))
    return pl.pallas_call(
        functools.partial(attention_kernel, part),
        grid_spec=pltpu.PrefetchScalarGridSpec(
            num_scalar_prefetch=1,
            grid=(chunks,),
            in_specs=[own, own, pair, pair, pair,
                      pl.BlockSpec((1, mp, PIECE), lambda m, place: (place[0], 0, 0)),
                      line, pl.BlockSpec((1, width), lambda m, place: (0, 0)), chunk],
            out_specs=[pair] * 4 + [chunk, pl.BlockSpec((8, 128), lambda m, place: (0, 0))],
            scratch_shapes=[
                pltpu.VMEM((ROWS, width), BF16),
                pltpu.VMEM((ROWS, width), BF16),
                pltpu.VMEM((width, ROWS), BF16),
                pltpu.VMEM((width, ROWS), BF16),
                pltpu.VMEM((ROWS, 128), BF16),
                pltpu.VMEM((ROWS, 128), BF16),
                pltpu.VMEM((mp, PIECE, ROWS), BF16),
                pltpu.VMEM((ROWS, 640), F32),
                pltpu.VMEM((ROWS, 640), BF16),
                pltpu.VMEM((ROWS, 256), F32),
                pltpu.VMEM((ROWS, 256), BF16),
                pltpu.VMEM((ROWS, width), F32),
                pltpu.VMEM((ROWS, width), F32),
            ],
        ),
        out_shape=[jax.ShapeDtypeStruct((2, PIECE, width), BF16)] * 4
        + [jax.ShapeDtypeStruct(weights.shape, BF16), jax.ShapeDtypeStruct((8, 128), F32)],
        compiler_params=pltpu.CompilerParams(vmem_limit_bytes=VMEM),
        cost_estimate=pl.CostEstimate(
            flops=60_000_000_000, bytes_accessed=4 * chunks * width * width,
            transcendentals=ROWS * ROWS * 12,
        ),
        name="attention",
    )(place, normed, grads, *received, ids, gains, norm_gain, weights)


def finish_kernel(
    place, tok, cot, gain, branch, d_ff, ret0, ret1, ret2, ret3, output, input_grad
):
    step = pl.program_id(0)
    part = tok.shape[1]

    for index, back in enumerate((ret0, ret1, ret2, ret3)):

        @pl.when(step == index)
        def _():
            x = tok[0].astype(F32)
            output[0] = (x + (branch[0] + back[1].astype(F32))[:part]).astype(BF16)
            d_normed = (d_ff[0] + back[0].astype(F32))[:part]
            centered = x - jnp.mean(x, axis=-1, keepdims=True)
            spread = lax.rsqrt(jnp.mean(centered * centered, axis=-1, keepdims=True) + 1e-6)
            unit = centered * spread
            scaled = d_normed * gain[...]
            d_x = spread * (
                scaled
                - jnp.mean(scaled, axis=-1, keepdims=True)
                - unit * jnp.mean(scaled * unit, axis=-1, keepdims=True)
            )
            input_grad[0] = cot[0].astype(F32) + d_x


def finish_call(place, tokens, cotangent, gain, branch, d_ff, returned):
    count, part, width = tokens.shape
    block = pl.BlockSpec(
        (1, part, width), lambda k, place: (lax.rem(place[0] + k, count), 0, 0)
    )
    padded = pl.BlockSpec((1, PIECE, width), lambda k, place: (k, 0, 0))
    pair = pl.BlockSpec((2, PIECE, width), lambda k, place: (0, 0, 0))
    line = pl.BlockSpec((1, width), lambda k, place: (0, 0))
    return pl.pallas_call(
        finish_kernel,
        grid_spec=pltpu.PrefetchScalarGridSpec(
            num_scalar_prefetch=1,
            grid=(count,),
            in_specs=[block, block, line, padded, padded] + [pair] * 4,
            out_specs=[block, block],
        ),
        out_shape=[
            jax.ShapeDtypeStruct(tokens.shape, BF16),
            jax.ShapeDtypeStruct(tokens.shape, F32),
        ],
        compiler_params=pltpu.CompilerParams(vmem_limit_bytes=VMEM),
        name="finish",
    )(place, tokens, cotangent, gain, branch, d_ff, *returned)


def pack_attention(w_qkv, w_proj):
    rows, wide = w_qkv.shape[1:]
    heads = wide // HD
    qk = w_qkv[:2].reshape(2, rows, heads, HD).transpose(1, 2, 0, 3).reshape(rows, 2 * wide)
    return jnp.concatenate([qk, w_qkv[2], w_proj.T], axis=1)


def unpack_attention(grad, wide):
    rows = grad.shape[0]
    heads = wide // HD
    qk = grad[:, :2 * wide].reshape(rows, heads, 2, HD).transpose(2, 0, 1, 3)
    qk = qk.reshape(2, rows, wide)
    g_qkv = jnp.concatenate([qk, grad[None, :, 2 * wide:3 * wide]], axis=0)
    return g_qkv, grad[:, 3 * wide:].T


def body(
    dp, mp, tokens, w_qkv, w_up, w_proj, w_down, norm_gain, query_gain, key_gain, image_ids, cotangent
):
    micro, seqs, part, width = tokens.shape
    count = micro * seqs
    shard = w_up.shape[0]
    me = lax.axis_index("mp")
    place = me.astype(jnp.int32)[None]
    both = ("mp", "dp")
    w_attn = lax.all_gather(pack_attention(w_qkv, w_proj), both).reshape(mp, width, width)

    tok = tokens.reshape(count, part, width)
    cot = cotangent.reshape(count, part, width)
    gain = norm_gain.reshape(1, width)
    normed, grads, *sends = norm_call(place, tok, cot, gain)
    received = [
        lax.ppermute(send, "mp", [(i, (i + k) % mp) for i in range(mp)])
        for k, send in enumerate(sends, 1)
    ]
    ids = image_ids.reshape(count, mp, part)
    ids = jnp.pad(ids, ((0, 0), (0, 0), (0, PIECE - part)), constant_values=-1)
    gains = jnp.concatenate([query_gain, key_gain]).reshape(1, 2 * HD)
    w_ff, received = lax.optimization_barrier((jnp.stack([w_up, w_down.T]), received))
    w_ff = lax.all_gather(w_ff, both).reshape(mp, dp, 2, shard, width)
    *outs, g_attn, g_gains = attention_call(
        place, part, normed, grads, received, ids, gains, gain, w_attn
    )
    returned = [outs[0]] + [
        lax.ppermute(out, "mp", [(i, (i - k) % mp) for i in range(mp)])
        for k, out in enumerate(outs[1:], 1)
    ]
    flat_normed = normed.reshape(count * PIECE, width)
    flat_grads = grads.reshape(count * PIECE, width)
    if (dp, mp) == (8, 4):
        branch, d_ff, g_attn, g_up, g_down, g_gains = feed_remote_call(
            flat_normed, flat_grads, w_ff, g_attn.reshape(mp, 2, 2, 2, shard, width), gain, g_gains
        )
    else:
        branch, d_ff, g_up, g_down = feed_call(
            flat_normed, flat_grads,
            w_ff[:, :, 0].reshape(mp, width, width), w_ff[:, :, 1].reshape(mp, width, width),
        )
        g_attn, g_up, g_down = (
            lax.psum_scatter(
                grad.reshape(-1, shard, width), both, scatter_dimension=0
            ).astype(F32)
            for grad in (g_attn, g_up, g_down)
        )
        own = jnp.sum(d_ff * flat_normed.astype(F32), axis=0) / norm_gain
        g_gains = g_gains.at[:width // 128].add(own.reshape(-1, 128))
        g_gains = lax.psum(g_gains, ("dp", "mp"))
    output, input_grad = finish_call(
        place, tok, cot, gain,
        branch.reshape(count, PIECE, width), d_ff.reshape(count, PIECE, width), returned,
    )
    g_qkv, g_proj = unpack_attention(g_attn, w_qkv.shape[2])
    g_norm = g_gains[:width // 128].reshape(width)
    g_gains = g_gains[6]
    return (
        output.reshape(tokens.shape),
        input_grad.reshape(tokens.shape),
        g_qkv,
        g_up,
        g_proj,
        g_down.T,
        g_norm,
        g_gains[:HD],
        g_gains[HD:],
    )


def solution(mesh):
    rows = P(None, "dp", "mp", None)
    weights = (P(None, "dp", "mp"), P("dp", "mp"), P("mp", "dp"), P("mp", "dp"))
    gains = (P(), P(), P())
    return jax.shard_map(
        functools.partial(body, mesh.shape["dp"], mesh.shape["mp"]),
        mesh=mesh,
        in_specs=(rows,) + weights + gains + (P(None, "dp", None), rows),
        out_specs=(rows, rows) + weights + gains,
        check_vma=False,
    )
```

```python
import functools

import jax
import jax.numpy as jnp
from jax import lax
from jax.experimental import pallas as pl
from jax.experimental.pallas import tpu as pltpu
from jax.sharding import PartitionSpec as P

HD = 64
MOST = 709
IMAGES = 8
PIECE = 240
BIG = 768
REST = 256
ROWS = BIG + REST
VMEM = 60 * 1024 * 1024
F32 = jnp.float32
BF16 = jnp.bfloat16


def nn(left, right):
    return lax.dot_general(left, right, (((1,), (0,)), ((), ())), preferred_element_type=F32)


def nt(left, right):
    return lax.dot_general(left, right, (((1,), (1,)), ((), ())), preferred_element_type=F32)


def norm_kernel(place, tok, cot, gain, normed, grads, send1, send2, send3):
    step = pl.program_id(0)
    part = tok.shape[1]
    x = tok[0].astype(F32)
    centered = x - jnp.mean(x, axis=-1, keepdims=True)
    spread = lax.rsqrt(jnp.mean(centered * centered, axis=-1, keepdims=True) + 1e-6)
    value = (centered * spread * gain[...]).astype(BF16)
    normed[...] = jnp.zeros_like(normed)
    grads[...] = jnp.zeros_like(grads)
    normed[0, :part] = value
    grads[0, :part] = cot[0]
    for index, send in ((1, send1), (2, send2), (3, send3)):

        @pl.when(step == index)
        def _():
            send[0] = normed[0]
            send[1] = grads[0]


def norm_call(place, tokens, cotangent, gain):
    count, part, width = tokens.shape
    block = lambda k, place: (lax.rem(place[0] + k, count), 0, 0)
    fixed = lambda k, place: (0, 0, 0)
    return pl.pallas_call(
        norm_kernel,
        grid_spec=pltpu.PrefetchScalarGridSpec(
            num_scalar_prefetch=1,
            grid=(count,),
            in_specs=[
                pl.BlockSpec((1, part, width), block),
                pl.BlockSpec((1, part, width), block),
                pl.BlockSpec((1, width), lambda k, place: (0, 0)),
            ],
            out_specs=[pl.BlockSpec((1, PIECE, width), lambda k, place: (k, 0, 0))] * 2
            + [pl.BlockSpec((2, PIECE, width), fixed)] * 3,
        ),
        out_shape=[jax.ShapeDtypeStruct((count, PIECE, width), BF16)] * 2
        + [jax.ShapeDtypeStruct((2, PIECE, width), BF16)] * 3,
        compiler_params=pltpu.CompilerParams(vmem_limit_bytes=VMEM),
        name="norm_rows",
    )(place, tokens, cotangent, gain)


def feed_kernel(normed, grads, w_up, w_down, branch, d_normed, g_up, g_down, xt, dt):
    step = pl.program_id(0)
    x = normed[...]
    dy = grads[...]

    @pl.when(step == 0)
    def _():
        xt[...] = x.T
        dt[...] = dy.T

    up = nn(x, w_up[0])
    value, slope = gelu_parts(up)
    hidden = value.astype(BF16)
    d_up = (nn(dy, w_down[0]) * slope).astype(BF16)
    g_up[0] = nn(xt[...], d_up).astype(BF16)
    g_down[0] = nn(dt[...], hidden).astype(BF16)
    out = nt(hidden, w_down[0])
    back = nt(d_up, w_up[0])

    @pl.when(step == 0)
    def _():
        branch[...] = out
        d_normed[...] = back

    @pl.when(step > 0)
    def _():
        branch[...] += out
        d_normed[...] += back


def feed_call(normed, grads, w_up, w_down):
    rows, width = normed.shape
    chunks, _, hidden = w_up.shape
    whole = pl.BlockSpec((rows, width), lambda m: (0, 0))
    chunk = pl.BlockSpec((1, width, hidden), lambda m: (m, 0, 0))
    return pl.pallas_call(
        feed_kernel,
        grid=(chunks,),
        in_specs=[whole, whole, chunk, chunk],
        out_specs=[whole, whole, chunk, chunk],
        out_shape=[jax.ShapeDtypeStruct((rows, width), F32)] * 2
        + [jax.ShapeDtypeStruct(w_up.shape, BF16)] * 2,
        scratch_shapes=[pltpu.VMEM((width, rows), BF16)] * 2,
        compiler_params=pltpu.CompilerParams(vmem_limit_bytes=VMEM),
        cost_estimate=pl.CostEstimate(
            flops=12 * rows * width * hidden * chunks,
            bytes_accessed=4 * chunks * width * hidden * 2,
            transcendentals=rows * hidden * chunks,
        ),
        name="feed_forward",
    )(normed, grads, w_up, w_down)


class Place:
    def __init__(self, planes):
        d = lax.axis_index("dp")
        self.z = lax.axis_index("mp")
        self.d, self.planes = d, planes
        self.core, self.x, self.y = d % 2, (d // 2) % 2, d // 4
        self.sibling = d + 1 - 2 * self.core
        self.beside = d + 2 - 4 * self.x
        self.above = d + 4 - 8 * self.y

    def along(self, k):
        return lax.rem(self.z + k + self.planes, self.planes)

    def copy(self, src, dst, send, recv, dp=None, mp=None):
        return pltpu.make_async_remote_copy(
            src_ref=src, dst_ref=dst, send_sem=send, recv_sem=recv,
            device_id={"dp": self.d if dp is None else dp, "mp": self.z if mp is None else mp},
            device_id_type=pl.DeviceIdType.MESH,
        )

    def greet(self):
        barrier = pltpu.get_barrier_semaphore()
        for other in (self.sibling, self.beside, self.above):
            pl.semaphore_signal(barrier, 1, device_id={"dp": other, "mp": self.z},
                                device_id_type=pl.DeviceIdType.MESH)
        for k in range(1, self.planes):
            pl.semaphore_signal(barrier, 1, device_id={"dp": self.d, "mp": self.along(k)},
                                device_id_type=pl.DeviceIdType.MESH)
        pl.semaphore_wait(barrier, self.planes + 2)


class Scatter:
    def __init__(self, at, items, src, got_core, got_first, got_second, send_sem, recv_sem):
        self.at, self.items, self.src = at, items, src
        self.got_core, self.got_first, self.got_second = got_core, got_first, got_second
        self.send_sem, self.recv_sem = send_sem, recv_sem

    def copy(self, stage, step, item):
        at = self.at
        kind, cols, x_first = self.items[item]
        if stage == 0:
            src = self.src.at[step, kind, :, :, 1 - at.core, :, cols]
            dst = self.got_core.at[step, kind, :, :, :, cols]
            to = at.sibling
        elif stage == 1:
            if x_first:
                src = self.got_core.at[step, kind, :, 1 - at.x, :, cols]
            else:
                src = self.got_core.at[step, kind, 1 - at.y, :, :, cols]
            dst = self.got_first.at[step, kind, :, :, cols]
            to = at.beside if x_first else at.above
        else:
            src = self.got_first.at[step, kind, 1 - at.y if x_first else 1 - at.x, :, cols]
            dst = self.got_second.at[step, kind, :, cols]
            to = at.above if x_first else at.beside
        sem = (stage, item, step)
        return at.copy(src, dst, self.send_sem.at[sem], self.recv_sem.at[sem], dp=to)

    def start(self, step):
        for item in range(len(self.items)):
            self.copy(0, step, item).start()

    def after_core(self, step):
        for item, (kind, cols, _) in enumerate(self.items):
            self.copy(0, step, item).wait_recv()
            for row in ((0, 0), (0, 1), (1, 0), (1, 1)):
                own = self.src[(step, kind, *row, self.at.core, slice(None), cols)]
                to = (step, kind, *row, slice(None), cols)
                total = own.astype(F32) + self.got_core[to].astype(F32)
                self.got_core[to] = total.astype(BF16)
            self.copy(1, step, item).start()

    def after_first(self, step):
        for item, (kind, cols, x_first) in enumerate(self.items):
            self.copy(1, step, item).wait_recv()
            for row in range(2):
                if x_first:
                    own = self.got_core[step, kind, row, self.at.x, :, cols]
                else:
                    own = self.got_core[step, kind, self.at.y, row, :, cols]
                total = own.astype(F32) + self.got_first[step, kind, row, :, cols].astype(F32)
                self.got_first[step, kind, row, :, cols] = total.astype(BF16)
            self.copy(2, step, item).start()

    def total(self, step, item):
        kind, cols, x_first = self.items[item]
        self.copy(2, step, item).wait_recv()
        own = self.got_first[step, kind, self.at.y if x_first else self.at.x, :, cols]
        return own.astype(F32) + self.got_second[step, kind, :, cols].astype(F32)

    def after_second(self, step):
        for item, (kind, cols, _) in enumerate(self.items):
            self.got_second[step, kind, :, cols] = self.total(step, item).astype(BF16)

    def wait_send(self, step):
        for item in range(len(self.items)):
            for stage in range(3):
                self.copy(stage, step, item).wait_send()


class Gather:
    def __init__(self, at, shard, full, send_sem, recv_sem):
        self.at, self.shard, self.full = at, shard, full
        self.send_sem, self.recv_sem = send_sem, recv_sem

    def piece(self, k, y=False, x=False, core=False):
        at = self.at
        return self.full.at[at.along(-k), 1 - at.y if y else at.y, 1 - at.x if x else at.x,
                            1 - at.core if core else at.core]

    def move(self, kind, k, src, **to):
        sem = (kind, k)
        self.at.copy(src, src, self.send_sem.at[sem], self.recv_sem.at[sem], **to).start()

    def arrived(self, kind, k, ref):
        sem = (kind, k)
        self.at.copy(ref, ref, self.send_sem.at[sem], self.recv_sem.at[sem],
                     dp=self.at.sibling).wait_recv()

    def start(self):
        for k in range(1, self.at.planes):
            sem = (0, k)
            self.at.copy(self.shard, self.piece(0), self.send_sem.at[sem], self.recv_sem.at[sem],
                         mp=self.at.along(k)).start()

    def spread(self, k):
        at = self.at
        src = self.piece(k)
        if k:
            self.arrived(0, k, src)
        self.move(1, k, src, dp=at.beside)
        self.move(2, k, src, dp=at.above)
        self.move(3, k, src, dp=at.sibling)

    def forward(self, k):
        at = self.at
        from_x, from_y = self.piece(k, x=True), self.piece(k, y=True)
        self.arrived(1, k, from_x)
        if k % 2 == 0:
            self.move(5, k, from_x, dp=at.above)
        self.move(4, k, from_x, dp=at.sibling)
        self.arrived(2, k, from_y)
        if k % 2 == 1:
            self.move(5, k, from_y, dp=at.beside)
        self.move(6, k, from_y, dp=at.sibling)

    def across(self, k):
        src = self.piece(k, y=True, x=True)
        self.arrived(5, k, src)
        self.move(7, k, src, dp=self.at.sibling)

    def last(self, k):
        self.arrived(3, k, self.piece(k, core=True))
        self.arrived(4, k, self.piece(k, x=True, core=True))
        self.arrived(6, k, self.piece(k, y=True, core=True))
        self.arrived(7, k, self.piece(k, y=True, x=True, core=True))

    def wait_send(self):
        for k in range(self.at.planes):
            for kind in range(0 if k else 1, 8):
                sem = (kind, k)
                self.at.copy(self.piece(k), self.piece(k), self.send_sem.at[sem],
                             self.recv_sem.at[sem], dp=self.at.sibling).wait_send()


def gelu_parts(up):
    inner = 0.7978845608028654 * (up + 0.044715 * up * up * up)
    th = jnp.tanh(inner)
    half = 0.5 * (1.0 + th)
    slope = half + 0.5 * up * (1.0 - th * th) * (
        0.7978845608028654 * (1.0 + 3 * 0.044715 * up * up)
    )
    return up * half, slope


def halves(width):
    return (0, slice(0, width // 2), True), (0, slice(width // 2, width), False)


def feed_remote_kernel(
    x_ref, dy_ref, w_hbm, g_attn, z_attn, gain, gains_in,
    branch, d_normed, out_attn, out_up, out_down, out_gains,
    xt, dt, w_buf, g_ff, ff_core, ff_first, ff_second, at_core, at_first, at_second, got_z,
    sums, got_sums, z_sums,
    w_sem, ff_send, ff_recv, at_send, at_recv, z_send, z_recv, sum_send, sum_recv,
):
    width = x_ref.shape[1]
    steps, shard = w_hbm.shape[0], w_hbm.shape[3]
    half = width // 2
    at = Place(steps)
    at.greet()
    attn = Scatter(at, halves(width), g_attn, at_core, at_first, at_second, at_send, at_recv)
    both = (0, slice(0, width), True), (1, slice(0, width), False)
    feed = Scatter(at, both, g_ff, ff_core, ff_first, ff_second, ff_send, ff_recv)
    last = steps - 1

    def z_copy(step, kind):
        return at.copy(ff_second.at[step, kind], got_z.at[kind, step],
                       z_send.at[kind, step], z_recv.at[kind, step], mp=at.along(1 + step))

    def to_z(step):
        feed.after_second(step)
        for kind in range(2):
            z_copy(step, kind).start()

    def w_copy(step, kind):
        slot = lax.rem(step, 2)
        return pltpu.make_async_copy(
            w_hbm.at[at.along(1 + step), :, kind], w_buf.at[slot, kind], w_sem.at[slot, kind]
        )

    def feed_half(step, index):
        cols = slice(half * index, half * index + half)
        slot = lax.rem(step, 2)
        upper = w_buf[slot, 0, :, :, cols].reshape(width, half)
        lower = w_buf[slot, 1, :, :, cols].reshape(width, half)
        value, slope = gelu_parts(nn(x_ref[...], upper))
        hidden = value.astype(BF16)
        d_up = (nn(dy_ref[...], lower) * slope).astype(BF16)
        split = (2, 2, 2, shard, half)
        g_ff[step, 0, :, :, :, :, cols] = nn(xt[...], d_up).astype(BF16).reshape(split)
        g_ff[step, 1, :, :, :, :, cols] = nn(dt[...], hidden).astype(BF16).reshape(split)
        branch[...] += nt(hidden, lower)
        d_normed[...] += nt(d_up, upper)

    attn.start(0)
    for kind in range(2):
        w_copy(0, kind).start()
    xt[...] = x_ref[...].T
    dt[...] = dy_ref[...].T
    branch[...] = jnp.zeros_like(branch)
    d_normed[...] = jnp.zeros_like(d_normed)

    def one_step(step, carry):
        for kind in range(2):
            w_copy(step, kind).wait()

        @pl.when(step + 1 < steps)
        def _():
            for kind in range(2):
                w_copy(step + 1, kind).start()

        feed_half(step, 0)

        @pl.when(step == 0)
        def _():
            attn.after_core(0)

        @pl.when(step >= 1)
        def _():
            feed.after_core(step - 1)

        @pl.when(step >= 2)
        def _():
            to_z(step - 2)

        feed_half(step, 1)
        feed.start(step)

        @pl.when(step == 0)
        def _():
            attn.after_first(0)

        @pl.when(step >= 1)
        def _():
            feed.after_first(step - 1)

        return carry

    lax.fori_loop(0, steps, one_step, 0)

    sums[0] = gains_in[...]
    store_gain(sums.at[0], d_normed[...], x_ref[...], gain[...])

    def sum_copy(stage):
        to = (at.sibling, at.beside, at.above)[stage]
        return at.copy(sums.at[stage], got_sums.at[stage], sum_send.at[stage],
                       sum_recv.at[stage], dp=to)

    def sum_z_copy(k):
        return at.copy(sums.at[3], z_sums.at[at.z], sum_send.at[2 + k], sum_recv.at[2 + k],
                       mp=at.along(k))

    def next_sum(stage):
        sum_copy(stage).wait_recv()
        sums[stage + 1] = sums[stage] + got_sums[stage]

    sum_copy(0).start()
    feed.after_core(last)
    next_sum(0)
    sum_copy(1).start()
    to_z(last - 1)
    next_sum(1)
    sum_copy(2).start()
    for item in range(2):
        cols = attn.items[item][1]
        out_attn[:, cols] = attn.total(0, item) + z_attn[:, cols]
    feed.after_first(last)
    next_sum(2)
    for k in range(1, steps):
        sum_z_copy(k).start()
    z_sums[at.z] = sums[3]
    for kind, out in enumerate((out_up, out_down)):
        total = feed.total(last, kind)
        for step in range(last):
            z_copy(step, kind).wait_recv()
            total = total + got_z[kind, step].astype(F32)
        out[...] = total
    for k in range(1, steps):
        sum_z_copy(k).wait_recv()
    total = z_sums[0]
    for k in range(1, steps):
        total = total + z_sums[k]
    out_gains[...] = total

    attn.wait_send(0)
    for step in range(steps):
        feed.wait_send(step)
    for step in range(last):
        for kind in range(2):
            z_copy(step, kind).wait_send()
    for stage in range(3):
        sum_copy(stage).wait_send()
    for k in range(1, steps):
        sum_z_copy(k).wait_send()


def feed_remote_call(normed, grads, w_ff, g_attn, z_attn, gain, gains):
    rows, width = normed.shape
    steps, _, _, shard, _ = w_ff.shape
    vmem = pl.BlockSpec(memory_space=pltpu.VMEM)
    return pl.pallas_call(
        feed_remote_kernel,
        in_specs=[vmem, vmem, pl.BlockSpec(memory_space=pl.ANY)] + [vmem] * 4,
        out_specs=[vmem] * 6,
        out_shape=[jax.ShapeDtypeStruct((rows, width), F32)] * 2
        + [jax.ShapeDtypeStruct((shard, width), F32)] * 3
        + [jax.ShapeDtypeStruct((8, 128), F32)],
        scratch_shapes=[
            pltpu.VMEM((width, rows), BF16),
            pltpu.VMEM((width, rows), BF16),
            pltpu.VMEM((2, 2, 8, shard, width), BF16),
            pltpu.VMEM((steps, 2, 2, 2, 2, shard, width), BF16),
            pltpu.VMEM((steps, 2, 2, 2, shard, width), BF16),
            pltpu.VMEM((steps, 2, 2, shard, width), BF16),
            pltpu.VMEM((steps, 2, shard, width), BF16),
            pltpu.VMEM((1, 1, 2, 2, shard, width), BF16),
            pltpu.VMEM((1, 1, 2, shard, width), BF16),
            pltpu.VMEM((1, 1, shard, width), BF16),
            pltpu.VMEM((2, steps - 1, shard, width), BF16),
            pltpu.VMEM((4, 8, 128), F32),
            pltpu.VMEM((3, 8, 128), F32),
            pltpu.VMEM((steps, 8, 128), F32),
            pltpu.SemaphoreType.DMA((2, 2)),
            pltpu.SemaphoreType.DMA((3, 2, steps)),
            pltpu.SemaphoreType.DMA((3, 2, steps)),
            pltpu.SemaphoreType.DMA((3, 2, 1)),
            pltpu.SemaphoreType.DMA((3, 2, 1)),
            pltpu.SemaphoreType.DMA((2, steps - 1)),
            pltpu.SemaphoreType.DMA((2, steps - 1)),
            pltpu.SemaphoreType.DMA((6,)),
            pltpu.SemaphoreType.DMA((6,)),
        ],
        compiler_params=pltpu.CompilerParams(
            collective_id=0, has_side_effects=True, vmem_limit_bytes=VMEM
        ),
        cost_estimate=pl.CostEstimate(
            flops=12 * rows * width * width * steps,
            bytes_accessed=4 * steps * width * width * 2,
            transcendentals=rows * width * steps,
        ),
        name="feed_forward_scatter",
    )(normed, grads, w_ff, g_attn, z_attn, gain, gains)


def iota(shape, axis):
    return lax.broadcasted_iota(jnp.int32, shape, axis)


def source_of(index, start, total):
    rest = index - BIG
    other = jnp.where(rest < start, rest, rest + MOST)
    held = jnp.where(index < MOST, start + index, -1)
    return jnp.where((rest >= 0) & (rest < total - MOST), other, held)


def store_gain(out, d_normed, normed, gain):
    total = jnp.sum(d_normed * normed.astype(F32), axis=0, keepdims=True) / gain
    for row in range(total.shape[1] // 128):
        out[row:row + 1] += total[:, 128 * row:128 * row + 128]


def prepare(
    me, part, ids, pieces, x_ref, dy_ref, xt, dt, feat_q, feat_k, pt, d_normed, branch, g_gains
):
    mp = ids.shape[1]
    total = mp * part
    numbers = ids[me]
    start = jnp.zeros((1, 1), jnp.int32)
    for image in range(IMAGES):
        count = jnp.sum((numbers == image).astype(F32), axis=(0, 1), keepdims=True)
        ahead = jnp.sum(
            ((numbers >= 0) & (numbers < image)).astype(F32), axis=(0, 1), keepdims=True
        )
        start = start + jnp.where(count == MOST, ahead, 0.0).astype(jnp.int32)
    column = source_of(iota((ROWS, 1), 0), start, total)
    line = source_of(iota((1, ROWS), 1), start, total)
    x_sum, dy_sum, feats = 0.0, 0.0, 0.0
    for k, piece in enumerate(pieces):
        chunk = lax.rem(me - k + mp, mp)
        offset = iota((1, PIECE), 1)
        pos = jnp.where(offset < part, chunk * part + offset, -2)
        pick = (column == pos).astype(F32).astype(BF16)
        offset = iota((PIECE, 1), 0)
        pos = jnp.where(offset < part, chunk * part + offset, -2)
        pt[k] = (line == pos).astype(F32).astype(BF16)
        x_sum = x_sum + nn(pick, piece[0][...])
        dy_sum = dy_sum + nn(pick, piece[1][...])
        marks = (iota((128, 1), 0) - HD == ids[me, pl.ds(chunk, 1), :]).astype(F32)
        feats = feats + nt(pick, marks.astype(BF16))
    x = x_sum.astype(BF16)
    dy = dy_sum.astype(BF16)
    x_ref[...] = x
    dy_ref[...] = dy
    xt[...] = x.T
    dt[...] = dy.T
    lane = iota((1, 128), 1)
    feat_q[...] = (feats * 128.0).astype(BF16)
    marked = (lane >= HD) & (lane < HD + IMAGES)
    feat_k[...] = jnp.where(marked, (feats - 1.0) * 256.0, 0.0).astype(BF16)
    d_normed[...] = jnp.zeros_like(d_normed)
    branch[...] = jnp.zeros_like(branch)
    g_gains[...] = jnp.zeros_like(g_gains)


def attention_chunk(
    weights, gain, x_ref, dy_ref, xt, dt, feat_q, feat_k, raw, d_raw, d_att, att,
    d_normed, branch, g_gains, store, poll,
):
    raw[...] = nn(x_ref[...], weights(slice(0, 640)))
    d_att[...] = nn(dy_ref[...], weights(slice(512, 768)))
    lane = iota((1, 128), 1)
    low = lane < HD
    same = (iota((128, 128), 0) // HD == iota((128, 128), 1) // HD).astype(F32)
    mean_of = (same * (1.0 / HD)).astype(BF16)

    def half_mean(value):
        return nn(value.astype(BF16), mean_of)

    d_gain = jnp.zeros((1, 128), F32)
    for head in range(3):
        qk = raw[:, 128 * head:128 * head + 128]
        high = qk.astype(BF16)
        mean = nn(high, mean_of) + half_mean(qk - high.astype(F32))
        centered = qk - mean
        spread = lax.rsqrt(half_mean(centered * centered) + 1e-6)
        unit = centered * spread
        rounded = (unit * gain).astype(BF16).astype(F32)
        q_aug = jnp.where(low, rounded * 0.125, feat_q[...].astype(F32)).astype(BF16)
        k_aug = jnp.where(low, pltpu.roll(rounded, HD, 1), feat_k[...].astype(F32)).astype(BF16)
        v_tile = 384 + 128 * (head // 2)
        v = raw[:, v_tile:v_tile + 128]
        if head == 1:
            v = pltpu.roll(v, HD, 1)
        one = ((lane == HD) | (lane == HD + 1)).astype(F32)
        v_aug = jnp.where(low, v, one).astype(BF16)
        a_tile = 128 * ((head + 1) // 2)
        da = d_att[:, a_tile:a_tile + 128]
        if head != 1:
            da = pltpu.roll(da, HD, 1)
        q_t = q_aug.astype(F32).T.astype(BF16)
        d_queries, attended, d_keys, d_values = [], [], [], []
        for base, count in ((0, BIG), (BIG, REST)):
            keys = k_aug[base:base + count]
            values = v_aug[base:base + count]
            dk_t = jnp.zeros((128, count), F32)
            dv_t = jnp.zeros((128, count), F32)
            for row in range(base, base + count, 256):
                rows = slice(row, row + 256)
                prob = jnp.exp(nt(q_aug[rows], keys))
                prob_low = prob.astype(BF16)
                gathered = nn(prob_low, values)
                inverse = 1.0 / gathered[:, HD:HD + 1]
                out = jnp.where(low, gathered * inverse, 0.0)
                attended.append(out)
                scaled = jnp.where(low, da[rows] * inverse, 0.0).astype(BF16).astype(F32)
                dot = jnp.sum(scaled * out, axis=-1, keepdims=True)
                dot_high = dot.astype(BF16).astype(F32)
                d_aug = jnp.where(
                    lane == HD, -dot_high, jnp.where(lane == HD + 1, dot_high - dot, scaled)
                )
                d_low = d_aug.astype(BF16)
                d_score = (prob * nt(d_low, values)).astype(BF16)
                d_queries.append(nn(d_score, keys))
                dk_t = dk_t + nn(q_t[:, rows], d_score)
                dv_t = dv_t + nn(d_aug.T.astype(BF16), prob_low)
            d_keys.append(dk_t.T)
            d_values.append(dv_t.T)
        d_query = jnp.concatenate(d_queries, axis=0) * 0.125
        d_key = jnp.concatenate(d_keys, axis=0)
        d_value = jnp.concatenate(d_values, axis=0)
        attend = jnp.concatenate(attended, axis=0)
        d_qk = jnp.where(low, d_query, pltpu.roll(d_key, HD, 1))
        d_gain = d_gain + jnp.sum(d_qk * unit, axis=0, keepdims=True)
        scaled = d_qk * gain
        d_qk = spread * (scaled - half_mean(scaled) - unit * half_mean(scaled * unit))
        d_raw[:, 128 * head:128 * head + 128] = d_qk.astype(BF16)
        if head == 0:
            first_value = d_value
            att[:, 0:128] = jnp.where(low, 0.0, pltpu.roll(attend, HD, 1)).astype(BF16)
        elif head == 1:
            both = jnp.where(low, first_value, pltpu.roll(d_value, HD, 1))
            d_raw[:, 384:512] = both.astype(BF16)
            first_att = attend
        else:
            d_raw[:, 512:640] = jnp.where(low, d_value, 0.0).astype(BF16)
            both = jnp.where(low, first_att, pltpu.roll(attend, HD, 1))
            att[:, 128:256] = both.astype(BF16)
        poll(head)
    g_gains[6:7] += d_gain
    d_projected = d_raw[...]
    attended = att[...]
    d_normed[...] += nt(d_projected, weights(slice(0, 640)))
    branch[...] += nt(attended, weights(slice(512, 768)))
    left = nn(xt[...], d_projected)
    right = nn(dt[...], attended)
    store(slice(0, 512), left[:, :512].astype(BF16))
    store(slice(512, 640), (left[:, 512:] + right[:, :128]).astype(BF16))
    store(slice(640, 768), right[:, 128:].astype(BF16))


def take_back(outs, pt, x_ref, norm_gain, d_normed, branch, g_gains):
    store_gain(g_gains, d_normed[...], x_ref[...], norm_gain[...])
    d_rows = d_normed[...].astype(BF16)
    b_rows = branch[...].astype(BF16)
    for k, out in enumerate(outs):
        out[0] = nn(pt[k], d_rows).astype(BF16)
        out[1] = nn(pt[k], b_rows).astype(BF16)


def attention_kernel(
    part, place, own_x, own_dy, in1, in2, in3, ids, gains, norm_gain, weights,
    out0, out1, out2, out3, g_weights, g_gains,
    x_ref, dy_ref, xt, dt, feat_q, feat_k, pt, raw, d_raw, d_att, att, d_normed, branch,
):
    step = pl.program_id(0)

    @pl.when(step == 0)
    def _():
        pieces = [(own_x.at[0], own_dy.at[0])] + [(got.at[0], got.at[1]) for got in (in1, in2, in3)]
        prepare(place[0], part, ids, pieces, x_ref, dy_ref, xt, dt, feat_q, feat_k, pt,
                d_normed, branch, g_gains)

    def store(cols, value):
        g_weights[0, :, cols] = value

    attention_chunk(
        lambda cols: weights[0, :, cols], gains[...], x_ref, dy_ref, xt, dt, feat_q, feat_k,
        raw, d_raw, d_att, att, d_normed, branch, g_gains, store, lambda head: None,
    )

    @pl.when(step == pl.num_programs(0) - 1)
    def _():
        take_back((out0, out1, out2, out3), pt, x_ref, norm_gain, d_normed, branch, g_gains)


def attention_call(place, part, normed, grads, received, ids, gains, norm_gain, weights):
    width = normed.shape[-1]
    chunks = weights.shape[0]
    mp = ids.shape[1]
    own = pl.BlockSpec((1, PIECE, width), lambda m, place: (0, 0, 0))
    pair = pl.BlockSpec((2, PIECE, width), lambda m, place: (0, 0, 0))
    chunk = pl.BlockSpec((1, width, width), lambda m, place: (m, 0, 0))
    line = pl.BlockSpec((1, 128), lambda m, place: (0, 0))
    return pl.pallas_call(
        functools.partial(attention_kernel, part),
        grid_spec=pltpu.PrefetchScalarGridSpec(
            num_scalar_prefetch=1,
            grid=(chunks,),
            in_specs=[own, own, pair, pair, pair,
                      pl.BlockSpec(ids.shape, lambda m, place: (0, 0, 0)),
                      line, pl.BlockSpec((1, width), lambda m, place: (0, 0)), chunk],
            out_specs=[pair] * 4 + [chunk, pl.BlockSpec((8, 128), lambda m, place: (0, 0))],
            scratch_shapes=[
                pltpu.VMEM((ROWS, width), BF16),
                pltpu.VMEM((ROWS, width), BF16),
                pltpu.VMEM((width, ROWS), BF16),
                pltpu.VMEM((width, ROWS), BF16),
                pltpu.VMEM((ROWS, 128), BF16),
                pltpu.VMEM((ROWS, 128), BF16),
                pltpu.VMEM((mp, PIECE, ROWS), BF16),
                pltpu.VMEM((ROWS, 640), F32),
                pltpu.VMEM((ROWS, 640), BF16),
                pltpu.VMEM((ROWS, 256), F32),
                pltpu.VMEM((ROWS, 256), BF16),
                pltpu.VMEM((ROWS, width), F32),
                pltpu.VMEM((ROWS, width), F32),
            ],
        ),
        out_shape=[jax.ShapeDtypeStruct((2, PIECE, width), BF16)] * 4
        + [jax.ShapeDtypeStruct(weights.shape, BF16), jax.ShapeDtypeStruct((8, 128), F32)],
        compiler_params=pltpu.CompilerParams(vmem_limit_bytes=VMEM),
        cost_estimate=pl.CostEstimate(
            flops=60_000_000_000, bytes_accessed=4 * chunks * width * width,
            transcendentals=ROWS * ROWS * 12,
        ),
        name="attention",
    )(place, normed, grads, *received, ids, gains, norm_gain, weights)


def front_kernel(
    tok, cot, ids, gains, norm_gain, w_attn, w_feed,
    normed, grads, out0, out1, out2, out3, w_ff, g_last, z_attn, g_gains,
    got_rows, w_full, g_buf, at_core, at_first, at_second, got_z,
    x_ref, dy_ref, xt, dt, feat_q, feat_k, pt, raw, d_raw, d_att, att, d_normed, branch,
    row_send, row_recv, wa_send, wa_recv, wf_send, wf_recv, own_sem, at_send, at_recv,
    z_send, z_recv,
):
    count, part, width = tok.shape
    shard = w_attn.shape[0]
    at = Place(count)
    at.greet()
    gather = Gather(at, w_attn, w_full, wa_send, wa_recv)
    gather_ff = Gather(at, w_feed, w_ff, wf_send, wf_recv)
    scatter = Scatter(at, halves(width), g_buf, at_core, at_first, at_second, at_send, at_recv)
    own_ff = pltpu.make_async_copy(w_feed, gather_ff.piece(0), own_sem)

    def row_copy(kind, k):
        src = (normed, grads)[kind].at[k]
        return at.copy(src, got_rows.at[k - 1, kind], row_send.at[kind, k - 1],
                       row_recv.at[kind, k - 1], mp=at.along(k))

    gather.start()
    own_ff.start()
    w_full[at.z, at.y, at.x, at.core] = w_attn[...]
    gather.spread(0)
    gain = norm_gain[...]
    for k in (1, 3, 2, 0):
        sequence = at.along(k)
        x = tok[sequence].astype(F32)
        centered = x - jnp.mean(x, axis=-1, keepdims=True)
        spread = lax.rsqrt(jnp.mean(centered * centered, axis=-1, keepdims=True) + 1e-6)
        pad = jnp.zeros((PIECE - part, width), BF16)
        normed[k, :part] = (centered * spread * gain).astype(BF16)
        normed[k, part:] = pad
        if k:
            row_copy(0, k).start()
        grads[k, :part] = cot[sequence]
        grads[k, part:] = pad
    gather.spread(1)
    gather.spread(3)
    gather.forward(0)
    gather.spread(2)
    own_ff.wait()
    gather_ff.spread(0)
    gather.forward(1)
    gather.across(0)
    gather.forward(3)
    for k in (1, 3, 2):
        row_copy(0, k).wait_recv()
    for k in (1, 3, 2):
        row_copy(1, k).start()
    gather_ff.start()
    gather.across(1)
    gather.forward(2)
    gather.across(3)
    gather.across(2)
    for k in range(count):
        gather.last(k)
    for k in (1, 3, 2):
        row_copy(1, k).wait_recv()
    pieces = [(normed.at[0], grads.at[0])]
    pieces += [(got_rows.at[k, 0], got_rows.at[k, 1]) for k in range(count - 1)]
    prepare(at.z, part, ids, pieces, x_ref, dy_ref, xt, dt, feat_q, feat_k, pt,
            d_normed, branch, g_gains)

    def z_copy(step):
        return at.copy(at_second.at[step, 0], got_z.at[step], z_send.at[step], z_recv.at[step],
                       mp=at.along(1 + step))

    def one_step(step, carry):
        chunk = at.along(1 + step)

        def weights(cols):
            return w_full[chunk, :, :, :, :, cols].reshape(width, cols.stop - cols.start)

        def store(cols, value):
            split = (2, 2, 2, shard, cols.stop - cols.start)
            g_buf[step, 0, :, :, :, :, cols] = value.reshape(split)

        def poll(head):
            @pl.when(step >= 1)
            def _():
                if head == 0:
                    scatter.after_core(step - 1)
                elif head == 1:
                    scatter.after_first(step - 1)
                else:
                    scatter.after_second(step - 1)
                    z_copy(step - 1).start()

            @pl.when(step == 0)
            def _():
                if head == 0:
                    gather_ff.spread(1)
                    gather_ff.forward(0)
                elif head == 1:
                    gather_ff.spread(3)
                    gather_ff.across(0)
                else:
                    gather_ff.spread(2)
                    gather_ff.forward(1)

            @pl.when(step == 1)
            def _():
                if head == 0:
                    gather_ff.forward(3)
                    gather_ff.across(1)
                elif head == 1:
                    gather_ff.forward(2)
                    gather_ff.across(3)
                else:
                    gather_ff.across(2)

        attention_chunk(
            weights, gains[...], x_ref, dy_ref, xt, dt, feat_q, feat_k,
            raw, d_raw, d_att, att, d_normed, branch, g_gains, store, poll,
        )

        @pl.when(step < count - 1)
        def _():
            scatter.start(step)

        return carry

    lax.fori_loop(0, count, one_step, 0)
    take_back((out0, out1, out2, out3), pt, x_ref, norm_gain, d_normed, branch, g_gains)
    g_last[...] = g_buf[count - 1:]
    total = 0.0
    for step in range(count - 1):
        z_copy(step).wait_recv()
        total = total + got_z[step].astype(F32)
    z_attn[...] = total
    for k in range(count):
        gather_ff.last(k)

    gather.wait_send()
    gather_ff.wait_send()
    for k in range(1, count):
        for kind in range(2):
            row_copy(kind, k).wait_send()
    for step in range(count - 1):
        scatter.wait_send(step)
        z_copy(step).wait_send()


def front_call(tokens, cotangent, ids, gains, norm_gain, w_attn, w_feed):
    count, part, width = tokens.shape
    shard = w_attn.shape[0]
    vmem = pl.BlockSpec(memory_space=pltpu.VMEM)
    hbm = pl.BlockSpec(memory_space=pl.ANY)
    rows = jax.ShapeDtypeStruct((count, PIECE, width), BF16)
    return pl.pallas_call(
        front_kernel,
        in_specs=[vmem] * 6 + [hbm],
        out_specs=[vmem] * 6 + [hbm] + [vmem] * 3,
        out_shape=[rows, rows]
        + [jax.ShapeDtypeStruct((2, PIECE, width), BF16)] * 4
        + [
            jax.ShapeDtypeStruct((count, 2, 2, 2, 2, shard, width), BF16),
            jax.ShapeDtypeStruct((1, 1, 2, 2, 2, shard, width), BF16),
            jax.ShapeDtypeStruct((shard, width), F32),
            jax.ShapeDtypeStruct((8, 128), F32),
        ],
        scratch_shapes=[
            pltpu.VMEM((count - 1, 2, PIECE, width), BF16),
            pltpu.VMEM((count, 2, 2, 2, shard, width), BF16),
            pltpu.VMEM((count, 1, 2, 2, 2, shard, width), BF16),
            pltpu.VMEM((count - 1, 1, 2, 2, shard, width), BF16),
            pltpu.VMEM((count - 1, 1, 2, shard, width), BF16),
            pltpu.VMEM((count - 1, 1, shard, width), BF16),
            pltpu.VMEM((count - 1, shard, width), BF16),
            pltpu.VMEM((ROWS, width), BF16),
            pltpu.VMEM((ROWS, width), BF16),
            pltpu.VMEM((width, ROWS), BF16),
            pltpu.VMEM((width, ROWS), BF16),
            pltpu.VMEM((ROWS, 128), BF16),
            pltpu.VMEM((ROWS, 128), BF16),
            pltpu.VMEM((count, PIECE, ROWS), BF16),
            pltpu.VMEM((ROWS, 640), F32),
            pltpu.VMEM((ROWS, 640), BF16),
            pltpu.VMEM((ROWS, 256), F32),
            pltpu.VMEM((ROWS, 256), BF16),
            pltpu.VMEM((ROWS, width), F32),
            pltpu.VMEM((ROWS, width), F32),
            pltpu.SemaphoreType.DMA((2, count - 1)),
            pltpu.SemaphoreType.DMA((2, count - 1)),
            pltpu.SemaphoreType.DMA((8, count)),
            pltpu.SemaphoreType.DMA((8, count)),
            pltpu.SemaphoreType.DMA((8, count)),
            pltpu.SemaphoreType.DMA((8, count)),
            pltpu.SemaphoreType.DMA,
            pltpu.SemaphoreType.DMA((3, 2, count - 1)),
            pltpu.SemaphoreType.DMA((3, 2, count - 1)),
            pltpu.SemaphoreType.DMA((count - 1,)),
            pltpu.SemaphoreType.DMA((count - 1,)),
        ],
        compiler_params=pltpu.CompilerParams(
            collective_id=1, has_side_effects=True, vmem_limit_bytes=VMEM
        ),
        name="front",
    )(tokens, cotangent, ids, gains, norm_gain, w_attn, w_feed)


def finish_kernel(
    place, tok, cot, gain, branch, d_ff, ret0, ret1, ret2, ret3, output, input_grad
):
    step = pl.program_id(0)
    part = tok.shape[1]

    for index, back in enumerate((ret0, ret1, ret2, ret3)):

        @pl.when(step == index)
        def _():
            x = tok[0].astype(F32)
            output[0] = (x + (branch[0] + back[1].astype(F32))[:part]).astype(BF16)
            d_normed = (d_ff[0] + back[0].astype(F32))[:part]
            centered = x - jnp.mean(x, axis=-1, keepdims=True)
            spread = lax.rsqrt(jnp.mean(centered * centered, axis=-1, keepdims=True) + 1e-6)
            unit = centered * spread
            scaled = d_normed * gain[...]
            d_x = spread * (
                scaled
                - jnp.mean(scaled, axis=-1, keepdims=True)
                - unit * jnp.mean(scaled * unit, axis=-1, keepdims=True)
            )
            input_grad[0] = cot[0].astype(F32) + d_x


def finish_call(place, tokens, cotangent, gain, branch, d_ff, returned):
    count, part, width = tokens.shape
    block = pl.BlockSpec(
        (1, part, width), lambda k, place: (lax.rem(place[0] + k, count), 0, 0)
    )
    padded = pl.BlockSpec((1, PIECE, width), lambda k, place: (k, 0, 0))
    pair = pl.BlockSpec((2, PIECE, width), lambda k, place: (0, 0, 0))
    line = pl.BlockSpec((1, width), lambda k, place: (0, 0))
    return pl.pallas_call(
        finish_kernel,
        grid_spec=pltpu.PrefetchScalarGridSpec(
            num_scalar_prefetch=1,
            grid=(count,),
            in_specs=[block, block, line, padded, padded] + [pair] * 4,
            out_specs=[block, block],
        ),
        out_shape=[
            jax.ShapeDtypeStruct(tokens.shape, BF16),
            jax.ShapeDtypeStruct(tokens.shape, F32),
        ],
        compiler_params=pltpu.CompilerParams(vmem_limit_bytes=VMEM),
        name="finish",
    )(place, tokens, cotangent, gain, branch, d_ff, *returned)


def pack_attention(w_qkv, w_proj):
    rows, wide = w_qkv.shape[1:]
    heads = wide // HD
    qk = w_qkv[:2].reshape(2, rows, heads, HD).transpose(1, 2, 0, 3).reshape(rows, 2 * wide)
    return jnp.concatenate([qk, w_qkv[2], w_proj.T], axis=1)


def unpack_attention(grad, wide):
    rows = grad.shape[0]
    heads = wide // HD
    qk = grad[:, :2 * wide].reshape(rows, heads, 2, HD).transpose(2, 0, 1, 3)
    qk = qk.reshape(2, rows, wide)
    g_qkv = jnp.concatenate([qk, grad[None, :, 2 * wide:3 * wide]], axis=0)
    return g_qkv, grad[:, 3 * wide:].T


def body(
    dp, mp, tokens, w_qkv, w_up, w_proj, w_down, norm_gain, query_gain, key_gain, image_ids, cotangent
):
    micro, seqs, part, width = tokens.shape
    count = micro * seqs
    shard = w_up.shape[0]
    me = lax.axis_index("mp")
    place = me.astype(jnp.int32)[None]
    both = ("mp", "dp")
    tok = tokens.reshape(count, part, width)
    cot = cotangent.reshape(count, part, width)
    gain = norm_gain.reshape(1, width)
    ids = image_ids.reshape(count, mp, part)
    ids = jnp.pad(ids, ((0, 0), (0, 0), (0, PIECE - part)), constant_values=-1)
    gains = jnp.concatenate([query_gain, key_gain]).reshape(1, 2 * HD)
    w_attn = pack_attention(w_qkv, w_proj)
    w_ff = jnp.stack([w_up, w_down.T])

    def send_back(outs):
        return [outs[0]] + [
            lax.ppermute(out, "mp", [(i, (i - k) % mp) for i in range(mp)])
            for k, out in enumerate(outs[1:], 1)
        ]

    if (dp, mp) == (8, 4):
        normed, grads, *outs, w_ff, g_attn, z_attn, g_gains = front_call(
            tok, cot, ids, gains, gain, w_attn, w_ff
        )
        returned = send_back(outs)
        branch, d_ff, g_attn, g_up, g_down, g_gains = feed_remote_call(
            normed.reshape(count * PIECE, width), grads.reshape(count * PIECE, width),
            w_ff.reshape(mp, dp, 2, shard, width), g_attn, z_attn, gain, g_gains,
        )
    else:
        w_attn = lax.all_gather(w_attn, both).reshape(mp, width, width)
        w_ff = lax.all_gather(w_ff, both).reshape(mp, dp, 2, shard, width)
        normed, grads, *sends = norm_call(place, tok, cot, gain)
        received = [
            lax.ppermute(send, "mp", [(i, (i + k) % mp) for i in range(mp)])
            for k, send in enumerate(sends, 1)
        ]
        *outs, g_attn, g_gains = attention_call(
            place, part, normed, grads, received, ids, gains, gain, w_attn
        )
        returned = send_back(outs)
        flat_normed = normed.reshape(count * PIECE, width)
        branch, d_ff, g_up, g_down = feed_call(
            flat_normed, grads.reshape(count * PIECE, width),
            w_ff[:, :, 0].reshape(mp, width, width), w_ff[:, :, 1].reshape(mp, width, width),
        )
        g_attn, g_up, g_down = (
            lax.psum_scatter(
                grad.reshape(-1, shard, width), both, scatter_dimension=0
            ).astype(F32)
            for grad in (g_attn, g_up, g_down)
        )
        own = jnp.sum(d_ff * flat_normed.astype(F32), axis=0) / norm_gain
        g_gains = g_gains.at[:width // 128].add(own.reshape(-1, 128))
        g_gains = lax.psum(g_gains, both)
    output, input_grad = finish_call(
        place, tok, cot, gain,
        branch.reshape(count, PIECE, width), d_ff.reshape(count, PIECE, width), returned,
    )
    g_qkv, g_proj = unpack_attention(g_attn, w_qkv.shape[2])
    g_norm = g_gains[:width // 128].reshape(width)
    g_gains = g_gains[6]
    return (
        output.reshape(tokens.shape),
        input_grad.reshape(tokens.shape),
        g_qkv,
        g_up,
        g_proj,
        g_down.T,
        g_norm,
        g_gains[:HD],
        g_gains[HD:],
    )


def solution(mesh):
    rows = P(None, "dp", "mp", None)
    weights = (P(None, "dp", "mp"), P("dp", "mp"), P("mp", "dp"), P("mp", "dp"))
    gains = (P(), P(), P())
    return jax.shard_map(
        functools.partial(body, mesh.shape["dp"], mesh.shape["mp"]),
        mesh=mesh,
        in_specs=(rows,) + weights + gains + (P(None, "dp", None), rows),
        out_specs=(rows, rows) + weights + gains,
        check_vma=False,
    )
```

```python
import functools

import jax
import jax.numpy as jnp
from jax import lax
from jax.experimental import pallas as pl
from jax.experimental.pallas import tpu as pltpu
from jax.sharding import PartitionSpec as P

HD = 64
MOST = 709
IMAGES = 8
PIECE = 240
BIG = 768
REST = 256
ROWS = BIG + REST
VMEM = 60 * 1024 * 1024
F32 = jnp.float32
BF16 = jnp.bfloat16


def nn(left, right):
    return lax.dot_general(left, right, (((1,), (0,)), ((), ())), preferred_element_type=F32)


def nt(left, right):
    return lax.dot_general(left, right, (((1,), (1,)), ((), ())), preferred_element_type=F32)


def norm_kernel(place, tok, cot, gain, normed, grads, send1, send2, send3):
    step = pl.program_id(0)
    part = tok.shape[1]
    x = tok[0].astype(F32)
    centered = x - jnp.mean(x, axis=-1, keepdims=True)
    spread = lax.rsqrt(jnp.mean(centered * centered, axis=-1, keepdims=True) + 1e-6)
    value = (centered * spread * gain[...]).astype(BF16)
    normed[...] = jnp.zeros_like(normed)
    grads[...] = jnp.zeros_like(grads)
    normed[0, :part] = value
    grads[0, :part] = cot[0]
    for index, send in ((1, send1), (2, send2), (3, send3)):

        @pl.when(step == index)
        def _():
            send[0] = normed[0]
            send[1] = grads[0]


def norm_call(place, tokens, cotangent, gain):
    count, part, width = tokens.shape
    block = lambda k, place: (lax.rem(place[0] + k, count), 0, 0)
    fixed = lambda k, place: (0, 0, 0)
    return pl.pallas_call(
        norm_kernel,
        grid_spec=pltpu.PrefetchScalarGridSpec(
            num_scalar_prefetch=1,
            grid=(count,),
            in_specs=[
                pl.BlockSpec((1, part, width), block),
                pl.BlockSpec((1, part, width), block),
                pl.BlockSpec((1, width), lambda k, place: (0, 0)),
            ],
            out_specs=[pl.BlockSpec((1, PIECE, width), lambda k, place: (k, 0, 0))] * 2
            + [pl.BlockSpec((2, PIECE, width), fixed)] * 3,
        ),
        out_shape=[jax.ShapeDtypeStruct((count, PIECE, width), BF16)] * 2
        + [jax.ShapeDtypeStruct((2, PIECE, width), BF16)] * 3,
        compiler_params=pltpu.CompilerParams(vmem_limit_bytes=VMEM),
        name="norm_rows",
    )(place, tokens, cotangent, gain)


def feed_kernel(normed, grads, w_up, w_down, branch, d_normed, g_up, g_down, xt, dt):
    step = pl.program_id(0)
    x = normed[...]
    dy = grads[...]

    @pl.when(step == 0)
    def _():
        xt[...] = x.T
        dt[...] = dy.T

    up = nn(x, w_up[0])
    value, slope = gelu_parts(up)
    hidden = value.astype(BF16)
    d_up = (nn(dy, w_down[0]) * slope).astype(BF16)
    g_up[0] = nn(xt[...], d_up).astype(BF16)
    g_down[0] = nn(dt[...], hidden).astype(BF16)
    out = nt(hidden, w_down[0])
    back = nt(d_up, w_up[0])

    @pl.when(step == 0)
    def _():
        branch[...] = out
        d_normed[...] = back

    @pl.when(step > 0)
    def _():
        branch[...] += out
        d_normed[...] += back


def feed_call(normed, grads, w_up, w_down):
    rows, width = normed.shape
    chunks, _, hidden = w_up.shape
    whole = pl.BlockSpec((rows, width), lambda m: (0, 0))
    chunk = pl.BlockSpec((1, width, hidden), lambda m: (m, 0, 0))
    return pl.pallas_call(
        feed_kernel,
        grid=(chunks,),
        in_specs=[whole, whole, chunk, chunk],
        out_specs=[whole, whole, chunk, chunk],
        out_shape=[jax.ShapeDtypeStruct((rows, width), F32)] * 2
        + [jax.ShapeDtypeStruct(w_up.shape, BF16)] * 2,
        scratch_shapes=[pltpu.VMEM((width, rows), BF16)] * 2,
        compiler_params=pltpu.CompilerParams(vmem_limit_bytes=VMEM),
        cost_estimate=pl.CostEstimate(
            flops=12 * rows * width * hidden * chunks,
            bytes_accessed=4 * chunks * width * hidden * 2,
            transcendentals=rows * hidden * chunks,
        ),
        name="feed_forward",
    )(normed, grads, w_up, w_down)


class Place:
    def __init__(self, planes):
        d = lax.axis_index("dp")
        self.z = lax.axis_index("mp")
        self.d, self.planes = d, planes
        self.core, self.x, self.y = d % 2, (d // 2) % 2, d // 4
        self.sibling = d + 1 - 2 * self.core
        self.beside = d + 2 - 4 * self.x
        self.above = d + 4 - 8 * self.y

    def along(self, k):
        return lax.rem(self.z + k + self.planes, self.planes)

    def copy(self, src, dst, send, recv, dp=None, mp=None):
        return pltpu.make_async_remote_copy(
            src_ref=src, dst_ref=dst, send_sem=send, recv_sem=recv,
            device_id={"dp": self.d if dp is None else dp, "mp": self.z if mp is None else mp},
            device_id_type=pl.DeviceIdType.MESH,
        )

    def greet(self):
        barrier = pltpu.get_barrier_semaphore()
        for other in (self.sibling, self.beside, self.above):
            pl.semaphore_signal(barrier, 1, device_id={"dp": other, "mp": self.z},
                                device_id_type=pl.DeviceIdType.MESH)
        for k in range(1, self.planes):
            pl.semaphore_signal(barrier, 1, device_id={"dp": self.d, "mp": self.along(k)},
                                device_id_type=pl.DeviceIdType.MESH)
        pl.semaphore_wait(barrier, self.planes + 2)


class Scatter:
    def __init__(self, at, items, src, got_core, got_first, got_second, send_sem, recv_sem):
        self.at, self.items, self.src = at, items, src
        self.got_core, self.got_first, self.got_second = got_core, got_first, got_second
        self.send_sem, self.recv_sem = send_sem, recv_sem

    def copy(self, stage, step, item):
        at = self.at
        kind, cols, x_first = self.items[item]
        if stage == 0:
            src = self.src.at[step, kind, :, :, 1 - at.core, :, cols]
            dst = self.got_core.at[step, kind, :, :, :, cols]
            to = at.sibling
        elif stage == 1:
            if x_first:
                src = self.got_core.at[step, kind, :, 1 - at.x, :, cols]
            else:
                src = self.got_core.at[step, kind, 1 - at.y, :, :, cols]
            dst = self.got_first.at[step, kind, :, :, cols]
            to = at.beside if x_first else at.above
        else:
            src = self.got_first.at[step, kind, 1 - at.y if x_first else 1 - at.x, :, cols]
            dst = self.got_second.at[step, kind, :, cols]
            to = at.above if x_first else at.beside
        sem = (stage, item, step)
        return at.copy(src, dst, self.send_sem.at[sem], self.recv_sem.at[sem], dp=to)

    def start(self, step):
        for item in range(len(self.items)):
            self.copy(0, step, item).start()

    def after_core(self, step):
        for item, (kind, cols, _) in enumerate(self.items):
            self.copy(0, step, item).wait_recv()
            for row in ((0, 0), (0, 1), (1, 0), (1, 1)):
                own = self.src[(step, kind, *row, self.at.core, slice(None), cols)]
                to = (step, kind, *row, slice(None), cols)
                total = own.astype(F32) + self.got_core[to].astype(F32)
                self.got_core[to] = total.astype(BF16)
            self.copy(1, step, item).start()

    def after_first(self, step):
        for item, (kind, cols, x_first) in enumerate(self.items):
            self.copy(1, step, item).wait_recv()
            for row in range(2):
                if x_first:
                    own = self.got_core[step, kind, row, self.at.x, :, cols]
                else:
                    own = self.got_core[step, kind, self.at.y, row, :, cols]
                total = own.astype(F32) + self.got_first[step, kind, row, :, cols].astype(F32)
                self.got_first[step, kind, row, :, cols] = total.astype(BF16)
            self.copy(2, step, item).start()

    def total(self, step, item):
        kind, cols, x_first = self.items[item]
        self.copy(2, step, item).wait_recv()
        own = self.got_first[step, kind, self.at.y if x_first else self.at.x, :, cols]
        return own.astype(F32) + self.got_second[step, kind, :, cols].astype(F32)

    def after_second(self, step):
        for item, (kind, cols, _) in enumerate(self.items):
            self.got_second[step, kind, :, cols] = self.total(step, item).astype(BF16)

    def wait_send(self, step):
        for item in range(len(self.items)):
            for stage in range(3):
                self.copy(stage, step, item).wait_send()


class Gather:
    def __init__(self, at, shard, full, send_sem, recv_sem):
        self.at, self.shard, self.full = at, shard, full
        self.send_sem, self.recv_sem = send_sem, recv_sem

    def piece(self, k, y=False, x=False, core=False):
        at = self.at
        return self.full.at[at.along(-k), 1 - at.y if y else at.y, 1 - at.x if x else at.x,
                            1 - at.core if core else at.core]

    def move(self, kind, k, src, **to):
        sem = (kind, k)
        self.at.copy(src, src, self.send_sem.at[sem], self.recv_sem.at[sem], **to).start()

    def arrived(self, kind, k, ref):
        sem = (kind, k)
        self.at.copy(ref, ref, self.send_sem.at[sem], self.recv_sem.at[sem],
                     dp=self.at.sibling).wait_recv()

    def start(self):
        for k in range(1, self.at.planes):
            sem = (0, k)
            self.at.copy(self.shard, self.piece(0), self.send_sem.at[sem], self.recv_sem.at[sem],
                         mp=self.at.along(k)).start()

    def spread(self, k):
        at = self.at
        src = self.piece(k)
        if k:
            self.arrived(0, k, src)
        self.move(1, k, src, dp=at.beside)
        self.move(2, k, src, dp=at.above)
        self.move(3, k, src, dp=at.sibling)

    def forward(self, k):
        at = self.at
        from_x, from_y = self.piece(k, x=True), self.piece(k, y=True)
        self.arrived(1, k, from_x)
        if k % 2 == 0:
            self.move(5, k, from_x, dp=at.above)
        self.move(4, k, from_x, dp=at.sibling)
        self.arrived(2, k, from_y)
        if k % 2 == 1:
            self.move(5, k, from_y, dp=at.beside)
        self.move(6, k, from_y, dp=at.sibling)

    def across(self, k):
        src = self.piece(k, y=True, x=True)
        self.arrived(5, k, src)
        self.move(7, k, src, dp=self.at.sibling)

    def last(self, k):
        self.arrived(3, k, self.piece(k, core=True))
        self.arrived(4, k, self.piece(k, x=True, core=True))
        self.arrived(6, k, self.piece(k, y=True, core=True))
        self.arrived(7, k, self.piece(k, y=True, x=True, core=True))

    def wait_send(self):
        for k in range(self.at.planes):
            for kind in range(0 if k else 1, 8):
                sem = (kind, k)
                self.at.copy(self.piece(k), self.piece(k), self.send_sem.at[sem],
                             self.recv_sem.at[sem], dp=self.at.sibling).wait_send()


def gelu_parts(up):
    inner = 0.7978845608028654 * (up + 0.044715 * up * up * up)
    th = jnp.tanh(inner)
    half = 0.5 * (1.0 + th)
    slope = half + 0.5 * up * (1.0 - th * th) * (
        0.7978845608028654 * (1.0 + 3 * 0.044715 * up * up)
    )
    return up * half, slope


def halves(width):
    return (0, slice(0, width // 2), True), (0, slice(width // 2, width), False)


def feed_remote_kernel(
    x_ref, dy_ref, w_hbm, g_attn, z_attn, gain, gains_in,
    branch, d_normed, out_attn, out_up, out_down, out_gains,
    xt, dt, w_buf, g_ff, ff_core, ff_first, ff_second, at_core, at_first, at_second, got_z,
    sums, got_sums, z_sums,
    w_sem, ff_send, ff_recv, at_send, at_recv, z_send, z_recv, sum_send, sum_recv,
):
    width = x_ref.shape[1]
    steps, shard = w_hbm.shape[0], w_hbm.shape[3]
    half = width // 2
    at = Place(steps)
    at.greet()
    attn = Scatter(at, halves(width), g_attn, at_core, at_first, at_second, at_send, at_recv)
    both = (0, slice(0, width), True), (1, slice(0, width), False)
    feed = Scatter(at, both, g_ff, ff_core, ff_first, ff_second, ff_send, ff_recv)
    last = steps - 1

    def z_copy(step, kind):
        return at.copy(ff_second.at[step, kind], got_z.at[kind, step],
                       z_send.at[kind, step], z_recv.at[kind, step], mp=at.along(1 + step))

    def to_z(step):
        feed.after_second(step)
        for kind in range(2):
            z_copy(step, kind).start()

    def w_copy(step, kind):
        slot = lax.rem(step, 2)
        return pltpu.make_async_copy(
            w_hbm.at[at.along(1 + step), :, kind], w_buf.at[slot, kind], w_sem.at[slot, kind]
        )

    def feed_half(step, index):
        cols = slice(half * index, half * index + half)
        slot = lax.rem(step, 2)
        upper = w_buf[slot, 0, :, :, cols].reshape(width, half)
        lower = w_buf[slot, 1, :, :, cols].reshape(width, half)
        value, slope = gelu_parts(nn(x_ref[...], upper))
        hidden = value.astype(BF16)
        d_up = (nn(dy_ref[...], lower) * slope).astype(BF16)
        split = (2, 2, 2, shard, half)
        g_ff[step, 0, :, :, :, :, cols] = nn(xt[...], d_up).astype(BF16).reshape(split)
        g_ff[step, 1, :, :, :, :, cols] = nn(dt[...], hidden).astype(BF16).reshape(split)
        branch[...] += nt(hidden, lower)
        d_normed[...] += nt(d_up, upper)

    attn.start(0)
    for kind in range(2):
        w_copy(0, kind).start()
    xt[...] = x_ref[...].T
    dt[...] = dy_ref[...].T
    branch[...] = jnp.zeros_like(branch)
    d_normed[...] = jnp.zeros_like(d_normed)

    def one_step(step, carry):
        for kind in range(2):
            w_copy(step, kind).wait()

        @pl.when(step + 1 < steps)
        def _():
            for kind in range(2):
                w_copy(step + 1, kind).start()

        feed_half(step, 0)

        @pl.when(step == 0)
        def _():
            attn.after_core(0)

        @pl.when(step >= 1)
        def _():
            feed.after_core(step - 1)

        @pl.when(step >= 2)
        def _():
            to_z(step - 2)

        feed_half(step, 1)
        feed.start(step)

        @pl.when(step == 0)
        def _():
            attn.after_first(0)

        @pl.when(step >= 1)
        def _():
            feed.after_first(step - 1)

        return carry

    lax.fori_loop(0, steps, one_step, 0)

    sums[0] = gains_in[...]
    store_gain(sums.at[0], d_normed[...], x_ref[...], gain[...])

    def sum_copy(stage):
        to = (at.sibling, at.beside, at.above)[stage]
        return at.copy(sums.at[stage], got_sums.at[stage], sum_send.at[stage],
                       sum_recv.at[stage], dp=to)

    def sum_z_copy(k):
        return at.copy(sums.at[3], z_sums.at[at.z], sum_send.at[2 + k], sum_recv.at[2 + k],
                       mp=at.along(k))

    def next_sum(stage):
        sum_copy(stage).wait_recv()
        sums[stage + 1] = sums[stage] + got_sums[stage]

    sum_copy(0).start()
    feed.after_core(last)
    next_sum(0)
    sum_copy(1).start()
    to_z(last - 1)
    next_sum(1)
    sum_copy(2).start()
    for item in range(2):
        cols = attn.items[item][1]
        out_attn[:, cols] = attn.total(0, item) + z_attn[:, cols]
    feed.after_first(last)
    next_sum(2)
    for k in range(1, steps):
        sum_z_copy(k).start()
    z_sums[at.z] = sums[3]
    for kind, out in enumerate((out_up, out_down)):
        total = feed.total(last, kind)
        for step in range(last):
            z_copy(step, kind).wait_recv()
            total = total + got_z[kind, step].astype(F32)
        out[...] = total
    for k in range(1, steps):
        sum_z_copy(k).wait_recv()
    total = z_sums[0]
    for k in range(1, steps):
        total = total + z_sums[k]
    out_gains[...] = total

    attn.wait_send(0)
    for step in range(steps):
        feed.wait_send(step)
    for step in range(last):
        for kind in range(2):
            z_copy(step, kind).wait_send()
    for stage in range(3):
        sum_copy(stage).wait_send()
    for k in range(1, steps):
        sum_z_copy(k).wait_send()


def feed_remote_call(normed, grads, w_ff, g_attn, z_attn, gain, gains):
    rows, width = normed.shape
    steps, _, _, shard, _ = w_ff.shape
    vmem = pl.BlockSpec(memory_space=pltpu.VMEM)
    return pl.pallas_call(
        feed_remote_kernel,
        in_specs=[vmem, vmem, pl.BlockSpec(memory_space=pl.ANY)] + [vmem] * 4,
        out_specs=[vmem] * 6,
        out_shape=[jax.ShapeDtypeStruct((rows, width), F32)] * 2
        + [jax.ShapeDtypeStruct((shard, width), F32)] * 3
        + [jax.ShapeDtypeStruct((8, 128), F32)],
        scratch_shapes=[
            pltpu.VMEM((width, rows), BF16),
            pltpu.VMEM((width, rows), BF16),
            pltpu.VMEM((2, 2, 8, shard, width), BF16),
            pltpu.VMEM((steps, 2, 2, 2, 2, shard, width), BF16),
            pltpu.VMEM((steps, 2, 2, 2, shard, width), BF16),
            pltpu.VMEM((steps, 2, 2, shard, width), BF16),
            pltpu.VMEM((steps, 2, shard, width), BF16),
            pltpu.VMEM((1, 1, 2, 2, shard, width), BF16),
            pltpu.VMEM((1, 1, 2, shard, width), BF16),
            pltpu.VMEM((1, 1, shard, width), BF16),
            pltpu.VMEM((2, steps - 1, shard, width), BF16),
            pltpu.VMEM((4, 8, 128), F32),
            pltpu.VMEM((3, 8, 128), F32),
            pltpu.VMEM((steps, 8, 128), F32),
            pltpu.SemaphoreType.DMA((2, 2)),
            pltpu.SemaphoreType.DMA((3, 2, steps)),
            pltpu.SemaphoreType.DMA((3, 2, steps)),
            pltpu.SemaphoreType.DMA((3, 2, 1)),
            pltpu.SemaphoreType.DMA((3, 2, 1)),
            pltpu.SemaphoreType.DMA((2, steps - 1)),
            pltpu.SemaphoreType.DMA((2, steps - 1)),
            pltpu.SemaphoreType.DMA((6,)),
            pltpu.SemaphoreType.DMA((6,)),
        ],
        compiler_params=pltpu.CompilerParams(
            collective_id=0, has_side_effects=True, vmem_limit_bytes=VMEM
        ),
        cost_estimate=pl.CostEstimate(
            flops=12 * rows * width * width * steps,
            bytes_accessed=4 * steps * width * width * 2,
            transcendentals=rows * width * steps,
        ),
        name="feed_forward_scatter",
    )(normed, grads, w_ff, g_attn, z_attn, gain, gains)


def iota(shape, axis):
    return lax.broadcasted_iota(jnp.int32, shape, axis)


def source_of(index, start, total):
    rest = index - BIG
    other = jnp.where(rest < start, rest, rest + MOST)
    held = jnp.where(index < MOST, start + index, -1)
    return jnp.where((rest >= 0) & (rest < total - MOST), other, held)


def store_gain(out, d_normed, normed, gain):
    total = jnp.sum(d_normed * normed.astype(F32), axis=0, keepdims=True) / gain
    for row in range(total.shape[1] // 128):
        out[row:row + 1] += total[:, 128 * row:128 * row + 128]


def prepare(
    me, part, ids, pieces, x_ref, dy_ref, xt, dt, feat_q, feat_k, pt, d_normed, branch, g_gains
):
    mp = ids.shape[1]
    total = mp * part
    numbers = ids[me]
    start = jnp.zeros((1, 1), jnp.int32)
    for image in range(IMAGES):
        count = jnp.sum((numbers == image).astype(F32), axis=(0, 1), keepdims=True)
        ahead = jnp.sum(
            ((numbers >= 0) & (numbers < image)).astype(F32), axis=(0, 1), keepdims=True
        )
        start = start + jnp.where(count == MOST, ahead, 0.0).astype(jnp.int32)
    column = source_of(iota((ROWS, 1), 0), start, total)
    line = source_of(iota((1, ROWS), 1), start, total)
    x_sum, dy_sum, feats = 0.0, 0.0, 0.0
    for k, piece in enumerate(pieces):
        chunk = lax.rem(me - k + mp, mp)
        offset = iota((1, PIECE), 1)
        pos = jnp.where(offset < part, chunk * part + offset, -2)
        pick = (column == pos).astype(F32).astype(BF16)
        offset = iota((PIECE, 1), 0)
        pos = jnp.where(offset < part, chunk * part + offset, -2)
        pt[k] = (line == pos).astype(F32).astype(BF16)
        x_sum = x_sum + nn(pick, piece[0][...])
        dy_sum = dy_sum + nn(pick, piece[1][...])
        marks = (iota((128, 1), 0) - HD == ids[me, pl.ds(chunk, 1), :]).astype(F32)
        feats = feats + nt(pick, marks.astype(BF16))
    x = x_sum.astype(BF16)
    dy = dy_sum.astype(BF16)
    x_ref[...] = x
    dy_ref[...] = dy
    xt[...] = x.T
    dt[...] = dy.T
    lane = iota((1, 128), 1)
    feat_q[...] = (feats * 128.0).astype(BF16)
    marked = (lane >= HD) & (lane < HD + IMAGES)
    feat_k[...] = jnp.where(marked, (feats - 1.0) * 256.0, 0.0).astype(BF16)
    d_normed[...] = jnp.zeros_like(d_normed)
    branch[...] = jnp.zeros_like(branch)
    g_gains[...] = jnp.zeros_like(g_gains)


def attention_chunk(
    weights, gain, x_ref, dy_ref, xt, dt, feat_q, feat_k, raw, d_raw, d_att, att,
    d_normed, branch, g_gains, store, poll,
):
    raw[...] = nn(x_ref[...], weights(slice(0, 640)))
    d_att[...] = nn(dy_ref[...], weights(slice(512, 768)))
    lane = iota((1, 128), 1)
    low = lane < HD
    same = (iota((128, 128), 0) // HD == iota((128, 128), 1) // HD).astype(F32)
    mean_of = (same * (1.0 / HD)).astype(BF16)

    def half_mean(value):
        return nn(value.astype(BF16), mean_of)

    d_gain = jnp.zeros((1, 128), F32)
    for head in range(3):
        qk = raw[:, 128 * head:128 * head + 128]
        high = qk.astype(BF16)
        mean = nn(high, mean_of) + half_mean(qk - high.astype(F32))
        centered = qk - mean
        spread = lax.rsqrt(half_mean(centered * centered) + 1e-6)
        unit = centered * spread
        rounded = (unit * gain).astype(BF16).astype(F32)
        q_aug = jnp.where(low, rounded * 0.125, feat_q[...].astype(F32)).astype(BF16)
        k_aug = jnp.where(low, pltpu.roll(rounded, HD, 1), feat_k[...].astype(F32)).astype(BF16)
        v_tile = 384 + 128 * (head // 2)
        v = raw[:, v_tile:v_tile + 128]
        if head == 1:
            v = pltpu.roll(v, HD, 1)
        one = ((lane == HD) | (lane == HD + 1)).astype(F32)
        v_aug = jnp.where(low, v, one).astype(BF16)
        a_tile = 128 * ((head + 1) // 2)
        da = d_att[:, a_tile:a_tile + 128]
        if head != 1:
            da = pltpu.roll(da, HD, 1)
        q_t = q_aug.astype(F32).T.astype(BF16)
        d_queries, attended, d_keys, d_values = [], [], [], []
        for base, count in ((0, BIG), (BIG, REST)):
            keys = k_aug[base:base + count]
            values = v_aug[base:base + count]
            dk_t = jnp.zeros((128, count), F32)
            dv_t = jnp.zeros((128, count), F32)
            for row in range(base, base + count, 256):
                rows = slice(row, row + 256)
                prob = jnp.exp(nt(q_aug[rows], keys))
                prob_low = prob.astype(BF16)
                gathered = nn(prob_low, values)
                inverse = 1.0 / gathered[:, HD:HD + 1]
                out = jnp.where(low, gathered * inverse, 0.0)
                attended.append(out)
                scaled = jnp.where(low, da[rows] * inverse, 0.0).astype(BF16).astype(F32)
                dot = jnp.sum(scaled * out, axis=-1, keepdims=True)
                dot_high = dot.astype(BF16).astype(F32)
                d_aug = jnp.where(
                    lane == HD, -dot_high, jnp.where(lane == HD + 1, dot_high - dot, scaled)
                )
                d_low = d_aug.astype(BF16)
                d_score = (prob * nt(d_low, values)).astype(BF16)
                d_queries.append(nn(d_score, keys))
                dk_t = dk_t + nn(q_t[:, rows], d_score)
                dv_t = dv_t + nn(d_aug.T.astype(BF16), prob_low)
            d_keys.append(dk_t.T)
            d_values.append(dv_t.T)
        d_query = jnp.concatenate(d_queries, axis=0) * 0.125
        d_key = jnp.concatenate(d_keys, axis=0)
        d_value = jnp.concatenate(d_values, axis=0)
        attend = jnp.concatenate(attended, axis=0)
        d_qk = jnp.where(low, d_query, pltpu.roll(d_key, HD, 1))
        d_gain = d_gain + jnp.sum(d_qk * unit, axis=0, keepdims=True)
        scaled = d_qk * gain
        d_qk = spread * (scaled - half_mean(scaled) - unit * half_mean(scaled * unit))
        d_raw[:, 128 * head:128 * head + 128] = d_qk.astype(BF16)
        if head == 0:
            first_value = d_value
            att[:, 0:128] = jnp.where(low, 0.0, pltpu.roll(attend, HD, 1)).astype(BF16)
        elif head == 1:
            both = jnp.where(low, first_value, pltpu.roll(d_value, HD, 1))
            d_raw[:, 384:512] = both.astype(BF16)
            first_att = attend
        else:
            d_raw[:, 512:640] = jnp.where(low, d_value, 0.0).astype(BF16)
            both = jnp.where(low, first_att, pltpu.roll(attend, HD, 1))
            att[:, 128:256] = both.astype(BF16)
        poll(head)
    g_gains[6:7] += d_gain
    d_projected = d_raw[...]
    attended = att[...]
    d_normed[...] += nt(d_projected, weights(slice(0, 640)))
    branch[...] += nt(attended, weights(slice(512, 768)))
    left = nn(xt[...], d_projected)
    right = nn(dt[...], attended)
    store(slice(0, 512), left[:, :512].astype(BF16))
    store(slice(512, 640), (left[:, 512:] + right[:, :128]).astype(BF16))
    store(slice(640, 768), right[:, 128:].astype(BF16))


def take_back(outs, pt, x_ref, norm_gain, d_normed, branch, g_gains):
    store_gain(g_gains, d_normed[...], x_ref[...], norm_gain[...])
    d_rows = d_normed[...].astype(BF16)
    b_rows = branch[...].astype(BF16)
    for k, out in enumerate(outs):
        out[0] = nn(pt[k], d_rows).astype(BF16)
        out[1] = nn(pt[k], b_rows).astype(BF16)


def attention_kernel(
    part, place, own_x, own_dy, in1, in2, in3, ids, gains, norm_gain, weights,
    out0, out1, out2, out3, g_weights, g_gains,
    x_ref, dy_ref, xt, dt, feat_q, feat_k, pt, raw, d_raw, d_att, att, d_normed, branch,
):
    step = pl.program_id(0)

    @pl.when(step == 0)
    def _():
        pieces = [(own_x.at[0], own_dy.at[0])] + [(got.at[0], got.at[1]) for got in (in1, in2, in3)]
        prepare(place[0], part, ids, pieces, x_ref, dy_ref, xt, dt, feat_q, feat_k, pt,
                d_normed, branch, g_gains)

    def store(cols, value):
        g_weights[0, :, cols] = value

    attention_chunk(
        lambda cols: weights[0, :, cols], gains[...], x_ref, dy_ref, xt, dt, feat_q, feat_k,
        raw, d_raw, d_att, att, d_normed, branch, g_gains, store, lambda head: None,
    )

    @pl.when(step == pl.num_programs(0) - 1)
    def _():
        take_back((out0, out1, out2, out3), pt, x_ref, norm_gain, d_normed, branch, g_gains)


def attention_call(place, part, normed, grads, received, ids, gains, norm_gain, weights):
    width = normed.shape[-1]
    chunks = weights.shape[0]
    mp = ids.shape[1]
    own = pl.BlockSpec((1, PIECE, width), lambda m, place: (0, 0, 0))
    pair = pl.BlockSpec((2, PIECE, width), lambda m, place: (0, 0, 0))
    chunk = pl.BlockSpec((1, width, width), lambda m, place: (m, 0, 0))
    line = pl.BlockSpec((1, 128), lambda m, place: (0, 0))
    return pl.pallas_call(
        functools.partial(attention_kernel, part),
        grid_spec=pltpu.PrefetchScalarGridSpec(
            num_scalar_prefetch=1,
            grid=(chunks,),
            in_specs=[own, own, pair, pair, pair,
                      pl.BlockSpec(ids.shape, lambda m, place: (0, 0, 0)),
                      line, pl.BlockSpec((1, width), lambda m, place: (0, 0)), chunk],
            out_specs=[pair] * 4 + [chunk, pl.BlockSpec((8, 128), lambda m, place: (0, 0))],
            scratch_shapes=[
                pltpu.VMEM((ROWS, width), BF16),
                pltpu.VMEM((ROWS, width), BF16),
                pltpu.VMEM((width, ROWS), BF16),
                pltpu.VMEM((width, ROWS), BF16),
                pltpu.VMEM((ROWS, 128), BF16),
                pltpu.VMEM((ROWS, 128), BF16),
                pltpu.VMEM((mp, PIECE, ROWS), BF16),
                pltpu.VMEM((ROWS, 640), F32),
                pltpu.VMEM((ROWS, 640), BF16),
                pltpu.VMEM((ROWS, 256), F32),
                pltpu.VMEM((ROWS, 256), BF16),
                pltpu.VMEM((ROWS, width), F32),
                pltpu.VMEM((ROWS, width), F32),
            ],
        ),
        out_shape=[jax.ShapeDtypeStruct((2, PIECE, width), BF16)] * 4
        + [jax.ShapeDtypeStruct(weights.shape, BF16), jax.ShapeDtypeStruct((8, 128), F32)],
        compiler_params=pltpu.CompilerParams(vmem_limit_bytes=VMEM),
        cost_estimate=pl.CostEstimate(
            flops=60_000_000_000, bytes_accessed=4 * chunks * width * width,
            transcendentals=ROWS * ROWS * 12,
        ),
        name="attention",
    )(place, normed, grads, *received, ids, gains, norm_gain, weights)


def front_kernel(
    tok, cot, ids, gains, norm_gain, w_attn, w_feed,
    normed, grads, out0, out1, out2, out3, w_ff, g_last, z_attn, g_gains,
    got_rows, w_full, g_buf, at_core, at_first, at_second, got_z,
    x_ref, dy_ref, xt, dt, feat_q, feat_k, pt, raw, d_raw, d_att, att, d_normed, branch,
    row_send, row_recv, wa_send, wa_recv, wf_send, wf_recv, own_sem, at_send, at_recv,
    z_send, z_recv,
):
    count, part, width = tok.shape
    shard = w_attn.shape[0]
    at = Place(count)
    at.greet()
    gather = Gather(at, w_attn, w_full, wa_send, wa_recv)
    gather_ff = Gather(at, w_feed, w_ff, wf_send, wf_recv)
    scatter = Scatter(at, halves(width), g_buf, at_core, at_first, at_second, at_send, at_recv)
    own_ff = pltpu.make_async_copy(w_feed, gather_ff.piece(0), own_sem)

    def row_copy(kind, k):
        src = (normed, grads)[kind].at[k]
        return at.copy(src, got_rows.at[k - 1, kind], row_send.at[kind, k - 1],
                       row_recv.at[kind, k - 1], mp=at.along(k))

    gather.start()
    own_ff.start()
    w_full[at.z, at.y, at.x, at.core] = w_attn[...]
    gather.spread(0)
    gain = norm_gain[...]
    for k in (1, 3, 2, 0):
        sequence = at.along(k)
        x = tok[sequence].astype(F32)
        centered = x - jnp.mean(x, axis=-1, keepdims=True)
        spread = lax.rsqrt(jnp.mean(centered * centered, axis=-1, keepdims=True) + 1e-6)
        pad = jnp.zeros((PIECE - part, width), BF16)
        normed[k, :part] = (centered * spread * gain).astype(BF16)
        normed[k, part:] = pad
        if k:
            row_copy(0, k).start()
        grads[k, :part] = cot[sequence]
        grads[k, part:] = pad
    gather.spread(1)
    gather.spread(3)
    gather.forward(0)
    gather.spread(2)
    own_ff.wait()
    gather_ff.spread(0)
    gather.forward(1)
    gather.across(0)
    gather.forward(3)
    for k in (1, 3, 2):
        row_copy(0, k).wait_recv()
    for k in (1, 3, 2):
        row_copy(1, k).start()
    gather.across(1)
    gather.forward(2)
    gather.across(3)
    gather.across(2)
    for k in range(count):
        gather.last(k)
    for k in (1, 3, 2):
        row_copy(1, k).wait_recv()
    gather_ff.start()
    pieces = [(normed.at[0], grads.at[0])]
    pieces += [(got_rows.at[k, 0], got_rows.at[k, 1]) for k in range(count - 1)]
    prepare(at.z, part, ids, pieces, x_ref, dy_ref, xt, dt, feat_q, feat_k, pt,
            d_normed, branch, g_gains)

    def z_copy(step):
        return at.copy(at_second.at[step, 0], got_z.at[step], z_send.at[step], z_recv.at[step],
                       mp=at.along(1 + step))

    def one_step(step, carry):
        chunk = at.along(1 + step)

        def weights(cols):
            return w_full[chunk, :, :, :, :, cols].reshape(width, cols.stop - cols.start)

        def store(cols, value):
            split = (2, 2, 2, shard, cols.stop - cols.start)
            g_buf[step, 0, :, :, :, :, cols] = value.reshape(split)

        def poll(head):
            @pl.when(step >= 1)
            def _():
                if head == 0:
                    scatter.after_core(step - 1)
                elif head == 1:
                    scatter.after_first(step - 1)
                else:
                    scatter.after_second(step - 1)
                    z_copy(step - 1).start()

            @pl.when(step == 0)
            def _():
                if head == 0:
                    gather_ff.spread(1)
                    gather_ff.forward(0)
                elif head == 1:
                    gather_ff.spread(3)
                    gather_ff.across(0)
                else:
                    gather_ff.spread(2)
                    gather_ff.forward(1)

            @pl.when(step == 1)
            def _():
                if head == 0:
                    gather_ff.forward(3)
                    gather_ff.across(1)
                elif head == 1:
                    gather_ff.forward(2)
                    gather_ff.across(3)
                else:
                    gather_ff.across(2)

        attention_chunk(
            weights, gains[...], x_ref, dy_ref, xt, dt, feat_q, feat_k,
            raw, d_raw, d_att, att, d_normed, branch, g_gains, store, poll,
        )

        @pl.when(step < count - 1)
        def _():
            scatter.start(step)

        return carry

    lax.fori_loop(0, count, one_step, 0)
    take_back((out0, out1, out2, out3), pt, x_ref, norm_gain, d_normed, branch, g_gains)
    g_last[...] = g_buf[count - 1:]
    total = 0.0
    for step in range(count - 1):
        z_copy(step).wait_recv()
        total = total + got_z[step].astype(F32)
    z_attn[...] = total
    for k in range(count):
        gather_ff.last(k)

    gather.wait_send()
    gather_ff.wait_send()
    for k in range(1, count):
        for kind in range(2):
            row_copy(kind, k).wait_send()
    for step in range(count - 1):
        scatter.wait_send(step)
        z_copy(step).wait_send()


def front_call(tokens, cotangent, ids, gains, norm_gain, w_attn, w_feed):
    count, part, width = tokens.shape
    shard = w_attn.shape[0]
    vmem = pl.BlockSpec(memory_space=pltpu.VMEM)
    hbm = pl.BlockSpec(memory_space=pl.ANY)
    rows = jax.ShapeDtypeStruct((count, PIECE, width), BF16)
    return pl.pallas_call(
        front_kernel,
        in_specs=[vmem] * 6 + [hbm],
        out_specs=[vmem] * 6 + [hbm] + [vmem] * 3,
        out_shape=[rows, rows]
        + [jax.ShapeDtypeStruct((2, PIECE, width), BF16)] * 4
        + [
            jax.ShapeDtypeStruct((count, 2, 2, 2, 2, shard, width), BF16),
            jax.ShapeDtypeStruct((1, 1, 2, 2, 2, shard, width), BF16),
            jax.ShapeDtypeStruct((shard, width), F32),
            jax.ShapeDtypeStruct((8, 128), F32),
        ],
        scratch_shapes=[
            pltpu.VMEM((count - 1, 2, PIECE, width), BF16),
            pltpu.VMEM((count, 2, 2, 2, shard, width), BF16),
            pltpu.VMEM((count, 1, 2, 2, 2, shard, width), BF16),
            pltpu.VMEM((count - 1, 1, 2, 2, shard, width), BF16),
            pltpu.VMEM((count - 1, 1, 2, shard, width), BF16),
            pltpu.VMEM((count - 1, 1, shard, width), BF16),
            pltpu.VMEM((count - 1, shard, width), BF16),
            pltpu.VMEM((ROWS, width), BF16),
            pltpu.VMEM((ROWS, width), BF16),
            pltpu.VMEM((width, ROWS), BF16),
            pltpu.VMEM((width, ROWS), BF16),
            pltpu.VMEM((ROWS, 128), BF16),
            pltpu.VMEM((ROWS, 128), BF16),
            pltpu.VMEM((count, PIECE, ROWS), BF16),
            pltpu.VMEM((ROWS, 640), F32),
            pltpu.VMEM((ROWS, 640), BF16),
            pltpu.VMEM((ROWS, 256), F32),
            pltpu.VMEM((ROWS, 256), BF16),
            pltpu.VMEM((ROWS, width), F32),
            pltpu.VMEM((ROWS, width), F32),
            pltpu.SemaphoreType.DMA((2, count - 1)),
            pltpu.SemaphoreType.DMA((2, count - 1)),
            pltpu.SemaphoreType.DMA((8, count)),
            pltpu.SemaphoreType.DMA((8, count)),
            pltpu.SemaphoreType.DMA((8, count)),
            pltpu.SemaphoreType.DMA((8, count)),
            pltpu.SemaphoreType.DMA,
            pltpu.SemaphoreType.DMA((3, 2, count - 1)),
            pltpu.SemaphoreType.DMA((3, 2, count - 1)),
            pltpu.SemaphoreType.DMA((count - 1,)),
            pltpu.SemaphoreType.DMA((count - 1,)),
        ],
        compiler_params=pltpu.CompilerParams(
            collective_id=1, has_side_effects=True, vmem_limit_bytes=VMEM
        ),
        name="front",
    )(tokens, cotangent, ids, gains, norm_gain, w_attn, w_feed)


def finish_kernel(
    place, tok, cot, gain, branch, d_ff, ret0, ret1, ret2, ret3, output, input_grad
):
    step = pl.program_id(0)
    part = tok.shape[1]

    for index, back in enumerate((ret0, ret1, ret2, ret3)):

        @pl.when(step == index)
        def _():
            x = tok[0].astype(F32)
            output[0] = (x + (branch[0] + back[1].astype(F32))[:part]).astype(BF16)
            d_normed = (d_ff[0] + back[0].astype(F32))[:part]
            centered = x - jnp.mean(x, axis=-1, keepdims=True)
            spread = lax.rsqrt(jnp.mean(centered * centered, axis=-1, keepdims=True) + 1e-6)
            unit = centered * spread
            scaled = d_normed * gain[...]
            d_x = spread * (
                scaled
                - jnp.mean(scaled, axis=-1, keepdims=True)
                - unit * jnp.mean(scaled * unit, axis=-1, keepdims=True)
            )
            input_grad[0] = cot[0].astype(F32) + d_x


def finish_call(place, tokens, cotangent, gain, branch, d_ff, returned):
    count, part, width = tokens.shape
    block = pl.BlockSpec(
        (1, part, width), lambda k, place: (lax.rem(place[0] + k, count), 0, 0)
    )
    padded = pl.BlockSpec((1, PIECE, width), lambda k, place: (k, 0, 0))
    pair = pl.BlockSpec((2, PIECE, width), lambda k, place: (0, 0, 0))
    line = pl.BlockSpec((1, width), lambda k, place: (0, 0))
    return pl.pallas_call(
        finish_kernel,
        grid_spec=pltpu.PrefetchScalarGridSpec(
            num_scalar_prefetch=1,
            grid=(count,),
            in_specs=[block, block, line, padded, padded] + [pair] * 4,
            out_specs=[block, block],
        ),
        out_shape=[
            jax.ShapeDtypeStruct(tokens.shape, BF16),
            jax.ShapeDtypeStruct(tokens.shape, F32),
        ],
        compiler_params=pltpu.CompilerParams(vmem_limit_bytes=VMEM),
        name="finish",
    )(place, tokens, cotangent, gain, branch, d_ff, *returned)


def pack_attention(w_qkv, w_proj):
    rows, wide = w_qkv.shape[1:]
    heads = wide // HD
    qk = w_qkv[:2].reshape(2, rows, heads, HD).transpose(1, 2, 0, 3).reshape(rows, 2 * wide)
    return jnp.concatenate([qk, w_qkv[2], w_proj.T], axis=1)


def unpack_attention(grad, wide):
    rows = grad.shape[0]
    heads = wide // HD
    qk = grad[:, :2 * wide].reshape(rows, heads, 2, HD).transpose(2, 0, 1, 3)
    qk = qk.reshape(2, rows, wide)
    g_qkv = jnp.concatenate([qk, grad[None, :, 2 * wide:3 * wide]], axis=0)
    return g_qkv, grad[:, 3 * wide:].T


def body(
    dp, mp, tokens, w_qkv, w_up, w_proj, w_down, norm_gain, query_gain, key_gain, image_ids, cotangent
):
    micro, seqs, part, width = tokens.shape
    count = micro * seqs
    shard = w_up.shape[0]
    me = lax.axis_index("mp")
    place = me.astype(jnp.int32)[None]
    both = ("mp", "dp")
    tok = tokens.reshape(count, part, width)
    cot = cotangent.reshape(count, part, width)
    gain = norm_gain.reshape(1, width)
    ids = image_ids.reshape(count, mp, part)
    ids = jnp.pad(ids, ((0, 0), (0, 0), (0, PIECE - part)), constant_values=-1)
    gains = jnp.concatenate([query_gain, key_gain]).reshape(1, 2 * HD)
    w_attn = pack_attention(w_qkv, w_proj)
    w_ff = jnp.stack([w_up, w_down.T])

    def send_back(outs):
        return [outs[0]] + [
            lax.ppermute(out, "mp", [(i, (i - k) % mp) for i in range(mp)])
            for k, out in enumerate(outs[1:], 1)
        ]

    if (dp, mp) == (8, 4):
        normed, grads, *outs, w_ff, g_attn, z_attn, g_gains = front_call(
            tok, cot, ids, gains, gain, w_attn, w_ff
        )
        returned = send_back(outs)
        branch, d_ff, g_attn, g_up, g_down, g_gains = feed_remote_call(
            normed.reshape(count * PIECE, width), grads.reshape(count * PIECE, width),
            w_ff.reshape(mp, dp, 2, shard, width), g_attn, z_attn, gain, g_gains,
        )
    else:
        w_attn = lax.all_gather(w_attn, both).reshape(mp, width, width)
        w_ff = lax.all_gather(w_ff, both).reshape(mp, dp, 2, shard, width)
        normed, grads, *sends = norm_call(place, tok, cot, gain)
        received = [
            lax.ppermute(send, "mp", [(i, (i + k) % mp) for i in range(mp)])
            for k, send in enumerate(sends, 1)
        ]
        *outs, g_attn, g_gains = attention_call(
            place, part, normed, grads, received, ids, gains, gain, w_attn
        )
        returned = send_back(outs)
        flat_normed = normed.reshape(count * PIECE, width)
        branch, d_ff, g_up, g_down = feed_call(
            flat_normed, grads.reshape(count * PIECE, width),
            w_ff[:, :, 0].reshape(mp, width, width), w_ff[:, :, 1].reshape(mp, width, width),
        )
        g_attn, g_up, g_down = (
            lax.psum_scatter(
                grad.reshape(-1, shard, width), both, scatter_dimension=0
            ).astype(F32)
            for grad in (g_attn, g_up, g_down)
        )
        own = jnp.sum(d_ff * flat_normed.astype(F32), axis=0) / norm_gain
        g_gains = g_gains.at[:width // 128].add(own.reshape(-1, 128))
        g_gains = lax.psum(g_gains, both)
    output, input_grad = finish_call(
        place, tok, cot, gain,
        branch.reshape(count, PIECE, width), d_ff.reshape(count, PIECE, width), returned,
    )
    g_qkv, g_proj = unpack_attention(g_attn, w_qkv.shape[2])
    g_norm = g_gains[:width // 128].reshape(width)
    g_gains = g_gains[6]
    return (
        output.reshape(tokens.shape),
        input_grad.reshape(tokens.shape),
        g_qkv,
        g_up,
        g_proj,
        g_down.T,
        g_norm,
        g_gains[:HD],
        g_gains[HD:],
    )


def solution(mesh):
    rows = P(None, "dp", "mp", None)
    weights = (P(None, "dp", "mp"), P("dp", "mp"), P("mp", "dp"), P("mp", "dp"))
    gains = (P(), P(), P())
    return jax.shard_map(
        functools.partial(body, mesh.shape["dp"], mesh.shape["mp"]),
        mesh=mesh,
        in_specs=(rows,) + weights + gains + (P(None, "dp", None), rows),
        out_specs=(rows, rows) + weights + gains,
        check_vma=False,
    )
```

```python
import functools

import jax
import jax.numpy as jnp
from jax import lax
from jax.experimental import pallas as pl
from jax.experimental.pallas import tpu as pltpu
from jax.sharding import PartitionSpec as P

HD = 64
MOST = 709
IMAGES = 8
PIECE = 240
BIG = 768
REST = 256
ROWS = BIG + REST
VMEM = 60 * 1024 * 1024
FRONT_VMEM = 63 * 1024 * 1024
F32 = jnp.float32
BF16 = jnp.bfloat16


def nn(left, right):
    return lax.dot_general(left, right, (((1,), (0,)), ((), ())), preferred_element_type=F32)


def nt(left, right):
    return lax.dot_general(left, right, (((1,), (1,)), ((), ())), preferred_element_type=F32)


def norm_kernel(place, tok, cot, gain, normed, grads, send1, send2, send3):
    step = pl.program_id(0)
    part = tok.shape[1]
    x = tok[0].astype(F32)
    centered = x - jnp.mean(x, axis=-1, keepdims=True)
    spread = lax.rsqrt(jnp.mean(centered * centered, axis=-1, keepdims=True) + 1e-6)
    value = (centered * spread * gain[...]).astype(BF16)
    normed[...] = jnp.zeros_like(normed)
    grads[...] = jnp.zeros_like(grads)
    normed[0, :part] = value
    grads[0, :part] = cot[0]
    for index, send in ((1, send1), (2, send2), (3, send3)):

        @pl.when(step == index)
        def _():
            send[0] = normed[0]
            send[1] = grads[0]


def norm_call(place, tokens, cotangent, gain):
    count, part, width = tokens.shape
    block = lambda k, place: (lax.rem(place[0] + k, count), 0, 0)
    fixed = lambda k, place: (0, 0, 0)
    return pl.pallas_call(
        norm_kernel,
        grid_spec=pltpu.PrefetchScalarGridSpec(
            num_scalar_prefetch=1,
            grid=(count,),
            in_specs=[
                pl.BlockSpec((1, part, width), block),
                pl.BlockSpec((1, part, width), block),
                pl.BlockSpec((1, width), lambda k, place: (0, 0)),
            ],
            out_specs=[pl.BlockSpec((1, PIECE, width), lambda k, place: (k, 0, 0))] * 2
            + [pl.BlockSpec((2, PIECE, width), fixed)] * 3,
        ),
        out_shape=[jax.ShapeDtypeStruct((count, PIECE, width), BF16)] * 2
        + [jax.ShapeDtypeStruct((2, PIECE, width), BF16)] * 3,
        compiler_params=pltpu.CompilerParams(vmem_limit_bytes=VMEM),
        name="norm_rows",
    )(place, tokens, cotangent, gain)


def feed_kernel(normed, grads, w_up, w_down, branch, d_normed, g_up, g_down, xt, dt):
    step = pl.program_id(0)
    x = normed[...]
    dy = grads[...]

    @pl.when(step == 0)
    def _():
        xt[...] = x.T
        dt[...] = dy.T

    up = nn(x, w_up[0])
    value, slope = gelu_parts(up)
    hidden = value.astype(BF16)
    d_up = (nn(dy, w_down[0]) * slope).astype(BF16)
    g_up[0] = nn(xt[...], d_up).astype(BF16)
    g_down[0] = nn(dt[...], hidden).astype(BF16)
    out = nt(hidden, w_down[0])
    back = nt(d_up, w_up[0])

    @pl.when(step == 0)
    def _():
        branch[...] = out
        d_normed[...] = back

    @pl.when(step > 0)
    def _():
        branch[...] += out
        d_normed[...] += back


def feed_call(normed, grads, w_up, w_down):
    rows, width = normed.shape
    chunks, _, hidden = w_up.shape
    whole = pl.BlockSpec((rows, width), lambda m: (0, 0))
    chunk = pl.BlockSpec((1, width, hidden), lambda m: (m, 0, 0))
    return pl.pallas_call(
        feed_kernel,
        grid=(chunks,),
        in_specs=[whole, whole, chunk, chunk],
        out_specs=[whole, whole, chunk, chunk],
        out_shape=[jax.ShapeDtypeStruct((rows, width), F32)] * 2
        + [jax.ShapeDtypeStruct(w_up.shape, BF16)] * 2,
        scratch_shapes=[pltpu.VMEM((width, rows), BF16)] * 2,
        compiler_params=pltpu.CompilerParams(vmem_limit_bytes=VMEM),
        cost_estimate=pl.CostEstimate(
            flops=12 * rows * width * hidden * chunks,
            bytes_accessed=4 * chunks * width * hidden * 2,
            transcendentals=rows * hidden * chunks,
        ),
        name="feed_forward",
    )(normed, grads, w_up, w_down)


class Place:
    def __init__(self, planes):
        d = lax.axis_index("dp")
        self.z = lax.axis_index("mp")
        self.d, self.planes = d, planes
        self.core, self.x, self.y = d % 2, (d // 2) % 2, d // 4
        self.sibling = d + 1 - 2 * self.core
        self.beside = d + 2 - 4 * self.x
        self.above = d + 4 - 8 * self.y

    def along(self, k):
        return lax.rem(self.z + k + self.planes, self.planes)

    def copy(self, src, dst, send, recv, dp=None, mp=None):
        return pltpu.make_async_remote_copy(
            src_ref=src, dst_ref=dst, send_sem=send, recv_sem=recv,
            device_id={"dp": self.d if dp is None else dp, "mp": self.z if mp is None else mp},
            device_id_type=pl.DeviceIdType.MESH,
        )

    def greet(self):
        barrier = pltpu.get_barrier_semaphore()
        for other in (self.sibling, self.beside, self.above):
            pl.semaphore_signal(barrier, 1, device_id={"dp": other, "mp": self.z},
                                device_id_type=pl.DeviceIdType.MESH)
        for k in range(1, self.planes):
            pl.semaphore_signal(barrier, 1, device_id={"dp": self.d, "mp": self.along(k)},
                                device_id_type=pl.DeviceIdType.MESH)
        pl.semaphore_wait(barrier, self.planes + 2)


class Scatter:
    def __init__(self, at, items, src, got_core, got_first, got_second, send_sem, recv_sem):
        self.at, self.items, self.src = at, items, src
        self.got_core, self.got_first, self.got_second = got_core, got_first, got_second
        self.send_sem, self.recv_sem = send_sem, recv_sem

    def copy(self, stage, step, item):
        at = self.at
        kind, cols, x_first = self.items[item]
        if stage == 0:
            src = self.src.at[step, kind, :, :, 1 - at.core, :, cols]
            dst = self.got_core.at[step, kind, :, :, :, cols]
            to = at.sibling
        elif stage == 1:
            if x_first:
                src = self.got_core.at[step, kind, :, 1 - at.x, :, cols]
            else:
                src = self.got_core.at[step, kind, 1 - at.y, :, :, cols]
            dst = self.got_first.at[step, kind, :, :, cols]
            to = at.beside if x_first else at.above
        else:
            src = self.got_first.at[step, kind, 1 - at.y if x_first else 1 - at.x, :, cols]
            dst = self.got_second.at[step, kind, :, cols]
            to = at.above if x_first else at.beside
        sem = (stage, item, step)
        return at.copy(src, dst, self.send_sem.at[sem], self.recv_sem.at[sem], dp=to)

    def start(self, step):
        for item in range(len(self.items)):
            self.copy(0, step, item).start()

    def after_core(self, step):
        for item, (kind, cols, _) in enumerate(self.items):
            self.copy(0, step, item).wait_recv()
            for row in ((0, 0), (0, 1), (1, 0), (1, 1)):
                own = self.src[(step, kind, *row, self.at.core, slice(None), cols)]
                to = (step, kind, *row, slice(None), cols)
                total = own.astype(F32) + self.got_core[to].astype(F32)
                self.got_core[to] = total.astype(BF16)
            self.copy(1, step, item).start()

    def after_first(self, step):
        for item, (kind, cols, x_first) in enumerate(self.items):
            self.copy(1, step, item).wait_recv()
            for row in range(2):
                if x_first:
                    own = self.got_core[step, kind, row, self.at.x, :, cols]
                else:
                    own = self.got_core[step, kind, self.at.y, row, :, cols]
                total = own.astype(F32) + self.got_first[step, kind, row, :, cols].astype(F32)
                self.got_first[step, kind, row, :, cols] = total.astype(BF16)
            self.copy(2, step, item).start()

    def total(self, step, item):
        kind, cols, x_first = self.items[item]
        self.copy(2, step, item).wait_recv()
        own = self.got_first[step, kind, self.at.y if x_first else self.at.x, :, cols]
        return own.astype(F32) + self.got_second[step, kind, :, cols].astype(F32)

    def after_second(self, step):
        for item, (kind, cols, _) in enumerate(self.items):
            self.got_second[step, kind, :, cols] = self.total(step, item).astype(BF16)

    def wait_send(self, step):
        for item in range(len(self.items)):
            for stage in range(3):
                self.copy(stage, step, item).wait_send()


class Gather:
    def __init__(self, at, shard, full, send_sem, recv_sem):
        self.at, self.shard, self.full = at, shard, full
        self.send_sem, self.recv_sem = send_sem, recv_sem

    def piece(self, k, y=False, x=False, core=False):
        at = self.at
        return self.full.at[at.along(-k), 1 - at.y if y else at.y, 1 - at.x if x else at.x,
                            1 - at.core if core else at.core]

    def move(self, kind, k, src, **to):
        sem = (kind, k)
        self.at.copy(src, src, self.send_sem.at[sem], self.recv_sem.at[sem], **to).start()

    def arrived(self, kind, k, ref):
        sem = (kind, k)
        self.at.copy(ref, ref, self.send_sem.at[sem], self.recv_sem.at[sem],
                     dp=self.at.sibling).wait_recv()

    def start(self):
        for k in range(1, self.at.planes):
            sem = (0, k)
            self.at.copy(self.shard, self.piece(0), self.send_sem.at[sem], self.recv_sem.at[sem],
                         mp=self.at.along(k)).start()

    def spread(self, k):
        at = self.at
        src = self.piece(k)
        if k:
            self.arrived(0, k, src)
        self.move(1, k, src, dp=at.beside)
        self.move(2, k, src, dp=at.above)
        self.move(3, k, src, dp=at.sibling)

    def forward(self, k):
        at = self.at
        from_x, from_y = self.piece(k, x=True), self.piece(k, y=True)
        self.arrived(1, k, from_x)
        if k % 2 == 0:
            self.move(5, k, from_x, dp=at.above)
        self.move(4, k, from_x, dp=at.sibling)
        self.arrived(2, k, from_y)
        if k % 2 == 1:
            self.move(5, k, from_y, dp=at.beside)
        self.move(6, k, from_y, dp=at.sibling)

    def across(self, k):
        src = self.piece(k, y=True, x=True)
        self.arrived(5, k, src)
        self.move(7, k, src, dp=self.at.sibling)

    def last(self, k):
        self.arrived(3, k, self.piece(k, core=True))
        self.arrived(4, k, self.piece(k, x=True, core=True))
        self.arrived(6, k, self.piece(k, y=True, core=True))
        self.arrived(7, k, self.piece(k, y=True, x=True, core=True))

    def wait_send(self):
        for k in range(self.at.planes):
            for kind in range(0 if k else 1, 8):
                sem = (kind, k)
                self.at.copy(self.piece(k), self.piece(k), self.send_sem.at[sem],
                             self.recv_sem.at[sem], dp=self.at.sibling).wait_send()


def gelu_parts(up):
    inner = 0.7978845608028654 * (up + 0.044715 * up * up * up)
    th = jnp.tanh(inner)
    half = 0.5 * (1.0 + th)
    slope = half + 0.5 * up * (1.0 - th * th) * (
        0.7978845608028654 * (1.0 + 3 * 0.044715 * up * up)
    )
    return up * half, slope


def halves(width):
    return (0, slice(0, width // 2), True), (0, slice(width // 2, width), False)


def feed_remote_kernel(
    x_ref, dy_ref, w_hbm, g_attn, z_attn, gain, gains_in,
    branch, d_normed, out_attn, out_up, out_down, out_gains,
    xt, dt, w_buf, g_ff, ff_core, ff_first, ff_second, at_core, at_first, at_second, got_z,
    sums, got_sums, z_sums,
    w_sem, ff_send, ff_recv, at_send, at_recv, z_send, z_recv, sum_send, sum_recv,
):
    width = x_ref.shape[1]
    steps, shard = w_hbm.shape[0], w_hbm.shape[3]
    half = width // 2
    at = Place(steps)
    at.greet()
    attn = Scatter(at, halves(width), g_attn, at_core, at_first, at_second, at_send, at_recv)
    both = (0, slice(0, width), True), (1, slice(0, width), False)
    feed = Scatter(at, both, g_ff, ff_core, ff_first, ff_second, ff_send, ff_recv)
    last = steps - 1

    def z_copy(step, kind):
        return at.copy(ff_second.at[step, kind], got_z.at[kind, step],
                       z_send.at[kind, step], z_recv.at[kind, step], mp=at.along(1 + step))

    def to_z(step):
        feed.after_second(step)
        for kind in range(2):
            z_copy(step, kind).start()

    def w_copy(step, kind):
        slot = lax.rem(step, 2)
        return pltpu.make_async_copy(
            w_hbm.at[at.along(1 + step), :, kind], w_buf.at[slot, kind], w_sem.at[slot, kind]
        )

    def feed_half(step, index):
        cols = slice(half * index, half * index + half)
        slot = lax.rem(step, 2)
        upper = w_buf[slot, 0, :, :, cols].reshape(width, half)
        lower = w_buf[slot, 1, :, :, cols].reshape(width, half)
        value, slope = gelu_parts(nn(x_ref[...], upper))
        hidden = value.astype(BF16)
        d_up = (nn(dy_ref[...], lower) * slope).astype(BF16)
        split = (2, 2, 2, shard, half)
        g_ff[step, 0, :, :, :, :, cols] = nn(xt[...], d_up).astype(BF16).reshape(split)
        g_ff[step, 1, :, :, :, :, cols] = nn(dt[...], hidden).astype(BF16).reshape(split)
        branch[...] += nt(hidden, lower)
        d_normed[...] += nt(d_up, upper)

    attn.start(0)
    for kind in range(2):
        w_copy(0, kind).start()
    xt[...] = x_ref[...].T
    dt[...] = dy_ref[...].T
    branch[...] = jnp.zeros_like(branch)
    d_normed[...] = jnp.zeros_like(d_normed)

    def one_step(step, carry):
        for kind in range(2):
            w_copy(step, kind).wait()

        @pl.when(step + 1 < steps)
        def _():
            for kind in range(2):
                w_copy(step + 1, kind).start()

        feed_half(step, 0)

        @pl.when(step == 0)
        def _():
            attn.after_core(0)

        @pl.when(step >= 1)
        def _():
            feed.after_core(step - 1)

        @pl.when(step >= 2)
        def _():
            to_z(step - 2)

        feed_half(step, 1)
        feed.start(step)

        @pl.when(step == 0)
        def _():
            attn.after_first(0)

        @pl.when(step >= 1)
        def _():
            feed.after_first(step - 1)

        return carry

    lax.fori_loop(0, steps, one_step, 0)

    sums[0] = gains_in[...]
    store_gain(sums.at[0], d_normed[...], x_ref[...], gain[...])

    def sum_copy(stage):
        to = (at.sibling, at.beside, at.above)[stage]
        return at.copy(sums.at[stage], got_sums.at[stage], sum_send.at[stage],
                       sum_recv.at[stage], dp=to)

    def sum_z_copy(k):
        return at.copy(sums.at[3], z_sums.at[at.z], sum_send.at[2 + k], sum_recv.at[2 + k],
                       mp=at.along(k))

    def next_sum(stage):
        sum_copy(stage).wait_recv()
        sums[stage + 1] = sums[stage] + got_sums[stage]

    sum_copy(0).start()
    feed.after_core(last)
    next_sum(0)
    sum_copy(1).start()
    to_z(last - 1)
    next_sum(1)
    sum_copy(2).start()
    for item in range(2):
        cols = attn.items[item][1]
        out_attn[:, cols] = attn.total(0, item) + z_attn[:, cols]
    feed.after_first(last)
    next_sum(2)
    for k in range(1, steps):
        sum_z_copy(k).start()
    z_sums[at.z] = sums[3]
    for kind, out in enumerate((out_up, out_down)):
        total = feed.total(last, kind)
        for step in range(last):
            z_copy(step, kind).wait_recv()
            total = total + got_z[kind, step].astype(F32)
        out[...] = total
    for k in range(1, steps):
        sum_z_copy(k).wait_recv()
    total = z_sums[0]
    for k in range(1, steps):
        total = total + z_sums[k]
    out_gains[...] = total

    attn.wait_send(0)
    for step in range(steps):
        feed.wait_send(step)
    for step in range(last):
        for kind in range(2):
            z_copy(step, kind).wait_send()
    for stage in range(3):
        sum_copy(stage).wait_send()
    for k in range(1, steps):
        sum_z_copy(k).wait_send()


def feed_remote_call(normed, grads, w_ff, g_attn, z_attn, gain, gains):
    rows, width = normed.shape
    steps, _, _, shard, _ = w_ff.shape
    vmem = pl.BlockSpec(memory_space=pltpu.VMEM)
    return pl.pallas_call(
        feed_remote_kernel,
        in_specs=[vmem, vmem, pl.BlockSpec(memory_space=pl.ANY)] + [vmem] * 4,
        out_specs=[vmem] * 6,
        out_shape=[jax.ShapeDtypeStruct((rows, width), F32)] * 2
        + [jax.ShapeDtypeStruct((shard, width), F32)] * 3
        + [jax.ShapeDtypeStruct((8, 128), F32)],
        scratch_shapes=[
            pltpu.VMEM((width, rows), BF16),
            pltpu.VMEM((width, rows), BF16),
            pltpu.VMEM((2, 2, 8, shard, width), BF16),
            pltpu.VMEM((steps, 2, 2, 2, 2, shard, width), BF16),
            pltpu.VMEM((steps, 2, 2, 2, shard, width), BF16),
            pltpu.VMEM((steps, 2, 2, shard, width), BF16),
            pltpu.VMEM((steps, 2, shard, width), BF16),
            pltpu.VMEM((1, 1, 2, 2, shard, width), BF16),
            pltpu.VMEM((1, 1, 2, shard, width), BF16),
            pltpu.VMEM((1, 1, shard, width), BF16),
            pltpu.VMEM((2, steps - 1, shard, width), BF16),
            pltpu.VMEM((4, 8, 128), F32),
            pltpu.VMEM((3, 8, 128), F32),
            pltpu.VMEM((steps, 8, 128), F32),
            pltpu.SemaphoreType.DMA((2, 2)),
            pltpu.SemaphoreType.DMA((3, 2, steps)),
            pltpu.SemaphoreType.DMA((3, 2, steps)),
            pltpu.SemaphoreType.DMA((3, 2, 1)),
            pltpu.SemaphoreType.DMA((3, 2, 1)),
            pltpu.SemaphoreType.DMA((2, steps - 1)),
            pltpu.SemaphoreType.DMA((2, steps - 1)),
            pltpu.SemaphoreType.DMA((6,)),
            pltpu.SemaphoreType.DMA((6,)),
        ],
        compiler_params=pltpu.CompilerParams(
            collective_id=0, has_side_effects=True, vmem_limit_bytes=VMEM
        ),
        cost_estimate=pl.CostEstimate(
            flops=12 * rows * width * width * steps,
            bytes_accessed=4 * steps * width * width * 2,
            transcendentals=rows * width * steps,
        ),
        name="feed_forward_scatter",
    )(normed, grads, w_ff, g_attn, z_attn, gain, gains)


def iota(shape, axis):
    return lax.broadcasted_iota(jnp.int32, shape, axis)


def source_of(index, start, total):
    rest = index - BIG
    other = jnp.where(rest < start, rest, rest + MOST)
    held = jnp.where(index < MOST, start + index, -1)
    return jnp.where((rest >= 0) & (rest < total - MOST), other, held)


def store_gain(out, d_normed, normed, gain):
    total = jnp.sum(d_normed * normed.astype(F32), axis=0, keepdims=True) / gain
    for row in range(total.shape[1] // 128):
        out[row:row + 1] += total[:, 128 * row:128 * row + 128]


def prepare(
    me, part, ids, pieces, x_ref, dy_ref, xt, dt, feat_q, feat_k, pt, d_normed, branch, g_gains
):
    mp = ids.shape[1]
    total = mp * part
    numbers = ids[me]
    start = jnp.zeros((1, 1), jnp.int32)
    for image in range(IMAGES):
        count = jnp.sum((numbers == image).astype(F32), axis=(0, 1), keepdims=True)
        ahead = jnp.sum(
            ((numbers >= 0) & (numbers < image)).astype(F32), axis=(0, 1), keepdims=True
        )
        start = start + jnp.where(count == MOST, ahead, 0.0).astype(jnp.int32)
    column = source_of(iota((ROWS, 1), 0), start, total)
    line = source_of(iota((1, ROWS), 1), start, total)
    x_sum, dy_sum, feats = 0.0, 0.0, 0.0
    for k, piece in enumerate(pieces):
        chunk = lax.rem(me - k + mp, mp)
        offset = iota((1, PIECE), 1)
        pos = jnp.where(offset < part, chunk * part + offset, -2)
        pick = (column == pos).astype(F32).astype(BF16)
        offset = iota((PIECE, 1), 0)
        pos = jnp.where(offset < part, chunk * part + offset, -2)
        pt[k] = (line == pos).astype(F32).astype(BF16)
        x_sum = x_sum + nn(pick, piece[0][...])
        dy_sum = dy_sum + nn(pick, piece[1][...])
        marks = (iota((128, 1), 0) - HD == ids[me, pl.ds(chunk, 1), :]).astype(F32)
        feats = feats + nt(pick, marks.astype(BF16))
    x = x_sum.astype(BF16)
    dy = dy_sum.astype(BF16)
    x_ref[...] = x
    dy_ref[...] = dy
    xt[...] = x.T
    dt[...] = dy.T
    lane = iota((1, 128), 1)
    feat_q[...] = (feats * 128.0).astype(BF16)
    marked = (lane >= HD) & (lane < HD + IMAGES)
    feat_k[...] = jnp.where(marked, (feats - 1.0) * 256.0, 0.0).astype(BF16)
    d_normed[...] = jnp.zeros_like(d_normed)
    branch[...] = jnp.zeros_like(branch)
    g_gains[...] = jnp.zeros_like(g_gains)


def attention_chunk(
    weights, gain, x_ref, dy_ref, xt, dt, feat_q, feat_k, raw, d_raw, d_att, att,
    d_normed, branch, g_gains, store, poll,
):
    raw[...] = nn(x_ref[...], weights(slice(0, 640)))
    d_att[...] = nn(dy_ref[...], weights(slice(512, 768)))
    lane = iota((1, 128), 1)
    low = lane < HD
    same = (iota((128, 128), 0) // HD == iota((128, 128), 1) // HD).astype(F32)
    mean_of = (same * (1.0 / HD)).astype(BF16)

    def half_mean(value):
        return nn(value.astype(BF16), mean_of)

    d_gain = jnp.zeros((1, 128), F32)
    for head in range(3):
        qk = raw[:, 128 * head:128 * head + 128]
        high = qk.astype(BF16)
        mean = nn(high, mean_of) + half_mean(qk - high.astype(F32))
        centered = qk - mean
        spread = lax.rsqrt(half_mean(centered * centered) + 1e-6)
        unit = centered * spread
        rounded = (unit * gain).astype(BF16).astype(F32)
        q_aug = jnp.where(low, rounded * 0.125, feat_q[...].astype(F32)).astype(BF16)
        k_aug = jnp.where(low, pltpu.roll(rounded, HD, 1), feat_k[...].astype(F32)).astype(BF16)
        v_tile = 384 + 128 * (head // 2)
        v = raw[:, v_tile:v_tile + 128]
        if head == 1:
            v = pltpu.roll(v, HD, 1)
        one = ((lane == HD) | (lane == HD + 1)).astype(F32)
        v_aug = jnp.where(low, v, one).astype(BF16)
        a_tile = 128 * ((head + 1) // 2)
        da = d_att[:, a_tile:a_tile + 128]
        if head != 1:
            da = pltpu.roll(da, HD, 1)
        q_t = q_aug.astype(F32).T.astype(BF16)
        d_queries, attended, d_keys, d_values = [], [], [], []
        for base, count in ((0, BIG), (BIG, REST)):
            keys = k_aug[base:base + count]
            values = v_aug[base:base + count]
            dk_t = jnp.zeros((128, count), F32)
            dv_t = jnp.zeros((128, count), F32)
            for row in range(base, base + count, 256):
                rows = slice(row, row + 256)
                prob = jnp.exp(nt(q_aug[rows], keys))
                prob_low = prob.astype(BF16)
                gathered = nn(prob_low, values)
                inverse = 1.0 / gathered[:, HD:HD + 1]
                out = jnp.where(low, gathered * inverse, 0.0)
                attended.append(out)
                scaled = jnp.where(low, da[rows] * inverse, 0.0).astype(BF16).astype(F32)
                dot = jnp.sum(scaled * out, axis=-1, keepdims=True)
                dot_high = dot.astype(BF16).astype(F32)
                d_aug = jnp.where(
                    lane == HD, -dot_high, jnp.where(lane == HD + 1, dot_high - dot, scaled)
                )
                d_low = d_aug.astype(BF16)
                d_score = (prob * nt(d_low, values)).astype(BF16)
                d_queries.append(nn(d_score, keys))
                dk_t = dk_t + nn(q_t[:, rows], d_score)
                dv_t = dv_t + nn(d_aug.T.astype(BF16), prob_low)
            d_keys.append(dk_t.T)
            d_values.append(dv_t.T)
        d_query = jnp.concatenate(d_queries, axis=0) * 0.125
        d_key = jnp.concatenate(d_keys, axis=0)
        d_value = jnp.concatenate(d_values, axis=0)
        attend = jnp.concatenate(attended, axis=0)
        d_qk = jnp.where(low, d_query, pltpu.roll(d_key, HD, 1))
        d_gain = d_gain + jnp.sum(d_qk * unit, axis=0, keepdims=True)
        scaled = d_qk * gain
        d_qk = spread * (scaled - half_mean(scaled) - unit * half_mean(scaled * unit))
        d_raw[:, 128 * head:128 * head + 128] = d_qk.astype(BF16)
        if head == 0:
            first_value = d_value
            att[:, 0:128] = jnp.where(low, 0.0, pltpu.roll(attend, HD, 1)).astype(BF16)
        elif head == 1:
            both = jnp.where(low, first_value, pltpu.roll(d_value, HD, 1))
            d_raw[:, 384:512] = both.astype(BF16)
            first_att = attend
        else:
            d_raw[:, 512:640] = jnp.where(low, d_value, 0.0).astype(BF16)
            both = jnp.where(low, first_att, pltpu.roll(attend, HD, 1))
            att[:, 128:256] = both.astype(BF16)
        poll(head)
    g_gains[6:7] += d_gain
    d_projected = d_raw[...]
    attended = att[...]
    d_normed[...] += nt(d_projected, weights(slice(0, 640)))
    branch[...] += nt(attended, weights(slice(512, 768)))
    left = nn(xt[...], d_projected)
    right = nn(dt[...], attended)
    store(slice(0, 512), left[:, :512].astype(BF16))
    store(slice(512, 640), (left[:, 512:] + right[:, :128]).astype(BF16))
    store(slice(640, 768), right[:, 128:].astype(BF16))


def take_back(outs, pt, x_ref, norm_gain, d_normed, branch, g_gains):
    store_gain(g_gains, d_normed[...], x_ref[...], norm_gain[...])
    d_rows = d_normed[...].astype(BF16)
    b_rows = branch[...].astype(BF16)
    for k, out in enumerate(outs):
        out[0] = nn(pt[k], d_rows).astype(BF16)
        out[1] = nn(pt[k], b_rows).astype(BF16)


def attention_kernel(
    part, place, own_x, own_dy, in1, in2, in3, ids, gains, norm_gain, weights,
    out0, out1, out2, out3, g_weights, g_gains,
    x_ref, dy_ref, xt, dt, feat_q, feat_k, pt, raw, d_raw, d_att, att, d_normed, branch,
):
    step = pl.program_id(0)

    @pl.when(step == 0)
    def _():
        pieces = [(own_x.at[0], own_dy.at[0])] + [(got.at[0], got.at[1]) for got in (in1, in2, in3)]
        prepare(place[0], part, ids, pieces, x_ref, dy_ref, xt, dt, feat_q, feat_k, pt,
                d_normed, branch, g_gains)

    def store(cols, value):
        g_weights[0, :, cols] = value

    attention_chunk(
        lambda cols: weights[0, :, cols], gains[...], x_ref, dy_ref, xt, dt, feat_q, feat_k,
        raw, d_raw, d_att, att, d_normed, branch, g_gains, store, lambda head: None,
    )

    @pl.when(step == pl.num_programs(0) - 1)
    def _():
        take_back((out0, out1, out2, out3), pt, x_ref, norm_gain, d_normed, branch, g_gains)


def attention_call(place, part, normed, grads, received, ids, gains, norm_gain, weights):
    width = normed.shape[-1]
    chunks = weights.shape[0]
    mp = ids.shape[1]
    own = pl.BlockSpec((1, PIECE, width), lambda m, place: (0, 0, 0))
    pair = pl.BlockSpec((2, PIECE, width), lambda m, place: (0, 0, 0))
    chunk = pl.BlockSpec((1, width, width), lambda m, place: (m, 0, 0))
    line = pl.BlockSpec((1, 128), lambda m, place: (0, 0))
    return pl.pallas_call(
        functools.partial(attention_kernel, part),
        grid_spec=pltpu.PrefetchScalarGridSpec(
            num_scalar_prefetch=1,
            grid=(chunks,),
            in_specs=[own, own, pair, pair, pair,
                      pl.BlockSpec(ids.shape, lambda m, place: (0, 0, 0)),
                      line, pl.BlockSpec((1, width), lambda m, place: (0, 0)), chunk],
            out_specs=[pair] * 4 + [chunk, pl.BlockSpec((8, 128), lambda m, place: (0, 0))],
            scratch_shapes=[
                pltpu.VMEM((ROWS, width), BF16),
                pltpu.VMEM((ROWS, width), BF16),
                pltpu.VMEM((width, ROWS), BF16),
                pltpu.VMEM((width, ROWS), BF16),
                pltpu.VMEM((ROWS, 128), BF16),
                pltpu.VMEM((ROWS, 128), BF16),
                pltpu.VMEM((mp, PIECE, ROWS), BF16),
                pltpu.VMEM((ROWS, 640), F32),
                pltpu.VMEM((ROWS, 640), BF16),
                pltpu.VMEM((ROWS, 256), F32),
                pltpu.VMEM((ROWS, 256), BF16),
                pltpu.VMEM((ROWS, width), F32),
                pltpu.VMEM((ROWS, width), F32),
            ],
        ),
        out_shape=[jax.ShapeDtypeStruct((2, PIECE, width), BF16)] * 4
        + [jax.ShapeDtypeStruct(weights.shape, BF16), jax.ShapeDtypeStruct((8, 128), F32)],
        compiler_params=pltpu.CompilerParams(vmem_limit_bytes=VMEM),
        cost_estimate=pl.CostEstimate(
            flops=60_000_000_000, bytes_accessed=4 * chunks * width * width,
            transcendentals=ROWS * ROWS * 12,
        ),
        name="attention",
    )(place, normed, grads, *received, ids, gains, norm_gain, weights)


def group_means():
    same = (iota((128, 128), 0) // HD == iota((128, 128), 1) // HD).astype(F32)
    return (same * (1.0 / HD)).astype(BF16)


def forward_chunk(
    weights, gain, x_ref, feat_q, feat_k, raw, qk_all, v_all, stats, att, branch, begin, spill
):
    raw[...] = nn(x_ref[...], weights(slice(0, 640)))
    lane = iota((1, 128), 1)
    low = lane < HD
    mean_of = group_means()
    stat = jnp.zeros((ROWS, 128), F32)
    for head in range(3):
        qk = raw[:, 128 * head:128 * head + 128]
        high = qk.astype(BF16)
        mean = nn(high, mean_of) + nn((qk - high.astype(F32)).astype(BF16), mean_of)
        centered = qk - mean
        spread = lax.rsqrt(nn((centered * centered).astype(BF16), mean_of) + 1e-6)
        rounded = (centered * spread * gain).astype(BF16)
        qk_all[head] = rounded
        rounded = rounded.astype(F32)
        q_aug = jnp.where(low, rounded * 0.125, feat_q[...].astype(F32)).astype(BF16)
        k_aug = jnp.where(low, pltpu.roll(rounded, HD, 1), feat_k[...].astype(F32)).astype(BF16)
        v_tile = 384 + 128 * (head // 2)
        v = raw[:, v_tile:v_tile + 128]
        if head == 1:
            v = pltpu.roll(v, HD, 1)
        v_aug = jnp.where(low, v, 1.0).astype(BF16)
        v_all[head] = v_aug
        p_ref = begin(head)
        parts = []
        for base, count in ((0, BIG), (BIG, REST)):
            keys = k_aug[base:base + count]
            values = v_aug[base:base + count]
            for row in range(base, base + count, 256):
                rows = slice(row, row + 256)
                prob = jnp.exp(nt(q_aug[rows], keys)).astype(BF16)
                p_ref[rows, :count] = prob
                parts.append(nn(prob, values))
        spill(head)
        gathered = jnp.concatenate(parts, axis=0)
        inverse = 1.0 / gathered
        attend = gathered * pltpu.roll(inverse, HD, 1)
        stat = jnp.where((lane == head) | (lane == HD + head), spread, stat)
        stat = jnp.where(lane == HD + 8 + head, inverse, stat)
        if head == 0:
            att[:, 0:128] = jnp.where(low, 0.0, pltpu.roll(attend, HD, 1)).astype(BF16)
        elif head == 1:
            first = attend
        else:
            att[:, 128:256] = jnp.where(low, first, pltpu.roll(attend, HD, 1)).astype(BF16)
    stats[...] = stat
    branch[...] += nt(att[...], weights(slice(512, 768)))


def backward_chunk(
    weights, gain, dy_ref, xt, dt, raw, d_raw, d_score_ref, qk_all, v_all, stats, att,
    d_normed, g_gains, ready, store, poll,
):
    raw[:, :256] = nn(dy_ref[...], weights(slice(512, 768)))
    lane = iota((1, 128), 1)
    low = lane < HD
    mean_of = group_means()
    stat = stats[...]
    back_gain = 1.0 / gain
    d_gain = jnp.zeros((1, 128), F32)
    for head in range(3):
        qk = qk_all[head]
        v_aug = v_all[head]
        tile = 128 * ((head + 1) // 2)
        da = raw[:, tile:tile + 128]
        out = att[:, tile:tile + 128].astype(F32)
        if head != 1:
            da = pltpu.roll(da, HD, 1)
            out = pltpu.roll(out, HD, 1)
        inverse = stat[:, HD + 8 + head:HD + 9 + head]
        scaled = jnp.where(low, da * inverse, 0.0).astype(BF16).astype(F32)
        dot = jnp.sum(scaled * out, axis=-1, keepdims=True)
        dot_high = dot.astype(BF16).astype(F32)
        d_aug = jnp.where(
            lane == HD, -dot_high, jnp.where(lane == HD + 1, dot_high - dot, scaled)
        )
        d_low = d_aug.astype(BF16)
        d_t = d_aug.T.astype(BF16)
        qk_low = qk.astype(F32)
        qk_t = qk_low.T.astype(BF16)
        p_ref = ready(head)
        d_queries, d_keys, d_values = [], [], []
        for base, count in ((0, BIG), (BIG, REST)):
            block = slice(base, base + count)
            for row in range(base, base + count, 256):
                rows = slice(row, row + 256)
                d_prob = nt(d_low[rows], v_aug[block])
                d_score = (p_ref[rows, :count].astype(F32) * d_prob).astype(BF16)
                d_score_ref[rows, :count] = d_score
                d_queries.append(nn(d_score, qk[block]))
            d_keys.append(nn(qk_t[:, block], d_score_ref[block, :count]).T)
            d_values.append(nn(d_t[:, block], p_ref[block, :count]).T)
        d_query = jnp.concatenate(d_queries, axis=0)
        d_key = jnp.concatenate(d_keys, axis=0)
        d_value = jnp.concatenate(d_values, axis=0)
        d_qk = pltpu.roll(jnp.where(low, d_key, d_query), HD, 1) * 0.125
        unit = qk_low * back_gain
        spread = jnp.where(low, stat[:, head:head + 1], stat[:, HD + head:HD + head + 1])
        d_gain = d_gain + jnp.sum(d_qk * unit, axis=0, keepdims=True)
        scaled = d_qk * gain
        mean = nn(scaled.astype(BF16), mean_of)
        d_qk = spread * (scaled - mean - unit * nn((scaled * unit).astype(BF16), mean_of))
        d_raw[:, 128 * head:128 * head + 128] = d_qk.astype(BF16)
        if head == 0:
            first = d_value
        elif head == 1:
            both = jnp.where(low, first, pltpu.roll(d_value, HD, 1))
            d_raw[:, 384:512] = both.astype(BF16)
        else:
            d_raw[:, 512:640] = jnp.where(low, d_value, 0.0).astype(BF16)
        poll(head)
    g_gains[6:7] += d_gain
    d_projected = d_raw[...]
    d_normed[...] += nt(d_projected, weights(slice(0, 640)))
    left = nn(xt[...], d_projected)
    right = nn(dt[...], att[...])
    store(slice(0, 512), left[:, :512].astype(BF16))
    store(slice(512, 640), (left[:, 512:] + right[:, :128]).astype(BF16))
    store(slice(640, 768), right[:, 128:].astype(BF16))


def front_kernel(
    tok, cot, ids, gains, norm_gain, w_attn, w_feed,
    normed, grads, returned, out0, out1, out2, out3, w_ff, g_last, z_attn, g_gains, p_all,
    got_rows, back_rows, w_full, g_buf, at_core, at_first, at_second, got_z,
    x_ref, dy_ref, xt, dt, feat_q, feat_k, pt, raw, d_raw, d_score, p_buf,
    qk_all, v_all, stats, att, total,
    row_send, row_recv, back_send, back_recv, wa_send, wa_recv, wf_send, wf_recv, own_sem,
    p_out, p_in, at_send, at_recv, z_send, z_recv,
):
    count, part, width = tok.shape
    shard = w_attn.shape[0]
    at = Place(count)
    at.greet()
    gather = Gather(at, w_attn, w_full, wa_send, wa_recv)
    gather_ff = Gather(at, w_feed, w_ff, wf_send, wf_recv)
    scatter = Scatter(at, halves(width), g_buf, at_core, at_first, at_second, at_send, at_recv)
    own_ff = pltpu.make_async_copy(w_feed, gather_ff.piece(0), own_sem)

    def row_copy(kind, k):
        src = (normed, grads)[kind].at[k]
        return at.copy(src, got_rows.at[k - 1, kind], row_send.at[kind, k - 1],
                       row_recv.at[kind, k - 1], mp=at.along(k))

    def back_copy(k):
        return at.copy(back_rows.at[k - 1], returned.at[k], back_send.at[k - 1],
                       back_recv.at[k - 1], mp=at.along(-k))

    gather.start()
    own_ff.start()
    w_full[at.z, at.y, at.x, at.core] = w_attn[...]
    gather.spread(0)
    gain = norm_gain[...]
    for k in (1, 3, 2, 0):
        sequence = at.along(k)
        x = tok[sequence].astype(F32)
        centered = x - jnp.mean(x, axis=-1, keepdims=True)
        spread = lax.rsqrt(jnp.mean(centered * centered, axis=-1, keepdims=True) + 1e-6)
        pad = jnp.zeros((PIECE - part, width), BF16)
        normed[k, :part] = (centered * spread * gain).astype(BF16)
        normed[k, part:] = pad
        if k:
            row_copy(0, k).start()
        grads[k, :part] = cot[sequence]
        grads[k, part:] = pad
    place_rows(at.z, part, ids, pt, feat_q, feat_k)
    g_gains[...] = jnp.zeros_like(g_gains)
    total[...] = jnp.zeros_like(total)
    gather.spread(1)
    gather.spread(3)
    gather.forward(0)
    gather.spread(2)
    own_ff.wait()
    gather_ff.spread(0)
    gather.forward(1)
    gather.across(0)
    gather.forward(3)
    gather.across(1)
    gather.forward(2)
    gather.across(3)
    gather.across(2)
    for k in range(count):
        gather.last(k)
    for k in (1, 3, 2):
        row_copy(0, k).wait_recv()
    for k in (1, 3, 2):
        row_copy(1, k).start()

    def lay_out(kind, own, rows, columns):
        value = 0.0
        for k in range(count):
            piece = own[0] if k == 0 else got_rows[k - 1, kind]
            value = value + lax.dot_general(
                pt[k], piece, (((0,), (0,)), ((), ())), preferred_element_type=F32
            )
        value = value.astype(BF16)
        rows[...] = value
        columns[...] = value.T

    lay_out(0, normed, x_ref, xt)

    def weights_of(chunk):
        def weights(cols):
            return w_full[chunk, :, :, :, :, cols].reshape(width, cols.stop - cols.start)

        return weights

    def p_write(step, head):
        slot = lax.rem(step + head, 2)
        return pltpu.make_async_copy(p_buf.at[slot], p_all.at[at.along(step), head],
                                     p_out.at[slot])

    def p_read(step, head):
        slot = lax.rem(step + head, 2)
        return pltpu.make_async_copy(p_all.at[at.along(1 + step), head], p_buf.at[slot],
                                     p_in.at[slot])

    def forward_step(step, carry):
        chunk = at.along(step)

        def begin(head):
            if head == 2:
                p_write(step, 0).wait()
            else:
                @pl.when(step >= 1)
                def _():
                    p_write(step - 1, 1 + head).wait()
            return p_buf.at[lax.rem(step + head, 2)]

        forward_chunk(
            weights_of(chunk), gains[...], x_ref, feat_q, feat_k, raw, qk_all.at[chunk],
            v_all.at[chunk], stats.at[chunk], att.at[chunk], total, begin,
            lambda head: p_write(step, head).start(),
        )
        return carry

    lax.fori_loop(0, count, forward_step, 0)
    for head in (1, 2):
        p_write(count - 1, head).wait()
    p_read(0, 0).start()
    value = total[...].astype(BF16)
    returned[0] = nn(pt[0], value).astype(BF16)
    for k in range(1, count):
        back_rows[k - 1] = nn(pt[k], value).astype(BF16)
    total[...] = jnp.zeros_like(total)
    for k in (1, 3, 2):
        row_copy(1, k).wait_recv()
    gather_ff.start()
    lay_out(1, grads, dy_ref, dt)

    def z_copy(step):
        return at.copy(at_second.at[step, 0], got_z.at[step], z_send.at[step], z_recv.at[step],
                       mp=at.along(1 + step))

    def events(step, head):
        if step == 0 and head == 1:
            gather_ff.forward(0)
        elif step == 0 and head == 2:
            gather_ff.across(0)
        elif step == 1 and head == 0:
            for k in (1, 3, 2):
                back_copy(k).start()
            gather_ff.spread(1)
        elif step == 1 and head == 1:
            gather_ff.spread(3)
        elif step == 1 and head == 2:
            gather_ff.spread(2)
            gather_ff.forward(1)
        elif step == 2 and head == 0:
            gather_ff.forward(3)
            gather_ff.across(1)
        elif step == 2 and head == 1:
            gather_ff.forward(2)
            gather_ff.across(3)
        elif step == 2 and head == 2:
            gather_ff.across(2)

    def backward_step(step, carry):
        chunk = at.along(1 + step)

        def store(cols, value):
            split = (2, 2, 2, shard, cols.stop - cols.start)
            g_buf[step, 0, :, :, :, :, cols] = value.reshape(split)

        def ready(head):
            p_read(step, head).wait()
            if head < 2:
                p_read(step, head + 1).start()
            else:
                @pl.when(step + 1 < count)
                def _():
                    p_read(step + 1, 0).start()
            return p_buf.at[lax.rem(step + head, 2)]

        def poll(head):
            @pl.when(step >= 1)
            def _():
                if head == 0:
                    scatter.after_core(step - 1)
                elif head == 1:
                    scatter.after_first(step - 1)
                else:
                    scatter.after_second(step - 1)
                    z_copy(step - 1).start()

            for which in range(count):
                @pl.when(step == which)
                def _():
                    events(which, head)

        backward_chunk(
            weights_of(chunk), gains[...], dy_ref, xt, dt, raw, d_raw, d_score,
            qk_all.at[chunk], v_all.at[chunk], stats.at[chunk], att.at[chunk], total, g_gains,
            ready, store, poll,
        )

        @pl.when(step < count - 1)
        def _():
            scatter.start(step)

        return carry

    lax.fori_loop(0, count, backward_step, 0)
    store_gain(g_gains, total[...], x_ref[...], norm_gain[...])
    value = total[...].astype(BF16)
    for k, out in enumerate((out0, out1, out2, out3)):
        out[...] = nn(pt[k], value).astype(BF16)
    g_last[...] = g_buf[count - 1:]
    z_total = 0.0
    for step in range(count - 1):
        z_copy(step).wait_recv()
        z_total = z_total + got_z[step].astype(F32)
    z_attn[...] = z_total
    for k in range(count):
        gather_ff.last(k)
    for k in range(1, count):
        back_copy(k).wait_recv()

    gather.wait_send()
    gather_ff.wait_send()
    for k in range(1, count):
        back_copy(k).wait_send()
        for kind in range(2):
            row_copy(kind, k).wait_send()
    for step in range(count - 1):
        scatter.wait_send(step)
        z_copy(step).wait_send()


def place_rows(me, part, ids, pt, feat_q, feat_k):
    mp = ids.shape[1]
    total = mp * part
    numbers = ids[me]
    start = jnp.zeros((1, 1), jnp.int32)
    for image in range(IMAGES):
        count = jnp.sum((numbers == image).astype(F32), axis=(0, 1), keepdims=True)
        ahead = jnp.sum(
            ((numbers >= 0) & (numbers < image)).astype(F32), axis=(0, 1), keepdims=True
        )
        start = start + jnp.where(count == MOST, ahead, 0.0).astype(jnp.int32)
    line = source_of(iota((1, ROWS), 1), start, total)
    feats = 0.0
    for k in range(mp):
        chunk = lax.rem(me - k + mp, mp)
        offset = iota((PIECE, 1), 0)
        pos = jnp.where(offset < part, chunk * part + offset, -2)
        pick = (line == pos).astype(F32).astype(BF16)
        pt[k] = pick
        marks = (iota((128, 1), 0) - HD == ids[me, pl.ds(chunk, 1), :]).astype(F32)
        feats = feats + nn(marks.astype(BF16), pick)
    feats = feats.T
    lane = iota((1, 128), 1)
    feat_q[...] = (feats * 128.0).astype(BF16)
    marked = (lane >= HD) & (lane < HD + IMAGES)
    feat_k[...] = jnp.where(marked, (feats - 1.0) * 256.0, 0.0).astype(BF16)


def front_call(tokens, cotangent, ids, gains, norm_gain, w_attn, w_feed):
    count, part, width = tokens.shape
    shard = w_attn.shape[0]
    vmem = pl.BlockSpec(memory_space=pltpu.VMEM)
    hbm = pl.BlockSpec(memory_space=pl.ANY)
    rows = jax.ShapeDtypeStruct((count, PIECE, width), BF16)
    return pl.pallas_call(
        front_kernel,
        in_specs=[vmem] * 6 + [hbm],
        out_specs=[vmem] * 7 + [hbm] + [vmem] * 3 + [hbm],
        out_shape=[rows, rows, rows]
        + [jax.ShapeDtypeStruct((PIECE, width), BF16)] * 4
        + [
            jax.ShapeDtypeStruct((count, 2, 2, 2, 2, shard, width), BF16),
            jax.ShapeDtypeStruct((1, 1, 2, 2, 2, shard, width), BF16),
            jax.ShapeDtypeStruct((shard, width), F32),
            jax.ShapeDtypeStruct((8, 128), F32),
            jax.ShapeDtypeStruct((count, 3, ROWS, BIG), BF16),
        ],
        scratch_shapes=[
            pltpu.VMEM((count - 1, 2, PIECE, width), BF16),
            pltpu.VMEM((count - 1, PIECE, width), BF16),
            pltpu.VMEM((count, 2, 2, 2, shard, width), BF16),
            pltpu.VMEM((count, 1, 2, 2, 2, shard, width), BF16),
            pltpu.VMEM((count - 1, 1, 2, 2, shard, width), BF16),
            pltpu.VMEM((count - 1, 1, 2, shard, width), BF16),
            pltpu.VMEM((count - 1, 1, shard, width), BF16),
            pltpu.VMEM((count - 1, shard, width), BF16),
            pltpu.VMEM((ROWS, width), BF16),
            pltpu.VMEM((ROWS, width), BF16),
            pltpu.VMEM((width, ROWS), BF16),
            pltpu.VMEM((width, ROWS), BF16),
            pltpu.VMEM((ROWS, 128), BF16),
            pltpu.VMEM((ROWS, 128), BF16),
            pltpu.VMEM((count, PIECE, ROWS), BF16),
            pltpu.VMEM((ROWS, 640), F32),
            pltpu.VMEM((ROWS, 640), BF16),
            pltpu.VMEM((ROWS, BIG), BF16),
            pltpu.VMEM((2, ROWS, BIG), BF16),
            pltpu.VMEM((count, 3, ROWS, 128), BF16),
            pltpu.VMEM((count, 3, ROWS, 128), BF16),
            pltpu.VMEM((count, ROWS, 128), F32),
            pltpu.VMEM((count, ROWS, 256), BF16),
            pltpu.VMEM((ROWS, width), F32),
            pltpu.SemaphoreType.DMA((2, count - 1)),
            pltpu.SemaphoreType.DMA((2, count - 1)),
            pltpu.SemaphoreType.DMA((count - 1,)),
            pltpu.SemaphoreType.DMA((count - 1,)),
            pltpu.SemaphoreType.DMA((8, count)),
            pltpu.SemaphoreType.DMA((8, count)),
            pltpu.SemaphoreType.DMA((8, count)),
            pltpu.SemaphoreType.DMA((8, count)),
            pltpu.SemaphoreType.DMA,
            pltpu.SemaphoreType.DMA((2,)),
            pltpu.SemaphoreType.DMA((2,)),
            pltpu.SemaphoreType.DMA((3, 2, count - 1)),
            pltpu.SemaphoreType.DMA((3, 2, count - 1)),
            pltpu.SemaphoreType.DMA((count - 1,)),
            pltpu.SemaphoreType.DMA((count - 1,)),
        ],
        compiler_params=pltpu.CompilerParams(
            collective_id=1, has_side_effects=True, vmem_limit_bytes=FRONT_VMEM
        ),
        name="front",
    )(tokens, cotangent, ids, gains, norm_gain, w_attn, w_feed)


def finish_kernel(
    place, tok, cot, gain, branch, d_ff, back, ret0, ret1, ret2, ret3, output, input_grad
):
    step = pl.program_id(0)
    part = tok.shape[1]

    for index, ret in enumerate((ret0, ret1, ret2, ret3)):

        @pl.when(step == index)
        def _():
            x = tok[0].astype(F32)
            output[0] = (x + (branch[0] + back[0].astype(F32))[:part]).astype(BF16)
            d_normed = (d_ff[0] + ret[...].astype(F32))[:part]
            centered = x - jnp.mean(x, axis=-1, keepdims=True)
            spread = lax.rsqrt(jnp.mean(centered * centered, axis=-1, keepdims=True) + 1e-6)
            unit = centered * spread
            scaled = d_normed * gain[...]
            d_x = spread * (
                scaled
                - jnp.mean(scaled, axis=-1, keepdims=True)
                - unit * jnp.mean(scaled * unit, axis=-1, keepdims=True)
            )
            input_grad[0] = cot[0].astype(F32) + d_x


def finish_call(place, tokens, cotangent, gain, branch, d_ff, back, returned):
    count, part, width = tokens.shape
    block = pl.BlockSpec(
        (1, part, width), lambda k, place: (lax.rem(place[0] + k, count), 0, 0)
    )
    padded = pl.BlockSpec((1, PIECE, width), lambda k, place: (k, 0, 0))
    piece = pl.BlockSpec((PIECE, width), lambda k, place: (0, 0))
    line = pl.BlockSpec((1, width), lambda k, place: (0, 0))
    return pl.pallas_call(
        finish_kernel,
        grid_spec=pltpu.PrefetchScalarGridSpec(
            num_scalar_prefetch=1,
            grid=(count,),
            in_specs=[block, block, line, padded, padded, padded] + [piece] * 4,
            out_specs=[block, block],
        ),
        out_shape=[
            jax.ShapeDtypeStruct(tokens.shape, BF16),
            jax.ShapeDtypeStruct(tokens.shape, F32),
        ],
        compiler_params=pltpu.CompilerParams(vmem_limit_bytes=VMEM),
        name="finish",
    )(place, tokens, cotangent, gain, branch, d_ff, back, *returned)


def pack_attention(w_qkv, w_proj):
    rows, wide = w_qkv.shape[1:]
    heads = wide // HD
    qk = w_qkv[:2].reshape(2, rows, heads, HD).transpose(1, 2, 0, 3).reshape(rows, 2 * wide)
    return jnp.concatenate([qk, w_qkv[2], w_proj.T], axis=1)


def unpack_attention(grad, wide):
    rows = grad.shape[0]
    heads = wide // HD
    qk = grad[:, :2 * wide].reshape(rows, heads, 2, HD).transpose(2, 0, 1, 3)
    qk = qk.reshape(2, rows, wide)
    g_qkv = jnp.concatenate([qk, grad[None, :, 2 * wide:3 * wide]], axis=0)
    return g_qkv, grad[:, 3 * wide:].T


def body(
    dp, mp, tokens, w_qkv, w_up, w_proj, w_down, norm_gain, query_gain, key_gain, image_ids, cotangent
):
    micro, seqs, part, width = tokens.shape
    count = micro * seqs
    shard = w_up.shape[0]
    me = lax.axis_index("mp")
    place = me.astype(jnp.int32)[None]
    both = ("mp", "dp")
    tok = tokens.reshape(count, part, width)
    cot = cotangent.reshape(count, part, width)
    gain = norm_gain.reshape(1, width)
    ids = image_ids.reshape(count, mp, part)
    ids = jnp.pad(ids, ((0, 0), (0, 0), (0, PIECE - part)), constant_values=-1)
    gains = jnp.concatenate([query_gain, key_gain]).reshape(1, 2 * HD)
    w_attn = pack_attention(w_qkv, w_proj)
    w_ff = jnp.stack([w_up, w_down.T])

    def send_back(outs):
        return [outs[0]] + [
            lax.ppermute(out, "mp", [(i, (i - k) % mp) for i in range(mp)])
            for k, out in enumerate(outs[1:], 1)
        ]

    if (dp, mp) == (8, 4):
        normed, grads, back, *outs, w_ff, g_attn, z_attn, g_gains, _ = front_call(
            tok, cot, ids, gains, gain, w_attn, w_ff
        )
        returned = send_back(outs)
        branch, d_ff, g_attn, g_up, g_down, g_gains = feed_remote_call(
            normed.reshape(count * PIECE, width), grads.reshape(count * PIECE, width),
            w_ff.reshape(mp, dp, 2, shard, width), g_attn, z_attn, gain, g_gains,
        )
    else:
        w_attn = lax.all_gather(w_attn, both).reshape(mp, width, width)
        w_ff = lax.all_gather(w_ff, both).reshape(mp, dp, 2, shard, width)
        normed, grads, *sends = norm_call(place, tok, cot, gain)
        received = [
            lax.ppermute(send, "mp", [(i, (i + k) % mp) for i in range(mp)])
            for k, send in enumerate(sends, 1)
        ]
        *outs, g_attn, g_gains = attention_call(
            place, part, normed, grads, received, ids, gains, gain, w_attn
        )
        outs = send_back(outs)
        back = jnp.stack([out[1] for out in outs])
        returned = [out[0] for out in outs]
        flat_normed = normed.reshape(count * PIECE, width)
        branch, d_ff, g_up, g_down = feed_call(
            flat_normed, grads.reshape(count * PIECE, width),
            w_ff[:, :, 0].reshape(mp, width, width), w_ff[:, :, 1].reshape(mp, width, width),
        )
        g_attn, g_up, g_down = (
            lax.psum_scatter(
                grad.reshape(-1, shard, width), both, scatter_dimension=0
            ).astype(F32)
            for grad in (g_attn, g_up, g_down)
        )
        own = jnp.sum(d_ff * flat_normed.astype(F32), axis=0) / norm_gain
        g_gains = g_gains.at[:width // 128].add(own.reshape(-1, 128))
        g_gains = lax.psum(g_gains, both)
    output, input_grad = finish_call(
        place, tok, cot, gain,
        branch.reshape(count, PIECE, width), d_ff.reshape(count, PIECE, width), back, returned,
    )
    g_qkv, g_proj = unpack_attention(g_attn, w_qkv.shape[2])
    g_norm = g_gains[:width // 128].reshape(width)
    g_gains = g_gains[6]
    return (
        output.reshape(tokens.shape),
        input_grad.reshape(tokens.shape),
        g_qkv,
        g_up,
        g_proj,
        g_down.T,
        g_norm,
        g_gains[:HD],
        g_gains[HD:],
    )


def solution(mesh):
    rows = P(None, "dp", "mp", None)
    weights = (P(None, "dp", "mp"), P("dp", "mp"), P("mp", "dp"), P("mp", "dp"))
    gains = (P(), P(), P())
    return jax.shard_map(
        functools.partial(body, mesh.shape["dp"], mesh.shape["mp"]),
        mesh=mesh,
        in_specs=(rows,) + weights + gains + (P(None, "dp", None), rows),
        out_specs=(rows, rows) + weights + gains,
        check_vma=False,
    )
```

```python
import functools

import jax
import jax.numpy as jnp
from jax import lax
from jax.experimental import pallas as pl
from jax.experimental.pallas import tpu as pltpu
from jax.sharding import PartitionSpec as P

HD = 64
MOST = 709
IMAGES = 8
PIECE = 240
BIG = 768
REST = 256
ROWS = BIG + REST
VMEM = 60 * 1024 * 1024
FRONT_VMEM = 63 * 1024 * 1024
F32 = jnp.float32
BF16 = jnp.bfloat16


def nn(left, right):
    return lax.dot_general(left, right, (((1,), (0,)), ((), ())), preferred_element_type=F32)


def nt(left, right):
    return lax.dot_general(left, right, (((1,), (1,)), ((), ())), preferred_element_type=F32)


def norm_kernel(place, tok, cot, gain, normed, grads, send1, send2, send3):
    step = pl.program_id(0)
    part = tok.shape[1]
    x = tok[0].astype(F32)
    centered = x - jnp.mean(x, axis=-1, keepdims=True)
    spread = lax.rsqrt(jnp.mean(centered * centered, axis=-1, keepdims=True) + 1e-6)
    value = (centered * spread * gain[...]).astype(BF16)
    normed[...] = jnp.zeros_like(normed)
    grads[...] = jnp.zeros_like(grads)
    normed[0, :part] = value
    grads[0, :part] = cot[0]
    for index, send in ((1, send1), (2, send2), (3, send3)):

        @pl.when(step == index)
        def _():
            send[0] = normed[0]
            send[1] = grads[0]


def norm_call(place, tokens, cotangent, gain):
    count, part, width = tokens.shape
    block = lambda k, place: (lax.rem(place[0] + k, count), 0, 0)
    fixed = lambda k, place: (0, 0, 0)
    return pl.pallas_call(
        norm_kernel,
        grid_spec=pltpu.PrefetchScalarGridSpec(
            num_scalar_prefetch=1,
            grid=(count,),
            in_specs=[
                pl.BlockSpec((1, part, width), block),
                pl.BlockSpec((1, part, width), block),
                pl.BlockSpec((1, width), lambda k, place: (0, 0)),
            ],
            out_specs=[pl.BlockSpec((1, PIECE, width), lambda k, place: (k, 0, 0))] * 2
            + [pl.BlockSpec((2, PIECE, width), fixed)] * 3,
        ),
        out_shape=[jax.ShapeDtypeStruct((count, PIECE, width), BF16)] * 2
        + [jax.ShapeDtypeStruct((2, PIECE, width), BF16)] * 3,
        compiler_params=pltpu.CompilerParams(vmem_limit_bytes=VMEM),
        name="norm_rows",
    )(place, tokens, cotangent, gain)


def feed_kernel(normed, grads, w_up, w_down, branch, d_normed, g_up, g_down, xt, dt):
    step = pl.program_id(0)
    x = normed[...]
    dy = grads[...]

    @pl.when(step == 0)
    def _():
        xt[...] = x.T
        dt[...] = dy.T

    up = nn(x, w_up[0])
    value, slope = gelu_parts(up)
    hidden = value.astype(BF16)
    d_up = (nn(dy, w_down[0]) * slope).astype(BF16)
    g_up[0] = nn(xt[...], d_up).astype(BF16)
    g_down[0] = nn(dt[...], hidden).astype(BF16)
    out = nt(hidden, w_down[0])
    back = nt(d_up, w_up[0])

    @pl.when(step == 0)
    def _():
        branch[...] = out
        d_normed[...] = back

    @pl.when(step > 0)
    def _():
        branch[...] += out
        d_normed[...] += back


def feed_call(normed, grads, w_up, w_down):
    rows, width = normed.shape
    chunks, _, hidden = w_up.shape
    whole = pl.BlockSpec((rows, width), lambda m: (0, 0))
    chunk = pl.BlockSpec((1, width, hidden), lambda m: (m, 0, 0))
    return pl.pallas_call(
        feed_kernel,
        grid=(chunks,),
        in_specs=[whole, whole, chunk, chunk],
        out_specs=[whole, whole, chunk, chunk],
        out_shape=[jax.ShapeDtypeStruct((rows, width), F32)] * 2
        + [jax.ShapeDtypeStruct(w_up.shape, BF16)] * 2,
        scratch_shapes=[pltpu.VMEM((width, rows), BF16)] * 2,
        compiler_params=pltpu.CompilerParams(vmem_limit_bytes=VMEM),
        cost_estimate=pl.CostEstimate(
            flops=12 * rows * width * hidden * chunks,
            bytes_accessed=4 * chunks * width * hidden * 2,
            transcendentals=rows * hidden * chunks,
        ),
        name="feed_forward",
    )(normed, grads, w_up, w_down)


class Place:
    def __init__(self, planes):
        d = lax.axis_index("dp")
        self.z = lax.axis_index("mp")
        self.d, self.planes = d, planes
        self.core, self.x, self.y = d % 2, (d // 2) % 2, d // 4
        self.sibling = d + 1 - 2 * self.core
        self.beside = d + 2 - 4 * self.x
        self.above = d + 4 - 8 * self.y

    def target(self, step):
        z, high = self.z, self.z // 2
        near = jnp.where(step == 2, 1 - z + 4 * high, z)
        return jnp.where(step == 0, 3 - 3 * high, jnp.where(step == 1, 2 - high, near))

    def along(self, k):
        return lax.rem(self.z + k + self.planes, self.planes)

    def copy(self, src, dst, send, recv, dp=None, mp=None):
        return pltpu.make_async_remote_copy(
            src_ref=src, dst_ref=dst, send_sem=send, recv_sem=recv,
            device_id={"dp": self.d if dp is None else dp, "mp": self.z if mp is None else mp},
            device_id_type=pl.DeviceIdType.MESH,
        )

    def greet(self):
        barrier = pltpu.get_barrier_semaphore()
        for other in (self.sibling, self.beside, self.above):
            pl.semaphore_signal(barrier, 1, device_id={"dp": other, "mp": self.z},
                                device_id_type=pl.DeviceIdType.MESH)
        for k in range(1, self.planes):
            pl.semaphore_signal(barrier, 1, device_id={"dp": self.d, "mp": self.along(k)},
                                device_id_type=pl.DeviceIdType.MESH)
        pl.semaphore_wait(barrier, self.planes + 2)


class Scatter:
    def __init__(self, at, items, src, got_core, got_first, got_second, send_sem, recv_sem):
        self.at, self.items, self.src = at, items, src
        self.got_core, self.got_first, self.got_second = got_core, got_first, got_second
        self.send_sem, self.recv_sem = send_sem, recv_sem

    def copy(self, stage, step, item):
        at = self.at
        kind, cols, x_first = self.items[item]
        if stage == 0:
            src = self.src.at[step, kind, :, :, 1 - at.core, :, cols]
            dst = self.got_core.at[step, kind, :, :, :, cols]
            to = at.sibling
        elif stage == 1:
            if x_first:
                src = self.got_core.at[step, kind, :, 1 - at.x, :, cols]
            else:
                src = self.got_core.at[step, kind, 1 - at.y, :, :, cols]
            dst = self.got_first.at[step, kind, :, :, cols]
            to = at.beside if x_first else at.above
        else:
            src = self.got_first.at[step, kind, 1 - at.y if x_first else 1 - at.x, :, cols]
            dst = self.got_second.at[step, kind, :, cols]
            to = at.above if x_first else at.beside
        sem = (stage, item, step)
        return at.copy(src, dst, self.send_sem.at[sem], self.recv_sem.at[sem], dp=to)

    def start(self, step):
        for item in range(len(self.items)):
            self.copy(0, step, item).start()

    def after_core(self, step):
        for item, (kind, cols, _) in enumerate(self.items):
            self.copy(0, step, item).wait_recv()
            for row in ((0, 0), (0, 1), (1, 0), (1, 1)):
                own = self.src[(step, kind, *row, self.at.core, slice(None), cols)]
                to = (step, kind, *row, slice(None), cols)
                total = own.astype(F32) + self.got_core[to].astype(F32)
                self.got_core[to] = total.astype(BF16)
            self.copy(1, step, item).start()

    def after_first(self, step):
        for item, (kind, cols, x_first) in enumerate(self.items):
            self.copy(1, step, item).wait_recv()
            for row in range(2):
                if x_first:
                    own = self.got_core[step, kind, row, self.at.x, :, cols]
                else:
                    own = self.got_core[step, kind, self.at.y, row, :, cols]
                total = own.astype(F32) + self.got_first[step, kind, row, :, cols].astype(F32)
                self.got_first[step, kind, row, :, cols] = total.astype(BF16)
            self.copy(2, step, item).start()

    def total(self, step, item):
        kind, cols, x_first = self.items[item]
        self.copy(2, step, item).wait_recv()
        own = self.got_first[step, kind, self.at.y if x_first else self.at.x, :, cols]
        return own.astype(F32) + self.got_second[step, kind, :, cols].astype(F32)

    def after_second(self, step):
        for item, (kind, cols, _) in enumerate(self.items):
            self.got_second[step, kind, :, cols] = self.total(step, item).astype(BF16)

    def wait_send(self, step):
        for item in range(len(self.items)):
            for stage in range(3):
                self.copy(stage, step, item).wait_send()


class Gather:
    def __init__(self, at, shard, full, send_sem, recv_sem):
        self.at, self.shard, self.full = at, shard, full
        self.send_sem, self.recv_sem = send_sem, recv_sem

    def there(self, r, does):
        plane = self.at.z + r

        @pl.when((plane >= 0) & (plane < self.at.planes))
        def _():
            does(plane)

    def piece(self, plane, y=False, x=False, core=False):
        at = self.at
        return self.full.at[plane, 1 - at.y if y else at.y, 1 - at.x if x else at.x,
                            1 - at.core if core else at.core]

    def copy(self, kind, plane, src, dst=None, **to):
        return self.at.copy(
            src, src if dst is None else dst, self.send_sem.at[kind, plane],
            self.recv_sem.at[kind % 8, plane], **to
        )

    def arrived(self, kind, plane, ref):
        self.copy(kind, plane, ref, dp=self.at.sibling).wait_recv()

    def pass_on(self, kind, plane, src, act):
        z, dst = self.at.z, self.piece(plane)
        if kind == 0:
            @pl.when(z < self.at.planes - 1)
            def _():
                act(self.copy(0, plane, src, dst, mp=z + 1))
        else:
            @pl.when(z > 0)
            def _():
                act(self.copy(8, plane, src, dst, mp=z - 1))

    def start(self):
        for kind in (0, 8):
            self.pass_on(kind, self.at.z, self.shard, lambda copy: copy.start())

    def spread(self, *which):
        for r in which:
            def does(plane):
                src = self.piece(plane)
                if r:
                    self.arrived(0, plane, src)
                    self.pass_on(0 if r < 0 else 8, plane, src, lambda copy: copy.start())
                self.copy(1, plane, src, dp=self.at.beside).start()
                self.copy(2, plane, src, dp=self.at.above).start()
                self.copy(3, plane, src, dp=self.at.sibling).start()

            self.there(r, does)

    def forward(self, *which):
        at = self.at
        for r in which:
            def does(plane):
                from_x, from_y = self.piece(plane, x=True), self.piece(plane, y=True)
                self.arrived(1, plane, from_x)
                if r % 2 == 0:
                    self.copy(5, plane, from_x, dp=at.above).start()
                self.copy(4, plane, from_x, dp=at.sibling).start()
                self.arrived(2, plane, from_y)
                if r % 2 == 1:
                    self.copy(5, plane, from_y, dp=at.beside).start()
                self.copy(6, plane, from_y, dp=at.sibling).start()

            self.there(r, does)

    def across(self, *which):
        for r in which:
            def does(plane):
                src = self.piece(plane, y=True, x=True)
                self.arrived(5, plane, src)
                self.copy(7, plane, src, dp=self.at.sibling).start()

            self.there(r, does)

    def last(self):
        for plane in range(self.at.planes):
            self.arrived(3, plane, self.piece(plane, core=True))
            self.arrived(4, plane, self.piece(plane, x=True, core=True))
            self.arrived(6, plane, self.piece(plane, y=True, core=True))
            self.arrived(7, plane, self.piece(plane, y=True, x=True, core=True))

    def wait_send(self):
        for r in range(1 - self.at.planes, self.at.planes):
            def does(plane):
                src = self.piece(plane)
                if r <= 0:
                    self.pass_on(0, plane, src, lambda copy: copy.wait_send())
                if r >= 0:
                    self.pass_on(8, plane, src, lambda copy: copy.wait_send())
                for kind in range(1, 8):
                    self.copy(kind, plane, src, dp=self.at.sibling).wait_send()

            self.there(r, does)


class Along:
    def __init__(self, at, parts, got, send_sem, recv_sem):
        self.at, self.parts, self.got = at, parts, got
        self.send_sem, self.recv_sem = send_sem, recv_sem
        self.inner = (at.z == 1) | (at.z == 2)

    def copy(self, step, kind):
        at, inner = self.at, self.inner
        side = 1 - 2 * (at.z // 2)
        to = at.z + jnp.where(inner & (step == 2), -side, side)
        slot = jnp.where(inner, 2 + 2 * step - 3 * (step // 2), step + step // 2)
        return at.copy(self.parts.at[step, kind], self.got.at[kind, slot],
                       self.send_sem.at[kind, step], self.recv_sem.at[kind, slot], mp=to)

    def arrived(self, kind, slot):
        ref = self.got.at[kind, slot]
        self.at.copy(ref, ref, self.send_sem.at[kind, 0], self.recv_sem.at[kind, slot],
                     mp=self.at.along(1)).wait_recv()

    def send_outer(self, step):
        @pl.when(jnp.logical_not(self.inner))
        def _():
            for kind in range(self.got.shape[0]):
                self.copy(step, kind).start()

    def send_inner(self, step):
        @pl.when(self.inner)
        def _():
            for kind in range(self.got.shape[0]):
                self.arrived(kind, step)
                own = self.parts[step, kind].astype(F32)
                total = own + self.got[kind, step].astype(F32)
                self.parts[step, kind] = total.astype(BF16)
                self.copy(step, kind).start()

    def add(self, kind, out):
        self.arrived(kind, 3)
        out[...] += self.got[kind, 3].astype(F32)

        @pl.when(self.inner)
        def _():
            self.arrived(kind, 4)
            out[...] += self.got[kind, 4].astype(F32)

    def wait_send(self, step):
        for kind in range(self.got.shape[0]):
            self.copy(step, kind).wait_send()


def gelu_parts(up):
    inner = 0.7978845608028654 * (up + 0.044715 * up * up * up)
    th = jnp.tanh(inner)
    half = 0.5 * (1.0 + th)
    slope = half + 0.5 * up * (1.0 - th * th) * (
        0.7978845608028654 * (1.0 + 3 * 0.044715 * up * up)
    )
    return up * half, slope


def halves(width):
    return (0, slice(0, width // 2), True), (0, slice(width // 2, width), False)


def feed_remote_kernel(
    x_ref, dy_ref, w_hbm, g_attn, z_attn, gain, gains_in,
    branch, d_normed, out_attn, out_up, out_down, out_gains,
    xt, dt, w_buf, g_ff, ff_core, ff_first, ff_second, at_core, at_first, at_second, got_z,
    sums, got_sums, z_sums,
    w_sem, ff_send, ff_recv, at_send, at_recv, z_send, z_recv, sum_send, sum_recv,
):
    width = x_ref.shape[1]
    steps, shard = w_hbm.shape[0], w_hbm.shape[3]
    half = width // 2
    at = Place(steps)
    at.greet()
    attn = Scatter(at, halves(width), g_attn, at_core, at_first, at_second, at_send, at_recv)
    both = (0, slice(0, width), True), (1, slice(0, width), False)
    feed = Scatter(at, both, g_ff, ff_core, ff_first, ff_second, ff_send, ff_recv)
    along = Along(at, ff_second, got_z, z_send, z_recv)
    last = steps - 1

    def w_copy(step, kind):
        slot = lax.rem(step, 2)
        return pltpu.make_async_copy(
            w_hbm.at[at.target(step), :, kind], w_buf.at[slot, kind], w_sem.at[slot, kind]
        )

    def feed_half(step, index):
        cols = slice(half * index, half * index + half)
        slot = lax.rem(step, 2)
        upper = w_buf[slot, 0, :, :, cols].reshape(width, half)
        lower = w_buf[slot, 1, :, :, cols].reshape(width, half)
        value, slope = gelu_parts(nn(x_ref[...], upper))
        hidden = value.astype(BF16)
        d_up = (nn(dy_ref[...], lower) * slope).astype(BF16)
        split = (2, 2, 2, shard, half)
        g_ff[step, 0, :, :, :, :, cols] = nn(xt[...], d_up).astype(BF16).reshape(split)
        g_ff[step, 1, :, :, :, :, cols] = nn(dt[...], hidden).astype(BF16).reshape(split)
        branch[...] += nt(hidden, lower)
        d_normed[...] += nt(d_up, upper)

    attn.start(0)
    for kind in range(2):
        w_copy(0, kind).start()
    xt[...] = x_ref[...].T
    dt[...] = dy_ref[...].T
    branch[...] = jnp.zeros_like(branch)
    d_normed[...] = jnp.zeros_like(d_normed)

    def one_step(step, carry):
        for kind in range(2):
            w_copy(step, kind).wait()

        @pl.when(step + 1 < steps)
        def _():
            for kind in range(2):
                w_copy(step + 1, kind).start()

        feed_half(step, 0)

        @pl.when(step == 0)
        def _():
            attn.after_core(0)

        @pl.when(step >= 1)
        def _():
            feed.after_core(step - 1)

        @pl.when(step >= 2)
        def _():
            feed.after_second(step - 2)
            along.send_outer(step - 2)

        feed_half(step, 1)
        feed.start(step)

        @pl.when(step >= 2)
        def _():
            along.send_inner(step - 2)

        @pl.when(step == 0)
        def _():
            attn.after_first(0)

        @pl.when(step >= 1)
        def _():
            feed.after_first(step - 1)

        return carry

    lax.fori_loop(0, steps, one_step, 0)

    sums[0] = gains_in[...]
    store_gain(sums.at[0], d_normed[...], x_ref[...], gain[...])

    def sum_copy(stage):
        to = (at.sibling, at.beside, at.above)[stage]
        return at.copy(sums.at[stage], got_sums.at[stage], sum_send.at[stage],
                       sum_recv.at[stage], dp=to)

    def sum_z_copy(k):
        return at.copy(sums.at[3], z_sums.at[at.z], sum_send.at[2 + k], sum_recv.at[2 + k],
                       mp=at.along(k))

    def next_sum(stage):
        sum_copy(stage).wait_recv()
        sums[stage + 1] = sums[stage] + got_sums[stage]

    sum_copy(0).start()
    feed.after_core(last)
    next_sum(0)
    sum_copy(1).start()
    feed.after_second(last - 1)
    along.send_outer(last - 1)
    along.send_inner(last - 1)
    next_sum(1)
    sum_copy(2).start()
    for item in range(2):
        cols = attn.items[item][1]
        out_attn[:, cols] = attn.total(0, item) + z_attn[:, cols]
    feed.after_first(last)
    next_sum(2)
    for k in range(1, steps):
        sum_z_copy(k).start()
    z_sums[at.z] = sums[3]
    for kind, out in enumerate((out_up, out_down)):
        out[...] = feed.total(last, kind)
        along.add(kind, out)
    for k in range(1, steps):
        sum_z_copy(k).wait_recv()
    total = z_sums[0]
    for k in range(1, steps):
        total = total + z_sums[k]
    out_gains[...] = total

    attn.wait_send(0)
    for step in range(steps):
        feed.wait_send(step)
    for step in range(last):
        along.wait_send(step)
    for stage in range(3):
        sum_copy(stage).wait_send()
    for k in range(1, steps):
        sum_z_copy(k).wait_send()


def feed_remote_call(normed, grads, w_ff, g_attn, z_attn, gain, gains):
    rows, width = normed.shape
    steps, _, _, shard, _ = w_ff.shape
    vmem = pl.BlockSpec(memory_space=pltpu.VMEM)
    return pl.pallas_call(
        feed_remote_kernel,
        in_specs=[vmem, vmem, pl.BlockSpec(memory_space=pl.ANY)] + [vmem] * 4,
        out_specs=[vmem] * 6,
        out_shape=[jax.ShapeDtypeStruct((rows, width), F32)] * 2
        + [jax.ShapeDtypeStruct((shard, width), F32)] * 3
        + [jax.ShapeDtypeStruct((8, 128), F32)],
        scratch_shapes=[
            pltpu.VMEM((width, rows), BF16),
            pltpu.VMEM((width, rows), BF16),
            pltpu.VMEM((2, 2, 8, shard, width), BF16),
            pltpu.VMEM((steps, 2, 2, 2, 2, shard, width), BF16),
            pltpu.VMEM((steps, 2, 2, 2, shard, width), BF16),
            pltpu.VMEM((steps, 2, 2, shard, width), BF16),
            pltpu.VMEM((steps, 2, shard, width), BF16),
            pltpu.VMEM((1, 1, 2, 2, shard, width), BF16),
            pltpu.VMEM((1, 1, 2, shard, width), BF16),
            pltpu.VMEM((1, 1, shard, width), BF16),
            pltpu.VMEM((2, 5, shard, width), BF16),
            pltpu.VMEM((4, 8, 128), F32),
            pltpu.VMEM((3, 8, 128), F32),
            pltpu.VMEM((steps, 8, 128), F32),
            pltpu.SemaphoreType.DMA((2, 2)),
            pltpu.SemaphoreType.DMA((3, 2, steps)),
            pltpu.SemaphoreType.DMA((3, 2, steps)),
            pltpu.SemaphoreType.DMA((3, 2, 1)),
            pltpu.SemaphoreType.DMA((3, 2, 1)),
            pltpu.SemaphoreType.DMA((2, steps - 1)),
            pltpu.SemaphoreType.DMA((2, 5)),
            pltpu.SemaphoreType.DMA((6,)),
            pltpu.SemaphoreType.DMA((6,)),
        ],
        compiler_params=pltpu.CompilerParams(
            collective_id=0, has_side_effects=True, vmem_limit_bytes=VMEM
        ),
        cost_estimate=pl.CostEstimate(
            flops=12 * rows * width * width * steps,
            bytes_accessed=4 * steps * width * width * 2,
            transcendentals=rows * width * steps,
        ),
        name="feed_forward_scatter",
    )(normed, grads, w_ff, g_attn, z_attn, gain, gains)


def iota(shape, axis):
    return lax.broadcasted_iota(jnp.int32, shape, axis)


def source_of(index, start, total):
    rest = index - BIG
    other = jnp.where(rest < start, rest, rest + MOST)
    held = jnp.where(index < MOST, start + index, -1)
    return jnp.where((rest >= 0) & (rest < total - MOST), other, held)


def store_gain(out, d_normed, normed, gain):
    total = jnp.sum(d_normed * normed.astype(F32), axis=0, keepdims=True) / gain
    for row in range(total.shape[1] // 128):
        out[row:row + 1] += total[:, 128 * row:128 * row + 128]


def prepare(
    me, part, ids, pieces, x_ref, dy_ref, xt, dt, feat_q, feat_k, pt, d_normed, branch, g_gains
):
    mp = ids.shape[1]
    total = mp * part
    numbers = ids[me]
    start = jnp.zeros((1, 1), jnp.int32)
    for image in range(IMAGES):
        count = jnp.sum((numbers == image).astype(F32), axis=(0, 1), keepdims=True)
        ahead = jnp.sum(
            ((numbers >= 0) & (numbers < image)).astype(F32), axis=(0, 1), keepdims=True
        )
        start = start + jnp.where(count == MOST, ahead, 0.0).astype(jnp.int32)
    column = source_of(iota((ROWS, 1), 0), start, total)
    line = source_of(iota((1, ROWS), 1), start, total)
    x_sum, dy_sum, feats = 0.0, 0.0, 0.0
    for k, piece in enumerate(pieces):
        chunk = lax.rem(me - k + mp, mp)
        offset = iota((1, PIECE), 1)
        pos = jnp.where(offset < part, chunk * part + offset, -2)
        pick = (column == pos).astype(F32).astype(BF16)
        offset = iota((PIECE, 1), 0)
        pos = jnp.where(offset < part, chunk * part + offset, -2)
        pt[k] = (line == pos).astype(F32).astype(BF16)
        x_sum = x_sum + nn(pick, piece[0][...])
        dy_sum = dy_sum + nn(pick, piece[1][...])
        marks = (iota((128, 1), 0) - HD == ids[me, pl.ds(chunk, 1), :]).astype(F32)
        feats = feats + nt(pick, marks.astype(BF16))
    x = x_sum.astype(BF16)
    dy = dy_sum.astype(BF16)
    x_ref[...] = x
    dy_ref[...] = dy
    xt[...] = x.T
    dt[...] = dy.T
    lane = iota((1, 128), 1)
    feat_q[...] = (feats * 128.0).astype(BF16)
    marked = (lane >= HD) & (lane < HD + IMAGES)
    feat_k[...] = jnp.where(marked, (feats - 1.0) * 256.0, 0.0).astype(BF16)
    d_normed[...] = jnp.zeros_like(d_normed)
    branch[...] = jnp.zeros_like(branch)
    g_gains[...] = jnp.zeros_like(g_gains)


def attention_chunk(
    weights, gain, x_ref, dy_ref, xt, dt, feat_q, feat_k, raw, d_raw, d_att, att,
    d_normed, branch, g_gains, store, poll,
):
    raw[...] = nn(x_ref[...], weights(slice(0, 640)))
    d_att[...] = nn(dy_ref[...], weights(slice(512, 768)))
    lane = iota((1, 128), 1)
    low = lane < HD
    same = (iota((128, 128), 0) // HD == iota((128, 128), 1) // HD).astype(F32)
    mean_of = (same * (1.0 / HD)).astype(BF16)

    def half_mean(value):
        return nn(value.astype(BF16), mean_of)

    d_gain = jnp.zeros((1, 128), F32)
    for head in range(3):
        qk = raw[:, 128 * head:128 * head + 128]
        high = qk.astype(BF16)
        mean = nn(high, mean_of) + half_mean(qk - high.astype(F32))
        centered = qk - mean
        spread = lax.rsqrt(half_mean(centered * centered) + 1e-6)
        unit = centered * spread
        rounded = (unit * gain).astype(BF16).astype(F32)
        q_aug = jnp.where(low, rounded * 0.125, feat_q[...].astype(F32)).astype(BF16)
        k_aug = jnp.where(low, pltpu.roll(rounded, HD, 1), feat_k[...].astype(F32)).astype(BF16)
        v_tile = 384 + 128 * (head // 2)
        v = raw[:, v_tile:v_tile + 128]
        if head == 1:
            v = pltpu.roll(v, HD, 1)
        one = ((lane == HD) | (lane == HD + 1)).astype(F32)
        v_aug = jnp.where(low, v, one).astype(BF16)
        a_tile = 128 * ((head + 1) // 2)
        da = d_att[:, a_tile:a_tile + 128]
        if head != 1:
            da = pltpu.roll(da, HD, 1)
        q_t = q_aug.astype(F32).T.astype(BF16)
        d_queries, attended, d_keys, d_values = [], [], [], []
        for base, count in ((0, BIG), (BIG, REST)):
            keys = k_aug[base:base + count]
            values = v_aug[base:base + count]
            dk_t = jnp.zeros((128, count), F32)
            dv_t = jnp.zeros((128, count), F32)
            for row in range(base, base + count, 256):
                rows = slice(row, row + 256)
                prob = jnp.exp(nt(q_aug[rows], keys))
                prob_low = prob.astype(BF16)
                gathered = nn(prob_low, values)
                inverse = 1.0 / gathered[:, HD:HD + 1]
                out = jnp.where(low, gathered * inverse, 0.0)
                attended.append(out)
                scaled = jnp.where(low, da[rows] * inverse, 0.0).astype(BF16).astype(F32)
                dot = jnp.sum(scaled * out, axis=-1, keepdims=True)
                dot_high = dot.astype(BF16).astype(F32)
                d_aug = jnp.where(
                    lane == HD, -dot_high, jnp.where(lane == HD + 1, dot_high - dot, scaled)
                )
                d_low = d_aug.astype(BF16)
                d_score = (prob * nt(d_low, values)).astype(BF16)
                d_queries.append(nn(d_score, keys))
                dk_t = dk_t + nn(q_t[:, rows], d_score)
                dv_t = dv_t + nn(d_aug.T.astype(BF16), prob_low)
            d_keys.append(dk_t.T)
            d_values.append(dv_t.T)
        d_query = jnp.concatenate(d_queries, axis=0) * 0.125
        d_key = jnp.concatenate(d_keys, axis=0)
        d_value = jnp.concatenate(d_values, axis=0)
        attend = jnp.concatenate(attended, axis=0)
        d_qk = jnp.where(low, d_query, pltpu.roll(d_key, HD, 1))
        d_gain = d_gain + jnp.sum(d_qk * unit, axis=0, keepdims=True)
        scaled = d_qk * gain
        d_qk = spread * (scaled - half_mean(scaled) - unit * half_mean(scaled * unit))
        d_raw[:, 128 * head:128 * head + 128] = d_qk.astype(BF16)
        if head == 0:
            first_value = d_value
            att[:, 0:128] = jnp.where(low, 0.0, pltpu.roll(attend, HD, 1)).astype(BF16)
        elif head == 1:
            both = jnp.where(low, first_value, pltpu.roll(d_value, HD, 1))
            d_raw[:, 384:512] = both.astype(BF16)
            first_att = attend
        else:
            d_raw[:, 512:640] = jnp.where(low, d_value, 0.0).astype(BF16)
            both = jnp.where(low, first_att, pltpu.roll(attend, HD, 1))
            att[:, 128:256] = both.astype(BF16)
        poll(head)
    g_gains[6:7] += d_gain
    d_projected = d_raw[...]
    attended = att[...]
    d_normed[...] += nt(d_projected, weights(slice(0, 640)))
    branch[...] += nt(attended, weights(slice(512, 768)))
    left = nn(xt[...], d_projected)
    right = nn(dt[...], attended)
    store(slice(0, 512), left[:, :512].astype(BF16))
    store(slice(512, 640), (left[:, 512:] + right[:, :128]).astype(BF16))
    store(slice(640, 768), right[:, 128:].astype(BF16))


def take_back(outs, pt, x_ref, norm_gain, d_normed, branch, g_gains):
    store_gain(g_gains, d_normed[...], x_ref[...], norm_gain[...])
    d_rows = d_normed[...].astype(BF16)
    b_rows = branch[...].astype(BF16)
    for k, out in enumerate(outs):
        out[0] = nn(pt[k], d_rows).astype(BF16)
        out[1] = nn(pt[k], b_rows).astype(BF16)


def attention_kernel(
    part, place, own_x, own_dy, in1, in2, in3, ids, gains, norm_gain, weights,
    out0, out1, out2, out3, g_weights, g_gains,
    x_ref, dy_ref, xt, dt, feat_q, feat_k, pt, raw, d_raw, d_att, att, d_normed, branch,
):
    step = pl.program_id(0)

    @pl.when(step == 0)
    def _():
        pieces = [(own_x.at[0], own_dy.at[0])] + [(got.at[0], got.at[1]) for got in (in1, in2, in3)]
        prepare(place[0], part, ids, pieces, x_ref, dy_ref, xt, dt, feat_q, feat_k, pt,
                d_normed, branch, g_gains)

    def store(cols, value):
        g_weights[0, :, cols] = value

    attention_chunk(
        lambda cols: weights[0, :, cols], gains[...], x_ref, dy_ref, xt, dt, feat_q, feat_k,
        raw, d_raw, d_att, att, d_normed, branch, g_gains, store, lambda head: None,
    )

    @pl.when(step == pl.num_programs(0) - 1)
    def _():
        take_back((out0, out1, out2, out3), pt, x_ref, norm_gain, d_normed, branch, g_gains)


def attention_call(place, part, normed, grads, received, ids, gains, norm_gain, weights):
    width = normed.shape[-1]
    chunks = weights.shape[0]
    mp = ids.shape[1]
    own = pl.BlockSpec((1, PIECE, width), lambda m, place: (0, 0, 0))
    pair = pl.BlockSpec((2, PIECE, width), lambda m, place: (0, 0, 0))
    chunk = pl.BlockSpec((1, width, width), lambda m, place: (m, 0, 0))
    line = pl.BlockSpec((1, 128), lambda m, place: (0, 0))
    return pl.pallas_call(
        functools.partial(attention_kernel, part),
        grid_spec=pltpu.PrefetchScalarGridSpec(
            num_scalar_prefetch=1,
            grid=(chunks,),
            in_specs=[own, own, pair, pair, pair,
                      pl.BlockSpec(ids.shape, lambda m, place: (0, 0, 0)),
                      line, pl.BlockSpec((1, width), lambda m, place: (0, 0)), chunk],
            out_specs=[pair] * 4 + [chunk, pl.BlockSpec((8, 128), lambda m, place: (0, 0))],
            scratch_shapes=[
                pltpu.VMEM((ROWS, width), BF16),
                pltpu.VMEM((ROWS, width), BF16),
                pltpu.VMEM((width, ROWS), BF16),
                pltpu.VMEM((width, ROWS), BF16),
                pltpu.VMEM((ROWS, 128), BF16),
                pltpu.VMEM((ROWS, 128), BF16),
                pltpu.VMEM((mp, PIECE, ROWS), BF16),
                pltpu.VMEM((ROWS, 640), F32),
                pltpu.VMEM((ROWS, 640), BF16),
                pltpu.VMEM((ROWS, 256), F32),
                pltpu.VMEM((ROWS, 256), BF16),
                pltpu.VMEM((ROWS, width), F32),
                pltpu.VMEM((ROWS, width), F32),
            ],
        ),
        out_shape=[jax.ShapeDtypeStruct((2, PIECE, width), BF16)] * 4
        + [jax.ShapeDtypeStruct(weights.shape, BF16), jax.ShapeDtypeStruct((8, 128), F32)],
        compiler_params=pltpu.CompilerParams(vmem_limit_bytes=VMEM),
        cost_estimate=pl.CostEstimate(
            flops=60_000_000_000, bytes_accessed=4 * chunks * width * width,
            transcendentals=ROWS * ROWS * 12,
        ),
        name="attention",
    )(place, normed, grads, *received, ids, gains, norm_gain, weights)


def group_means():
    same = (iota((128, 128), 0) // HD == iota((128, 128), 1) // HD).astype(F32)
    return (same * (1.0 / HD)).astype(BF16)


def forward_chunk(
    weights, gain, x_ref, feat_q, feat_k, raw, qk_all, v_all, stats, att, branch, begin, spill
):
    raw[...] = nn(x_ref[...], weights(slice(0, 640)))
    lane = iota((1, 128), 1)
    low = lane < HD
    mean_of = group_means()
    stat = jnp.zeros((ROWS, 128), F32)
    for head in range(3):
        qk = raw[:, 128 * head:128 * head + 128]
        high = qk.astype(BF16)
        mean = nn(high, mean_of) + nn((qk - high.astype(F32)).astype(BF16), mean_of)
        centered = qk - mean
        spread = lax.rsqrt(nn((centered * centered).astype(BF16), mean_of) + 1e-6)
        rounded = (centered * spread * gain).astype(BF16)
        qk_all[head] = rounded
        rounded = rounded.astype(F32)
        q_aug = jnp.where(low, rounded * 0.125, feat_q[...].astype(F32)).astype(BF16)
        k_aug = jnp.where(low, pltpu.roll(rounded, HD, 1), feat_k[...].astype(F32)).astype(BF16)
        v_tile = 384 + 128 * (head // 2)
        v = raw[:, v_tile:v_tile + 128]
        if head == 1:
            v = pltpu.roll(v, HD, 1)
        v_aug = jnp.where(low, v, 1.0).astype(BF16)
        v_all[head] = v_aug
        p_ref = begin(head)
        parts = []
        for base, count in ((0, BIG), (BIG, REST)):
            keys = k_aug[base:base + count]
            values = v_aug[base:base + count]
            for row in range(base, base + count, 256):
                rows = slice(row, row + 256)
                prob = jnp.exp(nt(q_aug[rows], keys)).astype(BF16)
                p_ref[rows, :count] = prob
                parts.append(nn(prob, values))
        spill(head)
        gathered = jnp.concatenate(parts, axis=0)
        inverse = 1.0 / gathered
        attend = gathered * pltpu.roll(inverse, HD, 1)
        stat = jnp.where((lane == head) | (lane == HD + head), spread, stat)
        stat = jnp.where(lane == HD + 8 + head, inverse, stat)
        if head == 0:
            att[:, 0:128] = jnp.where(low, 0.0, pltpu.roll(attend, HD, 1)).astype(BF16)
        elif head == 1:
            first = attend
        else:
            att[:, 128:256] = jnp.where(low, first, pltpu.roll(attend, HD, 1)).astype(BF16)
    stats[...] = stat
    branch[...] += nt(att[...], weights(slice(512, 768)))


def backward_chunk(
    weights, gain, dy_ref, xt, dt, raw, d_raw, qk_all, v_all, stats, att,
    d_normed, g_gains, ready, store, poll,
):
    raw[:, :256] = nn(dy_ref[...], weights(slice(512, 768)))
    lane = iota((1, 128), 1)
    low = lane < HD
    mean_of = group_means()
    stat = stats[...]
    back_gain = 1.0 / gain
    d_gain = jnp.zeros((1, 128), F32)
    for head in range(3):
        qk = qk_all[head]
        v_aug = v_all[head]
        tile = 128 * ((head + 1) // 2)
        da = raw[:, tile:tile + 128]
        out = att[:, tile:tile + 128].astype(F32)
        if head != 1:
            da = pltpu.roll(da, HD, 1)
            out = pltpu.roll(out, HD, 1)
        inverse = stat[:, HD + 8 + head:HD + 9 + head]
        scaled = jnp.where(low, da * inverse, 0.0).astype(BF16).astype(F32)
        dot = jnp.sum(scaled * out, axis=-1, keepdims=True)
        dot_high = dot.astype(BF16).astype(F32)
        d_aug = jnp.where(
            lane == HD, -dot_high, jnp.where(lane == HD + 1, dot_high - dot, scaled)
        )
        d_low = d_aug.astype(BF16)
        d_t = d_aug.T.astype(BF16)
        qk_low = qk.astype(F32)
        qk_t = qk_low.T.astype(BF16)
        p_ref = ready(head)
        d_queries, d_keys, d_values = [], [], []
        for base, count in ((0, BIG), (BIG, REST)):
            block = slice(base, base + count)
            d_values.append(nn(d_t[:, block], p_ref[block, :count]).T)
            for row in range(base, base + count, 256):
                rows = slice(row, row + 256)
                d_prob = nt(d_low[rows], v_aug[block])
                d_score = (p_ref[rows, :count].astype(F32) * d_prob).astype(BF16)
                p_ref[rows, :count] = d_score
                d_queries.append(nn(d_score, qk[block]))
            d_keys.append(nn(qk_t[:, block], p_ref[block, :count]).T)
        d_query = jnp.concatenate(d_queries, axis=0)
        d_key = jnp.concatenate(d_keys, axis=0)
        d_value = jnp.concatenate(d_values, axis=0)
        d_qk = pltpu.roll(jnp.where(low, d_key, d_query), HD, 1) * 0.125
        unit = qk_low * back_gain
        spread = jnp.where(low, stat[:, head:head + 1], stat[:, HD + head:HD + head + 1])
        d_gain = d_gain + jnp.sum(d_qk * unit, axis=0, keepdims=True)
        scaled = d_qk * gain
        mean = nn(scaled.astype(BF16), mean_of)
        d_qk = spread * (scaled - mean - unit * nn((scaled * unit).astype(BF16), mean_of))
        d_raw[:, 128 * head:128 * head + 128] = d_qk.astype(BF16)
        if head == 0:
            first = d_value
        elif head == 1:
            both = jnp.where(low, first, pltpu.roll(d_value, HD, 1))
            d_raw[:, 384:512] = both.astype(BF16)
        else:
            d_raw[:, 512:640] = jnp.where(low, d_value, 0.0).astype(BF16)
        poll(head)
    g_gains[6:7] += d_gain
    d_projected = d_raw[...]
    d_normed[...] += nt(d_projected, weights(slice(0, 640)))
    left = nn(xt[...], d_projected)
    right = nn(dt[...], att[...])
    store(slice(0, 512), left[:, :512].astype(BF16))
    store(slice(512, 640), (left[:, 512:] + right[:, :128]).astype(BF16))
    store(slice(640, 768), right[:, 128:].astype(BF16))


def front_kernel(
    tok, cot, ids, gains, norm_gain, w_attn, w_feed,
    normed, grads, returned, out0, out1, out2, out3, w_ff, g_last, z_attn, g_gains, p_all,
    got_rows, w_full, g_buf, at_core, at_first, at_second, got_z,
    x_ref, dy_ref, xt, dt, feat_q, feat_k, pt, raw, d_raw, p_buf,
    qk_all, v_all, stats, att, total,
    row_send, row_recv, back_send, back_recv, wa_send, wa_recv, wf_send, wf_recv, own_sem,
    p_out, p_in, at_send, at_recv, z_send, z_recv,
):
    count, part, width = tok.shape
    shard = w_attn.shape[0]
    at = Place(count)
    at.greet()
    gather = Gather(at, w_attn, w_full, wa_send, wa_recv)
    gather_ff = Gather(at, w_feed, w_ff, wf_send, wf_recv)
    scatter = Scatter(at, halves(width), g_buf, at_core, at_first, at_second, at_send, at_recv)
    own_ff = pltpu.make_async_copy(w_feed, gather_ff.piece(at.z), own_sem)
    along = Along(at, at_second, got_z, z_send, z_recv)

    def row_copy(kind, k):
        src = (normed, grads)[kind].at[k]
        return at.copy(src, got_rows.at[k - 1, kind], row_send.at[kind, k - 1],
                       row_recv.at[kind, k - 1], mp=at.along(k))

    def back_copy(k):
        return at.copy(got_rows.at[k - 1, 0], returned.at[k], back_send.at[k - 1],
                       back_recv.at[k - 1], mp=at.along(-k))

    gather.start()
    own_ff.start()
    w_full[at.z, at.y, at.x, at.core] = w_attn[...]
    gather.spread(0)
    gain = norm_gain[...]
    for k in (1, 3, 2, 0):
        sequence = at.along(k)
        x = tok[sequence].astype(F32)
        centered = x - jnp.mean(x, axis=-1, keepdims=True)
        spread = lax.rsqrt(jnp.mean(centered * centered, axis=-1, keepdims=True) + 1e-6)
        pad = jnp.zeros((PIECE - part, width), BF16)
        normed[k, :part] = (centered * spread * gain).astype(BF16)
        normed[k, part:] = pad
        if k:
            row_copy(0, k).start()
        grads[k, :part] = cot[sequence]
        grads[k, part:] = pad
    place_rows(at.z, part, ids, pt, feat_q, feat_k)
    g_gains[...] = jnp.zeros_like(g_gains)
    total[...] = jnp.zeros_like(total)
    gather.spread(-1, 1)
    gather.forward(0)
    gather.spread(-2, 2)
    own_ff.wait()
    gather.forward(-1, 1)
    gather.across(0)
    gather.spread(-3, 3)
    gather_ff.spread(0)
    gather.forward(-2, 2)
    gather.across(-1, 1)
    gather.forward(-3, 3)
    gather.across(-2, 2)
    gather.across(-3, 3)
    gather.last()
    for k in (1, 3, 2):
        row_copy(0, k).wait_recv()
    for k in (1, 3, 2):
        row_copy(1, k).start()

    def lay_out(kind, own, rows, columns):
        value = 0.0
        for k in range(count):
            piece = own[0] if k == 0 else got_rows[k - 1, kind]
            value = value + lax.dot_general(
                pt[k], piece, (((0,), (0,)), ((), ())), preferred_element_type=F32
            )
        value = value.astype(BF16)
        rows[...] = value
        columns[...] = value.T

    lay_out(0, normed, x_ref, xt)

    def weights_of(chunk):
        def weights(cols):
            return w_full[chunk, :, :, :, :, cols].reshape(width, cols.stop - cols.start)

        return weights

    def p_write(step, head):
        slot = lax.rem(step + head, 2)
        return pltpu.make_async_copy(p_buf.at[slot], p_all.at[at.along(step), head],
                                     p_out.at[slot])

    def p_read(step, head):
        slot = lax.rem(step + head, 2)
        return pltpu.make_async_copy(p_all.at[at.target(step), head], p_buf.at[slot],
                                     p_in.at[slot])

    def forward_step(step, carry):
        chunk = at.along(step)

        def begin(head):
            if head == 2:
                p_write(step, 0).wait()
            else:
                @pl.when(step >= 1)
                def _():
                    p_write(step - 1, 1 + head).wait()
            return p_buf.at[lax.rem(step + head, 2)]

        forward_chunk(
            weights_of(chunk), gains[...], x_ref, feat_q, feat_k, raw, qk_all.at[chunk],
            v_all.at[chunk], stats.at[chunk], att.at[chunk], total, begin,
            lambda head: p_write(step, head).start(),
        )
        return carry

    lax.fori_loop(0, count, forward_step, 0)
    for head in (1, 2):
        p_write(count - 1, head).wait()
    p_read(0, 0).start()
    value = total[...].astype(BF16)
    returned[0] = nn(pt[0], value).astype(BF16)
    for k in range(1, count):
        got_rows[k - 1, 0] = nn(pt[k], value).astype(BF16)
    total[...] = jnp.zeros_like(total)
    for k in (1, 3, 2):
        row_copy(1, k).wait_recv()
    gather_ff.start()
    lay_out(1, grads, dy_ref, dt)

    def events(step, head):
        if step == 0 and head == 1:
            gather_ff.spread(-1, 1)
        elif step == 0 and head == 2:
            gather_ff.forward(0)
            gather_ff.spread(-2, 2)
        elif step == 1 and head == 0:
            for k in (1, 3, 2):
                back_copy(k).start()
            gather_ff.spread(-3, 3)
            gather_ff.across(0)
        elif step == 1 and head == 1:
            gather_ff.forward(-1, 1)
        elif step == 1 and head == 2:
            gather_ff.forward(-2, 2)
        elif step == 2 and head == 0:
            gather_ff.across(-1, 1)
            gather_ff.forward(-3, 3)
        elif step == 2 and head == 1:
            gather_ff.across(-2, 2)
        elif step == 2 and head == 2:
            gather_ff.across(-3, 3)
            along.send_inner(0)
        elif step == 3 and head == 1:
            along.send_inner(1)

    def backward_step(step, carry):
        chunk = at.target(step)

        def store(cols, value):
            split = (2, 2, 2, shard, cols.stop - cols.start)
            value = value.reshape(split)

            @pl.when(step < count - 1)
            def _():
                g_buf[step, 0, :, :, :, :, cols] = value

            @pl.when(step == count - 1)
            def _():
                g_last[0, 0, :, :, :, :, cols] = value

        def ready(head):
            p_read(step, head).wait()
            if head < 2:
                p_read(step, head + 1).start()
            else:
                @pl.when(step + 1 < count)
                def _():
                    p_read(step + 1, 0).start()
            return p_buf.at[lax.rem(step + head, 2)]

        def poll(head):
            @pl.when(step >= 1)
            def _():
                if head == 0:
                    scatter.after_core(step - 1)
                elif head == 1:
                    scatter.after_first(step - 1)
                else:
                    scatter.after_second(step - 1)
                    along.send_outer(step - 1)

            for which in range(count):
                @pl.when(step == which)
                def _():
                    events(which, head)

        backward_chunk(
            weights_of(chunk), gains[...], dy_ref, xt, dt, raw, d_raw,
            qk_all.at[chunk], v_all.at[chunk], stats.at[chunk], att.at[chunk], total, g_gains,
            ready, store, poll,
        )

        @pl.when(step < count - 1)
        def _():
            scatter.start(step)

        return carry

    lax.fori_loop(0, count, backward_step, 0)
    store_gain(g_gains, total[...], x_ref[...], norm_gain[...])
    value = total[...].astype(BF16)
    for k, out in enumerate((out0, out1, out2, out3)):
        out[...] = nn(pt[k], value).astype(BF16)
    along.send_inner(count - 2)
    z_attn[...] = jnp.zeros_like(z_attn)
    gather_ff.last()
    for k in range(1, count):
        back_copy(k).wait_recv()
    along.add(0, z_attn)

    gather.wait_send()
    gather_ff.wait_send()
    for k in range(1, count):
        back_copy(k).wait_send()
        for kind in range(2):
            row_copy(kind, k).wait_send()
    for step in range(count - 1):
        scatter.wait_send(step)
        along.wait_send(step)


def place_rows(me, part, ids, pt, feat_q, feat_k):
    mp = ids.shape[1]
    total = mp * part
    numbers = ids[me]
    start = jnp.zeros((1, 1), jnp.int32)
    for image in range(IMAGES):
        count = jnp.sum((numbers == image).astype(F32), axis=(0, 1), keepdims=True)
        ahead = jnp.sum(
            ((numbers >= 0) & (numbers < image)).astype(F32), axis=(0, 1), keepdims=True
        )
        start = start + jnp.where(count == MOST, ahead, 0.0).astype(jnp.int32)
    line = source_of(iota((1, ROWS), 1), start, total)
    feats = 0.0
    for k in range(mp):
        chunk = lax.rem(me - k + mp, mp)
        offset = iota((PIECE, 1), 0)
        pos = jnp.where(offset < part, chunk * part + offset, -2)
        pick = (line == pos).astype(F32).astype(BF16)
        pt[k] = pick
        marks = (iota((128, 1), 0) - HD == ids[me, pl.ds(chunk, 1), :]).astype(F32)
        feats = feats + nn(marks.astype(BF16), pick)
    feats = feats.T
    lane = iota((1, 128), 1)
    feat_q[...] = (feats * 128.0).astype(BF16)
    marked = (lane >= HD) & (lane < HD + IMAGES)
    feat_k[...] = jnp.where(marked, (feats - 1.0) * 256.0, 0.0).astype(BF16)


def front_call(tokens, cotangent, ids, gains, norm_gain, w_attn, w_feed):
    count, part, width = tokens.shape
    shard = w_attn.shape[0]
    vmem = pl.BlockSpec(memory_space=pltpu.VMEM)
    hbm = pl.BlockSpec(memory_space=pl.ANY)
    rows = jax.ShapeDtypeStruct((count, PIECE, width), BF16)
    return pl.pallas_call(
        front_kernel,
        in_specs=[vmem] * 6 + [hbm],
        out_specs=[vmem] * 7 + [hbm] + [vmem] * 3 + [hbm],
        out_shape=[rows, rows, rows]
        + [jax.ShapeDtypeStruct((PIECE, width), BF16)] * 4
        + [
            jax.ShapeDtypeStruct((count, 2, 2, 2, 2, shard, width), BF16),
            jax.ShapeDtypeStruct((1, 1, 2, 2, 2, shard, width), BF16),
            jax.ShapeDtypeStruct((shard, width), F32),
            jax.ShapeDtypeStruct((8, 128), F32),
            jax.ShapeDtypeStruct((count, 3, ROWS, BIG), BF16),
        ],
        scratch_shapes=[
            pltpu.VMEM((count - 1, 2, PIECE, width), BF16),
            pltpu.VMEM((count, 2, 2, 2, shard, width), BF16),
            pltpu.VMEM((count - 1, 1, 2, 2, 2, shard, width), BF16),
            pltpu.VMEM((count - 1, 1, 2, 2, shard, width), BF16),
            pltpu.VMEM((count - 1, 1, 2, shard, width), BF16),
            pltpu.VMEM((count - 1, 1, shard, width), BF16),
            pltpu.VMEM((1, 5, shard, width), BF16),
            pltpu.VMEM((ROWS, width), BF16),
            pltpu.VMEM((ROWS, width), BF16),
            pltpu.VMEM((width, ROWS), BF16),
            pltpu.VMEM((width, ROWS), BF16),
            pltpu.VMEM((ROWS, 128), BF16),
            pltpu.VMEM((ROWS, 128), BF16),
            pltpu.VMEM((count, PIECE, ROWS), BF16),
            pltpu.VMEM((ROWS, 640), F32),
            pltpu.VMEM((ROWS, 640), BF16),
            pltpu.VMEM((2, ROWS, BIG), BF16),
            pltpu.VMEM((count, 3, ROWS, 128), BF16),
            pltpu.VMEM((count, 3, ROWS, 128), BF16),
            pltpu.VMEM((count, ROWS, 128), F32),
            pltpu.VMEM((count, ROWS, 256), BF16),
            pltpu.VMEM((ROWS, width), F32),
            pltpu.SemaphoreType.DMA((2, count - 1)),
            pltpu.SemaphoreType.DMA((2, count - 1)),
            pltpu.SemaphoreType.DMA((count - 1,)),
            pltpu.SemaphoreType.DMA((count - 1,)),
            pltpu.SemaphoreType.DMA((9, count)),
            pltpu.SemaphoreType.DMA((8, count)),
            pltpu.SemaphoreType.DMA((9, count)),
            pltpu.SemaphoreType.DMA((8, count)),
            pltpu.SemaphoreType.DMA,
            pltpu.SemaphoreType.DMA((2,)),
            pltpu.SemaphoreType.DMA((2,)),
            pltpu.SemaphoreType.DMA((3, 2, count - 1)),
            pltpu.SemaphoreType.DMA((3, 2, count - 1)),
            pltpu.SemaphoreType.DMA((1, count - 1)),
            pltpu.SemaphoreType.DMA((1, 5)),
        ],
        compiler_params=pltpu.CompilerParams(
            collective_id=1, has_side_effects=True, vmem_limit_bytes=FRONT_VMEM
        ),
        name="front",
    )(tokens, cotangent, ids, gains, norm_gain, w_attn, w_feed)


def finish_kernel(
    place, tok, cot, gain, branch, d_ff, back, ret0, ret1, ret2, ret3, output, input_grad
):
    step = pl.program_id(0)
    part = tok.shape[1]

    for index, ret in enumerate((ret0, ret1, ret2, ret3)):

        @pl.when(step == index)
        def _():
            x = tok[0].astype(F32)
            output[0] = (x + (branch[0] + back[0].astype(F32))[:part]).astype(BF16)
            d_normed = (d_ff[0] + ret[...].astype(F32))[:part]
            centered = x - jnp.mean(x, axis=-1, keepdims=True)
            spread = lax.rsqrt(jnp.mean(centered * centered, axis=-1, keepdims=True) + 1e-6)
            unit = centered * spread
            scaled = d_normed * gain[...]
            d_x = spread * (
                scaled
                - jnp.mean(scaled, axis=-1, keepdims=True)
                - unit * jnp.mean(scaled * unit, axis=-1, keepdims=True)
            )
            input_grad[0] = cot[0].astype(F32) + d_x


def finish_call(place, tokens, cotangent, gain, branch, d_ff, back, returned):
    count, part, width = tokens.shape
    block = pl.BlockSpec(
        (1, part, width), lambda k, place: (lax.rem(place[0] + k, count), 0, 0)
    )
    padded = pl.BlockSpec((1, PIECE, width), lambda k, place: (k, 0, 0))
    piece = pl.BlockSpec((PIECE, width), lambda k, place: (0, 0))
    line = pl.BlockSpec((1, width), lambda k, place: (0, 0))
    return pl.pallas_call(
        finish_kernel,
        grid_spec=pltpu.PrefetchScalarGridSpec(
            num_scalar_prefetch=1,
            grid=(count,),
            in_specs=[block, block, line, padded, padded, padded] + [piece] * 4,
            out_specs=[block, block],
        ),
        out_shape=[
            jax.ShapeDtypeStruct(tokens.shape, BF16),
            jax.ShapeDtypeStruct(tokens.shape, F32),
        ],
        compiler_params=pltpu.CompilerParams(vmem_limit_bytes=VMEM),
        name="finish",
    )(place, tokens, cotangent, gain, branch, d_ff, back, *returned)


def pack_attention(w_qkv, w_proj):
    rows, wide = w_qkv.shape[1:]
    heads = wide // HD
    qk = w_qkv[:2].reshape(2, rows, heads, HD).transpose(1, 2, 0, 3).reshape(rows, 2 * wide)
    return jnp.concatenate([qk, w_qkv[2], w_proj.T], axis=1)


def unpack_attention(grad, wide):
    rows = grad.shape[0]
    heads = wide // HD
    qk = grad[:, :2 * wide].reshape(rows, heads, 2, HD).transpose(2, 0, 1, 3)
    qk = qk.reshape(2, rows, wide)
    g_qkv = jnp.concatenate([qk, grad[None, :, 2 * wide:3 * wide]], axis=0)
    return g_qkv, grad[:, 3 * wide:].T


def body(
    dp, mp, tokens, w_qkv, w_up, w_proj, w_down, norm_gain, query_gain, key_gain, image_ids, cotangent
):
    micro, seqs, part, width = tokens.shape
    count = micro * seqs
    shard = w_up.shape[0]
    me = lax.axis_index("mp")
    place = me.astype(jnp.int32)[None]
    both = ("mp", "dp")
    tok = tokens.reshape(count, part, width)
    cot = cotangent.reshape(count, part, width)
    gain = norm_gain.reshape(1, width)
    ids = image_ids.reshape(count, mp, part)
    ids = jnp.pad(ids, ((0, 0), (0, 0), (0, PIECE - part)), constant_values=-1)
    gains = jnp.concatenate([query_gain, key_gain]).reshape(1, 2 * HD)
    w_attn = pack_attention(w_qkv, w_proj)
    w_ff = jnp.stack([w_up, w_down.T])

    def send_back(outs):
        return [outs[0]] + [
            lax.ppermute(out, "mp", [(i, (i - k) % mp) for i in range(mp)])
            for k, out in enumerate(outs[1:], 1)
        ]

    if (dp, mp) == (8, 4):
        normed, grads, back, *outs, w_ff, g_attn, z_attn, g_gains, _ = front_call(
            tok, cot, ids, gains, gain, w_attn, w_ff
        )
        returned = send_back(outs)
        branch, d_ff, g_attn, g_up, g_down, g_gains = feed_remote_call(
            normed.reshape(count * PIECE, width), grads.reshape(count * PIECE, width),
            w_ff.reshape(mp, dp, 2, shard, width), g_attn, z_attn, gain, g_gains,
        )
    else:
        w_attn = lax.all_gather(w_attn, both).reshape(mp, width, width)
        w_ff = lax.all_gather(w_ff, both).reshape(mp, dp, 2, shard, width)
        normed, grads, *sends = norm_call(place, tok, cot, gain)
        received = [
            lax.ppermute(send, "mp", [(i, (i + k) % mp) for i in range(mp)])
            for k, send in enumerate(sends, 1)
        ]
        *outs, g_attn, g_gains = attention_call(
            place, part, normed, grads, received, ids, gains, gain, w_attn
        )
        outs = send_back(outs)
        back = jnp.stack([out[1] for out in outs])
        returned = [out[0] for out in outs]
        flat_normed = normed.reshape(count * PIECE, width)
        branch, d_ff, g_up, g_down = feed_call(
            flat_normed, grads.reshape(count * PIECE, width),
            w_ff[:, :, 0].reshape(mp, width, width), w_ff[:, :, 1].reshape(mp, width, width),
        )
        g_attn, g_up, g_down = (
            lax.psum_scatter(
                grad.reshape(-1, shard, width), both, scatter_dimension=0
            ).astype(F32)
            for grad in (g_attn, g_up, g_down)
        )
        own = jnp.sum(d_ff * flat_normed.astype(F32), axis=0) / norm_gain
        g_gains = g_gains.at[:width // 128].add(own.reshape(-1, 128))
        g_gains = lax.psum(g_gains, both)
    output, input_grad = finish_call(
        place, tok, cot, gain,
        branch.reshape(count, PIECE, width), d_ff.reshape(count, PIECE, width), back, returned,
    )
    g_qkv, g_proj = unpack_attention(g_attn, w_qkv.shape[2])
    g_norm = g_gains[:width // 128].reshape(width)
    g_gains = g_gains[6]
    return (
        output.reshape(tokens.shape),
        input_grad.reshape(tokens.shape),
        g_qkv,
        g_up,
        g_proj,
        g_down.T,
        g_norm,
        g_gains[:HD],
        g_gains[HD:],
    )


def solution(mesh):
    rows = P(None, "dp", "mp", None)
    weights = (P(None, "dp", "mp"), P("dp", "mp"), P("mp", "dp"), P("mp", "dp"))
    gains = (P(), P(), P())
    return jax.shard_map(
        functools.partial(body, mesh.shape["dp"], mesh.shape["mp"]),
        mesh=mesh,
        in_specs=(rows,) + weights + gains + (P(None, "dp", None), rows),
        out_specs=(rows, rows) + weights + gains,
        check_vma=False,
    )
```

```python
import functools

import jax
import jax.numpy as jnp
from jax import lax
from jax.experimental import pallas as pl
from jax.experimental.pallas import tpu as pltpu
from jax.sharding import PartitionSpec as P

HD = 64
MOST = 709
IMAGES = 8
STRIP = 48
EARLY = 144
PIECE = 240
BIG = 768
REST = 256
ROWS = BIG + REST
VMEM = 60 * 1024 * 1024
FRONT_VMEM = 63 * 1024 * 1024
F32 = jnp.float32
BF16 = jnp.bfloat16


def nn(left, right):
    return lax.dot_general(left, right, (((1,), (0,)), ((), ())), preferred_element_type=F32)


def nt(left, right):
    return lax.dot_general(left, right, (((1,), (1,)), ((), ())), preferred_element_type=F32)


def norm_kernel(place, tok, cot, gain, normed, grads, send1, send2, send3):
    step = pl.program_id(0)
    part = tok.shape[1]
    x = tok[0].astype(F32)
    centered = x - jnp.mean(x, axis=-1, keepdims=True)
    spread = lax.rsqrt(jnp.mean(centered * centered, axis=-1, keepdims=True) + 1e-6)
    value = (centered * spread * gain[...]).astype(BF16)
    normed[...] = jnp.zeros_like(normed)
    grads[...] = jnp.zeros_like(grads)
    normed[0, :part] = value
    grads[0, :part] = cot[0]
    for index, send in ((1, send1), (2, send2), (3, send3)):

        @pl.when(step == index)
        def _():
            send[0] = normed[0]
            send[1] = grads[0]


def norm_call(place, tokens, cotangent, gain):
    count, part, width = tokens.shape
    block = lambda k, place: (lax.rem(place[0] + k, count), 0, 0)
    fixed = lambda k, place: (0, 0, 0)
    return pl.pallas_call(
        norm_kernel,
        grid_spec=pltpu.PrefetchScalarGridSpec(
            num_scalar_prefetch=1,
            grid=(count,),
            in_specs=[
                pl.BlockSpec((1, part, width), block),
                pl.BlockSpec((1, part, width), block),
                pl.BlockSpec((1, width), lambda k, place: (0, 0)),
            ],
            out_specs=[pl.BlockSpec((1, PIECE, width), lambda k, place: (k, 0, 0))] * 2
            + [pl.BlockSpec((2, PIECE, width), fixed)] * 3,
        ),
        out_shape=[jax.ShapeDtypeStruct((count, PIECE, width), BF16)] * 2
        + [jax.ShapeDtypeStruct((2, PIECE, width), BF16)] * 3,
        compiler_params=pltpu.CompilerParams(vmem_limit_bytes=VMEM),
        name="norm_rows",
    )(place, tokens, cotangent, gain)


def feed_kernel(normed, grads, w_up, w_down, branch, d_normed, g_up, g_down, xt, dt):
    step = pl.program_id(0)
    x = normed[...]
    dy = grads[...]

    @pl.when(step == 0)
    def _():
        xt[...] = x.T
        dt[...] = dy.T

    up = nn(x, w_up[0])
    value, slope = gelu_parts(up)
    hidden = value.astype(BF16)
    d_up = (nn(dy, w_down[0]) * slope).astype(BF16)
    g_up[0] = nn(xt[...], d_up).astype(BF16)
    g_down[0] = nn(dt[...], hidden).astype(BF16)
    out = nt(hidden, w_down[0])
    back = nt(d_up, w_up[0])

    @pl.when(step == 0)
    def _():
        branch[...] = out
        d_normed[...] = back

    @pl.when(step > 0)
    def _():
        branch[...] += out
        d_normed[...] += back


def feed_call(normed, grads, w_up, w_down):
    rows, width = normed.shape
    chunks, _, hidden = w_up.shape
    whole = pl.BlockSpec((rows, width), lambda m: (0, 0))
    chunk = pl.BlockSpec((1, width, hidden), lambda m: (m, 0, 0))
    return pl.pallas_call(
        feed_kernel,
        grid=(chunks,),
        in_specs=[whole, whole, chunk, chunk],
        out_specs=[whole, whole, chunk, chunk],
        out_shape=[jax.ShapeDtypeStruct((rows, width), F32)] * 2
        + [jax.ShapeDtypeStruct(w_up.shape, BF16)] * 2,
        scratch_shapes=[pltpu.VMEM((width, rows), BF16)] * 2,
        compiler_params=pltpu.CompilerParams(vmem_limit_bytes=VMEM),
        cost_estimate=pl.CostEstimate(
            flops=12 * rows * width * hidden * chunks,
            bytes_accessed=4 * chunks * width * hidden * 2,
            transcendentals=rows * hidden * chunks,
        ),
        name="feed_forward",
    )(normed, grads, w_up, w_down)


class Place:
    def __init__(self, planes):
        d = lax.axis_index("dp")
        self.z = lax.axis_index("mp")
        self.d, self.planes = d, planes
        self.core, self.x, self.y = d % 2, (d // 2) % 2, d // 4
        self.sibling = d + 1 - 2 * self.core
        self.beside = d + 2 - 4 * self.x
        self.above = d + 4 - 8 * self.y

    def target(self, step):
        z, high = self.z, self.z // 2
        near = jnp.where(step == 2, 1 - z + 4 * high, z)
        return jnp.where(step == 0, 3 - 3 * high, jnp.where(step == 1, 2 - high, near))

    def along(self, k):
        return lax.rem(self.z + k + self.planes, self.planes)

    def copy(self, src, dst, send, recv, dp=None, mp=None):
        return pltpu.make_async_remote_copy(
            src_ref=src, dst_ref=dst, send_sem=send, recv_sem=recv,
            device_id={"dp": self.d if dp is None else dp, "mp": self.z if mp is None else mp},
            device_id_type=pl.DeviceIdType.MESH,
        )

    def greet(self):
        barrier = pltpu.get_barrier_semaphore()
        for other in (self.sibling, self.beside, self.above):
            pl.semaphore_signal(barrier, 1, device_id={"dp": other, "mp": self.z},
                                device_id_type=pl.DeviceIdType.MESH)
        for k in range(1, self.planes):
            pl.semaphore_signal(barrier, 1, device_id={"dp": self.d, "mp": self.along(k)},
                                device_id_type=pl.DeviceIdType.MESH)
        pl.semaphore_wait(barrier, self.planes + 2)


class Scatter:
    def __init__(self, at, items, src, got_core, got_first, got_second, send_sem, recv_sem):
        self.at, self.items, self.src = at, items, src
        self.got_core, self.got_first, self.got_second = got_core, got_first, got_second
        self.send_sem, self.recv_sem = send_sem, recv_sem

    def copy(self, stage, step, item):
        at = self.at
        kind, cols, x_first = self.items[item]
        if stage == 0:
            src = self.src.at[step, kind, :, :, 1 - at.core, :, cols]
            dst = self.got_core.at[step, kind, :, :, :, cols]
            to = at.sibling
        elif stage == 1:
            if x_first:
                src = self.got_core.at[step, kind, :, 1 - at.x, :, cols]
            else:
                src = self.got_core.at[step, kind, 1 - at.y, :, :, cols]
            dst = self.got_first.at[step, kind, :, :, cols]
            to = at.beside if x_first else at.above
        else:
            src = self.got_first.at[step, kind, 1 - at.y if x_first else 1 - at.x, :, cols]
            dst = self.got_second.at[step, kind, :, cols]
            to = at.above if x_first else at.beside
        sem = (stage, item, step)
        return at.copy(src, dst, self.send_sem.at[sem], self.recv_sem.at[sem], dp=to)

    def start(self, step):
        for item in range(len(self.items)):
            self.copy(0, step, item).start()

    def after_core(self, step):
        for item, (kind, cols, _) in enumerate(self.items):
            self.copy(0, step, item).wait_recv()
            for row in ((0, 0), (0, 1), (1, 0), (1, 1)):
                own = self.src[(step, kind, *row, self.at.core, slice(None), cols)]
                to = (step, kind, *row, slice(None), cols)
                total = own.astype(F32) + self.got_core[to].astype(F32)
                self.got_core[to] = total.astype(BF16)
            self.copy(1, step, item).start()

    def after_first(self, step):
        for item, (kind, cols, x_first) in enumerate(self.items):
            self.copy(1, step, item).wait_recv()
            for row in range(2):
                if x_first:
                    own = self.got_core[step, kind, row, self.at.x, :, cols]
                else:
                    own = self.got_core[step, kind, self.at.y, row, :, cols]
                total = own.astype(F32) + self.got_first[step, kind, row, :, cols].astype(F32)
                self.got_first[step, kind, row, :, cols] = total.astype(BF16)
            self.copy(2, step, item).start()

    def total(self, step, item):
        kind, cols, x_first = self.items[item]
        self.copy(2, step, item).wait_recv()
        own = self.got_first[step, kind, self.at.y if x_first else self.at.x, :, cols]
        return own.astype(F32) + self.got_second[step, kind, :, cols].astype(F32)

    def after_second(self, step):
        for item, (kind, cols, _) in enumerate(self.items):
            self.got_second[step, kind, :, cols] = self.total(step, item).astype(BF16)

    def wait_send(self, step):
        for item in range(len(self.items)):
            for stage in range(3):
                self.copy(stage, step, item).wait_send()


class Gather:
    def __init__(self, at, shard, full, send_sem, recv_sem):
        self.at, self.shard, self.full = at, shard, full
        self.send_sem, self.recv_sem = send_sem, recv_sem

    def there(self, r, does):
        plane = self.at.z + r

        @pl.when((plane >= 0) & (plane < self.at.planes))
        def _():
            does(plane)

    def piece(self, plane, y=False, x=False, core=False):
        at = self.at
        return self.full.at[plane, 1 - at.y if y else at.y, 1 - at.x if x else at.x,
                            1 - at.core if core else at.core]

    def copy(self, kind, plane, src, dst=None, **to):
        return self.at.copy(
            src, src if dst is None else dst, self.send_sem.at[kind, plane],
            self.recv_sem.at[kind % 8, plane], **to
        )

    def arrived(self, kind, plane, ref):
        self.copy(kind, plane, ref, dp=self.at.sibling).wait_recv()

    def pass_on(self, kind, plane, src, act):
        z, dst = self.at.z, self.piece(plane)
        if kind == 0:
            @pl.when(z < self.at.planes - 1)
            def _():
                act(self.copy(0, plane, src, dst, mp=z + 1))
        else:
            @pl.when(z > 0)
            def _():
                act(self.copy(8, plane, src, dst, mp=z - 1))

    def start(self):
        for kind in (0, 8):
            self.pass_on(kind, self.at.z, self.shard, lambda copy: copy.start())

    def spread(self, *which):
        for r in which:
            def does(plane):
                src = self.piece(plane)
                if r:
                    self.arrived(0, plane, src)
                    self.pass_on(0 if r < 0 else 8, plane, src, lambda copy: copy.start())
                self.copy(1, plane, src, dp=self.at.beside).start()
                self.copy(2, plane, src, dp=self.at.above).start()
                self.copy(3, plane, src, dp=self.at.sibling).start()

            self.there(r, does)

    def forward(self, *which):
        at = self.at
        for r in which:
            def does(plane):
                from_x, from_y = self.piece(plane, x=True), self.piece(plane, y=True)
                self.arrived(1, plane, from_x)
                if r % 2 == 0:
                    self.copy(5, plane, from_x, dp=at.above).start()
                self.copy(4, plane, from_x, dp=at.sibling).start()
                self.arrived(2, plane, from_y)
                if r % 2 == 1:
                    self.copy(5, plane, from_y, dp=at.beside).start()
                self.copy(6, plane, from_y, dp=at.sibling).start()

            self.there(r, does)

    def across(self, *which):
        for r in which:
            def does(plane):
                src = self.piece(plane, y=True, x=True)
                self.arrived(5, plane, src)
                self.copy(7, plane, src, dp=self.at.sibling).start()

            self.there(r, does)

    def last(self):
        for plane in range(self.at.planes):
            self.arrived(3, plane, self.piece(plane, core=True))
            self.arrived(4, plane, self.piece(plane, x=True, core=True))
            self.arrived(6, plane, self.piece(plane, y=True, core=True))
            self.arrived(7, plane, self.piece(plane, y=True, x=True, core=True))

    def wait_send(self):
        for r in range(1 - self.at.planes, self.at.planes):
            def does(plane):
                src = self.piece(plane)
                if r <= 0:
                    self.pass_on(0, plane, src, lambda copy: copy.wait_send())
                if r >= 0:
                    self.pass_on(8, plane, src, lambda copy: copy.wait_send())
                for kind in range(1, 8):
                    self.copy(kind, plane, src, dp=self.at.sibling).wait_send()

            self.there(r, does)


class Along:
    def __init__(self, at, parts, got, send_sem, recv_sem):
        self.at, self.parts, self.got = at, parts, got
        self.send_sem, self.recv_sem = send_sem, recv_sem
        self.inner = (at.z == 1) | (at.z == 2)

    def copy(self, step, kind):
        at, inner = self.at, self.inner
        side = 1 - 2 * (at.z // 2)
        to = at.z + jnp.where(inner & (step == 2), -side, side)
        slot = jnp.where(inner, 2 + 2 * step - 3 * (step // 2), step + step // 2)
        return at.copy(self.parts.at[step, kind], self.got.at[kind, slot],
                       self.send_sem.at[kind, step], self.recv_sem.at[kind, slot], mp=to)

    def arrived(self, kind, slot):
        ref = self.got.at[kind, slot]
        self.at.copy(ref, ref, self.send_sem.at[kind, 0], self.recv_sem.at[kind, slot],
                     mp=self.at.along(1)).wait_recv()

    def send_outer(self, step):
        @pl.when(jnp.logical_not(self.inner))
        def _():
            for kind in range(self.got.shape[0]):
                self.copy(step, kind).start()

    def send_inner(self, step):
        @pl.when(self.inner)
        def _():
            for kind in range(self.got.shape[0]):
                self.arrived(kind, step)
                own = self.parts[step, kind].astype(F32)
                total = own + self.got[kind, step].astype(F32)
                self.parts[step, kind] = total.astype(BF16)
                self.copy(step, kind).start()

    def add(self, kind, out):
        self.arrived(kind, 3)
        out[...] += self.got[kind, 3].astype(F32)

        @pl.when(self.inner)
        def _():
            self.arrived(kind, 4)
            out[...] += self.got[kind, 4].astype(F32)

    def wait_send(self, step):
        for kind in range(self.got.shape[0]):
            self.copy(step, kind).wait_send()


def gelu_parts(up):
    inner = 0.7978845608028654 * (up + 0.044715 * up * up * up)
    th = jnp.tanh(inner)
    half = 0.5 * (1.0 + th)
    slope = half + 0.5 * up * (1.0 - th * th) * (
        0.7978845608028654 * (1.0 + 3 * 0.044715 * up * up)
    )
    return up * half, slope


def halves(width):
    return (0, slice(0, width // 2), True), (0, slice(width // 2, width), False)


def feed_remote_kernel(
    x_ref, dy_ref, w_hbm, g_attn, z_attn, gain, gains_in,
    branch, d_normed, out_attn, out_up, out_down, out_gains,
    xt, dt, w_buf, hidden, d_up, g_ff, ff_core, ff_first, ff_second, at_core, at_first, at_second, got_z,
    sums, got_sums, z_sums,
    w_sem, ff_send, ff_recv, at_send, at_recv, z_send, z_recv, sum_send, sum_recv,
):
    width = x_ref.shape[1]
    steps, shard = w_hbm.shape[0], w_hbm.shape[3]
    at = Place(steps)
    at.greet()
    attn = Scatter(at, halves(width), g_attn, at_core, at_first, at_second, at_send, at_recv)
    both = (0, slice(0, width), True), (1, slice(0, width), False)
    feed = Scatter(at, both, g_ff, ff_core, ff_first, ff_second, ff_send, ff_recv)
    along = Along(at, ff_second, got_z, z_send, z_recv)
    last = steps - 1

    def w_copy(step, kind):
        slot = lax.rem(step, 2)
        return pltpu.make_async_copy(
            w_hbm.at[at.target(step), :, kind], w_buf.at[slot, kind], w_sem.at[slot, kind]
        )

    attn.start(0)
    for kind in range(2):
        w_copy(0, kind).start()
    xt[...] = x_ref[...].T
    dt[...] = dy_ref[...].T
    branch[...] = jnp.zeros_like(branch)
    d_normed[...] = jnp.zeros_like(d_normed)

    def one_step(step, carry):
        for kind in range(2):
            w_copy(step, kind).wait()

        @pl.when(step + 1 < steps)
        def _():
            for kind in range(2):
                w_copy(step + 1, kind).start()

        slot = lax.rem(step, 2)
        split = (2, 2, 2, shard, width)

        def weights(kind):
            return w_buf[slot, kind].reshape(width, width)

        value, slope = gelu_parts(nn(x_ref[...], weights(0)))
        hidden[...] = value.astype(BF16)
        d_up[...] = (nn(dy_ref[...], weights(1)) * slope).astype(BF16)

        @pl.when(step == 0)
        def _():
            attn.after_core(0)

        g_ff[step, 0] = nn(xt[...], d_up[...]).astype(BF16).reshape(split)
        g_ff[step, 1] = nn(dt[...], hidden[...]).astype(BF16).reshape(split)
        feed.start(step)

        @pl.when(step >= 1)
        def _():
            feed.after_first(step - 1)

        branch[...] += nt(hidden[...], weights(1))
        d_normed[...] += nt(d_up[...], weights(0))
        feed.after_core(step)

        @pl.when(step == 0)
        def _():
            attn.after_first(0)

        @pl.when(step >= 1)
        def _():
            feed.after_second(step - 1)
            along.send_outer(step - 1)

        return carry

    lax.fori_loop(0, steps, one_step, 0)

    sums[0] = gains_in[...]
    store_gain(sums.at[0], d_normed[...], x_ref[...], gain[...])

    def sum_copy(stage):
        to = (at.sibling, at.beside, at.above)[stage]
        return at.copy(sums.at[stage], got_sums.at[stage], sum_send.at[stage],
                       sum_recv.at[stage], dp=to)

    def sum_z_copy(k):
        return at.copy(sums.at[3], z_sums.at[at.z], sum_send.at[2 + k], sum_recv.at[2 + k],
                       mp=at.along(k))

    def next_sum(stage):
        sum_copy(stage).wait_recv()
        sums[stage + 1] = sums[stage] + got_sums[stage]

    sum_copy(0).start()
    for item in range(2):
        cols = attn.items[item][1]
        out_attn[:, cols] = attn.total(0, item) + z_attn[:, cols]
    next_sum(0)
    sum_copy(1).start()
    along.send_inner(0)
    along.send_inner(1)
    next_sum(1)
    sum_copy(2).start()
    feed.after_first(last)
    along.send_inner(2)
    next_sum(2)
    for k in range(1, steps):
        sum_z_copy(k).start()
    z_sums[at.z] = sums[3]
    for kind, out in enumerate((out_up, out_down)):
        out[...] = feed.total(last, kind)
        along.add(kind, out)
    for k in range(1, steps):
        sum_z_copy(k).wait_recv()
    total = z_sums[0]
    for k in range(1, steps):
        total = total + z_sums[k]
    out_gains[...] = total

    attn.wait_send(0)
    for step in range(steps):
        feed.wait_send(step)
    for step in range(last):
        along.wait_send(step)
    for stage in range(3):
        sum_copy(stage).wait_send()
    for k in range(1, steps):
        sum_z_copy(k).wait_send()


def feed_remote_call(normed, grads, w_ff, g_attn, z_attn, gain, gains):
    rows, width = normed.shape
    steps, _, _, shard, _ = w_ff.shape
    vmem = pl.BlockSpec(memory_space=pltpu.VMEM)
    return pl.pallas_call(
        feed_remote_kernel,
        in_specs=[vmem, vmem, pl.BlockSpec(memory_space=pl.ANY)] + [vmem] * 4,
        out_specs=[vmem] * 6,
        out_shape=[jax.ShapeDtypeStruct((rows, width), F32)] * 2
        + [jax.ShapeDtypeStruct((shard, width), F32)] * 3
        + [jax.ShapeDtypeStruct((8, 128), F32)],
        scratch_shapes=[
            pltpu.VMEM((width, rows), BF16),
            pltpu.VMEM((width, rows), BF16),
            pltpu.VMEM((2, 2, 8, shard, width), BF16),
            pltpu.VMEM((rows, width), BF16),
            pltpu.VMEM((rows, width), BF16),
            pltpu.VMEM((steps, 2, 2, 2, 2, shard, width), BF16),
            pltpu.VMEM((steps, 2, 2, 2, shard, width), BF16),
            pltpu.VMEM((steps, 2, 2, shard, width), BF16),
            pltpu.VMEM((steps, 2, shard, width), BF16),
            pltpu.VMEM((1, 1, 2, 2, shard, width), BF16),
            pltpu.VMEM((1, 1, 2, shard, width), BF16),
            pltpu.VMEM((1, 1, shard, width), BF16),
            pltpu.VMEM((2, 5, shard, width), BF16),
            pltpu.VMEM((4, 8, 128), F32),
            pltpu.VMEM((3, 8, 128), F32),
            pltpu.VMEM((steps, 8, 128), F32),
            pltpu.SemaphoreType.DMA((2, 2)),
            pltpu.SemaphoreType.DMA((3, 2, steps)),
            pltpu.SemaphoreType.DMA((3, 2, steps)),
            pltpu.SemaphoreType.DMA((3, 2, 1)),
            pltpu.SemaphoreType.DMA((3, 2, 1)),
            pltpu.SemaphoreType.DMA((2, steps - 1)),
            pltpu.SemaphoreType.DMA((2, 5)),
            pltpu.SemaphoreType.DMA((6,)),
            pltpu.SemaphoreType.DMA((6,)),
        ],
        compiler_params=pltpu.CompilerParams(
            collective_id=0, has_side_effects=True, vmem_limit_bytes=VMEM
        ),
        cost_estimate=pl.CostEstimate(
            flops=12 * rows * width * width * steps,
            bytes_accessed=4 * steps * width * width * 2,
            transcendentals=rows * width * steps,
        ),
        name="feed_forward_scatter",
    )(normed, grads, w_ff, g_attn, z_attn, gain, gains)


def iota(shape, axis):
    return lax.broadcasted_iota(jnp.int32, shape, axis)


def source_of(index, start, total):
    rest = index - BIG
    other = jnp.where(rest < start, rest, rest + MOST)
    held = jnp.where(index < MOST, start + index, -1)
    return jnp.where((rest >= 0) & (rest < total - MOST), other, held)


def store_gain(out, d_normed, normed, gain):
    total = jnp.sum(d_normed * normed.astype(F32), axis=0, keepdims=True) / gain
    for row in range(total.shape[1] // 128):
        out[row:row + 1] += total[:, 128 * row:128 * row + 128]


def prepare(
    me, part, ids, pieces, x_ref, dy_ref, xt, dt, feat_q, feat_k, pt, d_normed, branch, g_gains
):
    mp = ids.shape[1]
    total = mp * part
    numbers = ids[me]
    start = jnp.zeros((1, 1), jnp.int32)
    for image in range(IMAGES):
        count = jnp.sum((numbers == image).astype(F32), axis=(0, 1), keepdims=True)
        ahead = jnp.sum(
            ((numbers >= 0) & (numbers < image)).astype(F32), axis=(0, 1), keepdims=True
        )
        start = start + jnp.where(count == MOST, ahead, 0.0).astype(jnp.int32)
    column = source_of(iota((ROWS, 1), 0), start, total)
    line = source_of(iota((1, ROWS), 1), start, total)
    x_sum, dy_sum, feats = 0.0, 0.0, 0.0
    for k, piece in enumerate(pieces):
        chunk = lax.rem(me - k + mp, mp)
        offset = iota((1, PIECE), 1)
        pos = jnp.where(offset < part, chunk * part + offset, -2)
        pick = (column == pos).astype(F32).astype(BF16)
        offset = iota((PIECE, 1), 0)
        pos = jnp.where(offset < part, chunk * part + offset, -2)
        pt[k] = (line == pos).astype(F32).astype(BF16)
        x_sum = x_sum + nn(pick, piece[0][...])
        dy_sum = dy_sum + nn(pick, piece[1][...])
        marks = (iota((128, 1), 0) - HD == ids[me, pl.ds(chunk, 1), :]).astype(F32)
        feats = feats + nt(pick, marks.astype(BF16))
    x = x_sum.astype(BF16)
    dy = dy_sum.astype(BF16)
    x_ref[...] = x
    dy_ref[...] = dy
    xt[...] = x.T
    dt[...] = dy.T
    lane = iota((1, 128), 1)
    feat_q[...] = (feats * 128.0).astype(BF16)
    marked = (lane >= HD) & (lane < HD + IMAGES)
    feat_k[...] = jnp.where(marked, (feats - 1.0) * 256.0, 0.0).astype(BF16)
    d_normed[...] = jnp.zeros_like(d_normed)
    branch[...] = jnp.zeros_like(branch)
    g_gains[...] = jnp.zeros_like(g_gains)


def attention_chunk(
    weights, gain, x_ref, dy_ref, xt, dt, feat_q, feat_k, raw, d_raw, d_att, att,
    d_normed, branch, g_gains, store, poll,
):
    raw[...] = nn(x_ref[...], weights(slice(0, 640)))
    d_att[...] = nn(dy_ref[...], weights(slice(512, 768)))
    lane = iota((1, 128), 1)
    low = lane < HD
    same = (iota((128, 128), 0) // HD == iota((128, 128), 1) // HD).astype(F32)
    mean_of = (same * (1.0 / HD)).astype(BF16)

    def half_mean(value):
        return nn(value.astype(BF16), mean_of)

    d_gain = jnp.zeros((1, 128), F32)
    for head in range(3):
        qk = raw[:, 128 * head:128 * head + 128]
        high = qk.astype(BF16)
        mean = nn(high, mean_of) + half_mean(qk - high.astype(F32))
        centered = qk - mean
        spread = lax.rsqrt(half_mean(centered * centered) + 1e-6)
        unit = centered * spread
        rounded = (unit * gain).astype(BF16).astype(F32)
        q_aug = jnp.where(low, rounded * 0.125, feat_q[...].astype(F32)).astype(BF16)
        k_aug = jnp.where(low, pltpu.roll(rounded, HD, 1), feat_k[...].astype(F32)).astype(BF16)
        v_tile = 384 + 128 * (head // 2)
        v = raw[:, v_tile:v_tile + 128]
        if head == 1:
            v = pltpu.roll(v, HD, 1)
        one = ((lane == HD) | (lane == HD + 1)).astype(F32)
        v_aug = jnp.where(low, v, one).astype(BF16)
        a_tile = 128 * ((head + 1) // 2)
        da = d_att[:, a_tile:a_tile + 128]
        if head != 1:
            da = pltpu.roll(da, HD, 1)
        q_t = q_aug.astype(F32).T.astype(BF16)
        d_queries, attended, d_keys, d_values = [], [], [], []
        for base, count in ((0, BIG), (BIG, REST)):
            keys = k_aug[base:base + count]
            values = v_aug[base:base + count]
            dk_t = jnp.zeros((128, count), F32)
            dv_t = jnp.zeros((128, count), F32)
            for row in range(base, base + count, 256):
                rows = slice(row, row + 256)
                prob = jnp.exp(nt(q_aug[rows], keys))
                prob_low = prob.astype(BF16)
                gathered = nn(prob_low, values)
                inverse = 1.0 / gathered[:, HD:HD + 1]
                out = jnp.where(low, gathered * inverse, 0.0)
                attended.append(out)
                scaled = jnp.where(low, da[rows] * inverse, 0.0).astype(BF16).astype(F32)
                dot = jnp.sum(scaled * out, axis=-1, keepdims=True)
                dot_high = dot.astype(BF16).astype(F32)
                d_aug = jnp.where(
                    lane == HD, -dot_high, jnp.where(lane == HD + 1, dot_high - dot, scaled)
                )
                d_low = d_aug.astype(BF16)
                d_score = (prob * nt(d_low, values)).astype(BF16)
                d_queries.append(nn(d_score, keys))
                dk_t = dk_t + nn(q_t[:, rows], d_score)
                dv_t = dv_t + nn(d_aug.T.astype(BF16), prob_low)
            d_keys.append(dk_t.T)
            d_values.append(dv_t.T)
        d_query = jnp.concatenate(d_queries, axis=0) * 0.125
        d_key = jnp.concatenate(d_keys, axis=0)
        d_value = jnp.concatenate(d_values, axis=0)
        attend = jnp.concatenate(attended, axis=0)
        d_qk = jnp.where(low, d_query, pltpu.roll(d_key, HD, 1))
        d_gain = d_gain + jnp.sum(d_qk * unit, axis=0, keepdims=True)
        scaled = d_qk * gain
        d_qk = spread * (scaled - half_mean(scaled) - unit * half_mean(scaled * unit))
        d_raw[:, 128 * head:128 * head + 128] = d_qk.astype(BF16)
        if head == 0:
            first_value = d_value
            att[:, 0:128] = jnp.where(low, 0.0, pltpu.roll(attend, HD, 1)).astype(BF16)
        elif head == 1:
            both = jnp.where(low, first_value, pltpu.roll(d_value, HD, 1))
            d_raw[:, 384:512] = both.astype(BF16)
            first_att = attend
        else:
            d_raw[:, 512:640] = jnp.where(low, d_value, 0.0).astype(BF16)
            both = jnp.where(low, first_att, pltpu.roll(attend, HD, 1))
            att[:, 128:256] = both.astype(BF16)
        poll(head)
    g_gains[6:7] += d_gain
    d_projected = d_raw[...]
    attended = att[...]
    d_normed[...] += nt(d_projected, weights(slice(0, 640)))
    branch[...] += nt(attended, weights(slice(512, 768)))
    left = nn(xt[...], d_projected)
    right = nn(dt[...], attended)
    store(slice(0, 512), left[:, :512].astype(BF16))
    store(slice(512, 640), (left[:, 512:] + right[:, :128]).astype(BF16))
    store(slice(640, 768), right[:, 128:].astype(BF16))


def take_back(outs, pt, x_ref, norm_gain, d_normed, branch, g_gains):
    store_gain(g_gains, d_normed[...], x_ref[...], norm_gain[...])
    d_rows = d_normed[...].astype(BF16)
    b_rows = branch[...].astype(BF16)
    for k, out in enumerate(outs):
        out[0] = nn(pt[k], d_rows).astype(BF16)
        out[1] = nn(pt[k], b_rows).astype(BF16)


def attention_kernel(
    part, place, own_x, own_dy, in1, in2, in3, ids, gains, norm_gain, weights,
    out0, out1, out2, out3, g_weights, g_gains,
    x_ref, dy_ref, xt, dt, feat_q, feat_k, pt, raw, d_raw, d_att, att, d_normed, branch,
):
    step = pl.program_id(0)

    @pl.when(step == 0)
    def _():
        pieces = [(own_x.at[0], own_dy.at[0])] + [(got.at[0], got.at[1]) for got in (in1, in2, in3)]
        prepare(place[0], part, ids, pieces, x_ref, dy_ref, xt, dt, feat_q, feat_k, pt,
                d_normed, branch, g_gains)

    def store(cols, value):
        g_weights[0, :, cols] = value

    attention_chunk(
        lambda cols: weights[0, :, cols], gains[...], x_ref, dy_ref, xt, dt, feat_q, feat_k,
        raw, d_raw, d_att, att, d_normed, branch, g_gains, store, lambda head: None,
    )

    @pl.when(step == pl.num_programs(0) - 1)
    def _():
        take_back((out0, out1, out2, out3), pt, x_ref, norm_gain, d_normed, branch, g_gains)


def attention_call(place, part, normed, grads, received, ids, gains, norm_gain, weights):
    width = normed.shape[-1]
    chunks = weights.shape[0]
    mp = ids.shape[1]
    own = pl.BlockSpec((1, PIECE, width), lambda m, place: (0, 0, 0))
    pair = pl.BlockSpec((2, PIECE, width), lambda m, place: (0, 0, 0))
    chunk = pl.BlockSpec((1, width, width), lambda m, place: (m, 0, 0))
    line = pl.BlockSpec((1, 128), lambda m, place: (0, 0))
    return pl.pallas_call(
        functools.partial(attention_kernel, part),
        grid_spec=pltpu.PrefetchScalarGridSpec(
            num_scalar_prefetch=1,
            grid=(chunks,),
            in_specs=[own, own, pair, pair, pair,
                      pl.BlockSpec(ids.shape, lambda m, place: (0, 0, 0)),
                      line, pl.BlockSpec((1, width), lambda m, place: (0, 0)), chunk],
            out_specs=[pair] * 4 + [chunk, pl.BlockSpec((8, 128), lambda m, place: (0, 0))],
            scratch_shapes=[
                pltpu.VMEM((ROWS, width), BF16),
                pltpu.VMEM((ROWS, width), BF16),
                pltpu.VMEM((width, ROWS), BF16),
                pltpu.VMEM((width, ROWS), BF16),
                pltpu.VMEM((ROWS, 128), BF16),
                pltpu.VMEM((ROWS, 128), BF16),
                pltpu.VMEM((mp, PIECE, ROWS), BF16),
                pltpu.VMEM((ROWS, 640), F32),
                pltpu.VMEM((ROWS, 640), BF16),
                pltpu.VMEM((ROWS, 256), F32),
                pltpu.VMEM((ROWS, 256), BF16),
                pltpu.VMEM((ROWS, width), F32),
                pltpu.VMEM((ROWS, width), F32),
            ],
        ),
        out_shape=[jax.ShapeDtypeStruct((2, PIECE, width), BF16)] * 4
        + [jax.ShapeDtypeStruct(weights.shape, BF16), jax.ShapeDtypeStruct((8, 128), F32)],
        compiler_params=pltpu.CompilerParams(vmem_limit_bytes=VMEM),
        cost_estimate=pl.CostEstimate(
            flops=60_000_000_000, bytes_accessed=4 * chunks * width * width,
            transcendentals=ROWS * ROWS * 12,
        ),
        name="attention",
    )(place, normed, grads, *received, ids, gains, norm_gain, weights)


def group_means():
    same = (iota((128, 128), 0) // HD == iota((128, 128), 1) // HD).astype(F32)
    return (same * (1.0 / HD)).astype(BF16)


def forward_chunk(
    weights, gain, x_ref, feat_q, feat_k, raw, qk_all, v_all, stats, att, branch, begin, spill
):
    raw[...] = nn(x_ref[...], weights(slice(0, 640)))
    lane = iota((1, 128), 1)
    low = lane < HD
    mean_of = group_means()
    stat = jnp.zeros((ROWS, 128), F32)
    for head in range(3):
        qk = raw[:, 128 * head:128 * head + 128]
        high = qk.astype(BF16)
        mean = nn(high, mean_of) + nn((qk - high.astype(F32)).astype(BF16), mean_of)
        centered = qk - mean
        spread = lax.rsqrt(nn((centered * centered).astype(BF16), mean_of) + 1e-6)
        rounded = (centered * spread * gain).astype(BF16)
        qk_all[head] = rounded
        rounded = rounded.astype(F32)
        q_aug = jnp.where(low, rounded * 0.125, feat_q[...].astype(F32)).astype(BF16)
        k_aug = jnp.where(low, pltpu.roll(rounded, HD, 1), feat_k[...].astype(F32)).astype(BF16)
        v_tile = 384 + 128 * (head // 2)
        v = raw[:, v_tile:v_tile + 128]
        if head == 1:
            v = pltpu.roll(v, HD, 1)
        v_aug = jnp.where(low, v, 1.0).astype(BF16)
        v_all[head] = v_aug
        p_ref = begin(head)
        parts = []
        for base, count in ((0, BIG), (BIG, REST)):
            keys = k_aug[base:base + count]
            values = v_aug[base:base + count]
            for row in range(base, base + count, 256):
                rows = slice(row, row + 256)
                prob = jnp.exp(nt(q_aug[rows], keys)).astype(BF16)
                p_ref[rows, :count] = prob
                parts.append(nn(prob, values))
        spill(head)
        gathered = jnp.concatenate(parts, axis=0)
        inverse = 1.0 / gathered
        attend = gathered * pltpu.roll(inverse, HD, 1)
        stat = jnp.where((lane == head) | (lane == HD + head), spread, stat)
        stat = jnp.where(lane == HD + 8 + head, inverse, stat)
        if head == 0:
            att[:, 0:128] = jnp.where(low, 0.0, pltpu.roll(attend, HD, 1)).astype(BF16)
        elif head == 1:
            first = attend
        else:
            att[:, 128:256] = jnp.where(low, first, pltpu.roll(attend, HD, 1)).astype(BF16)
    stats[...] = stat
    branch[...] += nt(att[...], weights(slice(512, 768)))


def backward_chunk(
    weights, gain, dy_ref, xt, dt, raw, d_raw, qk_all, v_all, stats, att,
    d_normed, g_gains, ready, store, poll,
):
    raw[:, :256] = nn(dy_ref[...], weights(slice(512, 768)))
    lane = iota((1, 128), 1)
    low = lane < HD
    mean_of = group_means()
    stat = stats[...]
    back_gain = 1.0 / gain
    d_gain = jnp.zeros((1, 128), F32)
    for head in range(3):
        qk = qk_all[head]
        v_aug = v_all[head]
        tile = 128 * ((head + 1) // 2)
        da = raw[:, tile:tile + 128]
        out = att[:, tile:tile + 128].astype(F32)
        if head != 1:
            da = pltpu.roll(da, HD, 1)
            out = pltpu.roll(out, HD, 1)
        inverse = stat[:, HD + 8 + head:HD + 9 + head]
        scaled = jnp.where(low, da * inverse, 0.0).astype(BF16).astype(F32)
        dot = jnp.sum(scaled * out, axis=-1, keepdims=True)
        dot_high = dot.astype(BF16).astype(F32)
        d_aug = jnp.where(
            lane == HD, -dot_high, jnp.where(lane == HD + 1, dot_high - dot, scaled)
        )
        d_low = d_aug.astype(BF16)
        d_t = d_aug.T.astype(BF16)
        qk_low = qk.astype(F32)
        qk_t = qk_low.T.astype(BF16)
        p_ref = ready(head)
        d_queries, d_keys, d_values = [], [], []
        for base, count in ((0, BIG), (BIG, REST)):
            block = slice(base, base + count)
            d_values.append(nn(d_t[:, block], p_ref[block, :count]).T)
            for row in range(base, base + count, 256):
                rows = slice(row, row + 256)
                d_prob = nt(d_low[rows], v_aug[block])
                d_score = (p_ref[rows, :count].astype(F32) * d_prob).astype(BF16)
                p_ref[rows, :count] = d_score
                d_queries.append(nn(d_score, qk[block]))
            d_keys.append(nn(qk_t[:, block], p_ref[block, :count]).T)
        d_query = jnp.concatenate(d_queries, axis=0)
        d_key = jnp.concatenate(d_keys, axis=0)
        d_value = jnp.concatenate(d_values, axis=0)
        d_qk = pltpu.roll(jnp.where(low, d_key, d_query), HD, 1) * 0.125
        unit = qk_low * back_gain
        spread = jnp.where(low, stat[:, head:head + 1], stat[:, HD + head:HD + head + 1])
        d_gain = d_gain + jnp.sum(d_qk * unit, axis=0, keepdims=True)
        scaled = d_qk * gain
        mean = nn(scaled.astype(BF16), mean_of)
        d_qk = spread * (scaled - mean - unit * nn((scaled * unit).astype(BF16), mean_of))
        d_raw[:, 128 * head:128 * head + 128] = d_qk.astype(BF16)
        if head == 0:
            first = d_value
        elif head == 1:
            both = jnp.where(low, first, pltpu.roll(d_value, HD, 1))
            d_raw[:, 384:512] = both.astype(BF16)
        else:
            d_raw[:, 512:640] = jnp.where(low, d_value, 0.0).astype(BF16)
        poll(head)
    g_gains[6:7] += d_gain
    d_projected = d_raw[...]
    d_normed[...] += nt(d_projected, weights(slice(0, 640)))
    left = nn(xt[...], d_projected)
    right = nn(dt[...], att[...])
    store(slice(0, 512), left[:, :512].astype(BF16))
    store(slice(512, 640), (left[:, 512:] + right[:, :128]).astype(BF16))
    store(slice(640, 768), right[:, 128:].astype(BF16))


def front_kernel(
    tok, cot, ids, gains, norm_gain, w_attn, w_feed,
    normed, grads, returned, out0, out1, out2, out3, w_ff, g_last, z_attn, g_gains, p_all,
    got_rows, w_full, g_buf, at_core, at_first, at_second, got_z,
    x_ref, dy_ref, xt, dt, feat_q, feat_k, pt, raw, d_raw, p_buf,
    qk_all, v_all, stats, att, total,
    row_send, row_recv, back_send, back_recv, wa_send, wa_recv, wf_send, wf_recv, own_sem,
    p_out, p_in, at_send, at_recv, z_send, z_recv,
):
    count, part, width = tok.shape
    shard = w_attn.shape[0]
    at = Place(count)
    at.greet()
    gather = Gather(at, w_attn, w_full, wa_send, wa_recv)
    gather_ff = Gather(at, w_feed, w_ff, wf_send, wf_recv)
    scatter = Scatter(at, halves(width), g_buf, at_core, at_first, at_second, at_send, at_recv)
    own_ff = pltpu.make_async_copy(w_feed, gather_ff.piece(at.z), own_sem)
    along = Along(at, at_second, got_z, z_send, z_recv)

    def row_copy(kind, k):
        src = (normed, grads)[kind].at[k]
        return at.copy(src, got_rows.at[k - 1, kind], row_send.at[kind, k - 1],
                       row_recv.at[kind, k - 1], mp=at.along(k))

    def back_copy(k, strip):
        rows, sem = pl.ds(strip * STRIP, STRIP), (k - 1, strip)
        return at.copy(got_rows.at[k - 1, 0, rows], returned.at[k, rows], back_send.at[sem],
                       back_recv.at[sem], mp=at.along(-k))

    strips = [(k, strip) for strip in range(EARLY // STRIP) for k in (1, 3, 2)]

    gather.start()
    own_ff.start()
    w_full[at.z, at.y, at.x, at.core] = w_attn[...]
    gather.spread(0)
    gain = norm_gain[...]
    for k in (1, 3, 2, 0):
        sequence = at.along(k)
        x = tok[sequence].astype(F32)
        centered = x - jnp.mean(x, axis=-1, keepdims=True)
        spread = lax.rsqrt(jnp.mean(centered * centered, axis=-1, keepdims=True) + 1e-6)
        pad = jnp.zeros((PIECE - part, width), BF16)
        normed[k, :part] = (centered * spread * gain).astype(BF16)
        normed[k, part:] = pad
        grads[k, :part] = cot[sequence]
        grads[k, part:] = pad
        if k == 2:
            gather.spread(-1, 1)
    gather.spread(-2, 2)
    for kind in range(2):
        for k in (1, 3, 2):
            row_copy(kind, k).start()
    place_rows(at.z, part, ids, pt, feat_q, feat_k)
    g_gains[...] = jnp.zeros_like(g_gains)
    total[...] = jnp.zeros_like(total)
    gather.forward(0)
    gather.spread(-3, 3)
    own_ff.wait()
    gather.forward(-1, 1)
    gather.across(0)
    gather.forward(-2, 2)
    gather.across(-1, 1)
    gather.forward(-3, 3)
    gather.across(-2, 2)
    gather.across(-3, 3)
    gather.last()
    gather_ff.spread(0)
    gather_ff.start()
    for k in (1, 3, 2):
        row_copy(0, k).wait_recv()

    def lay_out(kind, own, rows, columns):
        value = 0.0
        for k in range(count):
            piece = own[0] if k == 0 else got_rows[k - 1, kind]
            value = value + lax.dot_general(
                pt[k], piece, (((0,), (0,)), ((), ())), preferred_element_type=F32
            )
        value = value.astype(BF16)
        rows[...] = value
        columns[...] = value.T

    lay_out(0, normed, x_ref, xt)

    def weights_of(chunk):
        def weights(cols):
            return w_full[chunk, :, :, :, :, cols].reshape(width, cols.stop - cols.start)

        return weights

    def p_write(step, head):
        slot = lax.rem(step + head, 2)
        return pltpu.make_async_copy(p_buf.at[slot], p_all.at[at.along(step), head],
                                     p_out.at[slot])

    def p_read(step, head):
        slot = lax.rem(step + head, 2)
        return pltpu.make_async_copy(p_all.at[at.target(step), head], p_buf.at[slot],
                                     p_in.at[slot])

    def forward_step(step, carry):
        chunk = at.along(step)

        @pl.when(step == 2)
        def _():
            gather_ff.forward(0)

        def begin(head):
            if head == 2:
                p_write(step, 0).wait()
            else:
                @pl.when(step >= 1)
                def _():
                    p_write(step - 1, 1 + head).wait()
            return p_buf.at[lax.rem(step + head, 2)]

        forward_chunk(
            weights_of(chunk), gains[...], x_ref, feat_q, feat_k, raw, qk_all.at[chunk],
            v_all.at[chunk], stats.at[chunk], att.at[chunk], total, begin,
            lambda head: p_write(step, head).start(),
        )
        return carry

    lax.fori_loop(0, count, forward_step, 0)
    for head in (1, 2):
        p_write(count - 1, head).wait()
    p_read(0, 0).start()
    value = total[...].astype(BF16)
    for k, out in enumerate((out0, out1, out2, out3)):
        piece = nn(pt[k], value).astype(BF16)
        out[PIECE:] = piece[EARLY:]
        if k == 0:
            returned[0, :EARLY] = piece[:EARLY]
        else:
            got_rows[k - 1, 0, :EARLY] = piece[:EARLY]
    total[...] = jnp.zeros_like(total)
    for k in (1, 3, 2):
        row_copy(1, k).wait_recv()
    gather_ff.across(0)
    lay_out(1, grads, dy_ref, dt)

    def events(poll):
        if poll == 1:
            gather_ff.spread(-1, 1)
        elif poll == 3:
            gather_ff.spread(-2, 2)
            scatter.after_core(0)
        elif poll == 4:
            gather_ff.forward(-1, 1)
        elif poll == 5:
            gather_ff.spread(-3, 3)
        elif poll == 6:
            gather_ff.forward(-2, 2)
            scatter.after_core(1)
        elif poll == 7:
            gather_ff.across(-1, 1)
            scatter.after_first(0)
        elif poll == 8:
            gather_ff.forward(-3, 3)
            scatter.after_second(0)
            along.send_outer(0)
        elif poll == 9:
            gather_ff.across(-2, 2)
            scatter.after_core(2)
            scatter.after_first(1)
        elif poll == 10:
            scatter.after_second(1)
            along.send_outer(1)
            gather_ff.across(-3, 3)
        elif poll == 11:
            along.send_inner(0)
            scatter.after_first(2)
        for k, strip in strips[max(0, poll - 3):max(0, poll - 2)]:
            back_copy(k, strip).start()

    def backward_step(step, carry):
        chunk = at.target(step)

        def store(cols, value):
            split = (2, 2, 2, shard, cols.stop - cols.start)
            value = value.reshape(split)

            @pl.when(step < count - 1)
            def _():
                g_buf[step, 0, :, :, :, :, cols] = value

            @pl.when(step == count - 1)
            def _():
                g_last[0, 0, :, :, :, :, cols] = value

        def ready(head):
            p_read(step, head).wait()
            if head < 2:
                p_read(step, head + 1).start()
            else:
                @pl.when(step + 1 < count)
                def _():
                    p_read(step + 1, 0).start()
            return p_buf.at[lax.rem(step + head, 2)]

        def poll(head):
            for which in range(count):
                @pl.when(step == which)
                def _():
                    events(3 * which + head)

        backward_chunk(
            weights_of(chunk), gains[...], dy_ref, xt, dt, raw, d_raw,
            qk_all.at[chunk], v_all.at[chunk], stats.at[chunk], att.at[chunk], total, g_gains,
            ready, store, poll,
        )

        @pl.when(step < count - 1)
        def _():
            scatter.start(step)

        return carry

    lax.fori_loop(0, count, backward_step, 0)
    along.send_inner(1)
    scatter.after_second(2)
    along.send_outer(2)
    along.send_inner(2)
    store_gain(g_gains, total[...], x_ref[...], norm_gain[...])
    value = total[...].astype(BF16)
    for k, out in enumerate((out0, out1, out2, out3)):
        out[:PIECE] = nn(pt[k], value).astype(BF16)
    z_attn[...] = jnp.zeros_like(z_attn)
    gather_ff.last()
    for k, strip in strips:
        back_copy(k, strip).wait_recv()
    along.add(0, z_attn)

    gather.wait_send()
    gather_ff.wait_send()
    for k, strip in strips:
        back_copy(k, strip).wait_send()
    for k in range(1, count):
        for kind in range(2):
            row_copy(kind, k).wait_send()
    for step in range(count - 1):
        scatter.wait_send(step)
        along.wait_send(step)


def place_rows(me, part, ids, pt, feat_q, feat_k):
    mp = ids.shape[1]
    total = mp * part
    numbers = ids[me]
    start = jnp.zeros((1, 1), jnp.int32)
    for image in range(IMAGES):
        count = jnp.sum((numbers == image).astype(F32), axis=(0, 1), keepdims=True)
        ahead = jnp.sum(
            ((numbers >= 0) & (numbers < image)).astype(F32), axis=(0, 1), keepdims=True
        )
        start = start + jnp.where(count == MOST, ahead, 0.0).astype(jnp.int32)
    line = source_of(iota((1, ROWS), 1), start, total)
    feats = 0.0
    for k in range(mp):
        chunk = lax.rem(me - k + mp, mp)
        offset = iota((PIECE, 1), 0)
        pos = jnp.where(offset < part, chunk * part + offset, -2)
        pick = (line == pos).astype(F32).astype(BF16)
        pt[k] = pick
        marks = (iota((128, 1), 0) - HD == ids[me, pl.ds(chunk, 1), :]).astype(F32)
        feats = feats + nn(marks.astype(BF16), pick)
    feats = feats.T
    lane = iota((1, 128), 1)
    feat_q[...] = (feats * 128.0).astype(BF16)
    marked = (lane >= HD) & (lane < HD + IMAGES)
    feat_k[...] = jnp.where(marked, (feats - 1.0) * 256.0, 0.0).astype(BF16)


def front_call(tokens, cotangent, ids, gains, norm_gain, w_attn, w_feed):
    count, part, width = tokens.shape
    shard = w_attn.shape[0]
    vmem = pl.BlockSpec(memory_space=pltpu.VMEM)
    hbm = pl.BlockSpec(memory_space=pl.ANY)
    rows = jax.ShapeDtypeStruct((count, PIECE, width), BF16)
    return pl.pallas_call(
        front_kernel,
        in_specs=[vmem] * 6 + [hbm],
        out_specs=[vmem] * 7 + [hbm] + [vmem] * 3 + [hbm],
        out_shape=[rows, rows, jax.ShapeDtypeStruct((count, EARLY, width), BF16)]
        + [jax.ShapeDtypeStruct((2 * PIECE - EARLY, width), BF16)] * 4
        + [
            jax.ShapeDtypeStruct((count, 2, 2, 2, 2, shard, width), BF16),
            jax.ShapeDtypeStruct((1, 1, 2, 2, 2, shard, width), BF16),
            jax.ShapeDtypeStruct((shard, width), F32),
            jax.ShapeDtypeStruct((8, 128), F32),
            jax.ShapeDtypeStruct((count, 3, ROWS, BIG), BF16),
        ],
        scratch_shapes=[
            pltpu.VMEM((count - 1, 2, PIECE, width), BF16),
            pltpu.VMEM((count, 2, 2, 2, shard, width), BF16),
            pltpu.VMEM((count - 1, 1, 2, 2, 2, shard, width), BF16),
            pltpu.VMEM((count - 1, 1, 2, 2, shard, width), BF16),
            pltpu.VMEM((count - 1, 1, 2, shard, width), BF16),
            pltpu.VMEM((count - 1, 1, shard, width), BF16),
            pltpu.VMEM((1, 5, shard, width), BF16),
            pltpu.VMEM((ROWS, width), BF16),
            pltpu.VMEM((ROWS, width), BF16),
            pltpu.VMEM((width, ROWS), BF16),
            pltpu.VMEM((width, ROWS), BF16),
            pltpu.VMEM((ROWS, 128), BF16),
            pltpu.VMEM((ROWS, 128), BF16),
            pltpu.VMEM((count, PIECE, ROWS), BF16),
            pltpu.VMEM((ROWS, 640), F32),
            pltpu.VMEM((ROWS, 640), BF16),
            pltpu.VMEM((2, ROWS, BIG), BF16),
            pltpu.VMEM((count, 3, ROWS, 128), BF16),
            pltpu.VMEM((count, 3, ROWS, 128), BF16),
            pltpu.VMEM((count, ROWS, 128), F32),
            pltpu.VMEM((count, ROWS, 256), BF16),
            pltpu.VMEM((ROWS, width), F32),
            pltpu.SemaphoreType.DMA((2, count - 1)),
            pltpu.SemaphoreType.DMA((2, count - 1)),
            pltpu.SemaphoreType.DMA((count - 1, EARLY // STRIP)),
            pltpu.SemaphoreType.DMA((count - 1, EARLY // STRIP)),
            pltpu.SemaphoreType.DMA((9, count)),
            pltpu.SemaphoreType.DMA((8, count)),
            pltpu.SemaphoreType.DMA((9, count)),
            pltpu.SemaphoreType.DMA((8, count)),
            pltpu.SemaphoreType.DMA,
            pltpu.SemaphoreType.DMA((2,)),
            pltpu.SemaphoreType.DMA((2,)),
            pltpu.SemaphoreType.DMA((3, 2, count - 1)),
            pltpu.SemaphoreType.DMA((3, 2, count - 1)),
            pltpu.SemaphoreType.DMA((1, count - 1)),
            pltpu.SemaphoreType.DMA((1, 5)),
        ],
        compiler_params=pltpu.CompilerParams(
            collective_id=1, has_side_effects=True, vmem_limit_bytes=FRONT_VMEM
        ),
        name="front",
    )(tokens, cotangent, ids, gains, norm_gain, w_attn, w_feed)


def finish_kernel(
    place, tok, cot, gain, branch, d_ff, back, ret0, ret1, ret2, ret3, output, input_grad
):
    step = pl.program_id(0)
    part = tok.shape[1]

    for index, ret in enumerate((ret0, ret1, ret2, ret3)):

        @pl.when(step == index)
        def _():
            x = tok[0].astype(F32)
            output[0] = (x + (branch[0] + jnp.concatenate([back[0], ret[PIECE:]]).astype(F32))[:part]).astype(BF16)
            d_normed = (d_ff[0] + ret[:PIECE].astype(F32))[:part]
            centered = x - jnp.mean(x, axis=-1, keepdims=True)
            spread = lax.rsqrt(jnp.mean(centered * centered, axis=-1, keepdims=True) + 1e-6)
            unit = centered * spread
            scaled = d_normed * gain[...]
            d_x = spread * (
                scaled
                - jnp.mean(scaled, axis=-1, keepdims=True)
                - unit * jnp.mean(scaled * unit, axis=-1, keepdims=True)
            )
            input_grad[0] = cot[0].astype(F32) + d_x


def finish_call(place, tokens, cotangent, gain, branch, d_ff, back, returned):
    count, part, width = tokens.shape
    block = pl.BlockSpec(
        (1, part, width), lambda k, place: (lax.rem(place[0] + k, count), 0, 0)
    )
    padded = pl.BlockSpec((1, PIECE, width), lambda k, place: (k, 0, 0))
    piece = pl.BlockSpec((2 * PIECE - EARLY, width), lambda k, place: (0, 0))
    early = pl.BlockSpec((1, EARLY, width), lambda k, place: (k, 0, 0))
    line = pl.BlockSpec((1, width), lambda k, place: (0, 0))
    return pl.pallas_call(
        finish_kernel,
        grid_spec=pltpu.PrefetchScalarGridSpec(
            num_scalar_prefetch=1,
            grid=(count,),
            in_specs=[block, block, line, padded, padded, early] + [piece] * 4,
            out_specs=[block, block],
        ),
        out_shape=[
            jax.ShapeDtypeStruct(tokens.shape, BF16),
            jax.ShapeDtypeStruct(tokens.shape, F32),
        ],
        compiler_params=pltpu.CompilerParams(vmem_limit_bytes=VMEM),
        name="finish",
    )(place, tokens, cotangent, gain, branch, d_ff, back, *returned)


def pack_attention(w_qkv, w_proj):
    rows, wide = w_qkv.shape[1:]
    heads = wide // HD
    qk = w_qkv[:2].reshape(2, rows, heads, HD).transpose(1, 2, 0, 3).reshape(rows, 2 * wide)
    return jnp.concatenate([qk, w_qkv[2], w_proj.T], axis=1)


def unpack_attention(grad, wide):
    rows = grad.shape[0]
    heads = wide // HD
    qk = grad[:, :2 * wide].reshape(rows, heads, 2, HD).transpose(2, 0, 1, 3)
    qk = qk.reshape(2, rows, wide)
    g_qkv = jnp.concatenate([qk, grad[None, :, 2 * wide:3 * wide]], axis=0)
    return g_qkv, grad[:, 3 * wide:].T


def body(
    dp, mp, tokens, w_qkv, w_up, w_proj, w_down, norm_gain, query_gain, key_gain, image_ids, cotangent
):
    micro, seqs, part, width = tokens.shape
    count = micro * seqs
    shard = w_up.shape[0]
    me = lax.axis_index("mp")
    place = me.astype(jnp.int32)[None]
    both = ("mp", "dp")
    tok = tokens.reshape(count, part, width)
    cot = cotangent.reshape(count, part, width)
    gain = norm_gain.reshape(1, width)
    ids = image_ids.reshape(count, mp, part)
    ids = jnp.pad(ids, ((0, 0), (0, 0), (0, PIECE - part)), constant_values=-1)
    gains = jnp.concatenate([query_gain, key_gain]).reshape(1, 2 * HD)
    w_attn = pack_attention(w_qkv, w_proj)
    w_ff = jnp.stack([w_up, w_down.T])

    def send_back(outs):
        return [outs[0]] + [
            lax.ppermute(out, "mp", [(i, (i - k) % mp) for i in range(mp)])
            for k, out in enumerate(outs[1:], 1)
        ]

    if (dp, mp) == (8, 4):
        normed, grads, back, *outs, w_ff, g_attn, z_attn, g_gains, _ = front_call(
            tok, cot, ids, gains, gain, w_attn, w_ff
        )
        returned = send_back(outs)
        branch, d_ff, g_attn, g_up, g_down, g_gains = feed_remote_call(
            normed.reshape(count * PIECE, width), grads.reshape(count * PIECE, width),
            w_ff.reshape(mp, dp, 2, shard, width), g_attn, z_attn, gain, g_gains,
        )
    else:
        w_attn = lax.all_gather(w_attn, both).reshape(mp, width, width)
        w_ff = lax.all_gather(w_ff, both).reshape(mp, dp, 2, shard, width)
        normed, grads, *sends = norm_call(place, tok, cot, gain)
        received = [
            lax.ppermute(send, "mp", [(i, (i + k) % mp) for i in range(mp)])
            for k, send in enumerate(sends, 1)
        ]
        *outs, g_attn, g_gains = attention_call(
            place, part, normed, grads, received, ids, gains, gain, w_attn
        )
        outs = send_back(outs)
        back = jnp.stack([out[1, :EARLY] for out in outs])
        returned = [jnp.concatenate([out[0], out[1, EARLY:]]) for out in outs]
        flat_normed = normed.reshape(count * PIECE, width)
        branch, d_ff, g_up, g_down = feed_call(
            flat_normed, grads.reshape(count * PIECE, width),
            w_ff[:, :, 0].reshape(mp, width, width), w_ff[:, :, 1].reshape(mp, width, width),
        )
        g_attn, g_up, g_down = (
            lax.psum_scatter(
                grad.reshape(-1, shard, width), both, scatter_dimension=0
            ).astype(F32)
            for grad in (g_attn, g_up, g_down)
        )
        own = jnp.sum(d_ff * flat_normed.astype(F32), axis=0) / norm_gain
        g_gains = g_gains.at[:width // 128].add(own.reshape(-1, 128))
        g_gains = lax.psum(g_gains, both)
    output, input_grad = finish_call(
        place, tok, cot, gain,
        branch.reshape(count, PIECE, width), d_ff.reshape(count, PIECE, width), back, returned,
    )
    g_qkv, g_proj = unpack_attention(g_attn, w_qkv.shape[2])
    g_norm = g_gains[:width // 128].reshape(width)
    g_gains = g_gains[6]
    return (
        output.reshape(tokens.shape),
        input_grad.reshape(tokens.shape),
        g_qkv,
        g_up,
        g_proj,
        g_down.T,
        g_norm,
        g_gains[:HD],
        g_gains[HD:],
    )


def solution(mesh):
    rows = P(None, "dp", "mp", None)
    weights = (P(None, "dp", "mp"), P("dp", "mp"), P("mp", "dp"), P("mp", "dp"))
    gains = (P(), P(), P())
    return jax.shard_map(
        functools.partial(body, mesh.shape["dp"], mesh.shape["mp"]),
        mesh=mesh,
        in_specs=(rows,) + weights + gains + (P(None, "dp", None), rows),
        out_specs=(rows, rows) + weights + gains,
        check_vma=False,
    )
```

```python
import functools

import jax
import jax.numpy as jnp
from jax import lax
from jax.experimental import pallas as pl
from jax.experimental.pallas import tpu as pltpu
from jax.sharding import PartitionSpec as P

HD = 64
MOST = 709
IMAGES = 8
STRIP = 48
EARLY = 144
PIECE = 240
BIG = 768
REST = 256
ROWS = BIG + REST
VMEM = 60 * 1024 * 1024
FRONT_VMEM = 63 * 1024 * 1024
F32 = jnp.float32
BF16 = jnp.bfloat16


def nn(left, right):
    return lax.dot_general(left, right, (((1,), (0,)), ((), ())), preferred_element_type=F32)


def nt(left, right):
    return lax.dot_general(left, right, (((1,), (1,)), ((), ())), preferred_element_type=F32)


def norm_kernel(place, tok, cot, gain, normed, grads, send1, send2, send3):
    step = pl.program_id(0)
    part = tok.shape[1]
    x = tok[0].astype(F32)
    centered = x - jnp.mean(x, axis=-1, keepdims=True)
    spread = lax.rsqrt(jnp.mean(centered * centered, axis=-1, keepdims=True) + 1e-6)
    value = (centered * spread * gain[...]).astype(BF16)
    normed[...] = jnp.zeros_like(normed)
    grads[...] = jnp.zeros_like(grads)
    normed[0, :part] = value
    grads[0, :part] = cot[0]
    for index, send in ((1, send1), (2, send2), (3, send3)):

        @pl.when(step == index)
        def _():
            send[0] = normed[0]
            send[1] = grads[0]


def norm_call(place, tokens, cotangent, gain):
    count, part, width = tokens.shape
    block = lambda k, place: (lax.rem(place[0] + k, count), 0, 0)
    fixed = lambda k, place: (0, 0, 0)
    return pl.pallas_call(
        norm_kernel,
        grid_spec=pltpu.PrefetchScalarGridSpec(
            num_scalar_prefetch=1,
            grid=(count,),
            in_specs=[
                pl.BlockSpec((1, part, width), block),
                pl.BlockSpec((1, part, width), block),
                pl.BlockSpec((1, width), lambda k, place: (0, 0)),
            ],
            out_specs=[pl.BlockSpec((1, PIECE, width), lambda k, place: (k, 0, 0))] * 2
            + [pl.BlockSpec((2, PIECE, width), fixed)] * 3,
        ),
        out_shape=[jax.ShapeDtypeStruct((count, PIECE, width), BF16)] * 2
        + [jax.ShapeDtypeStruct((2, PIECE, width), BF16)] * 3,
        compiler_params=pltpu.CompilerParams(vmem_limit_bytes=VMEM),
        name="norm_rows",
    )(place, tokens, cotangent, gain)


def feed_kernel(normed, grads, w_up, w_down, branch, d_normed, g_up, g_down, xt, dt):
    step = pl.program_id(0)
    x = normed[...]
    dy = grads[...]

    @pl.when(step == 0)
    def _():
        xt[...] = x.T
        dt[...] = dy.T

    up = nn(x, w_up[0])
    value, slope = gelu_parts(up)
    hidden = value.astype(BF16)
    d_up = (nn(dy, w_down[0]) * slope).astype(BF16)
    g_up[0] = nn(xt[...], d_up).astype(BF16)
    g_down[0] = nn(dt[...], hidden).astype(BF16)
    out = nt(hidden, w_down[0])
    back = nt(d_up, w_up[0])

    @pl.when(step == 0)
    def _():
        branch[...] = out
        d_normed[...] = back

    @pl.when(step > 0)
    def _():
        branch[...] += out
        d_normed[...] += back


def feed_call(normed, grads, w_up, w_down):
    rows, width = normed.shape
    chunks, _, hidden = w_up.shape
    whole = pl.BlockSpec((rows, width), lambda m: (0, 0))
    chunk = pl.BlockSpec((1, width, hidden), lambda m: (m, 0, 0))
    return pl.pallas_call(
        feed_kernel,
        grid=(chunks,),
        in_specs=[whole, whole, chunk, chunk],
        out_specs=[whole, whole, chunk, chunk],
        out_shape=[jax.ShapeDtypeStruct((rows, width), F32)] * 2
        + [jax.ShapeDtypeStruct(w_up.shape, BF16)] * 2,
        scratch_shapes=[pltpu.VMEM((width, rows), BF16)] * 2,
        compiler_params=pltpu.CompilerParams(vmem_limit_bytes=VMEM),
        cost_estimate=pl.CostEstimate(
            flops=12 * rows * width * hidden * chunks,
            bytes_accessed=4 * chunks * width * hidden * 2,
            transcendentals=rows * hidden * chunks,
        ),
        name="feed_forward",
    )(normed, grads, w_up, w_down)


class Place:
    def __init__(self, planes):
        d = lax.axis_index("dp")
        self.z = lax.axis_index("mp")
        self.d, self.planes = d, planes
        self.core, self.x, self.y = d % 2, (d // 2) % 2, d // 4
        self.sibling = d + 1 - 2 * self.core
        self.beside = d + 2 - 4 * self.x
        self.above = d + 4 - 8 * self.y

    def target(self, step):
        z, high = self.z, self.z // 2
        near = jnp.where(step == 2, 1 - z + 4 * high, z)
        return jnp.where(step == 0, 3 - 3 * high, jnp.where(step == 1, 2 - high, near))

    def along(self, k):
        return lax.rem(self.z + k + self.planes, self.planes)

    def copy(self, src, dst, send, recv, dp=None, mp=None):
        return pltpu.make_async_remote_copy(
            src_ref=src, dst_ref=dst, send_sem=send, recv_sem=recv,
            device_id={"dp": self.d if dp is None else dp, "mp": self.z if mp is None else mp},
            device_id_type=pl.DeviceIdType.MESH,
        )

    def greet(self):
        barrier = pltpu.get_barrier_semaphore()
        for other in (self.sibling, self.beside, self.above):
            pl.semaphore_signal(barrier, 1, device_id={"dp": other, "mp": self.z},
                                device_id_type=pl.DeviceIdType.MESH)
        for k in range(1, self.planes):
            pl.semaphore_signal(barrier, 1, device_id={"dp": self.d, "mp": self.along(k)},
                                device_id_type=pl.DeviceIdType.MESH)
        pl.semaphore_wait(barrier, self.planes + 2)


class Scatter:
    def __init__(self, at, items, src, got_core, got_first, got_second, send_sem, recv_sem):
        self.at, self.items, self.src = at, items, src
        self.got_core, self.got_first, self.got_second = got_core, got_first, got_second
        self.send_sem, self.recv_sem = send_sem, recv_sem

    def copy(self, stage, step, item):
        at = self.at
        kind, cols, x_first = self.items[item]
        if stage == 0:
            src = self.src.at[step, kind, :, :, 1 - at.core, :, cols]
            dst = self.got_core.at[step, kind, :, :, :, cols]
            to = at.sibling
        elif stage == 1:
            if x_first:
                src = self.got_core.at[step, kind, :, 1 - at.x, :, cols]
            else:
                src = self.got_core.at[step, kind, 1 - at.y, :, :, cols]
            dst = self.got_first.at[step, kind, :, :, cols]
            to = at.beside if x_first else at.above
        else:
            src = self.got_first.at[step, kind, 1 - at.y if x_first else 1 - at.x, :, cols]
            dst = self.got_second.at[step, kind, :, cols]
            to = at.above if x_first else at.beside
        sem = (stage, item, step)
        return at.copy(src, dst, self.send_sem.at[sem], self.recv_sem.at[sem], dp=to)

    def start(self, step):
        for item in range(len(self.items)):
            self.copy(0, step, item).start()

    def after_core(self, step):
        for item, (kind, cols, _) in enumerate(self.items):
            self.copy(0, step, item).wait_recv()
            for row in ((0, 0), (0, 1), (1, 0), (1, 1)):
                own = self.src[(step, kind, *row, self.at.core, slice(None), cols)]
                to = (step, kind, *row, slice(None), cols)
                total = own.astype(F32) + self.got_core[to].astype(F32)
                self.got_core[to] = total.astype(BF16)
            self.copy(1, step, item).start()

    def after_first(self, step):
        for item, (kind, cols, x_first) in enumerate(self.items):
            self.copy(1, step, item).wait_recv()
            for row in range(2):
                if x_first:
                    own = self.got_core[step, kind, row, self.at.x, :, cols]
                else:
                    own = self.got_core[step, kind, self.at.y, row, :, cols]
                total = own.astype(F32) + self.got_first[step, kind, row, :, cols].astype(F32)
                self.got_first[step, kind, row, :, cols] = total.astype(BF16)
            self.copy(2, step, item).start()

    def total(self, step, item):
        kind, cols, x_first = self.items[item]
        self.copy(2, step, item).wait_recv()
        own = self.got_first[step, kind, self.at.y if x_first else self.at.x, :, cols]
        return own.astype(F32) + self.got_second[step, kind, :, cols].astype(F32)

    def after_second(self, step):
        for item, (kind, cols, _) in enumerate(self.items):
            self.got_second[step, kind, :, cols] = self.total(step, item).astype(BF16)

    def wait_send(self, step):
        for item in range(len(self.items)):
            for stage in range(3):
                self.copy(stage, step, item).wait_send()


class Gather:
    def __init__(self, at, shard, full, send_sem, recv_sem):
        self.at, self.shard, self.full = at, shard, full
        self.send_sem, self.recv_sem = send_sem, recv_sem

    def there(self, r, does):
        plane = self.at.z + r

        @pl.when((plane >= 0) & (plane < self.at.planes))
        def _():
            does(plane)

    def piece(self, plane, y=False, x=False, core=False):
        at = self.at
        return self.full.at[plane, 1 - at.y if y else at.y, 1 - at.x if x else at.x,
                            1 - at.core if core else at.core]

    def copy(self, kind, plane, src, dst=None, **to):
        return self.at.copy(
            src, src if dst is None else dst, self.send_sem.at[kind, plane],
            self.recv_sem.at[kind % 8, plane], **to
        )

    def arrived(self, kind, plane, ref):
        self.copy(kind, plane, ref, dp=self.at.sibling).wait_recv()

    def pass_on(self, kind, plane, src, act):
        z, dst = self.at.z, self.piece(plane)
        if kind == 0:
            @pl.when(z < self.at.planes - 1)
            def _():
                act(self.copy(0, plane, src, dst, mp=z + 1))
        else:
            @pl.when(z > 0)
            def _():
                act(self.copy(8, plane, src, dst, mp=z - 1))

    def start(self):
        for kind in (0, 8):
            self.pass_on(kind, self.at.z, self.shard, lambda copy: copy.start())

    def spread(self, *which):
        for r in which:
            def does(plane):
                src = self.piece(plane)
                if r:
                    self.arrived(0, plane, src)
                    self.pass_on(0 if r < 0 else 8, plane, src, lambda copy: copy.start())
                self.copy(1, plane, src, dp=self.at.beside).start()
                self.copy(2, plane, src, dp=self.at.above).start()
                self.copy(3, plane, src, dp=self.at.sibling).start()

            self.there(r, does)

    def forward(self, *which):
        at = self.at
        for r in which:
            def does(plane):
                from_x, from_y = self.piece(plane, x=True), self.piece(plane, y=True)
                self.arrived(1, plane, from_x)
                if r in (0, 1, -3):
                    self.copy(5, plane, from_x, dp=at.above).start()
                self.copy(4, plane, from_x, dp=at.sibling).start()
                self.arrived(2, plane, from_y)
                if r not in (0, 1, -3):
                    self.copy(5, plane, from_y, dp=at.beside).start()
                self.copy(6, plane, from_y, dp=at.sibling).start()

            self.there(r, does)

    def across(self, *which):
        for r in which:
            def does(plane):
                src = self.piece(plane, y=True, x=True)
                self.arrived(5, plane, src)
                self.copy(7, plane, src, dp=self.at.sibling).start()

            self.there(r, does)

    def last(self):
        for plane in range(self.at.planes):
            self.arrived(3, plane, self.piece(plane, core=True))
            self.arrived(4, plane, self.piece(plane, x=True, core=True))
            self.arrived(6, plane, self.piece(plane, y=True, core=True))
            self.arrived(7, plane, self.piece(plane, y=True, x=True, core=True))

    def wait_send(self):
        for r in range(1 - self.at.planes, self.at.planes):
            def does(plane):
                src = self.piece(plane)
                if r <= 0:
                    self.pass_on(0, plane, src, lambda copy: copy.wait_send())
                if r >= 0:
                    self.pass_on(8, plane, src, lambda copy: copy.wait_send())
                for kind in range(1, 8):
                    self.copy(kind, plane, src, dp=self.at.sibling).wait_send()

            self.there(r, does)


class Along:
    def __init__(self, at, parts, got, send_sem, recv_sem):
        self.at, self.parts, self.got = at, parts, got
        self.send_sem, self.recv_sem = send_sem, recv_sem
        self.inner = (at.z == 1) | (at.z == 2)

    def copy(self, step, kind):
        at, inner = self.at, self.inner
        side = 1 - 2 * (at.z // 2)
        to = at.z + jnp.where(inner & (step == 2), -side, side)
        slot = jnp.where(inner, 2 + 2 * step - 3 * (step // 2), step + step // 2)
        return at.copy(self.parts.at[step, kind], self.got.at[kind, slot],
                       self.send_sem.at[kind, step], self.recv_sem.at[kind, slot], mp=to)

    def arrived(self, kind, slot):
        ref = self.got.at[kind, slot]
        self.at.copy(ref, ref, self.send_sem.at[kind, 0], self.recv_sem.at[kind, slot],
                     mp=self.at.along(1)).wait_recv()

    def send_outer(self, step):
        @pl.when(jnp.logical_not(self.inner))
        def _():
            for kind in range(self.got.shape[0]):
                self.copy(step, kind).start()

    def send_inner(self, step):
        @pl.when(self.inner)
        def _():
            for kind in range(self.got.shape[0]):
                self.arrived(kind, step)
                own = self.parts[step, kind].astype(F32)
                total = own + self.got[kind, step].astype(F32)
                self.parts[step, kind] = total.astype(BF16)
                self.copy(step, kind).start()

    def add(self, kind, out):
        self.arrived(kind, 3)
        out[...] += self.got[kind, 3].astype(F32)

        @pl.when(self.inner)
        def _():
            self.arrived(kind, 4)
            out[...] += self.got[kind, 4].astype(F32)

    def wait_send(self, step):
        for kind in range(self.got.shape[0]):
            self.copy(step, kind).wait_send()


def gelu_parts(up):
    inner = 0.7978845608028654 * (up + 0.044715 * up * up * up)
    th = jnp.tanh(inner)
    half = 0.5 * (1.0 + th)
    slope = half + 0.5 * up * (1.0 - th * th) * (
        0.7978845608028654 * (1.0 + 3 * 0.044715 * up * up)
    )
    return up * half, slope


def halves(width):
    return (0, slice(0, width // 2), True), (0, slice(width // 2, width), False)


def feed_remote_kernel(
    x_ref, dy_ref, w_hbm, g_attn, z_attn, gain, gains_in, back0, back1, back2, back3,
    branch, d_normed, out_attn, out_up, out_down, out_gains, returned,
    xt, dt, w_buf, hidden, d_up, g_ff, ff_core, ff_first, ff_second, at_core, at_first, at_second, got_z,
    parts, got_za, sums, got_sums, z_sums,
    w_sem, ff_send, ff_recv, at_send, at_recv, z_send, z_recv, za_send, za_recv,
    sum_send, sum_recv, back_send, back_recv, own_sem,
):
    width = x_ref.shape[1]
    steps, shard = w_hbm.shape[0], w_hbm.shape[3]
    at = Place(steps)
    at.greet()
    attn = Scatter(at, halves(width), g_attn, at_core, at_first, at_second, at_send, at_recv)
    both = (0, slice(0, width), True), (1, slice(0, width), False)
    feed = Scatter(at, both, g_ff, ff_core, ff_first, ff_second, ff_send, ff_recv)
    along = Along(at, ff_second, got_z, z_send, z_recv)
    along_attn = Along(at, parts, got_za, za_send, za_recv)
    last = steps - 1

    def w_copy(step, kind):
        slot = lax.rem(step, 2)
        return pltpu.make_async_copy(
            w_hbm.at[at.target(step), :, kind], w_buf.at[slot, kind], w_sem.at[slot, kind]
        )

    strips = [(k, strip) for strip in range(returned.shape[1] // STRIP) for k in (1, 3, 2)]
    first = len(strips) - 4 * steps + 1

    def back_copy(k, strip):
        rows, sem = pl.ds(strip * STRIP, STRIP), (k - 1, strip)
        return at.copy((back0, back1, back2, back3)[k].at[rows], returned.at[k, rows],
                       back_send.at[sem], back_recv.at[sem], mp=at.along(-k))

    own_back = pltpu.make_async_copy(back0, returned.at[0], own_sem)
    own_back.start()
    attn.start(0)
    for kind in range(2):
        w_copy(0, kind).start()
    for k, strip in strips[:first]:
        back_copy(k, strip).start()
    parts[...] = z_attn[...]
    for step in range(last):
        along_attn.send_outer(step)
    xt[...] = x_ref[...].T
    dt[...] = dy_ref[...].T
    branch[...] = jnp.zeros_like(branch)
    d_normed[...] = jnp.zeros_like(d_normed)

    def one_step(step, carry):
        for kind in range(2):
            w_copy(step, kind).wait()

        @pl.when(step + 1 < steps)
        def _():
            for kind in range(2):
                w_copy(step + 1, kind).start()

        slot = lax.rem(step, 2)
        split = (2, 2, 2, shard, width)

        def weights(kind):
            return w_buf[slot, kind].reshape(width, width)

        value, slope = gelu_parts(nn(x_ref[...], weights(0)))
        hidden[...] = value.astype(BF16)
        d_up[...] = (nn(dy_ref[...], weights(1)) * slope).astype(BF16)

        for which in range(steps):
            @pl.when(step == which)
            def _():
                for k, strip in strips[first + 4 * which:first + 4 * which + 4]:
                    back_copy(k, strip).start()

        @pl.when(step == 0)
        def _():
            attn.after_core(0)

        @pl.when(step == 2)
        def _():
            along_attn.send_inner(0)

        @pl.when(step == 3)
        def _():
            along_attn.send_inner(1)
            along_attn.send_inner(2)

        g_ff[step, 0] = nn(xt[...], d_up[...]).astype(BF16).reshape(split)
        g_ff[step, 1] = nn(dt[...], hidden[...]).astype(BF16).reshape(split)
        feed.start(step)

        @pl.when(step >= 1)
        def _():
            feed.after_first(step - 1)

        branch[...] += nt(hidden[...], weights(1))
        d_normed[...] += nt(d_up[...], weights(0))
        feed.after_core(step)

        @pl.when(step == 0)
        def _():
            attn.after_first(0)

        @pl.when(step >= 1)
        def _():
            feed.after_second(step - 1)
            along.send_outer(step - 1)

        return carry

    lax.fori_loop(0, steps, one_step, 0)

    sums[0] = gains_in[...]
    store_gain(sums.at[0], d_normed[...], x_ref[...], gain[...])

    def sum_copy(stage):
        to = (at.sibling, at.beside, at.above)[stage]
        return at.copy(sums.at[stage], got_sums.at[stage], sum_send.at[stage],
                       sum_recv.at[stage], dp=to)

    def sum_z_copy(k):
        return at.copy(sums.at[3], z_sums.at[at.z], sum_send.at[2 + k], sum_recv.at[2 + k],
                       mp=at.along(k))

    def next_sum(stage):
        sum_copy(stage).wait_recv()
        sums[stage + 1] = sums[stage] + got_sums[stage]

    sum_copy(0).start()
    for item in range(2):
        cols = attn.items[item][1]
        out_attn[:, cols] = attn.total(0, item)
    next_sum(0)
    sum_copy(1).start()
    along.send_inner(0)
    along.send_inner(1)
    next_sum(1)
    sum_copy(2).start()
    feed.after_first(last)
    along.send_inner(2)
    next_sum(2)
    for k in range(1, steps):
        sum_z_copy(k).start()
    z_sums[at.z] = sums[3]
    along_attn.add(0, out_attn)
    for kind, out in enumerate((out_up, out_down)):
        out[...] = feed.total(last, kind)
        along.add(kind, out)
    for k in range(1, steps):
        sum_z_copy(k).wait_recv()
    total = z_sums[0]
    for k in range(1, steps):
        total = total + z_sums[k]
    out_gains[...] = total

    own_back.wait()
    for k, strip in strips:
        back_copy(k, strip).wait_recv()
        back_copy(k, strip).wait_send()
    attn.wait_send(0)
    for step in range(steps):
        feed.wait_send(step)
    for step in range(last):
        along.wait_send(step)
        along_attn.wait_send(step)
    for stage in range(3):
        sum_copy(stage).wait_send()
    for k in range(1, steps):
        sum_z_copy(k).wait_send()


def feed_remote_call(normed, grads, w_ff, g_attn, z_attn, gain, gains, backs):
    rows, width = normed.shape
    steps, _, _, shard, _ = w_ff.shape
    vmem = pl.BlockSpec(memory_space=pltpu.VMEM)
    hbm = pl.BlockSpec(memory_space=pl.ANY)
    return pl.pallas_call(
        feed_remote_kernel,
        in_specs=[vmem, vmem, hbm] + [vmem] * 4 + [hbm] * 4,
        out_specs=[vmem] * 6 + [hbm],
        out_shape=[jax.ShapeDtypeStruct((rows, width), F32)] * 2
        + [jax.ShapeDtypeStruct((shard, width), F32)] * 3
        + [jax.ShapeDtypeStruct((8, 128), F32)]
        + [jax.ShapeDtypeStruct((steps,) + backs[0].shape, BF16)],
        scratch_shapes=[
            pltpu.VMEM((width, rows), BF16),
            pltpu.VMEM((width, rows), BF16),
            pltpu.VMEM((2, 2, 8, shard, width), BF16),
            pltpu.VMEM((rows, width), BF16),
            pltpu.VMEM((rows, width), BF16),
            pltpu.VMEM((steps, 2, 2, 2, 2, shard, width), BF16),
            pltpu.VMEM((steps, 2, 2, 2, shard, width), BF16),
            pltpu.VMEM((steps, 2, 2, shard, width), BF16),
            pltpu.VMEM((steps, 2, shard, width), BF16),
            pltpu.VMEM((1, 1, 2, 2, shard, width), BF16),
            pltpu.VMEM((1, 1, 2, shard, width), BF16),
            pltpu.VMEM((1, 1, shard, width), BF16),
            pltpu.VMEM((2, 5, shard, width), BF16),
            pltpu.VMEM((steps - 1, 1, shard, width), BF16),
            pltpu.VMEM((1, 5, shard, width), BF16),
            pltpu.VMEM((4, 8, 128), F32),
            pltpu.VMEM((3, 8, 128), F32),
            pltpu.VMEM((steps, 8, 128), F32),
            pltpu.SemaphoreType.DMA((2, 2)),
            pltpu.SemaphoreType.DMA((3, 2, steps)),
            pltpu.SemaphoreType.DMA((3, 2, steps)),
            pltpu.SemaphoreType.DMA((3, 2, 1)),
            pltpu.SemaphoreType.DMA((3, 2, 1)),
            pltpu.SemaphoreType.DMA((2, steps - 1)),
            pltpu.SemaphoreType.DMA((2, 5)),
            pltpu.SemaphoreType.DMA((1, steps - 1)),
            pltpu.SemaphoreType.DMA((1, 5)),
            pltpu.SemaphoreType.DMA((6,)),
            pltpu.SemaphoreType.DMA((6,)),
            pltpu.SemaphoreType.DMA((steps - 1, backs[0].shape[0] // STRIP)),
            pltpu.SemaphoreType.DMA((steps - 1, backs[0].shape[0] // STRIP)),
            pltpu.SemaphoreType.DMA,
        ],
        compiler_params=pltpu.CompilerParams(
            collective_id=0, has_side_effects=True, vmem_limit_bytes=VMEM
        ),
        cost_estimate=pl.CostEstimate(
            flops=12 * rows * width * width * steps,
            bytes_accessed=4 * steps * width * width * 2,
            transcendentals=rows * width * steps,
        ),
        name="feed_forward_scatter",
    )(normed, grads, w_ff, g_attn, z_attn, gain, gains, *backs)


def iota(shape, axis):
    return lax.broadcasted_iota(jnp.int32, shape, axis)


def source_of(index, start, total):
    rest = index - BIG
    other = jnp.where(rest < start, rest, rest + MOST)
    held = jnp.where(index < MOST, start + index, -1)
    return jnp.where((rest >= 0) & (rest < total - MOST), other, held)


def store_gain(out, d_normed, normed, gain):
    total = jnp.sum(d_normed * normed.astype(F32), axis=0, keepdims=True) / gain
    for row in range(total.shape[1] // 128):
        out[row:row + 1] += total[:, 128 * row:128 * row + 128]


def prepare(
    me, part, ids, pieces, x_ref, dy_ref, xt, dt, feat_q, feat_k, pt, d_normed, branch, g_gains
):
    mp = ids.shape[1]
    total = mp * part
    numbers = ids[me]
    start = jnp.zeros((1, 1), jnp.int32)
    for image in range(IMAGES):
        count = jnp.sum((numbers == image).astype(F32), axis=(0, 1), keepdims=True)
        ahead = jnp.sum(
            ((numbers >= 0) & (numbers < image)).astype(F32), axis=(0, 1), keepdims=True
        )
        start = start + jnp.where(count == MOST, ahead, 0.0).astype(jnp.int32)
    column = source_of(iota((ROWS, 1), 0), start, total)
    line = source_of(iota((1, ROWS), 1), start, total)
    x_sum, dy_sum, feats = 0.0, 0.0, 0.0
    for k, piece in enumerate(pieces):
        chunk = lax.rem(me - k + mp, mp)
        offset = iota((1, PIECE), 1)
        pos = jnp.where(offset < part, chunk * part + offset, -2)
        pick = (column == pos).astype(F32).astype(BF16)
        offset = iota((PIECE, 1), 0)
        pos = jnp.where(offset < part, chunk * part + offset, -2)
        pt[k] = (line == pos).astype(F32).astype(BF16)
        x_sum = x_sum + nn(pick, piece[0][...])
        dy_sum = dy_sum + nn(pick, piece[1][...])
        marks = (iota((128, 1), 0) - HD == ids[me, pl.ds(chunk, 1), :]).astype(F32)
        feats = feats + nt(pick, marks.astype(BF16))
    x = x_sum.astype(BF16)
    dy = dy_sum.astype(BF16)
    x_ref[...] = x
    dy_ref[...] = dy
    xt[...] = x.T
    dt[...] = dy.T
    lane = iota((1, 128), 1)
    feat_q[...] = (feats * 128.0).astype(BF16)
    marked = (lane >= HD) & (lane < HD + IMAGES)
    feat_k[...] = jnp.where(marked, (feats - 1.0) * 256.0, 0.0).astype(BF16)
    d_normed[...] = jnp.zeros_like(d_normed)
    branch[...] = jnp.zeros_like(branch)
    g_gains[...] = jnp.zeros_like(g_gains)


def attention_chunk(
    weights, gain, x_ref, dy_ref, xt, dt, feat_q, feat_k, raw, d_raw, d_att, att,
    d_normed, branch, g_gains, store, poll,
):
    raw[...] = nn(x_ref[...], weights(slice(0, 640)))
    d_att[...] = nn(dy_ref[...], weights(slice(512, 768)))
    lane = iota((1, 128), 1)
    low = lane < HD
    same = (iota((128, 128), 0) // HD == iota((128, 128), 1) // HD).astype(F32)
    mean_of = (same * (1.0 / HD)).astype(BF16)

    def half_mean(value):
        return nn(value.astype(BF16), mean_of)

    d_gain = jnp.zeros((1, 128), F32)
    for head in range(3):
        qk = raw[:, 128 * head:128 * head + 128]
        high = qk.astype(BF16)
        mean = nn(high, mean_of) + half_mean(qk - high.astype(F32))
        centered = qk - mean
        spread = lax.rsqrt(half_mean(centered * centered) + 1e-6)
        unit = centered * spread
        rounded = (unit * gain).astype(BF16).astype(F32)
        q_aug = jnp.where(low, rounded * 0.125, feat_q[...].astype(F32)).astype(BF16)
        k_aug = jnp.where(low, pltpu.roll(rounded, HD, 1), feat_k[...].astype(F32)).astype(BF16)
        v_tile = 384 + 128 * (head // 2)
        v = raw[:, v_tile:v_tile + 128]
        if head == 1:
            v = pltpu.roll(v, HD, 1)
        one = ((lane == HD) | (lane == HD + 1)).astype(F32)
        v_aug = jnp.where(low, v, one).astype(BF16)
        a_tile = 128 * ((head + 1) // 2)
        da = d_att[:, a_tile:a_tile + 128]
        if head != 1:
            da = pltpu.roll(da, HD, 1)
        q_t = q_aug.astype(F32).T.astype(BF16)
        d_queries, attended, d_keys, d_values = [], [], [], []
        for base, count in ((0, BIG), (BIG, REST)):
            keys = k_aug[base:base + count]
            values = v_aug[base:base + count]
            dk_t = jnp.zeros((128, count), F32)
            dv_t = jnp.zeros((128, count), F32)
            for row in range(base, base + count, 256):
                rows = slice(row, row + 256)
                prob = jnp.exp(nt(q_aug[rows], keys))
                prob_low = prob.astype(BF16)
                gathered = nn(prob_low, values)
                inverse = 1.0 / gathered[:, HD:HD + 1]
                out = jnp.where(low, gathered * inverse, 0.0)
                attended.append(out)
                scaled = jnp.where(low, da[rows] * inverse, 0.0).astype(BF16).astype(F32)
                dot = jnp.sum(scaled * out, axis=-1, keepdims=True)
                dot_high = dot.astype(BF16).astype(F32)
                d_aug = jnp.where(
                    lane == HD, -dot_high, jnp.where(lane == HD + 1, dot_high - dot, scaled)
                )
                d_low = d_aug.astype(BF16)
                d_score = (prob * nt(d_low, values)).astype(BF16)
                d_queries.append(nn(d_score, keys))
                dk_t = dk_t + nn(q_t[:, rows], d_score)
                dv_t = dv_t + nn(d_aug.T.astype(BF16), prob_low)
            d_keys.append(dk_t.T)
            d_values.append(dv_t.T)
        d_query = jnp.concatenate(d_queries, axis=0) * 0.125
        d_key = jnp.concatenate(d_keys, axis=0)
        d_value = jnp.concatenate(d_values, axis=0)
        attend = jnp.concatenate(attended, axis=0)
        d_qk = jnp.where(low, d_query, pltpu.roll(d_key, HD, 1))
        d_gain = d_gain + jnp.sum(d_qk * unit, axis=0, keepdims=True)
        scaled = d_qk * gain
        d_qk = spread * (scaled - half_mean(scaled) - unit * half_mean(scaled * unit))
        d_raw[:, 128 * head:128 * head + 128] = d_qk.astype(BF16)
        if head == 0:
            first_value = d_value
            att[:, 0:128] = jnp.where(low, 0.0, pltpu.roll(attend, HD, 1)).astype(BF16)
        elif head == 1:
            both = jnp.where(low, first_value, pltpu.roll(d_value, HD, 1))
            d_raw[:, 384:512] = both.astype(BF16)
            first_att = attend
        else:
            d_raw[:, 512:640] = jnp.where(low, d_value, 0.0).astype(BF16)
            both = jnp.where(low, first_att, pltpu.roll(attend, HD, 1))
            att[:, 128:256] = both.astype(BF16)
        poll(head)
    g_gains[6:7] += d_gain
    d_projected = d_raw[...]
    attended = att[...]
    d_normed[...] += nt(d_projected, weights(slice(0, 640)))
    branch[...] += nt(attended, weights(slice(512, 768)))
    left = nn(xt[...], d_projected)
    right = nn(dt[...], attended)
    store(slice(0, 512), left[:, :512].astype(BF16))
    store(slice(512, 640), (left[:, 512:] + right[:, :128]).astype(BF16))
    store(slice(640, 768), right[:, 128:].astype(BF16))


def take_back(outs, pt, x_ref, norm_gain, d_normed, branch, g_gains):
    store_gain(g_gains, d_normed[...], x_ref[...], norm_gain[...])
    d_rows = d_normed[...].astype(BF16)
    b_rows = branch[...].astype(BF16)
    for k, out in enumerate(outs):
        out[0] = nn(pt[k], d_rows).astype(BF16)
        out[1] = nn(pt[k], b_rows).astype(BF16)


def attention_kernel(
    part, place, own_x, own_dy, in1, in2, in3, ids, gains, norm_gain, weights,
    out0, out1, out2, out3, g_weights, g_gains,
    x_ref, dy_ref, xt, dt, feat_q, feat_k, pt, raw, d_raw, d_att, att, d_normed, branch,
):
    step = pl.program_id(0)

    @pl.when(step == 0)
    def _():
        pieces = [(own_x.at[0], own_dy.at[0])] + [(got.at[0], got.at[1]) for got in (in1, in2, in3)]
        prepare(place[0], part, ids, pieces, x_ref, dy_ref, xt, dt, feat_q, feat_k, pt,
                d_normed, branch, g_gains)

    def store(cols, value):
        g_weights[0, :, cols] = value

    attention_chunk(
        lambda cols: weights[0, :, cols], gains[...], x_ref, dy_ref, xt, dt, feat_q, feat_k,
        raw, d_raw, d_att, att, d_normed, branch, g_gains, store, lambda head: None,
    )

    @pl.when(step == pl.num_programs(0) - 1)
    def _():
        take_back((out0, out1, out2, out3), pt, x_ref, norm_gain, d_normed, branch, g_gains)


def attention_call(place, part, normed, grads, received, ids, gains, norm_gain, weights):
    width = normed.shape[-1]
    chunks = weights.shape[0]
    mp = ids.shape[1]
    own = pl.BlockSpec((1, PIECE, width), lambda m, place: (0, 0, 0))
    pair = pl.BlockSpec((2, PIECE, width), lambda m, place: (0, 0, 0))
    chunk = pl.BlockSpec((1, width, width), lambda m, place: (m, 0, 0))
    line = pl.BlockSpec((1, 128), lambda m, place: (0, 0))
    return pl.pallas_call(
        functools.partial(attention_kernel, part),
        grid_spec=pltpu.PrefetchScalarGridSpec(
            num_scalar_prefetch=1,
            grid=(chunks,),
            in_specs=[own, own, pair, pair, pair,
                      pl.BlockSpec(ids.shape, lambda m, place: (0, 0, 0)),
                      line, pl.BlockSpec((1, width), lambda m, place: (0, 0)), chunk],
            out_specs=[pair] * 4 + [chunk, pl.BlockSpec((8, 128), lambda m, place: (0, 0))],
            scratch_shapes=[
                pltpu.VMEM((ROWS, width), BF16),
                pltpu.VMEM((ROWS, width), BF16),
                pltpu.VMEM((width, ROWS), BF16),
                pltpu.VMEM((width, ROWS), BF16),
                pltpu.VMEM((ROWS, 128), BF16),
                pltpu.VMEM((ROWS, 128), BF16),
                pltpu.VMEM((mp, PIECE, ROWS), BF16),
                pltpu.VMEM((ROWS, 640), F32),
                pltpu.VMEM((ROWS, 640), BF16),
                pltpu.VMEM((ROWS, 256), F32),
                pltpu.VMEM((ROWS, 256), BF16),
                pltpu.VMEM((ROWS, width), F32),
                pltpu.VMEM((ROWS, width), F32),
            ],
        ),
        out_shape=[jax.ShapeDtypeStruct((2, PIECE, width), BF16)] * 4
        + [jax.ShapeDtypeStruct(weights.shape, BF16), jax.ShapeDtypeStruct((8, 128), F32)],
        compiler_params=pltpu.CompilerParams(vmem_limit_bytes=VMEM),
        cost_estimate=pl.CostEstimate(
            flops=60_000_000_000, bytes_accessed=4 * chunks * width * width,
            transcendentals=ROWS * ROWS * 12,
        ),
        name="attention",
    )(place, normed, grads, *received, ids, gains, norm_gain, weights)


def group_means():
    same = (iota((128, 128), 0) // HD == iota((128, 128), 1) // HD).astype(F32)
    return (same * (1.0 / HD)).astype(BF16)


def forward_chunk(
    weights, gain, x_ref, feat_q, feat_k, raw, qk_all, v_all, stats, att, branch, begin, spill
):
    raw[...] = nn(x_ref[...], weights(slice(0, 640)))
    lane = iota((1, 128), 1)
    low = lane < HD
    mean_of = group_means()

    def ahead(head):
        qk = raw[:, 128 * head:128 * head + 128]
        high = qk.astype(BF16)
        mean = nn(high, mean_of) + nn((qk - high.astype(F32)).astype(BF16), mean_of)
        centered = qk - mean
        spread = lax.rsqrt(nn((centered * centered).astype(BF16), mean_of) + 1e-6)
        rounded = (centered * spread * gain).astype(BF16)
        qk_all[head] = rounded
        rounded = rounded.astype(F32)
        q_aug = jnp.where(low, rounded * 0.125, feat_q[...].astype(F32)).astype(BF16)
        k_aug = jnp.where(low, pltpu.roll(rounded, HD, 1), feat_k[...].astype(F32)).astype(BF16)
        v_tile = 384 + 128 * (head // 2)
        v = raw[:, v_tile:v_tile + 128]
        if head == 1:
            v = pltpu.roll(v, HD, 1)
        v_aug = jnp.where(low, v, 1.0).astype(BF16)
        v_all[head] = v_aug
        return spread, q_aug, k_aug, v_aug

    def products(p_ref, spread, q_aug, k_aug, v_aug):
        parts = []
        for base, count in ((0, BIG), (BIG, REST)):
            keys = k_aug[base:base + count]
            values = v_aug[base:base + count]
            for row in range(base, base + count, 256):
                rows = slice(row, row + 256)
                prob = jnp.exp(nt(q_aug[rows], keys)).astype(BF16)
                p_ref[rows, :count] = prob
                parts.append(nn(prob, values))
        return spread, jnp.concatenate(parts, axis=0)

    def after(head, stat, spread, gathered):
        inverse = 1.0 / gathered
        attend = gathered * pltpu.roll(inverse, HD, 1)
        stat = jnp.where((lane == head) | (lane == HD + head), spread, stat)
        return jnp.where(lane == HD + 8 + head, inverse, stat), attend

    held = ahead(0)
    p_ref = begin(0)
    done0 = products(p_ref, *held)
    held = ahead(1)
    spill(0)
    p_ref = begin(1)
    done1 = products(p_ref, *held)
    held = ahead(2)
    stat, first = after(0, jnp.zeros((ROWS, 128), F32), *done0)
    att[:, 0:128] = jnp.where(low, 0.0, pltpu.roll(first, HD, 1)).astype(BF16)
    spill(1)
    p_ref = begin(2)
    done2 = products(p_ref, *held)
    stat, second = after(1, stat, *done1)
    spill(2)
    stat, third = after(2, stat, *done2)
    att[:, 128:256] = jnp.where(low, second, pltpu.roll(third, HD, 1)).astype(BF16)
    stats[...] = stat
    branch[...] += nt(att[...], weights(slice(512, 768)))


def backward_chunk(
    weights, gain, dy_ref, xt, dt, raw, d_raw, qk_all, v_all, stats, att,
    d_normed, g_gains, ready, store, poll,
):
    raw[:, :256] = nn(dy_ref[...], weights(slice(512, 768)))
    lane = iota((1, 128), 1)
    low = lane < HD
    mean_of = group_means()
    back_gain = 1.0 / gain

    def ahead(head):
        tile = 128 * ((head + 1) // 2)
        da = raw[:, tile:tile + 128]
        out = att[:, tile:tile + 128].astype(F32)
        if head != 1:
            da = pltpu.roll(da, HD, 1)
            out = pltpu.roll(out, HD, 1)
        inverse = stats[:, HD + 8 + head:HD + 9 + head]
        scaled = jnp.where(low, da * inverse, 0.0).astype(BF16).astype(F32)
        dot = jnp.sum(scaled * out, axis=-1, keepdims=True)
        dot_high = dot.astype(BF16).astype(F32)
        d_aug = jnp.where(
            lane == HD, -dot_high, jnp.where(lane == HD + 1, dot_high - dot, scaled)
        )
        qk_t = qk_all[head].astype(F32).T.astype(BF16)
        return d_aug.astype(BF16), d_aug.T.astype(BF16), qk_t

    def products(head, p_ref, d_low, d_t, qk_t):
        qk = qk_all[head]
        v_aug = v_all[head]
        d_queries, d_keys, d_values = [], [], []
        for base, count in ((0, BIG), (BIG, REST)):
            block = slice(base, base + count)
            d_values.append(nn(d_t[:, block], p_ref[block, :count]))
            for row in range(base, base + count, 256):
                rows = slice(row, row + 256)
                d_prob = nt(d_low[rows], v_aug[block])
                d_score = (p_ref[rows, :count].astype(F32) * d_prob).astype(BF16)
                p_ref[rows, :count] = d_score
                d_queries.append(nn(d_score, qk[block]))
            d_keys.append(nn(qk_t[:, block], p_ref[block, :count]))
        return d_queries, d_keys, d_values

    def after(head, d_queries, d_keys, d_values):
        d_query = jnp.concatenate(d_queries, axis=0)
        d_key = jnp.concatenate([part.T for part in d_keys], axis=0)
        d_value = jnp.concatenate([part.T for part in d_values], axis=0)
        d_qk = pltpu.roll(jnp.where(low, d_key, d_query), HD, 1) * 0.125
        unit = qk_all[head].astype(F32) * back_gain
        spread = jnp.where(low, stats[:, head:head + 1], stats[:, HD + head:HD + head + 1])
        g_gains[6:7] += jnp.sum(d_qk * unit, axis=0, keepdims=True)
        scaled = d_qk * gain
        mean = nn(scaled.astype(BF16), mean_of)
        d_qk = spread * (scaled - mean - unit * nn((scaled * unit).astype(BF16), mean_of))
        d_raw[:, 128 * head:128 * head + 128] = d_qk.astype(BF16)
        return d_value

    held = ahead(0)
    p_ref = ready(0)
    done0 = products(0, p_ref, *held)
    held = ahead(1)
    poll(0)
    p_ref = ready(1)
    done1 = products(1, p_ref, *held)
    held = ahead(2)
    first = after(0, *done0)
    poll(1)
    p_ref = ready(2)
    done2 = products(2, p_ref, *held)
    second = after(1, *done1)
    d_raw[:, 384:512] = jnp.where(low, first, pltpu.roll(second, HD, 1)).astype(BF16)
    poll(2)
    third = after(2, *done2)
    d_raw[:, 512:640] = jnp.where(low, third, 0.0).astype(BF16)
    d_projected = d_raw[...]
    d_normed[...] += nt(d_projected, weights(slice(0, 640)))
    left = nn(xt[...], d_projected)
    right = nn(dt[...], att[...])
    store(slice(0, 512), left[:, :512].astype(BF16))
    store(slice(512, 640), (left[:, 512:] + right[:, :128]).astype(BF16))
    store(slice(640, 768), right[:, 128:].astype(BF16))


def front_kernel(
    tok, cot, ids, gains, norm_gain, w_attn, w_feed,
    normed, grads, returned, out0, out1, out2, out3, w_ff, g_last, at_second, g_gains, p_all,
    got_rows, w_full, g_buf, at_core, at_first,
    x_ref, dy_ref, xt, dt, feat_q, feat_k, pt, raw, d_raw, p_buf,
    qk_all, v_all, stats, att, total,
    row_send, row_recv, back_send, back_recv, wa_send, wa_recv, wf_send, wf_recv, own_sem,
    p_out, p_in, at_send, at_recv,
):
    count, part, width = tok.shape
    shard = w_attn.shape[0]
    at = Place(count)
    at.greet()
    gather = Gather(at, w_attn, w_full, wa_send, wa_recv)
    gather_ff = Gather(at, w_feed, w_ff, wf_send, wf_recv)
    scatter = Scatter(at, halves(width), g_buf, at_core, at_first, at_second, at_send, at_recv)
    own_ff = pltpu.make_async_copy(w_feed, gather_ff.piece(at.z), own_sem)

    def row_copy(kind, k):
        src = (normed, grads)[kind].at[k]
        return at.copy(src, got_rows.at[k - 1, kind], row_send.at[kind, k - 1],
                       row_recv.at[kind, k - 1], mp=at.along(k))

    def back_copy(k, strip):
        rows, sem = pl.ds(strip * STRIP, STRIP), (k - 1, strip)
        return at.copy(got_rows.at[k - 1, 0, rows], returned.at[k, rows], back_send.at[sem],
                       back_recv.at[sem], mp=at.along(-k))

    strips = [(k, strip) for strip in range(EARLY // STRIP) for k in (1, 3, 2)]

    gather.start()
    own_ff.start()
    w_full[at.z, at.y, at.x, at.core] = w_attn[...]
    gather.spread(0)
    gain = norm_gain[...]
    for k in (1, 3, 2, 0):
        sequence = at.along(k)
        x = tok[sequence].astype(F32)
        centered = x - jnp.mean(x, axis=-1, keepdims=True)
        spread = lax.rsqrt(jnp.mean(centered * centered, axis=-1, keepdims=True) + 1e-6)
        pad = jnp.zeros((PIECE - part, width), BF16)
        normed[k, :part] = (centered * spread * gain).astype(BF16)
        normed[k, part:] = pad
        grads[k, :part] = cot[sequence]
        grads[k, part:] = pad
        if k == 2:
            gather.spread(-1, 1)
    gather.spread(-2, 2)
    for k in (1, 3, 2):
        row_copy(0, k).start()
    place_rows(at.z, part, ids, pt, feat_q, feat_k)
    g_gains[...] = jnp.zeros_like(g_gains)
    total[...] = jnp.zeros_like(total)
    gather.forward(0)
    gather.spread(-3, 3)
    own_ff.wait()
    gather.forward(-1, 1)
    gather.across(0)
    gather.forward(-2, 2)
    gather.across(-1, 1)
    gather.forward(-3, 3)
    gather.across(-2, 2)
    gather.across(-3, 3)
    gather.last()
    gather_ff.spread(0)
    for k in (1, 3, 2):
        row_copy(0, k).wait_recv()
    for k in (1, 3, 2):
        row_copy(1, k).start()

    def lay_out(kind, own, rows, columns):
        value = 0.0
        for k in range(count):
            piece = own[0] if k == 0 else got_rows[k - 1, kind]
            value = value + lax.dot_general(
                pt[k], piece, (((0,), (0,)), ((), ())), preferred_element_type=F32
            )
        value = value.astype(BF16)
        rows[...] = value
        columns[...] = value.T

    lay_out(0, normed, x_ref, xt)

    def weights_of(chunk):
        def weights(cols):
            return w_full[chunk, :, :, :, :, cols].reshape(width, cols.stop - cols.start)

        return weights

    def p_write(step, head):
        slot = lax.rem(step + head, 2)
        return pltpu.make_async_copy(p_buf.at[slot], p_all.at[at.along(step), head],
                                     p_out.at[slot])

    def p_read(step, head):
        slot = lax.rem(step + head, 2)
        return pltpu.make_async_copy(p_all.at[at.target(step), head], p_buf.at[slot],
                                     p_in.at[slot])

    def forward_step(step, carry):
        chunk = at.along(step)

        @pl.when(step == 2)
        def _():
            gather_ff.forward(0)

        def begin(head):
            if head == 2:
                p_write(step, 0).wait()
            else:
                @pl.when(step >= 1)
                def _():
                    p_write(step - 1, 1 + head).wait()
            return p_buf.at[lax.rem(step + head, 2)]

        forward_chunk(
            weights_of(chunk), gains[...], x_ref, feat_q, feat_k, raw, qk_all.at[chunk],
            v_all.at[chunk], stats.at[chunk], att.at[chunk], total, begin,
            lambda head: p_write(step, head).start(),
        )
        return carry

    lax.fori_loop(0, count, forward_step, 0)
    for head in (1, 2):
        p_write(count - 1, head).wait()
    p_read(0, 0).start()
    value = total[...].astype(BF16)
    for k, out in enumerate((out0, out1, out2, out3)):
        piece = nn(pt[k], value).astype(BF16)
        out[PIECE:] = piece[EARLY:]
        if k == 0:
            returned[0, :EARLY] = piece[:EARLY]
        else:
            got_rows[k - 1, 0, :EARLY] = piece[:EARLY]
    total[...] = jnp.zeros_like(total)
    for k in (1, 3, 2):
        row_copy(1, k).wait_recv()
    gather_ff.start()
    gather_ff.across(0)
    lay_out(1, grads, dy_ref, dt)

    def events(poll):
        if poll == 2:
            gather_ff.spread(-1, 1)
        elif poll == 3:
            scatter.after_core(0)
        elif poll == 4:
            gather_ff.spread(-2, 2)
        elif poll == 5:
            gather_ff.forward(-1, 1)
        elif poll == 6:
            gather_ff.spread(-3, 3)
            scatter.after_core(1)
        elif poll == 7:
            gather_ff.forward(-2, 2)
            scatter.after_first(0)
        elif poll == 8:
            gather_ff.across(-1, 1)
        elif poll == 9:
            gather_ff.forward(-3, 3)
            scatter.after_core(2)
            scatter.after_first(1)
            scatter.after_second(0)
        elif poll == 10:
            gather_ff.across(-2, 2)
        elif poll == 11:
            gather_ff.across(-3, 3)
            scatter.after_second(1)
            scatter.after_first(2)
        for k, strip in strips[max(0, poll - 3):max(0, poll - 2)]:
            back_copy(k, strip).start()

    def backward_step(step, carry):
        chunk = at.target(step)

        def store(cols, value):
            split = (2, 2, 2, shard, cols.stop - cols.start)
            value = value.reshape(split)

            @pl.when(step < count - 1)
            def _():
                g_buf[step, 0, :, :, :, :, cols] = value

            @pl.when(step == count - 1)
            def _():
                g_last[0, 0, :, :, :, :, cols] = value

        def ready(head):
            p_read(step, head).wait()
            if head < 2:
                p_read(step, head + 1).start()
            else:
                @pl.when(step + 1 < count)
                def _():
                    p_read(step + 1, 0).start()
            return p_buf.at[lax.rem(step + head, 2)]

        def poll(head):
            for which in range(count):
                @pl.when(step == which)
                def _():
                    events(3 * which + head)

        backward_chunk(
            weights_of(chunk), gains[...], dy_ref, xt, dt, raw, d_raw,
            qk_all.at[chunk], v_all.at[chunk], stats.at[chunk], att.at[chunk], total, g_gains,
            ready, store, poll,
        )

        @pl.when(step < count - 1)
        def _():
            scatter.start(step)

        return carry

    lax.fori_loop(0, count, backward_step, 0)
    store_gain(g_gains, total[...], x_ref[...], norm_gain[...])
    value = total[...].astype(BF16)
    for k, out in enumerate((out0, out1, out2, out3)):
        out[:PIECE] = nn(pt[k], value).astype(BF16)
    scatter.after_second(2)
    gather_ff.last()
    for k, strip in strips:
        back_copy(k, strip).wait_recv()

    gather.wait_send()
    gather_ff.wait_send()
    for k, strip in strips:
        back_copy(k, strip).wait_send()
    for k in range(1, count):
        for kind in range(2):
            row_copy(kind, k).wait_send()
    for step in range(count - 1):
        scatter.wait_send(step)


def place_rows(me, part, ids, pt, feat_q, feat_k):
    mp = ids.shape[1]
    total = mp * part
    numbers = ids[me]
    start = jnp.zeros((1, 1), jnp.int32)
    for image in range(IMAGES):
        count = jnp.sum((numbers == image).astype(F32), axis=(0, 1), keepdims=True)
        ahead = jnp.sum(
            ((numbers >= 0) & (numbers < image)).astype(F32), axis=(0, 1), keepdims=True
        )
        start = start + jnp.where(count == MOST, ahead, 0.0).astype(jnp.int32)
    line = source_of(iota((1, ROWS), 1), start, total)
    feats = 0.0
    for k in range(mp):
        chunk = lax.rem(me - k + mp, mp)
        offset = iota((PIECE, 1), 0)
        pos = jnp.where(offset < part, chunk * part + offset, -2)
        pick = (line == pos).astype(F32).astype(BF16)
        pt[k] = pick
        marks = (iota((128, 1), 0) - HD == ids[me, pl.ds(chunk, 1), :]).astype(F32)
        feats = feats + nn(marks.astype(BF16), pick)
    feats = feats.T
    lane = iota((1, 128), 1)
    feat_q[...] = (feats * 128.0).astype(BF16)
    marked = (lane >= HD) & (lane < HD + IMAGES)
    feat_k[...] = jnp.where(marked, (feats - 1.0) * 256.0, 0.0).astype(BF16)


def front_call(tokens, cotangent, ids, gains, norm_gain, w_attn, w_feed):
    count, part, width = tokens.shape
    shard = w_attn.shape[0]
    vmem = pl.BlockSpec(memory_space=pltpu.VMEM)
    hbm = pl.BlockSpec(memory_space=pl.ANY)
    rows = jax.ShapeDtypeStruct((count, PIECE, width), BF16)
    return pl.pallas_call(
        front_kernel,
        in_specs=[vmem] * 6 + [hbm],
        out_specs=[vmem] * 7 + [hbm] + [vmem] * 3 + [hbm],
        out_shape=[rows, rows, jax.ShapeDtypeStruct((count, EARLY, width), BF16)]
        + [jax.ShapeDtypeStruct((2 * PIECE - EARLY, width), BF16)] * 4
        + [
            jax.ShapeDtypeStruct((count, 2, 2, 2, 2, shard, width), BF16),
            jax.ShapeDtypeStruct((1, 1, 2, 2, 2, shard, width), BF16),
            jax.ShapeDtypeStruct((count - 1, 1, shard, width), BF16),
            jax.ShapeDtypeStruct((8, 128), F32),
            jax.ShapeDtypeStruct((count, 3, ROWS, BIG), BF16),
        ],
        scratch_shapes=[
            pltpu.VMEM((count - 1, 2, PIECE, width), BF16),
            pltpu.VMEM((count, 2, 2, 2, shard, width), BF16),
            pltpu.VMEM((count - 1, 1, 2, 2, 2, shard, width), BF16),
            pltpu.VMEM((count - 1, 1, 2, 2, shard, width), BF16),
            pltpu.VMEM((count - 1, 1, 2, shard, width), BF16),
            pltpu.VMEM((ROWS, width), BF16),
            pltpu.VMEM((ROWS, width), BF16),
            pltpu.VMEM((width, ROWS), BF16),
            pltpu.VMEM((width, ROWS), BF16),
            pltpu.VMEM((ROWS, 128), BF16),
            pltpu.VMEM((ROWS, 128), BF16),
            pltpu.VMEM((count, PIECE, ROWS), BF16),
            pltpu.VMEM((ROWS, 640), F32),
            pltpu.VMEM((ROWS, 640), BF16),
            pltpu.VMEM((2, ROWS, BIG), BF16),
            pltpu.VMEM((count, 3, ROWS, 128), BF16),
            pltpu.VMEM((count, 3, ROWS, 128), BF16),
            pltpu.VMEM((count, ROWS, 128), F32),
            pltpu.VMEM((count, ROWS, 256), BF16),
            pltpu.VMEM((ROWS, width), F32),
            pltpu.SemaphoreType.DMA((2, count - 1)),
            pltpu.SemaphoreType.DMA((2, count - 1)),
            pltpu.SemaphoreType.DMA((count - 1, EARLY // STRIP)),
            pltpu.SemaphoreType.DMA((count - 1, EARLY // STRIP)),
            pltpu.SemaphoreType.DMA((9, count)),
            pltpu.SemaphoreType.DMA((8, count)),
            pltpu.SemaphoreType.DMA((9, count)),
            pltpu.SemaphoreType.DMA((8, count)),
            pltpu.SemaphoreType.DMA,
            pltpu.SemaphoreType.DMA((2,)),
            pltpu.SemaphoreType.DMA((2,)),
            pltpu.SemaphoreType.DMA((3, 2, count - 1)),
            pltpu.SemaphoreType.DMA((3, 2, count - 1)),
        ],
        compiler_params=pltpu.CompilerParams(
            collective_id=1, has_side_effects=True, vmem_limit_bytes=FRONT_VMEM
        ),
        name="front",
    )(tokens, cotangent, ids, gains, norm_gain, w_attn, w_feed)


def finish_kernel(
    place, tok, cot, gain, branch, d_ff, back, ret, output, input_grad
):
    part = tok.shape[1]
    x = tok[0].astype(F32)
    added = branch[0] + jnp.concatenate([back[0], ret[0, PIECE:]]).astype(F32)
    output[0] = (x + added[:part]).astype(BF16)
    d_normed = (d_ff[0] + ret[0, :PIECE].astype(F32))[:part]
    centered = x - jnp.mean(x, axis=-1, keepdims=True)
    spread = lax.rsqrt(jnp.mean(centered * centered, axis=-1, keepdims=True) + 1e-6)
    unit = centered * spread
    scaled = d_normed * gain[...]
    d_x = spread * (
        scaled
        - jnp.mean(scaled, axis=-1, keepdims=True)
        - unit * jnp.mean(scaled * unit, axis=-1, keepdims=True)
    )
    input_grad[0] = cot[0].astype(F32) + d_x


def finish_call(place, tokens, cotangent, gain, branch, d_ff, back, returned):
    count, part, width = tokens.shape
    block = pl.BlockSpec(
        (1, part, width), lambda k, place: (lax.rem(place[0] + k, count), 0, 0)
    )
    padded = pl.BlockSpec((1, PIECE, width), lambda k, place: (k, 0, 0))
    piece = pl.BlockSpec((1, 2 * PIECE - EARLY, width), lambda k, place: (k, 0, 0))
    early = pl.BlockSpec((1, EARLY, width), lambda k, place: (k, 0, 0))
    line = pl.BlockSpec((1, width), lambda k, place: (0, 0))
    return pl.pallas_call(
        finish_kernel,
        grid_spec=pltpu.PrefetchScalarGridSpec(
            num_scalar_prefetch=1,
            grid=(count,),
            in_specs=[block, block, line, padded, padded, early, piece],
            out_specs=[block, block],
        ),
        out_shape=[
            jax.ShapeDtypeStruct(tokens.shape, BF16),
            jax.ShapeDtypeStruct(tokens.shape, F32),
        ],
        compiler_params=pltpu.CompilerParams(vmem_limit_bytes=VMEM),
        name="finish",
    )(place, tokens, cotangent, gain, branch, d_ff, back, returned)


def pack_attention(w_qkv, w_proj):
    rows, wide = w_qkv.shape[1:]
    heads = wide // HD
    qk = w_qkv[:2].reshape(2, rows, heads, HD).transpose(1, 2, 0, 3).reshape(rows, 2 * wide)
    return jnp.concatenate([qk, w_qkv[2], w_proj.T], axis=1)


def unpack_attention(grad, wide):
    rows = grad.shape[0]
    heads = wide // HD
    qk = grad[:, :2 * wide].reshape(rows, heads, 2, HD).transpose(2, 0, 1, 3)
    qk = qk.reshape(2, rows, wide)
    g_qkv = jnp.concatenate([qk, grad[None, :, 2 * wide:3 * wide]], axis=0)
    return g_qkv, grad[:, 3 * wide:].T


def body(
    dp, mp, tokens, w_qkv, w_up, w_proj, w_down, norm_gain, query_gain, key_gain, image_ids, cotangent
):
    micro, seqs, part, width = tokens.shape
    count = micro * seqs
    shard = w_up.shape[0]
    me = lax.axis_index("mp")
    place = me.astype(jnp.int32)[None]
    both = ("mp", "dp")
    tok = tokens.reshape(count, part, width)
    cot = cotangent.reshape(count, part, width)
    gain = norm_gain.reshape(1, width)
    ids = image_ids.reshape(count, mp, part)
    ids = jnp.pad(ids, ((0, 0), (0, 0), (0, PIECE - part)), constant_values=-1)
    gains = jnp.concatenate([query_gain, key_gain]).reshape(1, 2 * HD)
    w_attn = pack_attention(w_qkv, w_proj)
    w_ff = jnp.stack([w_up, w_down.T])

    def send_back(outs):
        return [outs[0]] + [
            lax.ppermute(out, "mp", [(i, (i - k) % mp) for i in range(mp)])
            for k, out in enumerate(outs[1:], 1)
        ]

    if (dp, mp) == (8, 4):
        normed, grads, back, *outs, w_ff, g_attn, z_attn, g_gains, _ = front_call(
            tok, cot, ids, gains, gain, w_attn, w_ff
        )
        branch, d_ff, g_attn, g_up, g_down, g_gains, returned = feed_remote_call(
            normed.reshape(count * PIECE, width), grads.reshape(count * PIECE, width),
            w_ff.reshape(mp, dp, 2, shard, width), g_attn, z_attn, gain, g_gains, outs,
        )
    else:
        w_attn = lax.all_gather(w_attn, both).reshape(mp, width, width)
        w_ff = lax.all_gather(w_ff, both).reshape(mp, dp, 2, shard, width)
        normed, grads, *sends = norm_call(place, tok, cot, gain)
        received = [
            lax.ppermute(send, "mp", [(i, (i + k) % mp) for i in range(mp)])
            for k, send in enumerate(sends, 1)
        ]
        *outs, g_attn, g_gains = attention_call(
            place, part, normed, grads, received, ids, gains, gain, w_attn
        )
        outs = send_back(outs)
        back = jnp.stack([out[1, :EARLY] for out in outs])
        returned = jnp.stack([jnp.concatenate([out[0], out[1, EARLY:]]) for out in outs])
        flat_normed = normed.reshape(count * PIECE, width)
        branch, d_ff, g_up, g_down = feed_call(
            flat_normed, grads.reshape(count * PIECE, width),
            w_ff[:, :, 0].reshape(mp, width, width), w_ff[:, :, 1].reshape(mp, width, width),
        )
        g_attn, g_up, g_down = (
            lax.psum_scatter(
                grad.reshape(-1, shard, width), both, scatter_dimension=0
            ).astype(F32)
            for grad in (g_attn, g_up, g_down)
        )
        own = jnp.sum(d_ff * flat_normed.astype(F32), axis=0) / norm_gain
        g_gains = g_gains.at[:width // 128].add(own.reshape(-1, 128))
        g_gains = lax.psum(g_gains, both)
    output, input_grad = finish_call(
        place, tok, cot, gain,
        branch.reshape(count, PIECE, width), d_ff.reshape(count, PIECE, width), back, returned,
    )
    g_qkv, g_proj = unpack_attention(g_attn, w_qkv.shape[2])
    g_norm = g_gains[:width // 128].reshape(width)
    g_gains = g_gains[6]
    return (
        output.reshape(tokens.shape),
        input_grad.reshape(tokens.shape),
        g_qkv,
        g_up,
        g_proj,
        g_down.T,
        g_norm,
        g_gains[:HD],
        g_gains[HD:],
    )


def solution(mesh):
    rows = P(None, "dp", "mp", None)
    weights = (P(None, "dp", "mp"), P("dp", "mp"), P("mp", "dp"), P("mp", "dp"))
    gains = (P(), P(), P())
    return jax.shard_map(
        functools.partial(body, mesh.shape["dp"], mesh.shape["mp"]),
        mesh=mesh,
        in_specs=(rows,) + weights + gains + (P(None, "dp", None), rows),
        out_specs=(rows, rows) + weights + gains,
        check_vma=False,
    )
```

```python
import functools

import jax
import jax.numpy as jnp
from jax import lax
from jax.experimental import pallas as pl
from jax.experimental.pallas import tpu as pltpu
from jax.sharding import PartitionSpec as P

HD = 64
MOST = 709
IMAGES = 8
STRIP = 48
EARLY = 144
PIECE = 240
BIG = 768
REST = 256
ROWS = BIG + REST
VMEM = 60 * 1024 * 1024
FRONT_VMEM = 63 * 1024 * 1024
F32 = jnp.float32
BF16 = jnp.bfloat16


def nn(left, right):
    return lax.dot_general(left, right, (((1,), (0,)), ((), ())), preferred_element_type=F32)


def nt(left, right):
    return lax.dot_general(left, right, (((1,), (1,)), ((), ())), preferred_element_type=F32)


def norm_kernel(place, tok, cot, gain, normed, grads, send1, send2, send3):
    step = pl.program_id(0)
    part = tok.shape[1]
    x = tok[0].astype(F32)
    centered = x - jnp.mean(x, axis=-1, keepdims=True)
    spread = lax.rsqrt(jnp.mean(centered * centered, axis=-1, keepdims=True) + 1e-6)
    value = (centered * spread * gain[...]).astype(BF16)
    normed[...] = jnp.zeros_like(normed)
    grads[...] = jnp.zeros_like(grads)
    normed[0, :part] = value
    grads[0, :part] = cot[0]
    for index, send in ((1, send1), (2, send2), (3, send3)):

        @pl.when(step == index)
        def _():
            send[0] = normed[0]
            send[1] = grads[0]


def norm_call(place, tokens, cotangent, gain):
    count, part, width = tokens.shape
    block = lambda k, place: (lax.rem(place[0] + k, count), 0, 0)
    fixed = lambda k, place: (0, 0, 0)
    return pl.pallas_call(
        norm_kernel,
        grid_spec=pltpu.PrefetchScalarGridSpec(
            num_scalar_prefetch=1,
            grid=(count,),
            in_specs=[
                pl.BlockSpec((1, part, width), block),
                pl.BlockSpec((1, part, width), block),
                pl.BlockSpec((1, width), lambda k, place: (0, 0)),
            ],
            out_specs=[pl.BlockSpec((1, PIECE, width), lambda k, place: (k, 0, 0))] * 2
            + [pl.BlockSpec((2, PIECE, width), fixed)] * 3,
        ),
        out_shape=[jax.ShapeDtypeStruct((count, PIECE, width), BF16)] * 2
        + [jax.ShapeDtypeStruct((2, PIECE, width), BF16)] * 3,
        compiler_params=pltpu.CompilerParams(vmem_limit_bytes=VMEM),
        name="norm_rows",
    )(place, tokens, cotangent, gain)


def feed_kernel(normed, grads, w_up, w_down, branch, d_normed, g_up, g_down, xt, dt):
    step = pl.program_id(0)
    x = normed[...]
    dy = grads[...]

    @pl.when(step == 0)
    def _():
        xt[...] = x.T
        dt[...] = dy.T

    up = nn(x, w_up[0])
    value, slope = gelu_parts(up)
    hidden = value.astype(BF16)
    d_up = (nn(dy, w_down[0]) * slope).astype(BF16)
    g_up[0] = nn(xt[...], d_up).astype(BF16)
    g_down[0] = nn(dt[...], hidden).astype(BF16)
    out = nt(hidden, w_down[0])
    back = nt(d_up, w_up[0])

    @pl.when(step == 0)
    def _():
        branch[...] = out
        d_normed[...] = back

    @pl.when(step > 0)
    def _():
        branch[...] += out
        d_normed[...] += back


def feed_call(normed, grads, w_up, w_down):
    rows, width = normed.shape
    chunks, _, hidden = w_up.shape
    whole = pl.BlockSpec((rows, width), lambda m: (0, 0))
    chunk = pl.BlockSpec((1, width, hidden), lambda m: (m, 0, 0))
    return pl.pallas_call(
        feed_kernel,
        grid=(chunks,),
        in_specs=[whole, whole, chunk, chunk],
        out_specs=[whole, whole, chunk, chunk],
        out_shape=[jax.ShapeDtypeStruct((rows, width), F32)] * 2
        + [jax.ShapeDtypeStruct(w_up.shape, BF16)] * 2,
        scratch_shapes=[pltpu.VMEM((width, rows), BF16)] * 2,
        compiler_params=pltpu.CompilerParams(vmem_limit_bytes=VMEM),
        cost_estimate=pl.CostEstimate(
            flops=12 * rows * width * hidden * chunks,
            bytes_accessed=4 * chunks * width * hidden * 2,
            transcendentals=rows * hidden * chunks,
        ),
        name="feed_forward",
    )(normed, grads, w_up, w_down)


class Place:
    def __init__(self, planes):
        d = lax.axis_index("dp")
        self.z = lax.axis_index("mp")
        self.d, self.planes = d, planes
        self.core, self.x, self.y = d % 2, (d // 2) % 2, d // 4
        self.sibling = d + 1 - 2 * self.core
        self.beside = d + 2 - 4 * self.x
        self.above = d + 4 - 8 * self.y

    def target(self, step):
        z, high = self.z, self.z // 2
        near = jnp.where(step == 2, 1 - z + 4 * high, z)
        return jnp.where(step == 0, 3 - 3 * high, jnp.where(step == 1, 2 - high, near))

    def along(self, k):
        return lax.rem(self.z + k + self.planes, self.planes)

    def copy(self, src, dst, send, recv, dp=None, mp=None):
        return pltpu.make_async_remote_copy(
            src_ref=src, dst_ref=dst, send_sem=send, recv_sem=recv,
            device_id={"dp": self.d if dp is None else dp, "mp": self.z if mp is None else mp},
            device_id_type=pl.DeviceIdType.MESH,
        )

    def greet(self):
        barrier = pltpu.get_barrier_semaphore()
        for other in (self.sibling, self.beside, self.above):
            pl.semaphore_signal(barrier, 1, device_id={"dp": other, "mp": self.z},
                                device_id_type=pl.DeviceIdType.MESH)
        for k in range(1, self.planes):
            pl.semaphore_signal(barrier, 1, device_id={"dp": self.d, "mp": self.along(k)},
                                device_id_type=pl.DeviceIdType.MESH)
        pl.semaphore_wait(barrier, self.planes + 2)


class Scatter:
    def __init__(self, at, items, src, got_core, got_first, got_second, send_sem, recv_sem):
        self.at, self.items, self.src = at, items, src
        self.got_core, self.got_first, self.got_second = got_core, got_first, got_second
        self.send_sem, self.recv_sem = send_sem, recv_sem

    def copy(self, stage, step, item):
        at = self.at
        kind, cols, x_first = self.items[item]
        if stage == 0:
            src = self.src.at[step, kind, :, :, 1 - at.core, :, cols]
            dst = self.got_core.at[step, kind, :, :, :, cols]
            to = at.sibling
        elif stage == 1:
            if x_first:
                src = self.got_core.at[step, kind, :, 1 - at.x, :, cols]
            else:
                src = self.got_core.at[step, kind, 1 - at.y, :, :, cols]
            dst = self.got_first.at[step, kind, :, :, cols]
            to = at.beside if x_first else at.above
        else:
            src = self.got_first.at[step, kind, 1 - at.y if x_first else 1 - at.x, :, cols]
            dst = self.got_second.at[step, kind, :, cols]
            to = at.above if x_first else at.beside
        sem = (stage, item, step)
        return at.copy(src, dst, self.send_sem.at[sem], self.recv_sem.at[sem], dp=to)

    def start(self, step):
        for item in range(len(self.items)):
            self.copy(0, step, item).start()

    def after_core(self, step):
        for item, (kind, cols, _) in enumerate(self.items):
            self.copy(0, step, item).wait_recv()
            for row in ((0, 0), (0, 1), (1, 0), (1, 1)):
                own = self.src[(step, kind, *row, self.at.core, slice(None), cols)]
                to = (step, kind, *row, slice(None), cols)
                total = own.astype(F32) + self.got_core[to].astype(F32)
                self.got_core[to] = total.astype(BF16)
            self.copy(1, step, item).start()

    def after_first(self, step):
        for item, (kind, cols, x_first) in enumerate(self.items):
            self.copy(1, step, item).wait_recv()
            for row in range(2):
                if x_first:
                    own = self.got_core[step, kind, row, self.at.x, :, cols]
                else:
                    own = self.got_core[step, kind, self.at.y, row, :, cols]
                total = own.astype(F32) + self.got_first[step, kind, row, :, cols].astype(F32)
                self.got_first[step, kind, row, :, cols] = total.astype(BF16)
            self.copy(2, step, item).start()

    def total(self, step, item):
        kind, cols, x_first = self.items[item]
        self.copy(2, step, item).wait_recv()
        own = self.got_first[step, kind, self.at.y if x_first else self.at.x, :, cols]
        return own.astype(F32) + self.got_second[step, kind, :, cols].astype(F32)

    def after_second(self, step):
        for item, (kind, cols, _) in enumerate(self.items):
            self.got_second[step, kind, :, cols] = self.total(step, item).astype(BF16)

    def wait_send(self, step):
        for item in range(len(self.items)):
            for stage in range(3):
                self.copy(stage, step, item).wait_send()


class Gather:
    def __init__(self, at, shard, full, send_sem, recv_sem):
        self.at, self.shard, self.full = at, shard, full
        self.send_sem, self.recv_sem = send_sem, recv_sem

    def there(self, r, does):
        plane = self.at.z + r

        @pl.when((plane >= 0) & (plane < self.at.planes))
        def _():
            does(plane)

    def piece(self, plane, y=False, x=False, core=False):
        at = self.at
        return self.full.at[plane, 1 - at.y if y else at.y, 1 - at.x if x else at.x,
                            1 - at.core if core else at.core]

    def copy(self, kind, plane, src, dst=None, **to):
        return self.at.copy(
            src, src if dst is None else dst, self.send_sem.at[kind, plane],
            self.recv_sem.at[kind % 8, plane], **to
        )

    def arrived(self, kind, plane, ref):
        self.copy(kind, plane, ref, dp=self.at.sibling).wait_recv()

    def pass_on(self, kind, plane, src, act):
        z, dst = self.at.z, self.piece(plane)
        if kind == 0:
            @pl.when(z < self.at.planes - 1)
            def _():
                act(self.copy(0, plane, src, dst, mp=z + 1))
        else:
            @pl.when(z > 0)
            def _():
                act(self.copy(8, plane, src, dst, mp=z - 1))

    def start(self):
        for kind in (0, 8):
            self.pass_on(kind, self.at.z, self.shard, lambda copy: copy.start())

    def spread(self, *which):
        for r in which:
            def does(plane):
                src = self.piece(plane)
                if r:
                    self.arrived(0, plane, src)
                    self.pass_on(0 if r < 0 else 8, plane, src, lambda copy: copy.start())
                self.copy(1, plane, src, dp=self.at.beside).start()
                self.copy(2, plane, src, dp=self.at.above).start()
                self.copy(3, plane, src, dp=self.at.sibling).start()

            self.there(r, does)

    def forward(self, *which):
        at = self.at
        for r in which:
            def does(plane):
                from_x, from_y = self.piece(plane, x=True), self.piece(plane, y=True)
                self.arrived(1, plane, from_x)
                if r in (0, 1, -3):
                    self.copy(5, plane, from_x, dp=at.above).start()
                self.copy(4, plane, from_x, dp=at.sibling).start()
                self.arrived(2, plane, from_y)
                if r not in (0, 1, -3):
                    self.copy(5, plane, from_y, dp=at.beside).start()
                self.copy(6, plane, from_y, dp=at.sibling).start()

            self.there(r, does)

    def across(self, *which):
        for r in which:
            def does(plane):
                src = self.piece(plane, y=True, x=True)
                self.arrived(5, plane, src)
                self.copy(7, plane, src, dp=self.at.sibling).start()

            self.there(r, does)

    def last(self):
        for plane in range(self.at.planes):
            self.arrived(3, plane, self.piece(plane, core=True))
            self.arrived(4, plane, self.piece(plane, x=True, core=True))
            self.arrived(6, plane, self.piece(plane, y=True, core=True))
            self.arrived(7, plane, self.piece(plane, y=True, x=True, core=True))

    def wait_send(self):
        for r in range(1 - self.at.planes, self.at.planes):
            def does(plane):
                src = self.piece(plane)
                if r <= 0:
                    self.pass_on(0, plane, src, lambda copy: copy.wait_send())
                if r >= 0:
                    self.pass_on(8, plane, src, lambda copy: copy.wait_send())
                for kind in range(1, 8):
                    self.copy(kind, plane, src, dp=self.at.sibling).wait_send()

            self.there(r, does)


class Along:
    def __init__(self, at, parts, got, send_sem, recv_sem):
        self.at, self.parts, self.got = at, parts, got
        self.send_sem, self.recv_sem = send_sem, recv_sem
        self.inner = (at.z == 1) | (at.z == 2)

    def copy(self, step, kind):
        at, inner = self.at, self.inner
        side = 1 - 2 * (at.z // 2)
        to = at.z + jnp.where(inner & (step == 2), -side, side)
        slot = jnp.where(inner, 2 + 2 * step - 3 * (step // 2), step + step // 2)
        return at.copy(self.parts.at[step, kind], self.got.at[kind, slot],
                       self.send_sem.at[kind, step], self.recv_sem.at[kind, slot], mp=to)

    def arrived(self, kind, slot):
        ref = self.got.at[kind, slot]
        self.at.copy(ref, ref, self.send_sem.at[kind, 0], self.recv_sem.at[kind, slot],
                     mp=self.at.along(1)).wait_recv()

    def send_outer(self, step):
        @pl.when(jnp.logical_not(self.inner))
        def _():
            for kind in range(self.got.shape[0]):
                self.copy(step, kind).start()

    def send_inner(self, step):
        @pl.when(self.inner)
        def _():
            for kind in range(self.got.shape[0]):
                self.arrived(kind, step)
                own = self.parts[step, kind].astype(F32)
                total = own + self.got[kind, step].astype(F32)
                self.parts[step, kind] = total.astype(BF16)
                self.copy(step, kind).start()

    def add(self, kind, out):
        self.arrived(kind, 3)
        out[...] += self.got[kind, 3].astype(F32)

        @pl.when(self.inner)
        def _():
            self.arrived(kind, 4)
            out[...] += self.got[kind, 4].astype(F32)

    def wait_send(self, step):
        for kind in range(self.got.shape[0]):
            self.copy(step, kind).wait_send()


def gelu_parts(up):
    inner = 0.7978845608028654 * (up + 0.044715 * up * up * up)
    th = jnp.tanh(inner)
    half = 0.5 * (1.0 + th)
    slope = half + 0.5 * up * (1.0 - th * th) * (
        0.7978845608028654 * (1.0 + 3 * 0.044715 * up * up)
    )
    return up * half, slope


def halves(width):
    return (0, slice(0, width // 2), True), (0, slice(width // 2, width), False)


def feed_remote_kernel(
    x_ref, dy_ref, w_hbm, g_attn, z_attn, gain, gains_in, back0, back1, back2, back3,
    branch, d_normed, out_attn, out_up, out_down, out_gains, returned,
    xt, dt, w_buf, hidden, d_up, g_ff, ff_core, ff_first, ff_second, at_core, at_first, at_second, got_z,
    parts, got_za, sums, got_sums, z_sums,
    w_sem, ff_send, ff_recv, at_send, at_recv, z_send, z_recv, za_send, za_recv,
    sum_send, sum_recv, back_send, back_recv, own_sem,
):
    width = x_ref.shape[1]
    steps, shard = w_hbm.shape[0], w_hbm.shape[3]
    at = Place(steps)
    at.greet()
    attn = Scatter(at, halves(width), g_attn, at_core, at_first, at_second, at_send, at_recv)
    both = (0, slice(0, width), True), (1, slice(0, width), False)
    feed = Scatter(at, both, g_ff, ff_core, ff_first, ff_second, ff_send, ff_recv)
    along = Along(at, ff_second, got_z, z_send, z_recv)
    along_attn = Along(at, parts, got_za, za_send, za_recv)
    last = steps - 1

    def w_copy(step, kind):
        slot = lax.rem(step, 2)
        return pltpu.make_async_copy(
            w_hbm.at[at.target(step), :, kind], w_buf.at[slot, kind], w_sem.at[slot, kind]
        )

    strips = [(k, strip) for strip in range(returned.shape[1] // STRIP) for k in (1, 3, 2)]
    first = len(strips) - 4 * steps + 1

    def back_copy(k, strip):
        rows, sem = pl.ds(strip * STRIP, STRIP), (k - 1, strip)
        return at.copy((back0, back1, back2, back3)[k].at[rows], returned.at[k, rows],
                       back_send.at[sem], back_recv.at[sem], mp=at.along(-k))

    own_back = pltpu.make_async_copy(back0, returned.at[0], own_sem)
    own_back.start()
    attn.start(0)
    for kind in range(2):
        w_copy(0, kind).start()
    for k, strip in strips[:first]:
        back_copy(k, strip).start()
    parts[...] = z_attn[...]
    for step in range(last):
        along_attn.send_outer(step)
    xt[...] = x_ref[...].T
    dt[...] = dy_ref[...].T
    branch[...] = jnp.zeros_like(branch)
    d_normed[...] = jnp.zeros_like(d_normed)

    def one_step(step, carry):
        for kind in range(2):
            w_copy(step, kind).wait()

        @pl.when(step + 1 < steps)
        def _():
            for kind in range(2):
                w_copy(step + 1, kind).start()

        slot = lax.rem(step, 2)
        split = (2, 2, 2, shard, width)

        def weights(kind):
            return w_buf[slot, kind].reshape(width, width)

        value, slope = gelu_parts(nn(x_ref[...], weights(0)))
        hidden[...] = value.astype(BF16)
        d_up[...] = (nn(dy_ref[...], weights(1)) * slope).astype(BF16)

        for which in range(steps):
            @pl.when(step == which)
            def _():
                for k, strip in strips[first + 4 * which:first + 4 * which + 4]:
                    back_copy(k, strip).start()

        @pl.when(step == 0)
        def _():
            attn.after_core(0)

        @pl.when(step == 2)
        def _():
            along_attn.send_inner(0)

        @pl.when(step == 3)
        def _():
            along_attn.send_inner(1)
            along_attn.send_inner(2)

        g_ff[step, 0] = nn(xt[...], d_up[...]).astype(BF16).reshape(split)
        g_ff[step, 1] = nn(dt[...], hidden[...]).astype(BF16).reshape(split)
        feed.start(step)

        @pl.when(step >= 1)
        def _():
            feed.after_first(step - 1)

        branch[...] += nt(hidden[...], weights(1))
        d_normed[...] += nt(d_up[...], weights(0))
        feed.after_core(step)

        @pl.when(step == 0)
        def _():
            attn.after_first(0)

        @pl.when(step >= 1)
        def _():
            feed.after_second(step - 1)
            along.send_outer(step - 1)

        return carry

    lax.fori_loop(0, steps, one_step, 0)

    sums[0] = gains_in[...]
    store_gain(sums.at[0], d_normed[...], x_ref[...], gain[...])

    def sum_copy(stage):
        to = (at.sibling, at.beside, at.above)[stage]
        return at.copy(sums.at[stage], got_sums.at[stage], sum_send.at[stage],
                       sum_recv.at[stage], dp=to)

    def sum_z_copy(k):
        return at.copy(sums.at[3], z_sums.at[at.z], sum_send.at[2 + k], sum_recv.at[2 + k],
                       mp=at.along(k))

    def next_sum(stage):
        sum_copy(stage).wait_recv()
        sums[stage + 1] = sums[stage] + got_sums[stage]

    sum_copy(0).start()
    for item in range(2):
        cols = attn.items[item][1]
        out_attn[:, cols] = attn.total(0, item)
    next_sum(0)
    sum_copy(1).start()
    along.send_inner(0)
    along.send_inner(1)
    next_sum(1)
    sum_copy(2).start()
    feed.after_first(last)
    along.send_inner(2)
    next_sum(2)
    for k in range(1, steps):
        sum_z_copy(k).start()
    z_sums[at.z] = sums[3]
    along_attn.add(0, out_attn)
    for kind, out in enumerate((out_up, out_down)):
        out[...] = feed.total(last, kind)
        along.add(kind, out)
    for k in range(1, steps):
        sum_z_copy(k).wait_recv()
    total = z_sums[0]
    for k in range(1, steps):
        total = total + z_sums[k]
    out_gains[...] = total

    own_back.wait()
    for k, strip in strips:
        back_copy(k, strip).wait_recv()
        back_copy(k, strip).wait_send()
    attn.wait_send(0)
    for step in range(steps):
        feed.wait_send(step)
    for step in range(last):
        along.wait_send(step)
        along_attn.wait_send(step)
    for stage in range(3):
        sum_copy(stage).wait_send()
    for k in range(1, steps):
        sum_z_copy(k).wait_send()


def feed_remote_call(normed, grads, w_ff, g_attn, z_attn, gain, gains, backs):
    rows, width = normed.shape
    steps, _, _, shard, _ = w_ff.shape
    vmem = pl.BlockSpec(memory_space=pltpu.VMEM)
    hbm = pl.BlockSpec(memory_space=pl.ANY)
    return pl.pallas_call(
        feed_remote_kernel,
        in_specs=[vmem, vmem, hbm] + [vmem] * 4 + [hbm] * 4,
        out_specs=[vmem] * 6 + [hbm],
        out_shape=[jax.ShapeDtypeStruct((rows, width), F32)] * 2
        + [jax.ShapeDtypeStruct((shard, width), F32)] * 3
        + [jax.ShapeDtypeStruct((8, 128), F32)]
        + [jax.ShapeDtypeStruct((steps,) + backs[0].shape, BF16)],
        scratch_shapes=[
            pltpu.VMEM((width, rows), BF16),
            pltpu.VMEM((width, rows), BF16),
            pltpu.VMEM((2, 2, 8, shard, width), BF16),
            pltpu.VMEM((rows, width), BF16),
            pltpu.VMEM((rows, width), BF16),
            pltpu.VMEM((steps, 2, 2, 2, 2, shard, width), BF16),
            pltpu.VMEM((steps, 2, 2, 2, shard, width), BF16),
            pltpu.VMEM((steps, 2, 2, shard, width), BF16),
            pltpu.VMEM((steps, 2, shard, width), BF16),
            pltpu.VMEM((1, 1, 2, 2, shard, width), BF16),
            pltpu.VMEM((1, 1, 2, shard, width), BF16),
            pltpu.VMEM((1, 1, shard, width), BF16),
            pltpu.VMEM((2, 5, shard, width), BF16),
            pltpu.VMEM((steps - 1, 1, shard, width), BF16),
            pltpu.VMEM((1, 5, shard, width), BF16),
            pltpu.VMEM((4, 8, 128), F32),
            pltpu.VMEM((3, 8, 128), F32),
            pltpu.VMEM((steps, 8, 128), F32),
            pltpu.SemaphoreType.DMA((2, 2)),
            pltpu.SemaphoreType.DMA((3, 2, steps)),
            pltpu.SemaphoreType.DMA((3, 2, steps)),
            pltpu.SemaphoreType.DMA((3, 2, 1)),
            pltpu.SemaphoreType.DMA((3, 2, 1)),
            pltpu.SemaphoreType.DMA((2, steps - 1)),
            pltpu.SemaphoreType.DMA((2, 5)),
            pltpu.SemaphoreType.DMA((1, steps - 1)),
            pltpu.SemaphoreType.DMA((1, 5)),
            pltpu.SemaphoreType.DMA((6,)),
            pltpu.SemaphoreType.DMA((6,)),
            pltpu.SemaphoreType.DMA((steps - 1, backs[0].shape[0] // STRIP)),
            pltpu.SemaphoreType.DMA((steps - 1, backs[0].shape[0] // STRIP)),
            pltpu.SemaphoreType.DMA,
        ],
        compiler_params=pltpu.CompilerParams(
            collective_id=0, has_side_effects=True, vmem_limit_bytes=VMEM
        ),
        cost_estimate=pl.CostEstimate(
            flops=12 * rows * width * width * steps,
            bytes_accessed=4 * steps * width * width * 2,
            transcendentals=rows * width * steps,
        ),
        name="feed_forward_scatter",
    )(normed, grads, w_ff, g_attn, z_attn, gain, gains, *backs)


def iota(shape, axis):
    return lax.broadcasted_iota(jnp.int32, shape, axis)


def source_of(index, start, total):
    rest = index - BIG
    other = jnp.where(rest < start, rest, rest + MOST)
    held = jnp.where(index < MOST, start + index, -1)
    return jnp.where((rest >= 0) & (rest < total - MOST), other, held)


def store_gain(out, d_normed, normed, gain):
    total = jnp.sum(d_normed * normed.astype(F32), axis=0, keepdims=True) / gain
    for row in range(total.shape[1] // 128):
        out[row:row + 1] += total[:, 128 * row:128 * row + 128]


def prepare(
    me, part, ids, pieces, x_ref, dy_ref, xt, dt, feat_q, feat_k, pt, d_normed, branch, g_gains
):
    mp = ids.shape[1]
    total = mp * part
    numbers = ids[me]
    start = jnp.zeros((1, 1), jnp.int32)
    for image in range(IMAGES):
        count = jnp.sum((numbers == image).astype(F32), axis=(0, 1), keepdims=True)
        ahead = jnp.sum(
            ((numbers >= 0) & (numbers < image)).astype(F32), axis=(0, 1), keepdims=True
        )
        start = start + jnp.where(count == MOST, ahead, 0.0).astype(jnp.int32)
    column = source_of(iota((ROWS, 1), 0), start, total)
    line = source_of(iota((1, ROWS), 1), start, total)
    x_sum, dy_sum, feats = 0.0, 0.0, 0.0
    for k, piece in enumerate(pieces):
        chunk = lax.rem(me - k + mp, mp)
        offset = iota((1, PIECE), 1)
        pos = jnp.where(offset < part, chunk * part + offset, -2)
        pick = (column == pos).astype(F32).astype(BF16)
        offset = iota((PIECE, 1), 0)
        pos = jnp.where(offset < part, chunk * part + offset, -2)
        pt[k] = (line == pos).astype(F32).astype(BF16)
        x_sum = x_sum + nn(pick, piece[0][...])
        dy_sum = dy_sum + nn(pick, piece[1][...])
        marks = (iota((128, 1), 0) - HD == ids[me, pl.ds(chunk, 1), :]).astype(F32)
        feats = feats + nt(pick, marks.astype(BF16))
    x = x_sum.astype(BF16)
    dy = dy_sum.astype(BF16)
    x_ref[...] = x
    dy_ref[...] = dy
    xt[...] = x.T
    dt[...] = dy.T
    lane = iota((1, 128), 1)
    feat_q[...] = (feats * 128.0).astype(BF16)
    marked = (lane >= HD) & (lane < HD + IMAGES)
    feat_k[...] = jnp.where(marked, (feats - 1.0) * 256.0, 0.0).astype(BF16)
    d_normed[...] = jnp.zeros_like(d_normed)
    branch[...] = jnp.zeros_like(branch)
    g_gains[...] = jnp.zeros_like(g_gains)


def attention_chunk(
    weights, gain, x_ref, dy_ref, xt, dt, feat_q, feat_k, raw, d_raw, d_att, att,
    d_normed, branch, g_gains, store, poll,
):
    raw[...] = nn(x_ref[...], weights(slice(0, 640)))
    d_att[...] = nn(dy_ref[...], weights(slice(512, 768)))
    lane = iota((1, 128), 1)
    low = lane < HD
    same = (iota((128, 128), 0) // HD == iota((128, 128), 1) // HD).astype(F32)
    mean_of = (same * (1.0 / HD)).astype(BF16)

    def half_mean(value):
        return nn(value.astype(BF16), mean_of)

    d_gain = jnp.zeros((1, 128), F32)
    for head in range(3):
        qk = raw[:, 128 * head:128 * head + 128]
        high = qk.astype(BF16)
        mean = nn(high, mean_of) + half_mean(qk - high.astype(F32))
        centered = qk - mean
        spread = lax.rsqrt(half_mean(centered * centered) + 1e-6)
        unit = centered * spread
        rounded = (unit * gain).astype(BF16).astype(F32)
        q_aug = jnp.where(low, rounded * 0.125, feat_q[...].astype(F32)).astype(BF16)
        k_aug = jnp.where(low, pltpu.roll(rounded, HD, 1), feat_k[...].astype(F32)).astype(BF16)
        v_tile = 384 + 128 * (head // 2)
        v = raw[:, v_tile:v_tile + 128]
        if head == 1:
            v = pltpu.roll(v, HD, 1)
        one = ((lane == HD) | (lane == HD + 1)).astype(F32)
        v_aug = jnp.where(low, v, one).astype(BF16)
        a_tile = 128 * ((head + 1) // 2)
        da = d_att[:, a_tile:a_tile + 128]
        if head != 1:
            da = pltpu.roll(da, HD, 1)
        q_t = q_aug.astype(F32).T.astype(BF16)
        d_queries, attended, d_keys, d_values = [], [], [], []
        for base, count in ((0, BIG), (BIG, REST)):
            keys = k_aug[base:base + count]
            values = v_aug[base:base + count]
            dk_t = jnp.zeros((128, count), F32)
            dv_t = jnp.zeros((128, count), F32)
            for row in range(base, base + count, 256):
                rows = slice(row, row + 256)
                prob = jnp.exp(nt(q_aug[rows], keys))
                prob_low = prob.astype(BF16)
                gathered = nn(prob_low, values)
                inverse = 1.0 / gathered[:, HD:HD + 1]
                out = jnp.where(low, gathered * inverse, 0.0)
                attended.append(out)
                scaled = jnp.where(low, da[rows] * inverse, 0.0).astype(BF16).astype(F32)
                dot = jnp.sum(scaled * out, axis=-1, keepdims=True)
                dot_high = dot.astype(BF16).astype(F32)
                d_aug = jnp.where(
                    lane == HD, -dot_high, jnp.where(lane == HD + 1, dot_high - dot, scaled)
                )
                d_low = d_aug.astype(BF16)
                d_score = (prob * nt(d_low, values)).astype(BF16)
                d_queries.append(nn(d_score, keys))
                dk_t = dk_t + nn(q_t[:, rows], d_score)
                dv_t = dv_t + nn(d_aug.T.astype(BF16), prob_low)
            d_keys.append(dk_t.T)
            d_values.append(dv_t.T)
        d_query = jnp.concatenate(d_queries, axis=0) * 0.125
        d_key = jnp.concatenate(d_keys, axis=0)
        d_value = jnp.concatenate(d_values, axis=0)
        attend = jnp.concatenate(attended, axis=0)
        d_qk = jnp.where(low, d_query, pltpu.roll(d_key, HD, 1))
        d_gain = d_gain + jnp.sum(d_qk * unit, axis=0, keepdims=True)
        scaled = d_qk * gain
        d_qk = spread * (scaled - half_mean(scaled) - unit * half_mean(scaled * unit))
        d_raw[:, 128 * head:128 * head + 128] = d_qk.astype(BF16)
        if head == 0:
            first_value = d_value
            att[:, 0:128] = jnp.where(low, 0.0, pltpu.roll(attend, HD, 1)).astype(BF16)
        elif head == 1:
            both = jnp.where(low, first_value, pltpu.roll(d_value, HD, 1))
            d_raw[:, 384:512] = both.astype(BF16)
            first_att = attend
        else:
            d_raw[:, 512:640] = jnp.where(low, d_value, 0.0).astype(BF16)
            both = jnp.where(low, first_att, pltpu.roll(attend, HD, 1))
            att[:, 128:256] = both.astype(BF16)
        poll(head)
    g_gains[6:7] += d_gain
    d_projected = d_raw[...]
    attended = att[...]
    d_normed[...] += nt(d_projected, weights(slice(0, 640)))
    branch[...] += nt(attended, weights(slice(512, 768)))
    left = nn(xt[...], d_projected)
    right = nn(dt[...], attended)
    store(slice(0, 512), left[:, :512].astype(BF16))
    store(slice(512, 640), (left[:, 512:] + right[:, :128]).astype(BF16))
    store(slice(640, 768), right[:, 128:].astype(BF16))


def take_back(outs, pt, x_ref, norm_gain, d_normed, branch, g_gains):
    store_gain(g_gains, d_normed[...], x_ref[...], norm_gain[...])
    d_rows = d_normed[...].astype(BF16)
    b_rows = branch[...].astype(BF16)
    for k, out in enumerate(outs):
        out[0] = nn(pt[k], d_rows).astype(BF16)
        out[1] = nn(pt[k], b_rows).astype(BF16)


def attention_kernel(
    part, place, own_x, own_dy, in1, in2, in3, ids, gains, norm_gain, weights,
    out0, out1, out2, out3, g_weights, g_gains,
    x_ref, dy_ref, xt, dt, feat_q, feat_k, pt, raw, d_raw, d_att, att, d_normed, branch,
):
    step = pl.program_id(0)

    @pl.when(step == 0)
    def _():
        pieces = [(own_x.at[0], own_dy.at[0])] + [(got.at[0], got.at[1]) for got in (in1, in2, in3)]
        prepare(place[0], part, ids, pieces, x_ref, dy_ref, xt, dt, feat_q, feat_k, pt,
                d_normed, branch, g_gains)

    def store(cols, value):
        g_weights[0, :, cols] = value

    attention_chunk(
        lambda cols: weights[0, :, cols], gains[...], x_ref, dy_ref, xt, dt, feat_q, feat_k,
        raw, d_raw, d_att, att, d_normed, branch, g_gains, store, lambda head: None,
    )

    @pl.when(step == pl.num_programs(0) - 1)
    def _():
        take_back((out0, out1, out2, out3), pt, x_ref, norm_gain, d_normed, branch, g_gains)


def attention_call(place, part, normed, grads, received, ids, gains, norm_gain, weights):
    width = normed.shape[-1]
    chunks = weights.shape[0]
    mp = ids.shape[1]
    own = pl.BlockSpec((1, PIECE, width), lambda m, place: (0, 0, 0))
    pair = pl.BlockSpec((2, PIECE, width), lambda m, place: (0, 0, 0))
    chunk = pl.BlockSpec((1, width, width), lambda m, place: (m, 0, 0))
    line = pl.BlockSpec((1, 128), lambda m, place: (0, 0))
    return pl.pallas_call(
        functools.partial(attention_kernel, part),
        grid_spec=pltpu.PrefetchScalarGridSpec(
            num_scalar_prefetch=1,
            grid=(chunks,),
            in_specs=[own, own, pair, pair, pair,
                      pl.BlockSpec(ids.shape, lambda m, place: (0, 0, 0)),
                      line, pl.BlockSpec((1, width), lambda m, place: (0, 0)), chunk],
            out_specs=[pair] * 4 + [chunk, pl.BlockSpec((8, 128), lambda m, place: (0, 0))],
            scratch_shapes=[
                pltpu.VMEM((ROWS, width), BF16),
                pltpu.VMEM((ROWS, width), BF16),
                pltpu.VMEM((width, ROWS), BF16),
                pltpu.VMEM((width, ROWS), BF16),
                pltpu.VMEM((ROWS, 128), BF16),
                pltpu.VMEM((ROWS, 128), BF16),
                pltpu.VMEM((mp, PIECE, ROWS), BF16),
                pltpu.VMEM((ROWS, 640), F32),
                pltpu.VMEM((ROWS, 640), BF16),
                pltpu.VMEM((ROWS, 256), F32),
                pltpu.VMEM((ROWS, 256), BF16),
                pltpu.VMEM((ROWS, width), F32),
                pltpu.VMEM((ROWS, width), F32),
            ],
        ),
        out_shape=[jax.ShapeDtypeStruct((2, PIECE, width), BF16)] * 4
        + [jax.ShapeDtypeStruct(weights.shape, BF16), jax.ShapeDtypeStruct((8, 128), F32)],
        compiler_params=pltpu.CompilerParams(vmem_limit_bytes=VMEM),
        cost_estimate=pl.CostEstimate(
            flops=60_000_000_000, bytes_accessed=4 * chunks * width * width,
            transcendentals=ROWS * ROWS * 12,
        ),
        name="attention",
    )(place, normed, grads, *received, ids, gains, norm_gain, weights)


def group_means():
    same = (iota((128, 128), 0) // HD == iota((128, 128), 1) // HD).astype(F32)
    return (same * (1.0 / HD)).astype(BF16)


def forward_chunk(
    weights, gain, x_ref, feat_q, feat_k, raw, qk_all, v_all, stats, att, branch, begin, spill
):
    raw[...] = nn(x_ref[...], weights(slice(0, 640)))
    lane = iota((1, 128), 1)
    low = lane < HD
    mean_of = group_means()

    def ahead(head):
        qk = raw[:, 128 * head:128 * head + 128]
        high = qk.astype(BF16)
        mean = nn(high, mean_of) + nn((qk - high.astype(F32)).astype(BF16), mean_of)
        centered = qk - mean
        spread = lax.rsqrt(nn((centered * centered).astype(BF16), mean_of) + 1e-6)
        rounded = (centered * spread * gain).astype(BF16)
        qk_all[head] = rounded
        rounded = rounded.astype(F32)
        q_aug = jnp.where(low, rounded * 0.125, feat_q[...].astype(F32)).astype(BF16)
        k_aug = jnp.where(low, pltpu.roll(rounded, HD, 1), feat_k[...].astype(F32)).astype(BF16)
        v_tile = 384 + 128 * (head // 2)
        v = raw[:, v_tile:v_tile + 128]
        if head == 1:
            v = pltpu.roll(v, HD, 1)
        v_aug = jnp.where(low, v, 1.0).astype(BF16)
        v_all[head] = v_aug
        return spread, q_aug, k_aug, v_aug

    def products(p_ref, spread, q_aug, k_aug, v_aug):
        parts = []
        for base, count in ((0, BIG), (BIG, REST)):
            keys = k_aug[base:base + count]
            values = v_aug[base:base + count]
            for row in range(base, base + count, 256):
                rows = slice(row, row + 256)
                prob = jnp.exp(nt(q_aug[rows], keys)).astype(BF16)
                p_ref[rows, :count] = prob
                parts.append(nn(prob, values))
        return spread, jnp.concatenate(parts, axis=0)

    def after(head, stat, spread, gathered):
        inverse = 1.0 / gathered
        attend = gathered * pltpu.roll(inverse, HD, 1)
        stat = jnp.where((lane == head) | (lane == HD + head), spread, stat)
        return jnp.where(lane == HD + 8 + head, inverse, stat), attend

    held = ahead(0)
    p_ref = begin(0)
    done0 = products(p_ref, *held)
    held = ahead(1)
    spill(0)
    p_ref = begin(1)
    done1 = products(p_ref, *held)
    held = ahead(2)
    stat, first = after(0, jnp.zeros((ROWS, 128), F32), *done0)
    att[:, 0:128] = jnp.where(low, 0.0, pltpu.roll(first, HD, 1)).astype(BF16)
    spill(1)
    p_ref = begin(2)
    done2 = products(p_ref, *held)
    stat, second = after(1, stat, *done1)
    spill(2)
    stat, third = after(2, stat, *done2)
    att[:, 128:256] = jnp.where(low, second, pltpu.roll(third, HD, 1)).astype(BF16)
    stats[...] = stat
    branch[...] += nt(att[...], weights(slice(512, 768)))


def backward_chunk(
    weights, gain, dy_ref, xt, dt, raw, d_raw, qk_all, v_all, stats, att,
    d_normed, g_gains, ready, store, poll,
):
    raw[:, :256] = nn(dy_ref[...], weights(slice(512, 768)))
    lane = iota((1, 128), 1)
    low = lane < HD
    mean_of = group_means()
    back_gain = 1.0 / gain

    def ahead(head):
        tile = 128 * ((head + 1) // 2)
        da = raw[:, tile:tile + 128]
        out = att[:, tile:tile + 128].astype(F32)
        if head != 1:
            da = pltpu.roll(da, HD, 1)
            out = pltpu.roll(out, HD, 1)
        inverse = stats[:, HD + 8 + head:HD + 9 + head]
        scaled = jnp.where(low, da * inverse, 0.0).astype(BF16).astype(F32)
        dot = jnp.sum(scaled * out, axis=-1, keepdims=True)
        dot_high = dot.astype(BF16).astype(F32)
        d_aug = jnp.where(
            lane == HD, -dot_high, jnp.where(lane == HD + 1, dot_high - dot, scaled)
        )
        qk_t = qk_all[head].astype(F32).T.astype(BF16)
        return d_aug.astype(BF16), d_aug.T.astype(BF16), qk_t

    def products(head, p_ref, d_low, d_t, qk_t):
        qk = qk_all[head]
        v_aug = v_all[head]
        d_queries, d_keys, d_values = [], [], []
        for base, count in ((0, BIG), (BIG, REST)):
            block = slice(base, base + count)
            d_values.append(nn(d_t[:, block], p_ref[block, :count]))
            for row in range(base, base + count, 256):
                rows = slice(row, row + 256)
                d_prob = nt(d_low[rows], v_aug[block])
                d_score = (p_ref[rows, :count].astype(F32) * d_prob).astype(BF16)
                p_ref[rows, :count] = d_score
                d_queries.append(nn(d_score, qk[block]))
            d_keys.append(nn(qk_t[:, block], p_ref[block, :count]))
        return d_queries, d_keys, d_values

    def after(head, d_queries, d_keys, d_values):
        d_query = jnp.concatenate(d_queries, axis=0)
        d_key = jnp.concatenate([part.T for part in d_keys], axis=0)
        d_value = jnp.concatenate([part.T for part in d_values], axis=0)
        d_qk = pltpu.roll(jnp.where(low, d_key, d_query), HD, 1) * 0.125
        unit = qk_all[head].astype(F32) * back_gain
        spread = jnp.where(low, stats[:, head:head + 1], stats[:, HD + head:HD + head + 1])
        g_gains[6:7] += jnp.sum(d_qk * unit, axis=0, keepdims=True)
        scaled = d_qk * gain
        mean = nn(scaled.astype(BF16), mean_of)
        d_qk = spread * (scaled - mean - unit * nn((scaled * unit).astype(BF16), mean_of))
        d_raw[:, 128 * head:128 * head + 128] = d_qk.astype(BF16)
        return d_value

    held = ahead(0)
    p_ref = ready(0)
    done0 = products(0, p_ref, *held)
    held = ahead(1)
    poll(0)
    p_ref = ready(1)
    done1 = products(1, p_ref, *held)
    held = ahead(2)
    first = after(0, *done0)
    poll(1)
    p_ref = ready(2)
    done2 = products(2, p_ref, *held)
    second = after(1, *done1)
    d_raw[:, 384:512] = jnp.where(low, first, pltpu.roll(second, HD, 1)).astype(BF16)
    poll(2)
    third = after(2, *done2)
    d_raw[:, 512:640] = jnp.where(low, third, 0.0).astype(BF16)
    d_projected = d_raw[...]
    d_normed[...] += nt(d_projected, weights(slice(0, 640)))
    left = nn(xt[...], d_projected)
    right = nn(dt[...], att[...])
    store(slice(0, 512), left[:, :512].astype(BF16))
    store(slice(512, 640), (left[:, 512:] + right[:, :128]).astype(BF16))
    store(slice(640, 768), right[:, 128:].astype(BF16))


def front_kernel(
    tok, cot, ids, gains, norm_gain, w_attn, w_feed,
    normed, grads, returned, out0, out1, out2, out3, w_ff, g_last, at_second, g_gains, p_all,
    got_rows, w_full, g_buf, at_core, at_first,
    x_ref, dy_ref, xt, dt, feat_q, feat_k, pt, raw, d_raw, p_buf,
    qk_all, v_all, stats, att, total,
    row_send, row_recv, back_send, back_recv, wa_send, wa_recv, wf_send, wf_recv, own_sem,
    p_out, p_in, at_send, at_recv,
):
    count, part, width = tok.shape
    shard = w_attn.shape[0]
    at = Place(count)
    at.greet()
    gather = Gather(at, w_attn, w_full, wa_send, wa_recv)
    gather_ff = Gather(at, w_feed, w_ff, wf_send, wf_recv)
    scatter = Scatter(at, halves(width), g_buf, at_core, at_first, at_second, at_send, at_recv)
    own_ff = pltpu.make_async_copy(w_feed, gather_ff.piece(at.z), own_sem)

    def row_copy(kind, k):
        src = (normed, grads)[kind].at[k]
        return at.copy(src, got_rows.at[k - 1, kind], row_send.at[kind, k - 1],
                       row_recv.at[kind, k - 1], mp=at.along(k))

    def back_copy(k, strip):
        rows, sem = pl.ds(strip * STRIP, STRIP), (k - 1, strip)
        return at.copy(got_rows.at[k - 1, 0, rows], returned.at[k, rows], back_send.at[sem],
                       back_recv.at[sem], mp=at.along(-k))

    strips = [(k, strip) for strip in range(EARLY // STRIP) for k in (1, 3, 2)]

    gather.start()
    own_ff.start()
    w_full[at.z, at.y, at.x, at.core] = w_attn[...]
    gather.spread(0)
    gain = norm_gain[...]
    for k in (1, 3, 2, 0):
        sequence = at.along(k)
        x = tok[sequence].astype(F32)
        centered = x - jnp.mean(x, axis=-1, keepdims=True)
        spread = lax.rsqrt(jnp.mean(centered * centered, axis=-1, keepdims=True) + 1e-6)
        pad = jnp.zeros((PIECE - part, width), BF16)
        normed[k, :part] = (centered * spread * gain).astype(BF16)
        normed[k, part:] = pad
        grads[k, :part] = cot[sequence]
        grads[k, part:] = pad
        if k == 2:
            gather.spread(-1, 1)
    gather.spread(-2, 2)
    for k in (1, 3, 2):
        row_copy(0, k).start()
    place_rows(at.z, part, ids, pt, feat_q, feat_k)
    g_gains[...] = jnp.zeros_like(g_gains)
    total[...] = jnp.zeros_like(total)
    gather.forward(0)
    gather.spread(-3, 3)
    own_ff.wait()
    gather.forward(-1, 1)
    gather.across(0)
    gather.forward(-2, 2)
    gather.across(-1, 1)
    gather.forward(-3, 3)
    gather.across(-2, 2)
    gather.across(-3, 3)
    gather.last()
    gather_ff.spread(0)
    for k in (1, 3, 2):
        row_copy(0, k).wait_recv()
    for k in (1, 3, 2):
        row_copy(1, k).start()

    def lay_out(kind, own, rows, columns):
        value = 0.0
        for k in range(count):
            piece = own[0] if k == 0 else got_rows[k - 1, kind]
            value = value + lax.dot_general(
                pt[k], piece, (((0,), (0,)), ((), ())), preferred_element_type=F32
            )
        value = value.astype(BF16)
        rows[...] = value
        columns[...] = value.T

    lay_out(0, normed, x_ref, xt)

    def weights_of(chunk):
        def weights(cols):
            return w_full[chunk, :, :, :, :, cols].reshape(width, cols.stop - cols.start)

        return weights

    def p_write(step, head):
        slot = lax.rem(step + head, 2)
        return pltpu.make_async_copy(p_buf.at[slot], p_all.at[at.along(step), head],
                                     p_out.at[slot])

    def p_read(step, head):
        slot = lax.rem(step + head, 2)
        return pltpu.make_async_copy(p_all.at[at.target(step), head], p_buf.at[slot],
                                     p_in.at[slot])

    def forward_step(step, carry):
        chunk = at.along(step)

        @pl.when(step == 2)
        def _():
            gather_ff.forward(0)

        def begin(head):
            if head == 2:
                p_write(step, 0).wait()
            else:
                @pl.when(step >= 1)
                def _():
                    p_write(step - 1, 1 + head).wait()
            return p_buf.at[lax.rem(step + head, 2)]

        forward_chunk(
            weights_of(chunk), gains[...], x_ref, feat_q, feat_k, raw, qk_all.at[chunk],
            v_all.at[chunk], stats.at[chunk], att.at[chunk], total, begin,
            lambda head: p_write(step, head).start(),
        )
        return carry

    lax.fori_loop(0, count, forward_step, 0)
    for head in (1, 2):
        p_write(count - 1, head).wait()
    p_read(0, 0).start()
    value = total[...].astype(BF16)
    for k, out in enumerate((out0, out1, out2, out3)):
        piece = nn(pt[k], value).astype(BF16)
        out[PIECE:] = piece[EARLY:]
        if k == 0:
            returned[0, :EARLY] = piece[:EARLY]
        else:
            got_rows[k - 1, 0, :EARLY] = piece[:EARLY]
    total[...] = jnp.zeros_like(total)
    for k in (1, 3, 2):
        row_copy(1, k).wait_recv()
    gather_ff.start()
    gather_ff.across(0)
    lay_out(1, grads, dy_ref, dt)

    def events(poll):
        if poll == 2:
            gather_ff.spread(-1, 1)
        elif poll == 3:
            scatter.after_core(0)
        elif poll == 4:
            gather_ff.spread(-2, 2)
        elif poll == 5:
            gather_ff.forward(-1, 1)
        elif poll == 6:
            gather_ff.spread(-3, 3)
            scatter.after_core(1)
        elif poll == 7:
            gather_ff.forward(-2, 2)
            scatter.after_first(0)
        elif poll == 8:
            gather_ff.across(-1, 1)
        elif poll == 9:
            gather_ff.forward(-3, 3)
            scatter.after_core(2)
            scatter.after_first(1)
            scatter.after_second(0)
        elif poll == 10:
            gather_ff.across(-2, 2)
        elif poll == 11:
            gather_ff.across(-3, 3)
            scatter.after_second(1)
            scatter.after_first(2)
        for k, strip in strips[max(0, poll - 3):max(0, poll - 2)]:
            back_copy(k, strip).start()

    def backward_step(step, carry):
        chunk = at.target(step)

        def store(cols, value):
            split = (2, 2, 2, shard, cols.stop - cols.start)
            value = value.reshape(split)

            @pl.when(step < count - 1)
            def _():
                g_buf[step, 0, :, :, :, :, cols] = value

            @pl.when(step == count - 1)
            def _():
                g_last[0, 0, :, :, :, :, cols] = value

        def ready(head):
            p_read(step, head).wait()
            if head < 2:
                p_read(step, head + 1).start()
            else:
                @pl.when(step + 1 < count)
                def _():
                    p_read(step + 1, 0).start()
            return p_buf.at[lax.rem(step + head, 2)]

        def poll(head):
            for which in range(count):
                @pl.when(step == which)
                def _():
                    events(3 * which + head)

        backward_chunk(
            weights_of(chunk), gains[...], dy_ref, xt, dt, raw, d_raw,
            qk_all.at[chunk], v_all.at[chunk], stats.at[chunk], att.at[chunk], total, g_gains,
            ready, store, poll,
        )

        @pl.when(step < count - 1)
        def _():
            scatter.start(step)

        return carry

    lax.fori_loop(0, count, backward_step, 0)
    store_gain(g_gains, total[...], x_ref[...], norm_gain[...])
    value = total[...].astype(BF16)
    for k, out in enumerate((out0, out1, out2, out3)):
        out[:PIECE] = nn(pt[k], value).astype(BF16)
    scatter.after_second(2)
    gather_ff.last()
    for k, strip in strips:
        back_copy(k, strip).wait_recv()

    gather.wait_send()
    gather_ff.wait_send()
    for k, strip in strips:
        back_copy(k, strip).wait_send()
    for k in range(1, count):
        for kind in range(2):
            row_copy(kind, k).wait_send()
    for step in range(count - 1):
        scatter.wait_send(step)


def place_rows(me, part, ids, pt, feat_q, feat_k):
    mp = ids.shape[1]
    total = mp * part
    numbers = ids[me]
    start = jnp.zeros((1, 1), jnp.int32)
    for image in range(IMAGES):
        count = jnp.sum((numbers == image).astype(F32), axis=(0, 1), keepdims=True)
        ahead = jnp.sum(
            ((numbers >= 0) & (numbers < image)).astype(F32), axis=(0, 1), keepdims=True
        )
        start = start + jnp.where(count == MOST, ahead, 0.0).astype(jnp.int32)
    line = source_of(iota((1, ROWS), 1), start, total)
    feats = 0.0
    for k in range(mp):
        chunk = lax.rem(me - k + mp, mp)
        offset = iota((PIECE, 1), 0)
        pos = jnp.where(offset < part, chunk * part + offset, -2)
        pick = (line == pos).astype(F32).astype(BF16)
        pt[k] = pick
        marks = (iota((128, 1), 0) - HD == ids[me, pl.ds(chunk, 1), :]).astype(F32)
        feats = feats + nn(marks.astype(BF16), pick)
    feats = feats.T
    lane = iota((1, 128), 1)
    feat_q[...] = (feats * 128.0).astype(BF16)
    marked = (lane >= HD) & (lane < HD + IMAGES)
    feat_k[...] = jnp.where(marked, (feats - 1.0) * 256.0, 0.0).astype(BF16)


def front_call(tokens, cotangent, ids, gains, norm_gain, w_attn, w_feed):
    count, part, width = tokens.shape
    shard = w_attn.shape[0]
    vmem = pl.BlockSpec(memory_space=pltpu.VMEM)
    hbm = pl.BlockSpec(memory_space=pl.ANY)
    rows = jax.ShapeDtypeStruct((count, PIECE, width), BF16)
    return pl.pallas_call(
        front_kernel,
        in_specs=[vmem] * 6 + [hbm],
        out_specs=[vmem] * 7 + [hbm] + [vmem] * 3 + [hbm],
        out_shape=[rows, rows, jax.ShapeDtypeStruct((count, EARLY, width), BF16)]
        + [jax.ShapeDtypeStruct((2 * PIECE - EARLY, width), BF16)] * 4
        + [
            jax.ShapeDtypeStruct((count, 2, 2, 2, 2, shard, width), BF16),
            jax.ShapeDtypeStruct((1, 1, 2, 2, 2, shard, width), BF16),
            jax.ShapeDtypeStruct((count - 1, 1, shard, width), BF16),
            jax.ShapeDtypeStruct((8, 128), F32),
            jax.ShapeDtypeStruct((count, 3, ROWS, BIG), BF16),
        ],
        scratch_shapes=[
            pltpu.VMEM((count - 1, 2, PIECE, width), BF16),
            pltpu.VMEM((count, 2, 2, 2, shard, width), BF16),
            pltpu.VMEM((count - 1, 1, 2, 2, 2, shard, width), BF16),
            pltpu.VMEM((count - 1, 1, 2, 2, shard, width), BF16),
            pltpu.VMEM((count - 1, 1, 2, shard, width), BF16),
            pltpu.VMEM((ROWS, width), BF16),
            pltpu.VMEM((ROWS, width), BF16),
            pltpu.VMEM((width, ROWS), BF16),
            pltpu.VMEM((width, ROWS), BF16),
            pltpu.VMEM((ROWS, 128), BF16),
            pltpu.VMEM((ROWS, 128), BF16),
            pltpu.VMEM((count, PIECE, ROWS), BF16),
            pltpu.VMEM((ROWS, 640), F32),
            pltpu.VMEM((ROWS, 640), BF16),
            pltpu.VMEM((2, ROWS, BIG), BF16),
            pltpu.VMEM((count, 3, ROWS, 128), BF16),
            pltpu.VMEM((count, 3, ROWS, 128), BF16),
            pltpu.VMEM((count, ROWS, 128), F32),
            pltpu.VMEM((count, ROWS, 256), BF16),
            pltpu.VMEM((ROWS, width), F32),
            pltpu.SemaphoreType.DMA((2, count - 1)),
            pltpu.SemaphoreType.DMA((2, count - 1)),
            pltpu.SemaphoreType.DMA((count - 1, EARLY // STRIP)),
            pltpu.SemaphoreType.DMA((count - 1, EARLY // STRIP)),
            pltpu.SemaphoreType.DMA((9, count)),
            pltpu.SemaphoreType.DMA((8, count)),
            pltpu.SemaphoreType.DMA((9, count)),
            pltpu.SemaphoreType.DMA((8, count)),
            pltpu.SemaphoreType.DMA,
            pltpu.SemaphoreType.DMA((2,)),
            pltpu.SemaphoreType.DMA((2,)),
            pltpu.SemaphoreType.DMA((3, 2, count - 1)),
            pltpu.SemaphoreType.DMA((3, 2, count - 1)),
        ],
        compiler_params=pltpu.CompilerParams(
            collective_id=1, has_side_effects=True, vmem_limit_bytes=FRONT_VMEM
        ),
        name="front",
    )(tokens, cotangent, ids, gains, norm_gain, w_attn, w_feed)


def finish_kernel(
    seqs, place, tok, cot, gain, branch, d_ff, back, ret, output, input_grad
):
    part = tok.shape[1]
    x = tok[0].astype(F32)
    added = branch[0] + jnp.concatenate([back[0], ret[0, PIECE:]]).astype(F32)
    output[0] = (x + added[:part]).astype(BF16)
    d_normed = (d_ff[0] + ret[0, :PIECE].astype(F32))[:part]
    centered = x - jnp.mean(x, axis=-1, keepdims=True)
    spread = lax.rsqrt(jnp.mean(centered * centered, axis=-1, keepdims=True) + 1e-6)
    unit = centered * spread
    scaled = d_normed * gain[...]
    d_x = spread * (
        scaled
        - jnp.mean(scaled, axis=-1, keepdims=True)
        - unit * jnp.mean(scaled * unit, axis=-1, keepdims=True)
    )
    total = cot[0].astype(F32) + d_x
    sequence = lax.rem(place[0] + pl.program_id(0), pl.num_programs(0))
    for inner in range(seqs):

        @pl.when(lax.rem(sequence, seqs) == inner)
        def _():
            input_grad[sequence // seqs, :, inner, :] = total


def finish_call(place, seqs, tokens, cotangent, gain, branch, d_ff, back, returned):
    count, part, width = tokens.shape
    block = pl.BlockSpec(
        (1, part, width), lambda k, place: (lax.rem(place[0] + k, count), 0, 0)
    )
    padded = pl.BlockSpec((1, PIECE, width), lambda k, place: (k, 0, 0))
    piece = pl.BlockSpec((1, 2 * PIECE - EARLY, width), lambda k, place: (k, 0, 0))
    ordered = (count // seqs, part, seqs, width)
    early = pl.BlockSpec((1, EARLY, width), lambda k, place: (k, 0, 0))
    line = pl.BlockSpec((1, width), lambda k, place: (0, 0))
    return pl.pallas_call(
        functools.partial(finish_kernel, seqs),
        grid_spec=pltpu.PrefetchScalarGridSpec(
            num_scalar_prefetch=1,
            grid=(count,),
            in_specs=[block, block, line, padded, padded, early, piece],
            out_specs=[block, pl.BlockSpec(ordered, lambda k, place: (0, 0, 0, 0))],
        ),
        out_shape=[
            jax.ShapeDtypeStruct(tokens.shape, BF16),
            jax.ShapeDtypeStruct(ordered, F32),
        ],
        compiler_params=pltpu.CompilerParams(vmem_limit_bytes=VMEM),
        name="finish",
    )(place, tokens, cotangent, gain, branch, d_ff, back, returned)


def pack_attention(w_qkv, w_proj):
    rows, wide = w_qkv.shape[1:]
    heads = wide // HD
    qk = w_qkv[:2].reshape(2, rows, heads, HD).transpose(1, 2, 0, 3).reshape(rows, 2 * wide)
    return jnp.concatenate([qk, w_qkv[2], w_proj.T], axis=1)


def unpack_attention(grad, wide):
    rows = grad.shape[0]
    heads = wide // HD
    qk = grad[:, :2 * wide].reshape(rows, heads, 2, HD).transpose(2, 0, 1, 3)
    qk = qk.reshape(2, rows, wide)
    g_qkv = jnp.concatenate([qk, grad[None, :, 2 * wide:3 * wide]], axis=0)
    return g_qkv, grad[:, 3 * wide:].T


def body(
    dp, mp, tokens, w_qkv, w_up, w_proj, w_down, norm_gain, query_gain, key_gain, image_ids, cotangent
):
    micro, seqs, part, width = tokens.shape
    count = micro * seqs
    shard = w_up.shape[0]
    me = lax.axis_index("mp")
    place = me.astype(jnp.int32)[None]
    both = ("mp", "dp")
    tok = tokens.reshape(count, part, width)
    cot = cotangent.reshape(count, part, width)
    gain = norm_gain.reshape(1, width)
    ids = image_ids.reshape(count, mp, part)
    ids = jnp.pad(ids, ((0, 0), (0, 0), (0, PIECE - part)), constant_values=-1)
    gains = jnp.concatenate([query_gain, key_gain]).reshape(1, 2 * HD)
    w_attn = pack_attention(w_qkv, w_proj)
    w_ff = jnp.stack([w_up, w_down.T])

    def send_back(outs):
        return [outs[0]] + [
            lax.ppermute(out, "mp", [(i, (i - k) % mp) for i in range(mp)])
            for k, out in enumerate(outs[1:], 1)
        ]

    if (dp, mp) == (8, 4):
        normed, grads, back, *outs, w_ff, g_attn, z_attn, g_gains, _ = front_call(
            tok, cot, ids, gains, gain, w_attn, w_ff
        )
        branch, d_ff, g_attn, g_up, g_down, g_gains, returned = feed_remote_call(
            normed.reshape(count * PIECE, width), grads.reshape(count * PIECE, width),
            w_ff.reshape(mp, dp, 2, shard, width), g_attn, z_attn, gain, g_gains, outs,
        )
    else:
        w_attn = lax.all_gather(w_attn, both).reshape(mp, width, width)
        w_ff = lax.all_gather(w_ff, both).reshape(mp, dp, 2, shard, width)
        normed, grads, *sends = norm_call(place, tok, cot, gain)
        received = [
            lax.ppermute(send, "mp", [(i, (i + k) % mp) for i in range(mp)])
            for k, send in enumerate(sends, 1)
        ]
        *outs, g_attn, g_gains = attention_call(
            place, part, normed, grads, received, ids, gains, gain, w_attn
        )
        outs = send_back(outs)
        back = jnp.stack([out[1, :EARLY] for out in outs])
        returned = jnp.stack([jnp.concatenate([out[0], out[1, EARLY:]]) for out in outs])
        flat_normed = normed.reshape(count * PIECE, width)
        branch, d_ff, g_up, g_down = feed_call(
            flat_normed, grads.reshape(count * PIECE, width),
            w_ff[:, :, 0].reshape(mp, width, width), w_ff[:, :, 1].reshape(mp, width, width),
        )
        g_attn, g_up, g_down = (
            lax.psum_scatter(
                grad.reshape(-1, shard, width), both, scatter_dimension=0
            ).astype(F32)
            for grad in (g_attn, g_up, g_down)
        )
        own = jnp.sum(d_ff * flat_normed.astype(F32), axis=0) / norm_gain
        g_gains = g_gains.at[:width // 128].add(own.reshape(-1, 128))
        g_gains = lax.psum(g_gains, both)
    output, input_grad = finish_call(
        place, seqs, tok, cot, gain,
        branch.reshape(count, PIECE, width), d_ff.reshape(count, PIECE, width), back, returned,
    )
    input_grad = input_grad.transpose(0, 2, 1, 3)
    g_qkv, g_proj = unpack_attention(g_attn, w_qkv.shape[2])
    g_norm = g_gains[:width // 128].reshape(width)
    g_gains = g_gains[6]
    return (
        output.reshape(tokens.shape),
        input_grad,
        g_qkv,
        g_up,
        g_proj,
        g_down.T,
        g_norm,
        g_gains[:HD],
        g_gains[HD:],
    )


def solution(mesh):
    rows = P(None, "dp", "mp", None)
    weights = (P(None, "dp", "mp"), P("dp", "mp"), P("mp", "dp"), P("mp", "dp"))
    gains = (P(), P(), P())
    return jax.shard_map(
        functools.partial(body, mesh.shape["dp"], mesh.shape["mp"]),
        mesh=mesh,
        in_specs=(rows,) + weights + gains + (P(None, "dp", None), rows),
        out_specs=(rows, rows) + weights + gains,
        check_vma=False,
    )
```

```python
import functools

import jax
import jax.numpy as jnp
from jax import lax
from jax.experimental import pallas as pl
from jax.experimental.pallas import tpu as pltpu
from jax.sharding import PartitionSpec as P

HD = 64
MOST = 709
IMAGES = 8
STRIP = 48
EARLY = 192
PIECE = 240
BIG = 768
REST = 256
ROWS = BIG + REST
VMEM = 60 * 1024 * 1024
FRONT_VMEM = 63 * 1024 * 1024
F32 = jnp.float32
BF16 = jnp.bfloat16


def nn(left, right):
    return lax.dot_general(left, right, (((1,), (0,)), ((), ())), preferred_element_type=F32)


def nt(left, right):
    return lax.dot_general(left, right, (((1,), (1,)), ((), ())), preferred_element_type=F32)


def norm_kernel(place, tok, cot, gain, normed, grads, send1, send2, send3):
    step = pl.program_id(0)
    part = tok.shape[1]
    x = tok[0].astype(F32)
    centered = x - jnp.mean(x, axis=-1, keepdims=True)
    spread = lax.rsqrt(jnp.mean(centered * centered, axis=-1, keepdims=True) + 1e-6)
    value = (centered * spread * gain[...]).astype(BF16)
    normed[...] = jnp.zeros_like(normed)
    grads[...] = jnp.zeros_like(grads)
    normed[0, :part] = value
    grads[0, :part] = cot[0]
    for index, send in ((1, send1), (2, send2), (3, send3)):

        @pl.when(step == index)
        def _():
            send[0] = normed[0]
            send[1] = grads[0]


def norm_call(place, tokens, cotangent, gain):
    count, part, width = tokens.shape
    block = lambda k, place: (lax.rem(place[0] + k, count), 0, 0)
    fixed = lambda k, place: (0, 0, 0)
    return pl.pallas_call(
        norm_kernel,
        grid_spec=pltpu.PrefetchScalarGridSpec(
            num_scalar_prefetch=1,
            grid=(count,),
            in_specs=[
                pl.BlockSpec((1, part, width), block),
                pl.BlockSpec((1, part, width), block),
                pl.BlockSpec((1, width), lambda k, place: (0, 0)),
            ],
            out_specs=[pl.BlockSpec((1, PIECE, width), lambda k, place: (k, 0, 0))] * 2
            + [pl.BlockSpec((2, PIECE, width), fixed)] * 3,
        ),
        out_shape=[jax.ShapeDtypeStruct((count, PIECE, width), BF16)] * 2
        + [jax.ShapeDtypeStruct((2, PIECE, width), BF16)] * 3,
        compiler_params=pltpu.CompilerParams(vmem_limit_bytes=VMEM),
        name="norm_rows",
    )(place, tokens, cotangent, gain)


def feed_kernel(normed, grads, w_up, w_down, branch, d_normed, g_up, g_down, xt, dt):
    step = pl.program_id(0)
    x = normed[...]
    dy = grads[...]

    @pl.when(step == 0)
    def _():
        xt[...] = x.T
        dt[...] = dy.T

    up = nn(x, w_up[0])
    value, slope = gelu_parts(up)
    hidden = value.astype(BF16)
    d_up = (nn(dy, w_down[0]) * slope).astype(BF16)
    g_up[0] = nn(xt[...], d_up).astype(BF16)
    g_down[0] = nn(dt[...], hidden).astype(BF16)
    out = nt(hidden, w_down[0])
    back = nt(d_up, w_up[0])

    @pl.when(step == 0)
    def _():
        branch[...] = out
        d_normed[...] = back

    @pl.when(step > 0)
    def _():
        branch[...] += out
        d_normed[...] += back


def feed_call(normed, grads, w_up, w_down):
    rows, width = normed.shape
    chunks, _, hidden = w_up.shape
    whole = pl.BlockSpec((rows, width), lambda m: (0, 0))
    chunk = pl.BlockSpec((1, width, hidden), lambda m: (m, 0, 0))
    return pl.pallas_call(
        feed_kernel,
        grid=(chunks,),
        in_specs=[whole, whole, chunk, chunk],
        out_specs=[whole, whole, chunk, chunk],
        out_shape=[jax.ShapeDtypeStruct((rows, width), F32)] * 2
        + [jax.ShapeDtypeStruct(w_up.shape, BF16)] * 2,
        scratch_shapes=[pltpu.VMEM((width, rows), BF16)] * 2,
        compiler_params=pltpu.CompilerParams(vmem_limit_bytes=VMEM),
        cost_estimate=pl.CostEstimate(
            flops=12 * rows * width * hidden * chunks,
            bytes_accessed=4 * chunks * width * hidden * 2,
            transcendentals=rows * hidden * chunks,
        ),
        name="feed_forward",
    )(normed, grads, w_up, w_down)


class Place:
    def __init__(self, planes):
        d = lax.axis_index("dp")
        self.z = lax.axis_index("mp")
        self.d, self.planes = d, planes
        self.core, self.x, self.y = d % 2, (d // 2) % 2, d // 4
        self.sibling = d + 1 - 2 * self.core
        self.beside = d + 2 - 4 * self.x
        self.above = d + 4 - 8 * self.y

    def target(self, step):
        z, high = self.z, self.z // 2
        near = jnp.where(step == 2, 1 - z + 4 * high, z)
        return jnp.where(step == 0, 3 - 3 * high, jnp.where(step == 1, 2 - high, near))

    def along(self, k):
        return lax.rem(self.z + k + self.planes, self.planes)

    def copy(self, src, dst, send, recv, dp=None, mp=None):
        return pltpu.make_async_remote_copy(
            src_ref=src, dst_ref=dst, send_sem=send, recv_sem=recv,
            device_id={"dp": self.d if dp is None else dp, "mp": self.z if mp is None else mp},
            device_id_type=pl.DeviceIdType.MESH,
        )

    def greet(self):
        barrier = pltpu.get_barrier_semaphore()
        for other in (self.sibling, self.beside, self.above):
            pl.semaphore_signal(barrier, 1, device_id={"dp": other, "mp": self.z},
                                device_id_type=pl.DeviceIdType.MESH)
        for k in range(1, self.planes):
            pl.semaphore_signal(barrier, 1, device_id={"dp": self.d, "mp": self.along(k)},
                                device_id_type=pl.DeviceIdType.MESH)
        pl.semaphore_wait(barrier, self.planes + 2)


class Scatter:
    def __init__(self, at, items, src, got_core, got_first, got_second, send_sem, recv_sem):
        self.at, self.items, self.src = at, items, src
        self.got_core, self.got_first, self.got_second = got_core, got_first, got_second
        self.send_sem, self.recv_sem = send_sem, recv_sem

    def copy(self, stage, step, item):
        at = self.at
        kind, cols, x_first = self.items[item]
        if stage == 0:
            src = self.src.at[step, kind, :, :, 1 - at.core, :, cols]
            dst = self.got_core.at[step, kind, :, :, :, cols]
            to = at.sibling
        elif stage == 1:
            if x_first:
                src = self.got_core.at[step, kind, :, 1 - at.x, :, cols]
            else:
                src = self.got_core.at[step, kind, 1 - at.y, :, :, cols]
            dst = self.got_first.at[step, kind, :, :, cols]
            to = at.beside if x_first else at.above
        else:
            src = self.got_first.at[step, kind, 1 - at.y if x_first else 1 - at.x, :, cols]
            dst = self.got_second.at[step, kind, :, cols]
            to = at.above if x_first else at.beside
        sem = (stage, item, step)
        return at.copy(src, dst, self.send_sem.at[sem], self.recv_sem.at[sem], dp=to)

    def start(self, step):
        for item in range(len(self.items)):
            self.copy(0, step, item).start()

    def after_core(self, step):
        for item, (kind, cols, _) in enumerate(self.items):
            self.copy(0, step, item).wait_recv()
            for row in ((0, 0), (0, 1), (1, 0), (1, 1)):
                own = self.src[(step, kind, *row, self.at.core, slice(None), cols)]
                to = (step, kind, *row, slice(None), cols)
                total = own.astype(F32) + self.got_core[to].astype(F32)
                self.got_core[to] = total.astype(BF16)
            self.copy(1, step, item).start()

    def after_first(self, step):
        for item, (kind, cols, x_first) in enumerate(self.items):
            self.copy(1, step, item).wait_recv()
            for row in range(2):
                if x_first:
                    own = self.got_core[step, kind, row, self.at.x, :, cols]
                else:
                    own = self.got_core[step, kind, self.at.y, row, :, cols]
                total = own.astype(F32) + self.got_first[step, kind, row, :, cols].astype(F32)
                self.got_first[step, kind, row, :, cols] = total.astype(BF16)
            self.copy(2, step, item).start()

    def total(self, step, item):
        kind, cols, x_first = self.items[item]
        self.copy(2, step, item).wait_recv()
        own = self.got_first[step, kind, self.at.y if x_first else self.at.x, :, cols]
        return own.astype(F32) + self.got_second[step, kind, :, cols].astype(F32)

    def after_second(self, step):
        for item, (kind, cols, _) in enumerate(self.items):
            self.got_second[step, kind, :, cols] = self.total(step, item).astype(BF16)

    def wait_send(self, step):
        for item in range(len(self.items)):
            for stage in range(3):
                self.copy(stage, step, item).wait_send()


class Gather:
    def __init__(self, at, shard, full, send_sem, recv_sem):
        self.at, self.shard, self.full = at, shard, full
        self.send_sem, self.recv_sem = send_sem, recv_sem

    def there(self, r, does):
        plane = self.at.z + r

        @pl.when((plane >= 0) & (plane < self.at.planes))
        def _():
            does(plane)

    def piece(self, plane, y=False, x=False, core=False):
        at = self.at
        return self.full.at[plane, 1 - at.y if y else at.y, 1 - at.x if x else at.x,
                            1 - at.core if core else at.core]

    def copy(self, kind, plane, src, dst=None, **to):
        return self.at.copy(
            src, src if dst is None else dst, self.send_sem.at[kind, plane],
            self.recv_sem.at[kind % 8, plane], **to
        )

    def arrived(self, kind, plane, ref):
        self.copy(kind, plane, ref, dp=self.at.sibling).wait_recv()

    def pass_on(self, kind, plane, src, act):
        z, dst = self.at.z, self.piece(plane)
        if kind == 0:
            @pl.when(z < self.at.planes - 1)
            def _():
                act(self.copy(0, plane, src, dst, mp=z + 1))
        else:
            @pl.when(z > 0)
            def _():
                act(self.copy(8, plane, src, dst, mp=z - 1))

    def start(self):
        for kind in (0, 8):
            self.pass_on(kind, self.at.z, self.shard, lambda copy: copy.start())

    def spread(self, *which):
        for r in which:
            def does(plane):
                src = self.piece(plane)
                if r:
                    self.arrived(0, plane, src)
                    self.pass_on(0 if r < 0 else 8, plane, src, lambda copy: copy.start())
                self.copy(1, plane, src, dp=self.at.beside).start()
                self.copy(2, plane, src, dp=self.at.above).start()
                self.copy(3, plane, src, dp=self.at.sibling).start()

            self.there(r, does)

    def forward(self, *which):
        at = self.at
        for r in which:
            def does(plane):
                from_x, from_y = self.piece(plane, x=True), self.piece(plane, y=True)
                self.arrived(1, plane, from_x)
                if r in (0, 1, -3):
                    self.copy(5, plane, from_x, dp=at.above).start()
                self.copy(4, plane, from_x, dp=at.sibling).start()
                self.arrived(2, plane, from_y)
                if r not in (0, 1, -3):
                    self.copy(5, plane, from_y, dp=at.beside).start()
                self.copy(6, plane, from_y, dp=at.sibling).start()

            self.there(r, does)

    def across(self, *which):
        for r in which:
            def does(plane):
                src = self.piece(plane, y=True, x=True)
                self.arrived(5, plane, src)
                self.copy(7, plane, src, dp=self.at.sibling).start()

            self.there(r, does)

    def last(self):
        for plane in range(self.at.planes):
            self.arrived(3, plane, self.piece(plane, core=True))
            self.arrived(4, plane, self.piece(plane, x=True, core=True))
            self.arrived(6, plane, self.piece(plane, y=True, core=True))
            self.arrived(7, plane, self.piece(plane, y=True, x=True, core=True))

    def wait_send(self):
        for r in range(1 - self.at.planes, self.at.planes):
            def does(plane):
                src = self.piece(plane)
                if r <= 0:
                    self.pass_on(0, plane, src, lambda copy: copy.wait_send())
                if r >= 0:
                    self.pass_on(8, plane, src, lambda copy: copy.wait_send())
                for kind in range(1, 8):
                    self.copy(kind, plane, src, dp=self.at.sibling).wait_send()

            self.there(r, does)


class Along:
    def __init__(self, at, parts, got, send_sem, recv_sem):
        self.at, self.parts, self.got = at, parts, got
        self.send_sem, self.recv_sem = send_sem, recv_sem
        self.inner = (at.z == 1) | (at.z == 2)

    def copy(self, step, kind):
        at, inner = self.at, self.inner
        side = 1 - 2 * (at.z // 2)
        to = at.z + jnp.where(inner & (step == 2), -side, side)
        slot = jnp.where(inner, 2 + 2 * step - 3 * (step // 2), step + step // 2)
        return at.copy(self.parts.at[step, kind], self.got.at[kind, slot],
                       self.send_sem.at[kind, step], self.recv_sem.at[kind, slot], mp=to)

    def arrived(self, kind, slot):
        ref = self.got.at[kind, slot]
        self.at.copy(ref, ref, self.send_sem.at[kind, 0], self.recv_sem.at[kind, slot],
                     mp=self.at.along(1)).wait_recv()

    def send_outer(self, step):
        @pl.when(jnp.logical_not(self.inner))
        def _():
            for kind in range(self.got.shape[0]):
                self.copy(step, kind).start()

    def send_inner(self, step):
        @pl.when(self.inner)
        def _():
            for kind in range(self.got.shape[0]):
                self.arrived(kind, step)
                own = self.parts[step, kind].astype(F32)
                total = own + self.got[kind, step].astype(F32)
                self.parts[step, kind] = total.astype(BF16)
                self.copy(step, kind).start()

    def add(self, kind, out):
        self.arrived(kind, 3)
        out[...] += self.got[kind, 3].astype(F32)

        @pl.when(self.inner)
        def _():
            self.arrived(kind, 4)
            out[...] += self.got[kind, 4].astype(F32)

    def wait_send(self, step):
        for kind in range(self.got.shape[0]):
            self.copy(step, kind).wait_send()


def gelu_parts(up):
    inner = 0.7978845608028654 * (up + 0.044715 * up * up * up)
    th = jnp.tanh(inner)
    half = 0.5 * (1.0 + th)
    slope = half + 0.5 * up * (1.0 - th * th) * (
        0.7978845608028654 * (1.0 + 3 * 0.044715 * up * up)
    )
    return up * half, slope


def halves(width):
    return (0, slice(0, width // 2), True), (0, slice(width // 2, width), False)


def feed_remote_kernel(
    x_ref, dy_ref, w_hbm, g_attn, z_attn, gain, gains_in, back0, back1, back2, back3,
    branch, d_normed, out_attn, out_up, out_down, out_gains, returned,
    xt, dt, w_buf, hidden, d_up, g_ff, ff_core, ff_first, ff_second, at_core, at_first, at_second, got_z,
    parts, got_za, sums, got_sums, z_sums,
    w_sem, ff_send, ff_recv, at_send, at_recv, z_send, z_recv, za_send, za_recv,
    sum_send, sum_recv, back_send, back_recv, own_sem,
):
    width = x_ref.shape[1]
    steps, shard = w_hbm.shape[0], w_hbm.shape[3]
    at = Place(steps)
    at.greet()
    attn = Scatter(at, halves(width), g_attn, at_core, at_first, at_second, at_send, at_recv)
    both = (0, slice(0, width), True), (1, slice(0, width), False)
    feed = Scatter(at, both, g_ff, ff_core, ff_first, ff_second, ff_send, ff_recv)
    along = Along(at, ff_second, got_z, z_send, z_recv)
    along_attn = Along(at, parts, got_za, za_send, za_recv)
    last = steps - 1

    def w_copy(step, kind):
        slot = lax.rem(step, 2)
        return pltpu.make_async_copy(
            w_hbm.at[at.target(step), :, kind], w_buf.at[slot, kind], w_sem.at[slot, kind]
        )

    strips = [(k, strip) for strip in range(returned.shape[1] // STRIP) for k in (1, 3, 2)]
    first = len(strips) - 3 * steps

    def back_copy(k, strip):
        rows, sem = pl.ds(strip * STRIP, STRIP), (k - 1, strip)
        return at.copy((back0, back1, back2, back3)[k].at[rows], returned.at[k, rows],
                       back_send.at[sem], back_recv.at[sem], mp=at.along(-k))

    own_back = pltpu.make_async_copy(back0, returned.at[0], own_sem)
    own_back.start()
    attn.start(0)
    for kind in range(2):
        w_copy(0, kind).start()
    for k, strip in strips[:first]:
        back_copy(k, strip).start()
    parts[...] = z_attn[...]
    for step in range(last):
        along_attn.send_outer(step)
    xt[...] = x_ref[...].T
    dt[...] = dy_ref[...].T
    branch[...] = jnp.zeros_like(branch)
    d_normed[...] = jnp.zeros_like(d_normed)

    def one_step(step, carry):
        for kind in range(2):
            w_copy(step, kind).wait()

        @pl.when(step + 1 < steps)
        def _():
            for kind in range(2):
                w_copy(step + 1, kind).start()

        slot = lax.rem(step, 2)
        split = (2, 2, 2, shard, width)

        def weights(kind):
            return w_buf[slot, kind].reshape(width, width)

        value, slope = gelu_parts(nn(x_ref[...], weights(0)))
        hidden[...] = value.astype(BF16)
        d_up[...] = (nn(dy_ref[...], weights(1)) * slope).astype(BF16)

        for which in range(steps):
            @pl.when(step == which)
            def _():
                for k, strip in strips[first + 3 * which:first + 3 * which + 3]:
                    back_copy(k, strip).start()

        @pl.when(step == 0)
        def _():
            attn.after_core(0)

        @pl.when(step == 2)
        def _():
            along_attn.send_inner(0)

        @pl.when(step == 3)
        def _():
            along_attn.send_inner(1)
            along_attn.send_inner(2)

        g_ff[step, 0] = nn(xt[...], d_up[...]).astype(BF16).reshape(split)
        g_ff[step, 1] = nn(dt[...], hidden[...]).astype(BF16).reshape(split)
        feed.start(step)

        @pl.when(step >= 1)
        def _():
            feed.after_first(step - 1)

        branch[...] += nt(hidden[...], weights(1))
        d_normed[...] += nt(d_up[...], weights(0))
        feed.after_core(step)

        @pl.when(step == 0)
        def _():
            attn.after_first(0)

        @pl.when(step >= 1)
        def _():
            feed.after_second(step - 1)
            along.send_outer(step - 1)

        return carry

    lax.fori_loop(0, steps, one_step, 0)

    sums[0] = gains_in[...]
    store_gain(sums.at[0], d_normed[...], x_ref[...], gain[...])

    def sum_copy(stage):
        to = (at.sibling, at.beside, at.above)[stage]
        return at.copy(sums.at[stage], got_sums.at[stage], sum_send.at[stage],
                       sum_recv.at[stage], dp=to)

    def sum_z_copy(k):
        return at.copy(sums.at[3], z_sums.at[at.z], sum_send.at[2 + k], sum_recv.at[2 + k],
                       mp=at.along(k))

    def next_sum(stage):
        sum_copy(stage).wait_recv()
        sums[stage + 1] = sums[stage] + got_sums[stage]

    sum_copy(0).start()
    for item in range(2):
        cols = attn.items[item][1]
        out_attn[:, cols] = attn.total(0, item)
    next_sum(0)
    sum_copy(1).start()
    along.send_inner(0)
    along.send_inner(1)
    next_sum(1)
    sum_copy(2).start()
    feed.after_first(last)
    along.send_inner(2)
    next_sum(2)
    for k in range(1, steps):
        sum_z_copy(k).start()
    z_sums[at.z] = sums[3]
    along_attn.add(0, out_attn)
    for kind, out in enumerate((out_up, out_down)):
        out[...] = feed.total(last, kind)
        along.add(kind, out)
    for k in range(1, steps):
        sum_z_copy(k).wait_recv()
    total = z_sums[0]
    for k in range(1, steps):
        total = total + z_sums[k]
    out_gains[...] = total

    own_back.wait()
    for k, strip in strips:
        back_copy(k, strip).wait_recv()
        back_copy(k, strip).wait_send()
    attn.wait_send(0)
    for step in range(steps):
        feed.wait_send(step)
    for step in range(last):
        along.wait_send(step)
        along_attn.wait_send(step)
    for stage in range(3):
        sum_copy(stage).wait_send()
    for k in range(1, steps):
        sum_z_copy(k).wait_send()


def feed_remote_call(normed, grads, w_ff, g_attn, z_attn, gain, gains, backs):
    rows, width = normed.shape
    steps, _, _, shard, _ = w_ff.shape
    vmem = pl.BlockSpec(memory_space=pltpu.VMEM)
    hbm = pl.BlockSpec(memory_space=pl.ANY)
    return pl.pallas_call(
        feed_remote_kernel,
        in_specs=[vmem, vmem, hbm] + [vmem] * 4 + [hbm] * 4,
        out_specs=[vmem] * 6 + [hbm],
        out_shape=[jax.ShapeDtypeStruct((rows, width), F32)] * 2
        + [jax.ShapeDtypeStruct((shard, width), F32)] * 3
        + [jax.ShapeDtypeStruct((8, 128), F32)]
        + [jax.ShapeDtypeStruct((steps,) + backs[0].shape, BF16)],
        scratch_shapes=[
            pltpu.VMEM((width, rows), BF16),
            pltpu.VMEM((width, rows), BF16),
            pltpu.VMEM((2, 2, 8, shard, width), BF16),
            pltpu.VMEM((rows, width), BF16),
            pltpu.VMEM((rows, width), BF16),
            pltpu.VMEM((steps, 2, 2, 2, 2, shard, width), BF16),
            pltpu.VMEM((steps, 2, 2, 2, shard, width), BF16),
            pltpu.VMEM((steps, 2, 2, shard, width), BF16),
            pltpu.VMEM((steps, 2, shard, width), BF16),
            pltpu.VMEM((1, 1, 2, 2, shard, width), BF16),
            pltpu.VMEM((1, 1, 2, shard, width), BF16),
            pltpu.VMEM((1, 1, shard, width), BF16),
            pltpu.VMEM((2, 5, shard, width), BF16),
            pltpu.VMEM((steps - 1, 1, shard, width), BF16),
            pltpu.VMEM((1, 5, shard, width), BF16),
            pltpu.VMEM((4, 8, 128), F32),
            pltpu.VMEM((3, 8, 128), F32),
            pltpu.VMEM((steps, 8, 128), F32),
            pltpu.SemaphoreType.DMA((2, 2)),
            pltpu.SemaphoreType.DMA((3, 2, steps)),
            pltpu.SemaphoreType.DMA((3, 2, steps)),
            pltpu.SemaphoreType.DMA((3, 2, 1)),
            pltpu.SemaphoreType.DMA((3, 2, 1)),
            pltpu.SemaphoreType.DMA((2, steps - 1)),
            pltpu.SemaphoreType.DMA((2, 5)),
            pltpu.SemaphoreType.DMA((1, steps - 1)),
            pltpu.SemaphoreType.DMA((1, 5)),
            pltpu.SemaphoreType.DMA((6,)),
            pltpu.SemaphoreType.DMA((6,)),
            pltpu.SemaphoreType.DMA((steps - 1, backs[0].shape[0] // STRIP)),
            pltpu.SemaphoreType.DMA((steps - 1, backs[0].shape[0] // STRIP)),
            pltpu.SemaphoreType.DMA,
        ],
        compiler_params=pltpu.CompilerParams(
            collective_id=0, has_side_effects=True, vmem_limit_bytes=VMEM
        ),
        cost_estimate=pl.CostEstimate(
            flops=12 * rows * width * width * steps,
            bytes_accessed=4 * steps * width * width * 2,
            transcendentals=rows * width * steps,
        ),
        name="feed_forward_scatter",
    )(normed, grads, w_ff, g_attn, z_attn, gain, gains, *backs)


def iota(shape, axis):
    return lax.broadcasted_iota(jnp.int32, shape, axis)


def source_of(index, start, total):
    rest = index - BIG
    other = jnp.where(rest < start, rest, rest + MOST)
    held = jnp.where(index < MOST, start + index, -1)
    return jnp.where((rest >= 0) & (rest < total - MOST), other, held)


def store_gain(out, d_normed, normed, gain):
    total = jnp.sum(d_normed * normed.astype(F32), axis=0, keepdims=True) / gain
    for row in range(total.shape[1] // 128):
        out[row:row + 1] += total[:, 128 * row:128 * row + 128]


def prepare(
    me, part, ids, pieces, x_ref, dy_ref, xt, dt, feat_q, feat_k, pt, d_normed, branch, g_gains
):
    mp = ids.shape[1]
    total = mp * part
    numbers = ids[me]
    start = jnp.zeros((1, 1), jnp.int32)
    for image in range(IMAGES):
        count = jnp.sum((numbers == image).astype(F32), axis=(0, 1), keepdims=True)
        ahead = jnp.sum(
            ((numbers >= 0) & (numbers < image)).astype(F32), axis=(0, 1), keepdims=True
        )
        start = start + jnp.where(count == MOST, ahead, 0.0).astype(jnp.int32)
    column = source_of(iota((ROWS, 1), 0), start, total)
    line = source_of(iota((1, ROWS), 1), start, total)
    x_sum, dy_sum, feats = 0.0, 0.0, 0.0
    for k, piece in enumerate(pieces):
        chunk = lax.rem(me - k + mp, mp)
        offset = iota((1, PIECE), 1)
        pos = jnp.where(offset < part, chunk * part + offset, -2)
        pick = (column == pos).astype(F32).astype(BF16)
        offset = iota((PIECE, 1), 0)
        pos = jnp.where(offset < part, chunk * part + offset, -2)
        pt[k] = (line == pos).astype(F32).astype(BF16)
        x_sum = x_sum + nn(pick, piece[0][...])
        dy_sum = dy_sum + nn(pick, piece[1][...])
        marks = (iota((128, 1), 0) - HD == ids[me, pl.ds(chunk, 1), :]).astype(F32)
        feats = feats + nt(pick, marks.astype(BF16))
    x = x_sum.astype(BF16)
    dy = dy_sum.astype(BF16)
    x_ref[...] = x
    dy_ref[...] = dy
    xt[...] = x.T
    dt[...] = dy.T
    lane = iota((1, 128), 1)
    feat_q[...] = (feats * 128.0).astype(BF16)
    marked = (lane >= HD) & (lane < HD + IMAGES)
    feat_k[...] = jnp.where(marked, (feats - 1.0) * 256.0, 0.0).astype(BF16)
    d_normed[...] = jnp.zeros_like(d_normed)
    branch[...] = jnp.zeros_like(branch)
    g_gains[...] = jnp.zeros_like(g_gains)


def attention_chunk(
    weights, gain, x_ref, dy_ref, xt, dt, feat_q, feat_k, raw, d_raw, d_att, att,
    d_normed, branch, g_gains, store, poll,
):
    raw[...] = nn(x_ref[...], weights(slice(0, 640)))
    d_att[...] = nn(dy_ref[...], weights(slice(512, 768)))
    lane = iota((1, 128), 1)
    low = lane < HD
    same = (iota((128, 128), 0) // HD == iota((128, 128), 1) // HD).astype(F32)
    mean_of = (same * (1.0 / HD)).astype(BF16)

    def half_mean(value):
        return nn(value.astype(BF16), mean_of)

    d_gain = jnp.zeros((1, 128), F32)
    for head in range(3):
        qk = raw[:, 128 * head:128 * head + 128]
        high = qk.astype(BF16)
        mean = nn(high, mean_of) + half_mean(qk - high.astype(F32))
        centered = qk - mean
        spread = lax.rsqrt(half_mean(centered * centered) + 1e-6)
        unit = centered * spread
        rounded = (unit * gain).astype(BF16).astype(F32)
        q_aug = jnp.where(low, rounded * 0.125, feat_q[...].astype(F32)).astype(BF16)
        k_aug = jnp.where(low, pltpu.roll(rounded, HD, 1), feat_k[...].astype(F32)).astype(BF16)
        v_tile = 384 + 128 * (head // 2)
        v = raw[:, v_tile:v_tile + 128]
        if head == 1:
            v = pltpu.roll(v, HD, 1)
        one = ((lane == HD) | (lane == HD + 1)).astype(F32)
        v_aug = jnp.where(low, v, one).astype(BF16)
        a_tile = 128 * ((head + 1) // 2)
        da = d_att[:, a_tile:a_tile + 128]
        if head != 1:
            da = pltpu.roll(da, HD, 1)
        q_t = q_aug.astype(F32).T.astype(BF16)
        d_queries, attended, d_keys, d_values = [], [], [], []
        for base, count in ((0, BIG), (BIG, REST)):
            keys = k_aug[base:base + count]
            values = v_aug[base:base + count]
            dk_t = jnp.zeros((128, count), F32)
            dv_t = jnp.zeros((128, count), F32)
            for row in range(base, base + count, 256):
                rows = slice(row, row + 256)
                prob = jnp.exp(nt(q_aug[rows], keys))
                prob_low = prob.astype(BF16)
                gathered = nn(prob_low, values)
                inverse = 1.0 / gathered[:, HD:HD + 1]
                out = jnp.where(low, gathered * inverse, 0.0)
                attended.append(out)
                scaled = jnp.where(low, da[rows] * inverse, 0.0).astype(BF16).astype(F32)
                dot = jnp.sum(scaled * out, axis=-1, keepdims=True)
                dot_high = dot.astype(BF16).astype(F32)
                d_aug = jnp.where(
                    lane == HD, -dot_high, jnp.where(lane == HD + 1, dot_high - dot, scaled)
                )
                d_low = d_aug.astype(BF16)
                d_score = (prob * nt(d_low, values)).astype(BF16)
                d_queries.append(nn(d_score, keys))
                dk_t = dk_t + nn(q_t[:, rows], d_score)
                dv_t = dv_t + nn(d_aug.T.astype(BF16), prob_low)
            d_keys.append(dk_t.T)
            d_values.append(dv_t.T)
        d_query = jnp.concatenate(d_queries, axis=0) * 0.125
        d_key = jnp.concatenate(d_keys, axis=0)
        d_value = jnp.concatenate(d_values, axis=0)
        attend = jnp.concatenate(attended, axis=0)
        d_qk = jnp.where(low, d_query, pltpu.roll(d_key, HD, 1))
        d_gain = d_gain + jnp.sum(d_qk * unit, axis=0, keepdims=True)
        scaled = d_qk * gain
        d_qk = spread * (scaled - half_mean(scaled) - unit * half_mean(scaled * unit))
        d_raw[:, 128 * head:128 * head + 128] = d_qk.astype(BF16)
        if head == 0:
            first_value = d_value
            att[:, 0:128] = jnp.where(low, 0.0, pltpu.roll(attend, HD, 1)).astype(BF16)
        elif head == 1:
            both = jnp.where(low, first_value, pltpu.roll(d_value, HD, 1))
            d_raw[:, 384:512] = both.astype(BF16)
            first_att = attend
        else:
            d_raw[:, 512:640] = jnp.where(low, d_value, 0.0).astype(BF16)
            both = jnp.where(low, first_att, pltpu.roll(attend, HD, 1))
            att[:, 128:256] = both.astype(BF16)
        poll(head)
    g_gains[6:7] += d_gain
    d_projected = d_raw[...]
    attended = att[...]
    d_normed[...] += nt(d_projected, weights(slice(0, 640)))
    branch[...] += nt(attended, weights(slice(512, 768)))
    left = nn(xt[...], d_projected)
    right = nn(dt[...], attended)
    store(slice(0, 512), left[:, :512].astype(BF16))
    store(slice(512, 640), (left[:, 512:] + right[:, :128]).astype(BF16))
    store(slice(640, 768), right[:, 128:].astype(BF16))


def take_back(outs, pt, x_ref, norm_gain, d_normed, branch, g_gains):
    store_gain(g_gains, d_normed[...], x_ref[...], norm_gain[...])
    d_rows = d_normed[...].astype(BF16)
    b_rows = branch[...].astype(BF16)
    for k, out in enumerate(outs):
        out[0] = nn(pt[k], d_rows).astype(BF16)
        out[1] = nn(pt[k], b_rows).astype(BF16)


def attention_kernel(
    part, place, own_x, own_dy, in1, in2, in3, ids, gains, norm_gain, weights,
    out0, out1, out2, out3, g_weights, g_gains,
    x_ref, dy_ref, xt, dt, feat_q, feat_k, pt, raw, d_raw, d_att, att, d_normed, branch,
):
    step = pl.program_id(0)

    @pl.when(step == 0)
    def _():
        pieces = [(own_x.at[0], own_dy.at[0])] + [(got.at[0], got.at[1]) for got in (in1, in2, in3)]
        prepare(place[0], part, ids, pieces, x_ref, dy_ref, xt, dt, feat_q, feat_k, pt,
                d_normed, branch, g_gains)

    def store(cols, value):
        g_weights[0, :, cols] = value

    attention_chunk(
        lambda cols: weights[0, :, cols], gains[...], x_ref, dy_ref, xt, dt, feat_q, feat_k,
        raw, d_raw, d_att, att, d_normed, branch, g_gains, store, lambda head: None,
    )

    @pl.when(step == pl.num_programs(0) - 1)
    def _():
        take_back((out0, out1, out2, out3), pt, x_ref, norm_gain, d_normed, branch, g_gains)


def attention_call(place, part, normed, grads, received, ids, gains, norm_gain, weights):
    width = normed.shape[-1]
    chunks = weights.shape[0]
    mp = ids.shape[1]
    own = pl.BlockSpec((1, PIECE, width), lambda m, place: (0, 0, 0))
    pair = pl.BlockSpec((2, PIECE, width), lambda m, place: (0, 0, 0))
    chunk = pl.BlockSpec((1, width, width), lambda m, place: (m, 0, 0))
    line = pl.BlockSpec((1, 128), lambda m, place: (0, 0))
    return pl.pallas_call(
        functools.partial(attention_kernel, part),
        grid_spec=pltpu.PrefetchScalarGridSpec(
            num_scalar_prefetch=1,
            grid=(chunks,),
            in_specs=[own, own, pair, pair, pair,
                      pl.BlockSpec(ids.shape, lambda m, place: (0, 0, 0)),
                      line, pl.BlockSpec((1, width), lambda m, place: (0, 0)), chunk],
            out_specs=[pair] * 4 + [chunk, pl.BlockSpec((8, 128), lambda m, place: (0, 0))],
            scratch_shapes=[
                pltpu.VMEM((ROWS, width), BF16),
                pltpu.VMEM((ROWS, width), BF16),
                pltpu.VMEM((width, ROWS), BF16),
                pltpu.VMEM((width, ROWS), BF16),
                pltpu.VMEM((ROWS, 128), BF16),
                pltpu.VMEM((ROWS, 128), BF16),
                pltpu.VMEM((mp, PIECE, ROWS), BF16),
                pltpu.VMEM((ROWS, 640), F32),
                pltpu.VMEM((ROWS, 640), BF16),
                pltpu.VMEM((ROWS, 256), F32),
                pltpu.VMEM((ROWS, 256), BF16),
                pltpu.VMEM((ROWS, width), F32),
                pltpu.VMEM((ROWS, width), F32),
            ],
        ),
        out_shape=[jax.ShapeDtypeStruct((2, PIECE, width), BF16)] * 4
        + [jax.ShapeDtypeStruct(weights.shape, BF16), jax.ShapeDtypeStruct((8, 128), F32)],
        compiler_params=pltpu.CompilerParams(vmem_limit_bytes=VMEM),
        cost_estimate=pl.CostEstimate(
            flops=60_000_000_000, bytes_accessed=4 * chunks * width * width,
            transcendentals=ROWS * ROWS * 12,
        ),
        name="attention",
    )(place, normed, grads, *received, ids, gains, norm_gain, weights)


def group_means():
    same = (iota((128, 128), 0) // HD == iota((128, 128), 1) // HD).astype(F32)
    return (same * (1.0 / HD)).astype(BF16)


def forward_chunk(
    weights, gain, x_ref, feat_q, feat_k, raw, qk_all, v_all, stats, att, branch, begin, spill
):
    raw[...] = nn(x_ref[...], weights(slice(0, 640)))
    lane = iota((1, 128), 1)
    low = lane < HD
    mean_of = group_means()

    def ahead(head):
        qk = raw[:, 128 * head:128 * head + 128]
        high = qk.astype(BF16)
        mean = nn(high, mean_of) + nn((qk - high.astype(F32)).astype(BF16), mean_of)
        centered = qk - mean
        spread = lax.rsqrt(nn((centered * centered).astype(BF16), mean_of) + 1e-6)
        rounded = (centered * spread * gain).astype(BF16)
        qk_all[head] = rounded
        rounded = rounded.astype(F32)
        q_aug = jnp.where(low, rounded * 0.125, feat_q[...].astype(F32)).astype(BF16)
        k_aug = jnp.where(low, pltpu.roll(rounded, HD, 1), feat_k[...].astype(F32)).astype(BF16)
        v_tile = 384 + 128 * (head // 2)
        v = raw[:, v_tile:v_tile + 128]
        if head == 1:
            v = pltpu.roll(v, HD, 1)
        v_aug = jnp.where(low, v, 1.0).astype(BF16)
        v_all[head] = v_aug
        return spread, q_aug, k_aug, v_aug

    def products(p_ref, spread, q_aug, k_aug, v_aug):
        parts = []
        for base, count in ((0, BIG), (BIG, REST)):
            keys = k_aug[base:base + count]
            values = v_aug[base:base + count]
            for row in range(base, base + count, 256):
                rows = slice(row, row + 256)
                prob = jnp.exp(nt(q_aug[rows], keys)).astype(BF16)
                p_ref[rows, :count] = prob
                parts.append(nn(prob, values))
        return spread, jnp.concatenate(parts, axis=0)

    def after(head, stat, spread, gathered):
        inverse = 1.0 / gathered
        attend = gathered * pltpu.roll(inverse, HD, 1)
        stat = jnp.where((lane == head) | (lane == HD + head), spread, stat)
        return jnp.where(lane == HD + 8 + head, inverse, stat), attend

    held = ahead(0)
    p_ref = begin(0)
    done0 = products(p_ref, *held)
    held = ahead(1)
    spill(0)
    p_ref = begin(1)
    done1 = products(p_ref, *held)
    held = ahead(2)
    stat, first = after(0, jnp.zeros((ROWS, 128), F32), *done0)
    att[:, 0:128] = jnp.where(low, 0.0, pltpu.roll(first, HD, 1)).astype(BF16)
    spill(1)
    p_ref = begin(2)
    done2 = products(p_ref, *held)
    stat, second = after(1, stat, *done1)
    spill(2)
    stat, third = after(2, stat, *done2)
    att[:, 128:256] = jnp.where(low, second, pltpu.roll(third, HD, 1)).astype(BF16)
    stats[...] = stat
    branch[...] += nt(att[...], weights(slice(512, 768)))


def backward_chunk(
    weights, gain, dy_ref, xt, dt, raw, d_raw, qk_all, v_all, stats, att,
    d_normed, g_gains, ready, store, poll,
):
    raw[:, :256] = nn(dy_ref[...], weights(slice(512, 768)))
    lane = iota((1, 128), 1)
    low = lane < HD
    mean_of = group_means()
    back_gain = 1.0 / gain

    def ahead(head):
        tile = 128 * ((head + 1) // 2)
        da = raw[:, tile:tile + 128]
        out = att[:, tile:tile + 128].astype(F32)
        if head != 1:
            da = pltpu.roll(da, HD, 1)
            out = pltpu.roll(out, HD, 1)
        inverse = stats[:, HD + 8 + head:HD + 9 + head]
        scaled = jnp.where(low, da * inverse, 0.0).astype(BF16).astype(F32)
        dot = jnp.sum(scaled * out, axis=-1, keepdims=True)
        dot_high = dot.astype(BF16).astype(F32)
        d_aug = jnp.where(
            lane == HD, -dot_high, jnp.where(lane == HD + 1, dot_high - dot, scaled)
        )
        qk_t = qk_all[head].astype(F32).T.astype(BF16)
        return d_aug.astype(BF16), d_aug.T.astype(BF16), qk_t

    def products(head, p_ref, d_low, d_t, qk_t):
        qk = qk_all[head]
        v_aug = v_all[head]
        d_queries, d_keys, d_values = [], [], []
        for base, count in ((0, BIG), (BIG, REST)):
            block = slice(base, base + count)
            d_values.append(nn(d_t[:, block], p_ref[block, :count]))
            for row in range(base, base + count, 256):
                rows = slice(row, row + 256)
                d_prob = nt(d_low[rows], v_aug[block])
                d_score = (p_ref[rows, :count].astype(F32) * d_prob).astype(BF16)
                p_ref[rows, :count] = d_score
                d_queries.append(nn(d_score, qk[block]))
            d_keys.append(nn(qk_t[:, block], p_ref[block, :count]))
        return d_queries, d_keys, d_values

    def after(head, d_queries, d_keys, d_values):
        d_query = jnp.concatenate(d_queries, axis=0)
        d_key = jnp.concatenate([part.T for part in d_keys], axis=0)
        d_value = jnp.concatenate([part.T for part in d_values], axis=0)
        d_qk = pltpu.roll(jnp.where(low, d_key, d_query), HD, 1) * 0.125
        unit = qk_all[head].astype(F32) * back_gain
        spread = jnp.where(low, stats[:, head:head + 1], stats[:, HD + head:HD + head + 1])
        g_gains[6:7] += jnp.sum(d_qk * unit, axis=0, keepdims=True)
        scaled = d_qk * gain
        mean = nn(scaled.astype(BF16), mean_of)
        d_qk = spread * (scaled - mean - unit * nn((scaled * unit).astype(BF16), mean_of))
        d_raw[:, 128 * head:128 * head + 128] = d_qk.astype(BF16)
        return d_value

    held = ahead(0)
    p_ref = ready(0)
    done0 = products(0, p_ref, *held)
    held = ahead(1)
    poll(0)
    p_ref = ready(1)
    done1 = products(1, p_ref, *held)
    held = ahead(2)
    first = after(0, *done0)
    poll(1)
    p_ref = ready(2)
    done2 = products(2, p_ref, *held)
    second = after(1, *done1)
    d_raw[:, 384:512] = jnp.where(low, first, pltpu.roll(second, HD, 1)).astype(BF16)
    poll(2)
    third = after(2, *done2)
    d_raw[:, 512:640] = jnp.where(low, third, 0.0).astype(BF16)
    d_projected = d_raw[...]
    d_normed[...] += nt(d_projected, weights(slice(0, 640)))
    left = nn(xt[...], d_projected)
    right = nn(dt[...], att[...])
    store(slice(0, 512), left[:, :512].astype(BF16))
    store(slice(512, 640), (left[:, 512:] + right[:, :128]).astype(BF16))
    store(slice(640, 768), right[:, 128:].astype(BF16))


def front_kernel(
    tok, cot, ids, gains, norm_gain, w_attn, w_feed,
    normed, grads, returned, out0, out1, out2, out3, w_ff, g_last, at_second, g_gains, p_all,
    got_rows, w_full, g_buf, at_core, at_first,
    x_ref, dy_ref, xt, dt, feat_q, feat_k, pt, raw, d_raw, p_buf,
    qk_all, v_all, stats, att, total,
    row_send, row_recv, back_send, back_recv, wa_send, wa_recv, wf_send, wf_recv, own_sem,
    p_out, p_in, at_send, at_recv,
):
    count, part, width = tok.shape
    shard = w_attn.shape[0]
    at = Place(count)
    at.greet()
    gather = Gather(at, w_attn, w_full, wa_send, wa_recv)
    gather_ff = Gather(at, w_feed, w_ff, wf_send, wf_recv)
    scatter = Scatter(at, halves(width), g_buf, at_core, at_first, at_second, at_send, at_recv)
    own_ff = pltpu.make_async_copy(w_feed, gather_ff.piece(at.z), own_sem)

    def row_copy(kind, k):
        src = (normed, grads)[kind].at[k]
        return at.copy(src, got_rows.at[k - 1, kind], row_send.at[kind, k - 1],
                       row_recv.at[kind, k - 1], mp=at.along(k))

    def back_copy(k, strip):
        rows, sem = pl.ds(strip * STRIP, STRIP), (k - 1, strip)
        return at.copy(got_rows.at[k - 1, 0, rows], returned.at[k, rows], back_send.at[sem],
                       back_recv.at[sem], mp=at.along(-k))

    strips = [(k, strip) for strip in range(EARLY // STRIP) for k in (1, 3, 2)]

    gather.start()
    own_ff.start()
    w_full[at.z, at.y, at.x, at.core] = w_attn[...]
    gather.spread(0)
    gain = norm_gain[...]
    for k in (1, 3, 2, 0):
        sequence = at.along(k)
        x = tok[sequence].astype(F32)
        centered = x - jnp.mean(x, axis=-1, keepdims=True)
        spread = lax.rsqrt(jnp.mean(centered * centered, axis=-1, keepdims=True) + 1e-6)
        pad = jnp.zeros((PIECE - part, width), BF16)
        normed[k, :part] = (centered * spread * gain).astype(BF16)
        normed[k, part:] = pad
        grads[k, :part] = cot[sequence]
        grads[k, part:] = pad
        if k == 2:
            gather.spread(-1, 1)
    gather.spread(-2, 2)
    for k in (1, 3, 2):
        row_copy(0, k).start()
    place_rows(at.z, part, ids, pt, feat_q, feat_k)
    g_gains[...] = jnp.zeros_like(g_gains)
    total[...] = jnp.zeros_like(total)
    gather.forward(0)
    gather.spread(-3, 3)
    own_ff.wait()
    gather.forward(-1, 1)
    gather.across(0)
    gather.forward(-2, 2)
    gather.across(-1, 1)
    gather.forward(-3, 3)
    gather.across(-2, 2)
    gather.across(-3, 3)
    gather.last()
    gather_ff.spread(0)
    for k in (1, 3, 2):
        row_copy(0, k).wait_recv()
    for k in (1, 3, 2):
        row_copy(1, k).start()

    def lay_out(kind, own, rows, columns):
        value = 0.0
        for k in range(count):
            piece = own[0] if k == 0 else got_rows[k - 1, kind]
            value = value + lax.dot_general(
                pt[k], piece, (((0,), (0,)), ((), ())), preferred_element_type=F32
            )
        value = value.astype(BF16)
        rows[...] = value
        columns[...] = value.T

    lay_out(0, normed, x_ref, xt)

    def weights_of(chunk):
        def weights(cols):
            return w_full[chunk, :, :, :, :, cols].reshape(width, cols.stop - cols.start)

        return weights

    def p_write(step, head):
        slot = lax.rem(step + head, 2)
        return pltpu.make_async_copy(p_buf.at[slot], p_all.at[at.along(step), head],
                                     p_out.at[slot])

    def p_read(step, head):
        slot = lax.rem(step + head, 2)
        return pltpu.make_async_copy(p_all.at[at.target(step), head], p_buf.at[slot],
                                     p_in.at[slot])

    def forward_step(step, carry):
        chunk = at.along(step)

        @pl.when(step == 2)
        def _():
            gather_ff.forward(0)

        def begin(head):
            if head == 2:
                p_write(step, 0).wait()
            else:
                @pl.when(step >= 1)
                def _():
                    p_write(step - 1, 1 + head).wait()
            return p_buf.at[lax.rem(step + head, 2)]

        forward_chunk(
            weights_of(chunk), gains[...], x_ref, feat_q, feat_k, raw, qk_all.at[chunk],
            v_all.at[chunk], stats.at[chunk], att.at[chunk], total, begin,
            lambda head: p_write(step, head).start(),
        )
        return carry

    lax.fori_loop(0, count, forward_step, 0)
    for head in (1, 2):
        p_write(count - 1, head).wait()
    p_read(0, 0).start()
    value = total[...].astype(BF16)
    for k, out in enumerate((out0, out1, out2, out3)):
        piece = nn(pt[k], value).astype(BF16)
        out[PIECE:] = piece[EARLY:]
        if k == 0:
            returned[0, :EARLY] = piece[:EARLY]
        else:
            got_rows[k - 1, 0, :EARLY] = piece[:EARLY]
    total[...] = jnp.zeros_like(total)
    for k in (1, 3, 2):
        row_copy(1, k).wait_recv()
    gather_ff.start()
    gather_ff.across(0)
    lay_out(1, grads, dy_ref, dt)

    def events(poll):
        if poll == 2:
            gather_ff.spread(-1, 1)
        elif poll == 3:
            scatter.after_core(0)
        elif poll == 4:
            gather_ff.spread(-2, 2)
        elif poll == 5:
            gather_ff.forward(-1, 1)
        elif poll == 6:
            gather_ff.spread(-3, 3)
            scatter.after_core(1)
        elif poll == 7:
            gather_ff.forward(-2, 2)
            scatter.after_first(0)
        elif poll == 8:
            gather_ff.across(-1, 1)
        elif poll == 9:
            gather_ff.forward(-3, 3)
            scatter.after_core(2)
            scatter.after_first(1)
            scatter.after_second(0)
        elif poll == 10:
            gather_ff.across(-2, 2)
        elif poll == 11:
            gather_ff.across(-3, 3)
            scatter.after_second(1)
            scatter.after_first(2)
        for k, strip in strips[poll:poll + 1]:
            back_copy(k, strip).start()

    def backward_step(step, carry):
        chunk = at.target(step)

        def store(cols, value):
            split = (2, 2, 2, shard, cols.stop - cols.start)
            value = value.reshape(split)

            @pl.when(step < count - 1)
            def _():
                g_buf[step, 0, :, :, :, :, cols] = value

            @pl.when(step == count - 1)
            def _():
                g_last[0, 0, :, :, :, :, cols] = value

        def ready(head):
            p_read(step, head).wait()
            if head < 2:
                p_read(step, head + 1).start()
            else:
                @pl.when(step + 1 < count)
                def _():
                    p_read(step + 1, 0).start()
            return p_buf.at[lax.rem(step + head, 2)]

        def poll(head):
            for which in range(count):
                @pl.when(step == which)
                def _():
                    events(3 * which + head)

        backward_chunk(
            weights_of(chunk), gains[...], dy_ref, xt, dt, raw, d_raw,
            qk_all.at[chunk], v_all.at[chunk], stats.at[chunk], att.at[chunk], total, g_gains,
            ready, store, poll,
        )

        @pl.when(step < count - 1)
        def _():
            scatter.start(step)

        return carry

    lax.fori_loop(0, count, backward_step, 0)
    store_gain(g_gains, total[...], x_ref[...], norm_gain[...])
    value = total[...].astype(BF16)
    for k, out in enumerate((out0, out1, out2, out3)):
        out[:PIECE] = nn(pt[k], value).astype(BF16)
    scatter.after_second(2)
    gather_ff.last()
    for k, strip in strips:
        back_copy(k, strip).wait_recv()

    gather.wait_send()
    gather_ff.wait_send()
    for k, strip in strips:
        back_copy(k, strip).wait_send()
    for k in range(1, count):
        for kind in range(2):
            row_copy(kind, k).wait_send()
    for step in range(count - 1):
        scatter.wait_send(step)


def place_rows(me, part, ids, pt, feat_q, feat_k):
    mp = ids.shape[1]
    total = mp * part
    numbers = ids[me]
    start = jnp.zeros((1, 1), jnp.int32)
    for image in range(IMAGES):
        count = jnp.sum((numbers == image).astype(F32), axis=(0, 1), keepdims=True)
        ahead = jnp.sum(
            ((numbers >= 0) & (numbers < image)).astype(F32), axis=(0, 1), keepdims=True
        )
        start = start + jnp.where(count == MOST, ahead, 0.0).astype(jnp.int32)
    line = source_of(iota((1, ROWS), 1), start, total)
    feats = 0.0
    for k in range(mp):
        chunk = lax.rem(me - k + mp, mp)
        offset = iota((PIECE, 1), 0)
        pos = jnp.where(offset < part, chunk * part + offset, -2)
        pick = (line == pos).astype(F32).astype(BF16)
        pt[k] = pick
        marks = (iota((128, 1), 0) - HD == ids[me, pl.ds(chunk, 1), :]).astype(F32)
        feats = feats + nn(marks.astype(BF16), pick)
    feats = feats.T
    lane = iota((1, 128), 1)
    feat_q[...] = (feats * 128.0).astype(BF16)
    marked = (lane >= HD) & (lane < HD + IMAGES)
    feat_k[...] = jnp.where(marked, (feats - 1.0) * 256.0, 0.0).astype(BF16)


def front_call(tokens, cotangent, ids, gains, norm_gain, w_attn, w_feed):
    count, part, width = tokens.shape
    shard = w_attn.shape[0]
    vmem = pl.BlockSpec(memory_space=pltpu.VMEM)
    hbm = pl.BlockSpec(memory_space=pl.ANY)
    rows = jax.ShapeDtypeStruct((count, PIECE, width), BF16)
    return pl.pallas_call(
        front_kernel,
        in_specs=[vmem] * 6 + [hbm],
        out_specs=[vmem] * 7 + [hbm] + [vmem] * 3 + [hbm],
        out_shape=[rows, rows, jax.ShapeDtypeStruct((count, EARLY, width), BF16)]
        + [jax.ShapeDtypeStruct((2 * PIECE - EARLY, width), BF16)] * 4
        + [
            jax.ShapeDtypeStruct((count, 2, 2, 2, 2, shard, width), BF16),
            jax.ShapeDtypeStruct((1, 1, 2, 2, 2, shard, width), BF16),
            jax.ShapeDtypeStruct((count - 1, 1, shard, width), BF16),
            jax.ShapeDtypeStruct((8, 128), F32),
            jax.ShapeDtypeStruct((count, 3, ROWS, BIG), BF16),
        ],
        scratch_shapes=[
            pltpu.VMEM((count - 1, 2, PIECE, width), BF16),
            pltpu.VMEM((count, 2, 2, 2, shard, width), BF16),
            pltpu.VMEM((count - 1, 1, 2, 2, 2, shard, width), BF16),
            pltpu.VMEM((count - 1, 1, 2, 2, shard, width), BF16),
            pltpu.VMEM((count - 1, 1, 2, shard, width), BF16),
            pltpu.VMEM((ROWS, width), BF16),
            pltpu.VMEM((ROWS, width), BF16),
            pltpu.VMEM((width, ROWS), BF16),
            pltpu.VMEM((width, ROWS), BF16),
            pltpu.VMEM((ROWS, 128), BF16),
            pltpu.VMEM((ROWS, 128), BF16),
            pltpu.VMEM((count, PIECE, ROWS), BF16),
            pltpu.VMEM((ROWS, 640), F32),
            pltpu.VMEM((ROWS, 640), BF16),
            pltpu.VMEM((2, ROWS, BIG), BF16),
            pltpu.VMEM((count, 3, ROWS, 128), BF16),
            pltpu.VMEM((count, 3, ROWS, 128), BF16),
            pltpu.VMEM((count, ROWS, 128), F32),
            pltpu.VMEM((count, ROWS, 256), BF16),
            pltpu.VMEM((ROWS, width), F32),
            pltpu.SemaphoreType.DMA((2, count - 1)),
            pltpu.SemaphoreType.DMA((2, count - 1)),
            pltpu.SemaphoreType.DMA((count - 1, EARLY // STRIP)),
            pltpu.SemaphoreType.DMA((count - 1, EARLY // STRIP)),
            pltpu.SemaphoreType.DMA((9, count)),
            pltpu.SemaphoreType.DMA((8, count)),
            pltpu.SemaphoreType.DMA((9, count)),
            pltpu.SemaphoreType.DMA((8, count)),
            pltpu.SemaphoreType.DMA,
            pltpu.SemaphoreType.DMA((2,)),
            pltpu.SemaphoreType.DMA((2,)),
            pltpu.SemaphoreType.DMA((3, 2, count - 1)),
            pltpu.SemaphoreType.DMA((3, 2, count - 1)),
        ],
        compiler_params=pltpu.CompilerParams(
            collective_id=1, has_side_effects=True, vmem_limit_bytes=FRONT_VMEM
        ),
        name="front",
    )(tokens, cotangent, ids, gains, norm_gain, w_attn, w_feed)


def finish_kernel(
    seqs, place, tok, cot, gain, branch, d_ff, back, ret, output, input_grad
):
    part = tok.shape[1]
    x = tok[0].astype(F32)
    added = branch[0] + jnp.concatenate([back[0], ret[0, PIECE:]]).astype(F32)
    output[0] = (x + added[:part]).astype(BF16)
    d_normed = (d_ff[0] + ret[0, :PIECE].astype(F32))[:part]
    centered = x - jnp.mean(x, axis=-1, keepdims=True)
    spread = lax.rsqrt(jnp.mean(centered * centered, axis=-1, keepdims=True) + 1e-6)
    unit = centered * spread
    scaled = d_normed * gain[...]
    d_x = spread * (
        scaled
        - jnp.mean(scaled, axis=-1, keepdims=True)
        - unit * jnp.mean(scaled * unit, axis=-1, keepdims=True)
    )
    total = cot[0].astype(F32) + d_x
    sequence = lax.rem(place[0] + pl.program_id(0), pl.num_programs(0))
    for inner in range(seqs):

        @pl.when(lax.rem(sequence, seqs) == inner)
        def _():
            input_grad[sequence // seqs, :, inner, :] = total


def finish_call(place, seqs, tokens, cotangent, gain, branch, d_ff, back, returned):
    count, part, width = tokens.shape
    block = pl.BlockSpec(
        (1, part, width), lambda k, place: (lax.rem(place[0] + k, count), 0, 0)
    )
    padded = pl.BlockSpec((1, PIECE, width), lambda k, place: (k, 0, 0))
    piece = pl.BlockSpec((1, 2 * PIECE - EARLY, width), lambda k, place: (k, 0, 0))
    ordered = (count // seqs, part, seqs, width)
    early = pl.BlockSpec((1, EARLY, width), lambda k, place: (k, 0, 0))
    line = pl.BlockSpec((1, width), lambda k, place: (0, 0))
    return pl.pallas_call(
        functools.partial(finish_kernel, seqs),
        grid_spec=pltpu.PrefetchScalarGridSpec(
            num_scalar_prefetch=1,
            grid=(count,),
            in_specs=[block, block, line, padded, padded, early, piece],
            out_specs=[block, pl.BlockSpec(ordered, lambda k, place: (0, 0, 0, 0))],
        ),
        out_shape=[
            jax.ShapeDtypeStruct(tokens.shape, BF16),
            jax.ShapeDtypeStruct(ordered, F32),
        ],
        compiler_params=pltpu.CompilerParams(vmem_limit_bytes=VMEM),
        name="finish",
    )(place, tokens, cotangent, gain, branch, d_ff, back, returned)


def pack_attention(w_qkv, w_proj):
    rows, wide = w_qkv.shape[1:]
    heads = wide // HD
    qk = w_qkv[:2].reshape(2, rows, heads, HD).transpose(1, 2, 0, 3).reshape(rows, 2 * wide)
    return jnp.concatenate([qk, w_qkv[2], w_proj.T], axis=1)


def unpack_attention(grad, wide):
    rows = grad.shape[0]
    heads = wide // HD
    qk = grad[:, :2 * wide].reshape(rows, heads, 2, HD).transpose(2, 0, 1, 3)
    qk = qk.reshape(2, rows, wide)
    g_qkv = jnp.concatenate([qk, grad[None, :, 2 * wide:3 * wide]], axis=0)
    return g_qkv, grad[:, 3 * wide:].T


def body(
    dp, mp, tokens, w_qkv, w_up, w_proj, w_down, norm_gain, query_gain, key_gain, image_ids, cotangent
):
    micro, seqs, part, width = tokens.shape
    count = micro * seqs
    shard = w_up.shape[0]
    me = lax.axis_index("mp")
    place = me.astype(jnp.int32)[None]
    both = ("mp", "dp")
    tok = tokens.reshape(count, part, width)
    cot = cotangent.reshape(count, part, width)
    gain = norm_gain.reshape(1, width)
    ids = image_ids.reshape(count, mp, part)
    ids = jnp.pad(ids, ((0, 0), (0, 0), (0, PIECE - part)), constant_values=-1)
    gains = jnp.concatenate([query_gain, key_gain]).reshape(1, 2 * HD)
    w_attn = pack_attention(w_qkv, w_proj)
    w_ff = jnp.stack([w_up, w_down.T])

    def send_back(outs):
        return [outs[0]] + [
            lax.ppermute(out, "mp", [(i, (i - k) % mp) for i in range(mp)])
            for k, out in enumerate(outs[1:], 1)
        ]

    if (dp, mp) == (8, 4):
        normed, grads, back, *outs, w_ff, g_attn, z_attn, g_gains, _ = front_call(
            tok, cot, ids, gains, gain, w_attn, w_ff
        )
        branch, d_ff, g_attn, g_up, g_down, g_gains, returned = feed_remote_call(
            normed.reshape(count * PIECE, width), grads.reshape(count * PIECE, width),
            w_ff.reshape(mp, dp, 2, shard, width), g_attn, z_attn, gain, g_gains, outs,
        )
    else:
        w_attn = lax.all_gather(w_attn, both).reshape(mp, width, width)
        w_ff = lax.all_gather(w_ff, both).reshape(mp, dp, 2, shard, width)
        normed, grads, *sends = norm_call(place, tok, cot, gain)
        received = [
            lax.ppermute(send, "mp", [(i, (i + k) % mp) for i in range(mp)])
            for k, send in enumerate(sends, 1)
        ]
        *outs, g_attn, g_gains = attention_call(
            place, part, normed, grads, received, ids, gains, gain, w_attn
        )
        outs = send_back(outs)
        back = jnp.stack([out[1, :EARLY] for out in outs])
        returned = jnp.stack([jnp.concatenate([out[0], out[1, EARLY:]]) for out in outs])
        flat_normed = normed.reshape(count * PIECE, width)
        branch, d_ff, g_up, g_down = feed_call(
            flat_normed, grads.reshape(count * PIECE, width),
            w_ff[:, :, 0].reshape(mp, width, width), w_ff[:, :, 1].reshape(mp, width, width),
        )
        g_attn, g_up, g_down = (
            lax.psum_scatter(
                grad.reshape(-1, shard, width), both, scatter_dimension=0
            ).astype(F32)
            for grad in (g_attn, g_up, g_down)
        )
        own = jnp.sum(d_ff * flat_normed.astype(F32), axis=0) / norm_gain
        g_gains = g_gains.at[:width // 128].add(own.reshape(-1, 128))
        g_gains = lax.psum(g_gains, both)
    output, input_grad = finish_call(
        place, seqs, tok, cot, gain,
        branch.reshape(count, PIECE, width), d_ff.reshape(count, PIECE, width), back, returned,
    )
    input_grad = input_grad.transpose(0, 2, 1, 3)
    g_qkv, g_proj = unpack_attention(g_attn, w_qkv.shape[2])
    g_norm = g_gains[:width // 128].reshape(width)
    g_gains = g_gains[6]
    return (
        output.reshape(tokens.shape),
        input_grad,
        g_qkv,
        g_up,
        g_proj,
        g_down.T,
        g_norm,
        g_gains[:HD],
        g_gains[HD:],
    )


def solution(mesh):
    rows = P(None, "dp", "mp", None)
    weights = (P(None, "dp", "mp"), P("dp", "mp"), P("mp", "dp"), P("mp", "dp"))
    gains = (P(), P(), P())
    return jax.shard_map(
        functools.partial(body, mesh.shape["dp"], mesh.shape["mp"]),
        mesh=mesh,
        in_specs=(rows,) + weights + gains + (P(None, "dp", None), rows),
        out_specs=(rows, rows) + weights + gains,
        check_vma=False,
    )
```
